32 devices in a mesh: section: 2 (over x), gx: 4 (over y, core), gy: 4 (over z).
Axes of the slice: x: 2, y: 2, z: 4, core: 2. Of those that a mesh axis runs over, the one named last changes fastest.
Arguments:
- hidden_in: bfloat16 [4096, 2048], P('gx', 'gy'), may hold values from -6 to 6
- out_grad: bfloat16 [4096, 2048], P('gx', 'gy'), may hold values from -6 to 6
- lengths: int32 [4], replicated, may hold values from 512 to 1024, as said below
- dealing: int32 [4], replicated, may hold values from 0 to 3, each once
- attn_gain: bfloat16 [2, 2048], P('section', 'gx'), may hold values from 0.25 to 1.75
- w_query: bfloat16 [2, 2048, 2048], P('section', 'gx', 'gy'), may hold values from -0.125 to 0.125
- w_key: bfloat16 [2, 2048, 256], P('section', 'gx'), may hold values from -0.125 to 0.125
- w_value: bfloat16 [2, 2048, 256], P('section', 'gx'), may hold values from -0.125 to 0.125
- w_out: bfloat16 [2, 2048, 2048], P('section', 'gy', 'gx'), may hold values from -2 to 2
- mlp_gain: bfloat16 [2, 2048], P('section', 'gx'), may hold values from 0.25 to 1.75
- w_gate: bfloat16 [2, 2048, 5632], P('section', 'gx', 'gy'), may hold values from -0.125 to 0.125
- w_up: bfloat16 [2, 2048, 5632], P('section', 'gx', 'gy'), may hold values from -0.125 to 0.125
- w_down: bfloat16 [2, 5632, 2048], P('section', 'gy', 'gx'), may hold values from -0.078125 to 0.078125
Outputs:
- layer_outputs: bfloat16 [2, 4096, 2048], P('section', 'gx', 'gy')
- norm_rms: float32 [2, 2, 4096], P('section', None, 'gx')
- input_grads: bfloat16 [2, 4096, 2048], P('section', 'gx', 'gy')
- attn_gain_grad: float32 [2, 2048], P('section', 'gx')
- query_grad: float32 [2, 2048, 2048], P('section', 'gx', 'gy')
- key_grad: float32 [2, 2048, 256], P('section', 'gx')
- value_grad: float32 [2, 2048, 256], P('section', 'gx')
- out_proj_grad: float32 [2, 2048, 2048], P('section', 'gy', 'gx')
- mlp_gain_grad: float32 [2, 2048], P('section', 'gx')
- gate_grad: float32 [2, 2048, 5632], P('section', 'gx', 'gy')
- up_grad: float32 [2, 2048, 5632], P('section', 'gx', 'gy')
- down_grad: float32 [2, 5632, 2048], P('section', 'gy', 'gx')
The draws below stay inside these ranges and needn't reach their ends.
Inputs may be any that keep to these rules, and one draw needn't show every extreme that they name: `lengths`: one sequence has exactly 1024 tokens and one exactly 512. `dealing`: a permutation of the token shards.
All inputs are finite; a program needn't handle non-finite values.
Results may differ from the reference program's by a relative error of at most 0.04.
Values may be sent and summed in bfloat16 or wider, within the bound.
A program may use at most 320 MiB of HBM per device.

```python
import jax
import jax.numpy as jnp
from jax import lax

D = 2048
QH = 32
KVH = 4
HD = 64
FF = 5632
MBTOK = 256
LAYERS = 2
CAP = 1024
SHORTEST = 512
NSEQ = 4
TOKENS = 4096


def draw_lengths(key, part):
    key = jax.random.fold_in(key, 11)
    first_key, second_key = jax.random.split(key)
    picked = jax.random.randint(first_key, (NSEQ,), SHORTEST, CAP + 1)
    picked = picked.at[0].set(CAP).at[1].set(SHORTEST)
    return jax.random.permutation(second_key, picked).astype(jnp.int32)


def steps_of(own_key, extent, cuts, smallest, largest):
    factor_of = 1.0
    for position, blocks in cuts:
        heights = jax.random.uniform(jax.random.fold_in(jax.random.fold_in(own_key, 6), position), (blocks,), jnp.float32, smallest / len(cuts), largest / len(cuts))
        factor_of = factor_of * jnp.repeat(jnp.exp(heights), extent[position] // blocks).reshape((-1,) + (1,) * (len(extent) - 1 - position))
    return factor_of


def normal_values(rng, shape, width, most, cuts=(), held_as=jnp.bfloat16):
    drawn = width * jax.random.normal(rng, shape, jnp.float32)
    if cuts:
        drawn = drawn * steps_of(rng, shape, cuts, -0.22, 0.18)
    return jnp.clip(drawn, -most, most).astype(held_as)


def setup_inputs(seed: int = 0) -> dict:
    streams_of = jax.random.split(jax.random.key(seed), 14)
    return {
        "hidden_in": normal_values(streams_of[0], (TOKENS, D), 1.0, 6.0, ((0, 4), (1, 4))),
        "out_grad": normal_values(streams_of[1], (TOKENS, D), 1.0, 6.0, ((0, 4), (1, 4))),
        "lengths": draw_lengths(jax.random.fold_in(streams_of[13], 71), 0),
        "dealing": jax.random.permutation(streams_of[3], NSEQ).astype(jnp.int32),
        "attn_gain": jnp.clip(1.0 + 0.15 * jax.random.normal(streams_of[4], (LAYERS, D), jnp.float32), 0.25, 1.75).astype(jnp.bfloat16),
        "w_query": normal_values(streams_of[5], (LAYERS, D, QH * HD), D ** -0.5, 0.125, ((0, 2), (1, 4), (2, 4))),
        "w_key": normal_values(streams_of[6], (LAYERS, D, KVH * HD), D ** -0.5, 0.125, ((0, 2), (1, 4))),
        "w_value": normal_values(streams_of[7], (LAYERS, D, KVH * HD), D ** -0.5, 0.125, ((0, 2), (1, 4))),
        "w_out": normal_values(streams_of[8], (LAYERS, QH * HD, D), (D // 256 + 1) ** -0.5, 2.0, ((0, 2), (1, 4), (2, 4))),
        "mlp_gain": jnp.clip(1.0 + 0.15 * jax.random.normal(streams_of[9], (LAYERS, D), jnp.float32), 0.25, 1.75).astype(jnp.bfloat16),
        "w_gate": normal_values(streams_of[10], (LAYERS, D, FF), D ** -0.5, 0.125, ((0, 2), (1, 4), (2, 4))),
        "w_up": normal_values(streams_of[11], (LAYERS, D, FF), D ** -0.5, 0.125, ((0, 2), (1, 4), (2, 4))),
        "w_down": normal_values(streams_of[12], (LAYERS, FF, D), FF ** -0.5, 0.078125, ((0, 2), (1, 4), (2, 4))),
    }


EPS = 1e-05

@jax.custom_vjp
def low(v):
    return lax.optimization_barrier(v.astype(jnp.bfloat16)).astype(jnp.float32)

@jax.custom_vjp
def low_back(v):
    return v

def low_keep(v):
    return (low(v), None)

def low_pass(kept, grad):
    return (grad,)

def back_keep(v):
    return (v, None)

def back_low(kept, grad):
    return (low(grad),)
low.defvjp(low_keep, low_pass)
low_back.defvjp(back_keep, back_low)

def dot_hi(left, right):
    return jnp.dot(left, right, precision=lax.Precision.HIGHEST)

def rotate(values):
    half_width = HD // 2
    places = jnp.arange(values.shape[0]).astype(jnp.float32)
    frequency = jnp.power(10000.0, -2.0 * jnp.arange(half_width).astype(jnp.float32) / HD)
    angles = places[:, None] * frequency[None, :]
    cosine = jnp.cos(angles)[:, None, :]
    sines = jnp.sin(angles)[:, None, :]
    first_half = values[..., :half_width]
    second_half = values[..., half_width:]
    return jnp.concatenate([first_half * cosine - second_half * sines, second_half * cosine + first_half * sines], axis=-1)

def attention(q_rot, k_rot, value_heads, seq_length):
    group_size = QH // KVH
    block_rows = min(512, MBTOK)
    block_count = CAP // block_rows
    scaling = HD ** (-0.5)
    queries = q_rot.reshape(block_count, block_rows, KVH, group_size, HD)
    first_rows = jnp.arange(block_count) * block_rows
    keys_at = jnp.arange(CAP)

    def one_block(pieces):
        query_block, first_row = pieces
        raw_scores = jnp.einsum('ikgd,jkd->kgij', query_block, k_rot, precision=lax.Precision.HIGHEST) * scaling
        scores = low_back(raw_scores)
        places = first_row + jnp.arange(block_rows)
        allowed = (keys_at[None, :] <= places[:, None]) & (keys_at[None, :] < seq_length)
        scores = jnp.where(allowed[None, None], scores, -1e+30)
        row_top = lax.optimization_barrier(jnp.max(scores, axis=-1, keepdims=True))
        exponent = jnp.exp(scores - row_top)
        probs = exponent / lax.optimization_barrier(jnp.sum(exponent, axis=-1, keepdims=True))
        heads_out = jnp.einsum('kgij,jkd->ikgd', low(probs), value_heads, precision=lax.Precision.HIGHEST)
        return heads_out.reshape(block_rows, QH * HD)
    return lax.map(jax.checkpoint(one_block), (queries, first_rows)).reshape(CAP, QH * HD)

def layer_fwd(stream_in, seq_length, weights, layer_idx):
    gain_attn, q_weight, k_weight, v_weight, o_weight, gain_mlp, gate_weight, up_weight, down_weight = [w[layer_idx] for w in weights]
    stream = low_back(stream_in)
    valid_rows = (jnp.arange(CAP) < seq_length).astype(jnp.float32)[:, None]
    square_attn = lax.optimization_barrier(jnp.mean(stream * stream, axis=1, keepdims=True))
    normed_attn = low(stream * lax.rsqrt(square_attn + EPS) * gain_attn)
    query = low_back(dot_hi(normed_attn, q_weight))
    key_pre = dot_hi(normed_attn, k_weight)
    value = low(dot_hi(normed_attn, v_weight))
    q_rot = low(rotate(query.reshape(CAP, QH, HD)))
    k_rot = low(rotate(key_pre.reshape(CAP, KVH, HD)))
    heads = low_back(low(attention(q_rot, k_rot, value.reshape(CAP, KVH, HD), seq_length)))
    middle = low(stream + low_back(dot_hi(heads, o_weight)))
    square_mlp = lax.optimization_barrier(jnp.mean(middle * middle, axis=1, keepdims=True))
    normed_mlp = low(middle * lax.rsqrt(square_mlp + EPS) * gain_mlp)
    gate_pre = low_back(dot_hi(normed_mlp, gate_weight))
    up_pre = low_back(dot_hi(normed_mlp, up_weight))
    hidden = low(jax.nn.silu(gate_pre) * up_pre)
    mlp_out = low_back(dot_hi(hidden, down_weight))
    result = low(valid_rows * (middle + mlp_out))
    statistics = jnp.concatenate([jnp.sqrt(square_attn + EPS), jnp.sqrt(square_mlp + EPS)], axis=1).T * valid_rows[:, 0][None, :]
    return (result, statistics)

def reference(hidden_in, out_grad, lengths, dealing, attn_gain, w_query, w_key, w_value, w_out, mlp_gain, w_gate, w_up, w_down):
    params = tuple((array_in.astype(jnp.float32) for array_in in (attn_gain, w_query, w_key, w_value, w_out, mlp_gain, w_gate, w_up, w_down)))
    start_x = hidden_in.astype(jnp.float32).reshape(NSEQ, CAP, D)
    probes = jnp.zeros((LAYERS, NSEQ, CAP, D), jnp.float32)

    def forward(weights, extra):

        def one_seq(carried, pieces):
            sequence, seq_length, probe_in = pieces
            stream = sequence
            outputs = []
            statistics = []
            for layer_idx in range(LAYERS):
                stream, stat_rows = layer_fwd(stream + probe_in[layer_idx], seq_length, weights, layer_idx)
                outputs.append(stream)
                statistics.append(stat_rows)
            return (carried, (jnp.stack(outputs), jnp.stack(statistics)))
        _, result = lax.scan(jax.checkpoint(one_seq), jnp.zeros((), jnp.float32), (start_x, lengths, jnp.transpose(extra, (1, 0, 2, 3))))
        return result
    (outputs, statistics), pullback = jax.vjp(forward, params, probes)
    cot_seed = jnp.zeros_like(outputs).at[:, LAYERS - 1].set(out_grad.astype(jnp.float32).reshape(NSEQ, CAP, D))
    gradients, probe_grads = pullback((cot_seed, jnp.zeros_like(statistics)))
    dealt_out = jnp.zeros_like(outputs).at[dealing].set(outputs)
    dealt_stats = jnp.zeros_like(statistics).at[dealing].set(statistics)
    layer_outputs = jnp.transpose(dealt_out, (1, 0, 2, 3)).reshape(LAYERS, NSEQ * CAP, D).astype(jnp.bfloat16)
    norm_rms = jnp.transpose(dealt_stats, (1, 2, 0, 3)).reshape(LAYERS, 2, NSEQ * CAP)
    input_grads = probe_grads.reshape(LAYERS, NSEQ * CAP, D).astype(jnp.bfloat16)
    return (layer_outputs, norm_rms, input_grads, gradients[0], gradients[1], gradients[2], gradients[3], gradients[4], gradients[5], gradients[6], gradients[7], gradients[8])
```

```python
import jax
import jax.numpy as jnp
from jax import lax
from jax.sharding import PartitionSpec as P

QH = 32
KVH = 4
HD = 64
LAYERS = 2
EPS = 1e-05
BF = jnp.bfloat16
F32 = jnp.float32


def mm(left, right, dims=((1,), (0,))):
    return lax.dot_general(left, right, (dims, ((), ())), preferred_element_type=F32)


def swap_pairs(values, axis):
    count = lax.axis_size(axis)
    return lax.ppermute(values, axis, [(i, i ^ 1) for i in range(count)])


def rope_tables(places):
    half_width = HD // 2
    frequency = jnp.power(10000.0, -2.0 * jnp.arange(half_width).astype(F32) / HD)
    angles = places.astype(F32)[:, None] * frequency[None, :]
    return jnp.cos(angles)[:, None, :], jnp.sin(angles)[:, None, :]


def rotate(values, cosine, sines):
    half_width = HD // 2
    first, second = values[..., :half_width], values[..., half_width:]
    return jnp.concatenate(
        [first * cosine - second * sines, second * cosine + first * sines], axis=-1
    )


def core_rows(rows, core):
    quarter = rows.shape[0] // 4
    low = lax.dynamic_slice_in_dim(rows, core * quarter, quarter, 0)
    high = lax.dynamic_slice_in_dim(rows, (3 - core) * quarter, quarter, 0)
    return jnp.concatenate([low, high], axis=0)


def join_halves(first, second):
    quarter = first.shape[0] // 2
    return jnp.concatenate(
        [first[:quarter], second[:quarter], second[quarter:], first[quarter:]], axis=0
    )


def sum_columns(partial):
    scattered = lax.psum_scatter(partial.astype(BF), "gy", scatter_dimension=1, tiled=True)
    return lax.all_gather(scattered, "gy", axis=1, tiled=True).astype(F32)


def sum_shards(partial, dimension):
    return lax.psum_scatter(partial.astype(BF), "gx", scatter_dimension=dimension, tiled=True)


def normed(h, gain):
    values = h.astype(F32)
    square = jnp.mean(values * values, axis=1, keepdims=True)
    ratio = lax.rsqrt(square + EPS)
    return ratio, (values * ratio * gain).astype(BF), jnp.sqrt(square + EPS)[:, 0]


def norm_back(d_normed, h, ratio, gain):
    values = h.astype(F32)
    scaled = d_normed * gain
    mean_term = jnp.mean(scaled * values, axis=1, keepdims=True)
    grad = ratio * scaled - values * (ratio * ratio * ratio) * mean_term
    return grad, jnp.sum(d_normed * values * ratio, axis=0)


def probabilities(q_rot, k_all, allowed):
    scores = jnp.einsum("ihd,jd->hij", q_rot, k_all, preferred_element_type=F32) * HD ** (-0.5)
    scores = jnp.where(allowed[None], scores, -1e30)
    exponent = jnp.exp(scores - jnp.max(scores, axis=-1, keepdims=True))
    return exponent / jnp.sum(exponent, axis=-1, keepdims=True)


def forward_layer(h, weights, cosine, sines, allowed, valid):
    gain_attn, w_qkv, w_o, gain_mlp, w_gate, w_up, w_down = weights
    rows = h.shape[0]
    r1, n1, rms1 = normed(h, gain_attn)
    qkv = mm(n1, w_qkv)
    q_width = qkv.shape[1] - 2 * HD
    q_rot = rotate(qkv[:, :q_width].reshape(rows, -1, HD), cosine, sines).astype(BF)
    k_rot = rotate(qkv[:, None, q_width : q_width + HD], cosine, sines)[:, 0].astype(BF)
    kv = jnp.concatenate([k_rot, qkv[:, q_width + HD :].astype(BF)], axis=1)
    kv_all = jnp.concatenate([kv, swap_pairs(kv, "gx")], axis=0)
    k_all, v_all = kv_all[:, :HD], kv_all[:, HD:]
    probs = probabilities(q_rot, k_all, allowed).astype(BF)
    heads = jnp.einsum("hij,jd->ihd", probs, v_all, preferred_element_type=F32)
    heads = heads.reshape(rows, -1).astype(BF)
    h1 = (h.astype(F32) + sum_columns(mm(heads, w_o))).astype(BF)
    r2, n2, rms2 = normed(h1, gain_mlp)
    gate, up = mm(n2, w_gate), mm(n2, w_up)
    hidden = (gate * jax.nn.sigmoid(gate) * up).astype(BF)
    mlp = sum_columns(mm(hidden, w_down))
    result = jnp.where(valid, h1.astype(F32) + mlp, 0.0).astype(BF)
    statistics = jnp.where(valid[:, 0][None], jnp.stack([rms1, rms2]), 0.0)
    return result, statistics, (h, r1, n1, q_rot, k_all, v_all, heads, h1, r2, n2, gate, up, hidden)


def backward_layer(e2, weights, cosine, sines, allowed, saved):
    gain_attn, w_qkv, w_o, gain_mlp, w_gate, w_up, w_down = weights
    h, r1, n1, q_rot, k_all, v_all, heads, h1, r2, n2, gate, up, hidden = saved
    rows = h.shape[0]
    turn, down = ((0,), (0,)), ((1,), (1,))
    dm = e2.astype(BF)
    g_down = mm(hidden, dm, turn)
    d_hidden = mm(dm, w_down, down)
    sigmoid = jax.nn.sigmoid(gate)
    d_gate = (d_hidden * up * sigmoid * (1.0 + gate * (1.0 - sigmoid))).astype(BF)
    d_up = (d_hidden * (gate * sigmoid)).astype(BF)
    dn2 = sum_columns(mm(d_gate, w_gate, down) + mm(d_up, w_up, down))
    g_gate, g_up = mm(n2, d_gate, turn), mm(n2, d_up, turn)
    part, g_gain_mlp = norm_back(dn2, h1, r2, gain_mlp)
    e1 = e2 + part
    da = e1.astype(BF)
    g_o = mm(heads, da, turn)
    d_heads = mm(da, w_o, down).astype(BF).reshape(q_rot.shape)
    probs = probabilities(q_rot, k_all, allowed)
    d_probs = jnp.einsum("ihd,jd->hij", d_heads, v_all, preferred_element_type=F32)
    delta = jnp.sum(d_probs * probs, axis=-1, keepdims=True)
    d_scores = (probs * (d_probs - delta)).astype(BF)
    scaling = HD ** (-0.5)
    dq = jnp.einsum("hij,jd->ihd", d_scores, k_all, preferred_element_type=F32) * scaling
    dk = jnp.einsum("hij,ihd->jd", d_scores, q_rot, preferred_element_type=F32) * scaling
    dv = jnp.einsum("hij,ihd->jd", probs.astype(BF), d_heads, preferred_element_type=F32)
    dkv = jnp.concatenate([dk, dv], axis=1)
    dkv = dkv[:rows] + swap_pairs(dkv[rows:], "gx")
    dq = rotate(dq, cosine, -sines).reshape(rows, -1)
    dk = rotate(dkv[:, None, :HD], cosine, -sines)[:, 0]
    d_qkv = jnp.concatenate([dq, dk, dkv[:, HD:]], axis=1).astype(BF)
    dn1 = sum_columns(mm(d_qkv, w_qkv, down))
    g_qkv = mm(n1, d_qkv, turn)
    part, g_gain_attn = norm_back(dn1, h, r1, gain_attn)
    d_input = (e1 + part).astype(BF)
    grads = (
        sum_shards(g_qkv, 0),
        sum_shards(g_o, 1),
        sum_shards(g_gate, 0),
        sum_shards(g_up, 0),
        sum_shards(g_down, 1),
    )
    return d_input, jnp.stack([g_gain_attn, g_gain_mlp]), grads


def on_device(
    hidden_in, out_grad, lengths, dealing, attn_gain, w_query, w_key, w_value, w_out,
    mlp_gain, w_gate, w_up, w_down,
):
    shards = lax.axis_size("gx")
    shard = lax.axis_index("gx")
    section = lax.axis_index("section")
    column = lax.axis_index("gy")
    core = shard % 2
    sequence = (shard // 2) * 2 + section
    span, width = hidden_in.shape
    half = span // 2
    seq_length = lax.dynamic_index_in_dim(lengths, sequence, keepdims=False)

    both = jnp.concatenate([hidden_in, out_grad], axis=1)
    mine = core_rows(both, core)
    theirs = swap_pairs(core_rows(both, 1 - core), "gx")
    mine = jnp.where(core == section, mine, theirs)
    wide = lax.all_gather(mine.reshape(half, 2, width), "gy", axis=2, tiled=True)
    h, d_out = wide[:, 0], wide[:, 1]

    kv_head = column * (w_query.shape[2] // HD) // (QH // KVH)
    w_qkv = jnp.concatenate(
        [
            w_query[0],
            lax.dynamic_slice_in_dim(w_key[0], kv_head * HD, HD, 1),
            lax.dynamic_slice_in_dim(w_value[0], kv_head * HD, HD, 1),
        ],
        axis=1,
    )
    own = (attn_gain[0], w_qkv, w_out[0], mlp_gain[0], w_gate[0], w_up[0], w_down[0])
    layers = ([], [])
    for array, dimension in zip(own, (0, 0, 1, 0, 0, 0, 1)):
        other = swap_pairs(array, "section")
        for layer in range(LAYERS):
            block = jnp.where(section == layer, array, other)
            layers[layer].append(lax.all_gather(block, "gx", axis=dimension, tiled=True))
    for weights in layers:
        weights[0], weights[3] = weights[0].astype(F32), weights[3].astype(F32)

    here = core_rows(jnp.arange(span), core)
    there = core_rows(jnp.arange(span), 1 - core)
    keys_at = jnp.concatenate([here, there])
    allowed = (keys_at[None, :] <= here[:, None]) & (keys_at[None, :] < seq_length)
    valid = (here < seq_length)[:, None]
    cosine, sines = rope_tables(here)

    outputs, statistics, saved = [], [], []
    for layer in range(LAYERS):
        h, stat, kept = forward_layer(h, layers[layer], cosine, sines, allowed, valid)
        outputs.append(lax.dynamic_slice_in_dim(h, column * width, width, 1))
        statistics.append(stat)
        saved.append(kept)

    def to_section(per_layer):
        kept = jnp.where(section == 0, per_layer[0], per_layer[1])
        sent = swap_pairs(jnp.where(section == 0, per_layer[1], per_layer[0]), "section")
        return kept, sent

    kept, sent = to_section(outputs)
    by_section = jnp.stack([jnp.where(section == 0, kept, sent), jnp.where(section == 0, sent, kept)])
    everything = lax.all_gather(by_section, "gx", axis=0)
    stat_kept, stat_sent = to_section(statistics)
    stat_both = jnp.stack(
        [jnp.where(section == 0, stat_kept, stat_sent), jnp.where(section == 0, stat_sent, stat_kept)]
    )
    every_stat = lax.all_gather(stat_both, "gx", axis=0)
    owner = jnp.sum(jnp.where(dealing == shard, jnp.arange(shards), 0))
    halves = lax.dynamic_slice(
        everything, ((owner // 2) * 2, owner % 2, 0, 0), (2, 1, half, width)
    )
    layer_out = join_halves(halves[0, 0], halves[1, 0])
    stat_halves = lax.dynamic_slice(every_stat, ((owner // 2) * 2, owner % 2, 0, 0), (2, 1, 2, half))
    stats_out = join_halves(stat_halves[0, 0].T, stat_halves[1, 0].T).T

    gain_sums, received, local, input_grads = [None] * 2, [None] * 2, [None] * 2, [None] * 2
    e2 = d_out
    for layer in (1, 0):
        e2 = jnp.where(valid, e2.astype(F32), 0.0)
        e2, gain_sums[layer], grads = backward_layer(
            e2, layers[layer], cosine, sines, allowed, saved[layer]
        )
        input_grads[layer] = lax.dynamic_slice_in_dim(e2, column * width, width, 1)
        local[layer] = grads
        received[layer] = [lax.ppermute(g, "section", [(1 - layer, layer)]) for g in grads]
    totals = [
        jnp.where(section == 0, a0.astype(F32) + r0.astype(F32), a1.astype(F32) + r1.astype(F32))
        for a0, r0, a1, r1 in zip(local[0], received[0], local[1], received[1])
    ]
    s_qkv, s_o, s_gate, s_up, s_down = totals
    q_width = w_query.shape[2]
    kv_width = w_key.shape[2]

    def spread(part):
        blank = jnp.zeros((part.shape[0], kv_width), F32)
        return lax.dynamic_update_slice_in_dim(blank, part, kv_head * HD, 1)

    kv_sum = lax.psum(
        jnp.stack([spread(s_qkv[:, q_width : q_width + HD]), spread(s_qkv[:, q_width + HD :])]).astype(BF),
        "gy",
    ).astype(F32)
    gains = lax.psum(jnp.stack(gain_sums), ("section", "gx"))
    gains = lax.dynamic_index_in_dim(gains, section, 0, keepdims=False)
    part = attn_gain.shape[1]
    gains = lax.dynamic_slice_in_dim(gains, shard * part, part, 1)

    kept, sent = to_section(input_grads)
    keep = jnp.where(core == section, kept, sent)
    give = swap_pairs(jnp.where(core == section, sent, kept), "gx")
    back_home = join_halves(jnp.where(core == 0, keep, give), jnp.where(core == 0, give, keep))
    return (
        layer_out[None],
        stats_out[None],
        back_home[None],
        gains[None, 0],
        s_qkv[None, :, :q_width],
        kv_sum[None, 0],
        kv_sum[None, 1],
        s_o[None],
        gains[None, 1],
        s_gate[None],
        s_up[None],
        s_down[None],
    )


def solution(mesh):
    rows_cols = P("section", "gx", "gy")
    cols_rows = P("section", "gy", "gx")
    rows_only = P("section", "gx", None)
    gain = P("section", "gx")
    return jax.shard_map(
        on_device,
        mesh=mesh,
        in_specs=(
            P("gx", "gy"), P("gx", "gy"), P(), P(), gain, rows_cols, rows_only, rows_only,
            cols_rows, gain, rows_cols, rows_cols, cols_rows,
        ),
        out_specs=(
            rows_cols, P("section", None, "gx"), rows_cols, gain, rows_cols, rows_only, rows_only,
            cols_rows, gain, rows_cols, rows_cols, cols_rows,
        ),
        check_vma=False,
    )
```

```python
import functools

import jax
import jax.numpy as jnp
from jax import lax
from jax.experimental import pallas as pl
from jax.experimental.pallas import tpu as pltpu
from jax.sharding import PartitionSpec as P

QH = 32
KVH = 4
HD = 64
LAYERS = 2
EPS = 1e-05
BF = jnp.bfloat16
F32 = jnp.float32
MESH = pl.DeviceIdType.MESH
CHUNK = 32
VMEM_LIMIT = 56 * 1024 * 1024
ANY = pl.BlockSpec(memory_space=pl.ANY)
VMEM = pl.BlockSpec(memory_space=pltpu.VMEM)


def mm(left, right, dims=((1,), (0,))):
    return lax.dot_general(left, right, (dims, ((), ())), preferred_element_type=F32)


def swap_pairs(values, axis, by=1):
    count = lax.axis_size(axis)
    return lax.ppermute(values, axis, [(i, i ^ by) for i in range(count)])


def rope_tables(places):
    half_width = HD // 2
    frequency = jnp.power(10000.0, -2.0 * jnp.arange(half_width).astype(F32) / HD)
    angles = places.astype(F32)[:, None] * frequency[None, :]
    return jnp.cos(angles)[:, None, :], jnp.sin(angles)[:, None, :]


def rotate(values, cosine, sines):
    half_width = HD // 2
    first, second = values[..., :half_width], values[..., half_width:]
    return jnp.concatenate(
        [first * cosine - second * sines, second * cosine + first * sines], axis=-1
    )


def core_rows(rows, core):
    quarter = rows.shape[0] // 4
    low = lax.dynamic_slice_in_dim(rows, core * quarter, quarter, 0)
    high = lax.dynamic_slice_in_dim(rows, (3 - core) * quarter, quarter, 0)
    return jnp.concatenate([low, high], axis=0)


def join_halves(first, second):
    quarter = first.shape[0] // 2
    return jnp.concatenate(
        [first[:quarter], second[:quarter], second[quarter:], first[quarter:]], axis=0
    )


def gather_blocks(base):
    shards = lax.axis_size("gx")
    if shards != 4:
        every = lax.all_gather(base, "gx", axis=0)
        return [every[i] for i in range(shards)]
    far = swap_pairs(base, "gx", 2)
    return [base, swap_pairs(base, "gx"), far, swap_pairs(far, "gx")]


def wide_blocks(wide):
    shards = lax.axis_size("gx")
    own = lax.axis_index("gx")
    block = wide.shape[1] // shards
    order = [own ^ j if shards == 4 else j for j in range(shards)]
    return [lax.dynamic_slice_in_dim(wide, b * block, block, 1) for b in order]


def reduce_blocks(make):
    shards = lax.axis_size("gx")
    if shards != 4:
        every = jnp.stack([make(j).astype(BF) for j in range(shards)])
        return lax.psum_scatter(every, "gx", scatter_dimension=0, tiled=False)
    sent = [swap_pairs(make(j).astype(BF), "gx") for j in (3, 1)]
    far = (make(2) + sent[0].astype(F32)).astype(BF)
    near = make(0) + sent[1].astype(F32)
    return (near + swap_pairs(far, "gx", 2).astype(F32)).astype(BF)


def line_kernel(
    backward, transposed, low, high, order, masked,
    lhs_ref, gain_ref, resid_ref, valid_ref, h_ref, ratio_ref, *rest,
):
    blocks = len(order)
    w_refs = rest[:blocks]
    (
        out_ref, gacc_ref, w_all, part, from_end, from_mid, pair,
        w_sem, up_send, up_recv, mid_send, mid_recv, fin_send, fin_recv,
    ) = rest[blocks:]
    rows, width = resid_ref.shape
    columns = width // blocks
    count = rows // CHUNK
    z = lax.axis_index("gy")
    shard = lax.axis_index("gx")
    middle = (z == 1) | (z == 2)
    end_of = jnp.where(z == 1, 0, 3)
    mid_of = jnp.where(z == 0, 1, 2)
    across = 3 - z

    loads = [
        pltpu.make_async_copy(w_refs[j].at[:, low:high], w_all.at[j], w_sem.at[j])
        for j in range(blocks)
    ]
    for load in loads:
        load.start()

    barrier = pltpu.get_barrier_semaphore()

    @pl.when(middle)
    def _():
        pl.semaphore_signal(barrier, inc=1, device_id={"gy": end_of}, device_id_type=MESH)
        pl.semaphore_signal(barrier, inc=1, device_id={"gy": across}, device_id_type=MESH)
        pl.semaphore_wait(barrier, 2)

    @pl.when(jnp.logical_not(middle))
    def _():
        pl.semaphore_signal(barrier, inc=1, device_id={"gy": mid_of}, device_id_type=MESH)
        pl.semaphore_wait(barrier, 1)

    gacc_ref[...] = jnp.zeros_like(gacc_ref)
    for load in loads:
        load.wait()

    def at(ref, i):
        return ref.at[pl.ds(pl.multiple_of(i * CHUNK, CHUNK), CHUNK), :]

    def up_copy(i):
        return pltpu.make_async_remote_copy(
            src_ref=at(part, i), dst_ref=at(from_end, i), send_sem=up_send.at[i],
            recv_sem=up_recv.at[i], device_id={"gy": mid_of}, device_id_type=MESH,
        )

    def mid_copy(i):
        return pltpu.make_async_remote_copy(
            src_ref=at(pair, i), dst_ref=at(from_mid, i), send_sem=mid_send.at[i],
            recv_sem=mid_recv.at[i], device_id={"gy": across}, device_id_type=MESH,
        )

    def fin_copy(i):
        return pltpu.make_async_remote_copy(
            src_ref=at(out_ref, i), dst_ref=at(out_ref, i), send_sem=fin_send.at[i],
            recv_sem=fin_recv.at[i], device_id={"gy": end_of}, device_id_type=MESH,
        )

    half = rows // 2

    def product(step, carry):
        here = pl.ds(pl.multiple_of(step * half, half), half)
        for j in range(blocks):
            where = (shard ^ j) if order[j] else j
            dims = (((1,), (1 if transposed else 0,)), ((), ()))
            value = lax.dot_general(
                lhs_ref[here, :], w_all[j], dims, preferred_element_type=F32
            )
            part[here, pl.ds(pl.multiple_of(where * columns, columns), columns)] = value.astype(BF)

        @pl.when(jnp.logical_not(middle))
        def _():
            def send(i, inner):
                up_copy(step * (count // 2) + i).start()
                return inner

            lax.fori_loop(0, count // 2, send, 0)

        return carry

    lax.fori_loop(0, 2, product, 0)

    def finish(i):
        mid_copy(i).wait_recv()
        here = pl.ds(pl.multiple_of(i * CHUNK, CHUNK), CHUNK)
        total = pair[here, :].astype(F32) + from_mid[here, :].astype(F32)
        resid = resid_ref[here, :].astype(F32)
        if backward:
            values = h_ref[here, :].astype(F32)
            scaled = total * gain_ref[...]
            ratio = ratio_ref[here, :]
            mean_term = jnp.sum(scaled * values, axis=1, keepdims=True) * (1.0 / width)
            result = resid + ratio * scaled - values * (ratio * ratio * ratio) * mean_term
            gains = total * values * ratio
            gacc_ref[...] += jnp.sum(gains.reshape(CHUNK // 8, 8, width), axis=0)
        else:
            result = resid + total
            if masked:
                result = result * valid_ref[here, :]
        out_ref[here, :] = result.astype(BF)
        fin_copy(i).start()

    @pl.when(middle)
    def _():
        def step(i, carry):
            up_copy(i).wait_recv()
            here = pl.ds(pl.multiple_of(i * CHUNK, CHUNK), CHUNK)
            pair[here, :] = (part[here, :].astype(F32) + from_end[here, :].astype(F32)).astype(BF)
            mid_copy(i).start()

            @pl.when(i >= 1)
            def _():
                finish(i - 1)

            return carry

        lax.fori_loop(0, count, step, 0)
        finish(count - 1)

        def drain(i, carry):
            mid_copy(i).wait_send()
            fin_copy(i).wait_send()
            return carry

        lax.fori_loop(0, count, drain, 0)

    @pl.when(jnp.logical_not(middle))
    def _():
        def drain(i, carry):
            up_copy(i).wait_send()
            fin_copy(i).wait_recv()
            return carry

        lax.fori_loop(0, count, drain, 0)


def summed(lhs, w_blocks, low, high, transposed, resid, ident, valid=None, back=None):
    rows, width = resid.shape
    blocks = len(w_blocks)
    if lax.axis_size("gy") != 4:
        dims = ((1,), (1 if transposed else 0,))
        total = jnp.concatenate([mm(lhs, w[:, low:high], dims) for w in w_blocks_in_order(w_blocks)], axis=1)
        total = lax.psum(total.astype(BF), "gy").astype(F32)
        if back is None:
            result = resid.astype(F32) + total
            return (result if valid is None else result * valid).astype(BF), None
        h, ratio, gain = back
        grad, gains = norm_back(total, h, ratio, gain)
        first = lax.axis_index("gy") == 0
        return (resid.astype(F32) + grad).astype(BF), jnp.where(first, gains, 0.0)
    depth = lhs.shape[1]
    w_shape = (width // blocks, depth) if transposed else (depth, width // blocks)
    one = jnp.ones((rows, 1), F32)
    h, ratio, gain = back if back is not None else (jnp.zeros((16, 128), BF), jnp.zeros((8, 1), F32), jnp.zeros((width,), F32))
    body = functools.partial(
        line_kernel, back is not None, transposed, low, high, [blocks == 4] * blocks, valid is not None
    )
    count = rows // CHUNK
    dma = pltpu.SemaphoreType.DMA
    out, gains = pl.pallas_call(
        body,
        out_shape=(
            jax.ShapeDtypeStruct((rows, width), BF),
            jax.ShapeDtypeStruct((8, width), F32),
        ),
        in_specs=[VMEM] * 6 + [ANY] * blocks,
        out_specs=(VMEM, VMEM),
        scratch_shapes=[
            pltpu.VMEM((blocks,) + w_shape, BF),
            pltpu.VMEM((rows, width), BF),
            pltpu.VMEM((rows, width), BF),
            pltpu.VMEM((rows, width), BF),
            pltpu.VMEM((rows, width), BF),
            dma((blocks,)),
        ]
        + [dma((count,))] * 6,
        compiler_params=pltpu.CompilerParams(
            collective_id=ident, has_side_effects=True, vmem_limit_bytes=VMEM_LIMIT
        ),
        cost_estimate=pl.CostEstimate(
            flops=2 * rows * depth * width, bytes_accessed=150 * 1024 * 1024, transcendentals=0
        ),
        name="line_sum",
    )(lhs, gain[None], resid, one if valid is None else valid, h, ratio, *w_blocks)
    return out, jnp.sum(gains, axis=0)


def w_blocks_in_order(w_blocks):
    if len(w_blocks) != 4:
        return w_blocks
    own = lax.axis_index("gx")
    every = jnp.stack(w_blocks)
    return [lax.dynamic_index_in_dim(every, own ^ i, 0, keepdims=False) for i in range(4)]


def normed(h, gain):
    values = h.astype(F32)
    square = jnp.mean(values * values, axis=1, keepdims=True)
    ratio = lax.rsqrt(square + EPS)
    return ratio, (values * ratio * gain).astype(BF), jnp.sqrt(square + EPS)[:, 0]


def norm_back(d_normed, h, ratio, gain):
    values = h.astype(F32)
    scaled = d_normed * gain
    mean_term = jnp.mean(scaled * values, axis=1, keepdims=True)
    grad = ratio * scaled - values * (ratio * ratio * ratio) * mean_term
    return grad, jnp.sum(d_normed * values * ratio, axis=0)


def probabilities(q_rot, k_all, allowed):
    scores = jnp.einsum("ihd,jd->hij", q_rot, k_all, preferred_element_type=F32) * HD ** (-0.5)
    scores = jnp.where(allowed[None], scores, -1e30)
    exponent = jnp.exp(scores - jnp.max(scores, axis=-1, keepdims=True))
    return exponent / jnp.sum(exponent, axis=-1, keepdims=True)


def forward_layer(h, weights, cosine, sines, allowed, valid):
    gain_attn, gain_mlp, w_attn, w_gu, w_down = weights
    rows, width = h.shape
    q_width = w_attn[0].shape[1] - 2 * HD - width // len(w_attn)
    qkv_width = q_width + 2 * HD
    r1, n1, rms1 = normed(h, gain_attn)
    w_qkv = jnp.concatenate([w[:, :qkv_width] for w in w_attn], axis=0)
    qkv = mm(jnp.concatenate(wide_blocks(n1), axis=1), w_qkv)
    q_rot = rotate(qkv[:, :q_width].reshape(rows, -1, HD), cosine, sines).astype(BF)
    k_rot = rotate(qkv[:, None, q_width : q_width + HD], cosine, sines)[:, 0].astype(BF)
    kv = jnp.concatenate([k_rot, qkv[:, q_width + HD :].astype(BF)], axis=1)
    kv_all = jnp.concatenate([kv, swap_pairs(kv, "gx")], axis=0)
    k_all, v_all = kv_all[:, :HD], kv_all[:, HD:]
    probs = probabilities(q_rot, k_all, allowed).astype(BF)
    heads = jnp.einsum("hij,jd->ihd", probs, v_all, preferred_element_type=F32)
    heads = heads.reshape(rows, -1).astype(BF)
    h1, _ = summed(heads, w_attn, qkv_width, w_attn[0].shape[1], False, h, 0)
    r2, n2, rms2 = normed(h1, gain_mlp)
    gu = mm(jnp.concatenate(wide_blocks(n2), axis=1), jnp.concatenate(w_gu, axis=0))
    gu = gu.astype(BF)
    hidden_width = gu.shape[1] // 2
    gate, up = gu[:, :hidden_width].astype(F32), gu[:, hidden_width:].astype(F32)
    hidden = (gate * jax.nn.sigmoid(gate) * up).astype(BF)
    result, _ = summed(hidden, w_down, 0, w_down[0].shape[1], False, h1, 1, valid=valid)
    statistics = jnp.where(valid[:, 0][None] > 0, jnp.stack([rms1, rms2]), 0.0)
    return result, statistics, (h, r1, n1, q_rot, k_all, v_all, heads, h1, r2, n2, gu, hidden)


def backward_layer(dm, weights, cosine, sines, allowed, saved):
    gain_attn, gain_mlp, w_attn, w_gu, w_down = weights
    h, r1, n1, q_rot, k_all, v_all, heads, h1, r2, n2, gu, hidden = saved
    rows, width = h.shape
    turn, down = ((0,), (0,)), ((1,), (1,))
    hidden_width = gu.shape[1] // 2
    gate, up = gu[:, :hidden_width].astype(F32), gu[:, hidden_width:].astype(F32)
    dm_blocks = wide_blocks(dm)
    d_hidden = mm(jnp.concatenate(dm_blocks, axis=1), jnp.concatenate(w_down, axis=1), down)
    sigmoid = jax.nn.sigmoid(gate)
    d_gate = (d_hidden * up * sigmoid * (1.0 + gate * (1.0 - sigmoid))).astype(BF)
    d_up = (d_hidden * (gate * sigmoid)).astype(BF)
    d_gu = jnp.concatenate([d_gate, d_up], axis=1)
    e1, g_gain_mlp = summed(
        d_gu, w_gu, 0, d_gu.shape[1], True, dm, 2, back=(h1, r2, gain_mlp)
    )
    n2_blocks = wide_blocks(n2)
    g_gu = reduce_blocks(lambda j: mm(n2_blocks[j], d_gu, turn))
    g_down = reduce_blocks(lambda j: mm(hidden, dm_blocks[j], turn))
    da_blocks = wide_blocks(e1)
    qkv_width = w_attn[0].shape[1] - width // len(w_attn)
    w_o = jnp.concatenate([w[:, qkv_width:] for w in w_attn], axis=1)
    d_heads = mm(jnp.concatenate(da_blocks, axis=1), w_o, down).astype(BF).reshape(q_rot.shape)
    probs = probabilities(q_rot, k_all, allowed)
    d_probs = jnp.einsum("ihd,jd->hij", d_heads, v_all, preferred_element_type=F32)
    delta = jnp.sum(d_probs * probs, axis=-1, keepdims=True)
    d_scores = (probs * (d_probs - delta)).astype(BF)
    scaling = HD ** (-0.5)
    dq = jnp.einsum("hij,jd->ihd", d_scores, k_all, preferred_element_type=F32) * scaling
    dk = jnp.einsum("hij,ihd->jd", d_scores, q_rot, preferred_element_type=F32) * scaling
    dv = jnp.einsum("hij,ihd->jd", probs.astype(BF), d_heads, preferred_element_type=F32)
    dkv = jnp.concatenate([dk, dv], axis=1)
    dkv = dkv[:rows] + swap_pairs(dkv[rows:], "gx")
    dq = rotate(dq, cosine, -sines).reshape(rows, -1)
    dk = rotate(dkv[:, None, :HD], cosine, -sines)[:, 0]
    d_qkv = jnp.concatenate([dq, dk, dkv[:, HD:]], axis=1).astype(BF)
    d_input, g_gain_attn = summed(
        d_qkv, w_attn, 0, qkv_width, True, e1, 3, back=(h, r1, gain_attn)
    )
    n1_blocks = wide_blocks(n1)
    g_attn = reduce_blocks(
        lambda j: jnp.concatenate(
            [mm(n1_blocks[j], d_qkv, turn), mm(heads, da_blocks[j], turn)], axis=1
        )
    )
    return d_input, jnp.stack([g_gain_attn, g_gain_mlp]), (g_attn, g_gu, g_down)


def on_device(
    hidden_in, out_grad, lengths, dealing, attn_gain, w_query, w_key, w_value, w_out,
    mlp_gain, w_gate, w_up, w_down,
):
    shards = lax.axis_size("gx")
    shard = lax.axis_index("gx")
    section = lax.axis_index("section")
    column = lax.axis_index("gy")
    core = shard % 2
    sequence = (shard // 2) * 2 + section
    span, width = hidden_in.shape
    half = span // 2
    seq_length = lax.dynamic_index_in_dim(lengths, sequence, keepdims=False)

    both = jnp.concatenate([hidden_in, out_grad], axis=1)
    mine = core_rows(both, core)
    theirs = swap_pairs(core_rows(both, 1 - core), "gx")
    mine = jnp.where(core == section, mine, theirs)
    wide = lax.all_gather(mine.reshape(half, 2, width), "gy", axis=2, tiled=True)
    h, d_out = wide[:, 0], wide[:, 1]

    kv_head = column * (w_query.shape[2] // HD) // (QH // KVH)
    attn_own = jnp.concatenate(
        [
            w_query[0],
            lax.dynamic_slice_in_dim(w_key[0], kv_head * HD, HD, 1),
            lax.dynamic_slice_in_dim(w_value[0], kv_head * HD, HD, 1),
            w_out[0],
        ],
        axis=1,
    )
    own = (attn_own, jnp.concatenate([w_gate[0], w_up[0]], axis=1), w_down[0])
    gains_both = lax.all_gather(jnp.stack([attn_gain[0], mlp_gain[0]]), ("section", "gx"), axis=0)
    gains_both = gains_both.reshape(LAYERS, shards, 2, -1).transpose(0, 2, 1, 3).reshape(LAYERS, 2, -1)
    layers = []
    for layer in range(LAYERS):
        weights = [gains_both[layer, 0].astype(F32), gains_both[layer, 1].astype(F32)]
        for array in own:
            moved = lax.ppermute(array, "section", [(layer, 1 - layer)])
            weights.append(gather_blocks(jnp.where(section == layer, array, moved)))
        layers.append(weights)

    here = core_rows(jnp.arange(span), core)
    there = core_rows(jnp.arange(span), 1 - core)
    keys_at = jnp.concatenate([here, there])
    allowed = (keys_at[None, :] <= here[:, None]) & (keys_at[None, :] < seq_length)
    valid = (here < seq_length)[:, None].astype(F32)
    cosine, sines = rope_tables(here)

    outputs, statistics, saved = [], [], []
    for layer in range(LAYERS):
        h, stat, kept = forward_layer(h, layers[layer], cosine, sines, allowed, valid)
        outputs.append(lax.dynamic_slice_in_dim(h, column * width, width, 1))
        statistics.append(stat)
        saved.append(kept)

    def to_section(per_layer):
        kept = jnp.where(section == 0, per_layer[0], per_layer[1])
        sent = swap_pairs(jnp.where(section == 0, per_layer[1], per_layer[0]), "section")
        return kept, sent

    kept, sent = to_section(outputs)
    by_section = jnp.stack([jnp.where(section == 0, kept, sent), jnp.where(section == 0, sent, kept)])
    everything = lax.all_gather(by_section, "gx", axis=0)
    stat_kept, stat_sent = to_section(statistics)
    stat_both = jnp.stack(
        [jnp.where(section == 0, stat_kept, stat_sent), jnp.where(section == 0, stat_sent, stat_kept)]
    )
    every_stat = lax.all_gather(stat_both, "gx", axis=0)
    owner = jnp.sum(jnp.where(dealing == shard, jnp.arange(shards), 0))
    halves = lax.dynamic_slice(
        everything, ((owner // 2) * 2, owner % 2, 0, 0), (2, 1, half, width)
    )
    layer_out = join_halves(halves[0, 0], halves[1, 0])
    stat_halves = lax.dynamic_slice(every_stat, ((owner // 2) * 2, owner % 2, 0, 0), (2, 1, 2, half))
    stats_out = join_halves(stat_halves[0, 0].T, stat_halves[1, 0].T).T

    gain_sums, received, local, input_grads = [None] * 2, [None] * 2, [None] * 2, [None] * 2
    cotangent = d_out
    for layer in (1, 0):
        dm = (cotangent.astype(F32) * valid).astype(BF)
        cotangent, gain_sums[layer], grads = backward_layer(
            dm, layers[layer], cosine, sines, allowed, saved[layer]
        )
        input_grads[layer] = lax.dynamic_slice_in_dim(cotangent, column * width, width, 1)
        local[layer] = grads
        received[layer] = [lax.ppermute(g, "section", [(1 - layer, layer)]) for g in grads]
    totals = [
        jnp.where(section == 0, a0.astype(F32) + r0.astype(F32), a1.astype(F32) + r1.astype(F32))
        for a0, r0, a1, r1 in zip(local[0], received[0], local[1], received[1])
    ]
    s_attn, s_gu, s_down = totals
    q_width = w_query.shape[2]
    kv_width = w_key.shape[2]
    ff_width = w_gate.shape[2]

    def spread(part):
        blank = jnp.zeros((part.shape[0], kv_width), F32)
        return lax.dynamic_update_slice_in_dim(blank, part, kv_head * HD, 1)

    kv_sum = lax.psum(
        jnp.stack([spread(s_attn[:, q_width : q_width + HD]), spread(s_attn[:, q_width + HD : q_width + 2 * HD])]).astype(BF),
        "gy",
    ).astype(F32)
    gains = lax.psum(jnp.stack(gain_sums), ("section", "gx", "gy"))
    if lax.axis_size("gy") == 4:
        gains = gains * 0.5
    gains = lax.dynamic_index_in_dim(gains, section, 0, keepdims=False)
    part = attn_gain.shape[1]
    gains = lax.dynamic_slice_in_dim(gains, shard * part, part, 1)

    kept, sent = to_section(input_grads)
    keep = jnp.where(core == section, kept, sent)
    give = swap_pairs(jnp.where(core == section, sent, kept), "gx")
    back_home = join_halves(jnp.where(core == 0, keep, give), jnp.where(core == 0, give, keep))
    return (
        layer_out[None],
        stats_out[None],
        back_home[None],
        gains[None, 0],
        s_attn[None, :, :q_width],
        kv_sum[None, 0],
        kv_sum[None, 1],
        s_attn[None, :, q_width + 2 * HD :],
        gains[None, 1],
        s_gu[None, :, :ff_width],
        s_gu[None, :, ff_width:],
        s_down[None],
    )


def solution(mesh):
    rows_cols = P("section", "gx", "gy")
    cols_rows = P("section", "gy", "gx")
    rows_only = P("section", "gx", None)
    gain = P("section", "gx")
    return jax.shard_map(
        on_device,
        mesh=mesh,
        in_specs=(
            P("gx", "gy"), P("gx", "gy"), P(), P(), gain, rows_cols, rows_only, rows_only,
            cols_rows, gain, rows_cols, rows_cols, cols_rows,
        ),
        out_specs=(
            rows_cols, P("section", None, "gx"), rows_cols, gain, rows_cols, rows_only, rows_only,
            cols_rows, gain, rows_cols, rows_cols, cols_rows,
        ),
        check_vma=False,
    )
```

```python
import functools

import jax
import jax.numpy as jnp
from jax import lax
from jax.experimental import pallas as pl
from jax.experimental.pallas import tpu as pltpu
from jax.sharding import PartitionSpec as P

QH = 32
KVH = 4
HD = 64
LAYERS = 2
EPS = 1e-05
BF = jnp.bfloat16
F32 = jnp.float32
MESH = pl.DeviceIdType.MESH
CHUNK = 32
STEPS = 2
VMEM_LIMIT = 56 * 1024 * 1024
ANY = pl.BlockSpec(memory_space=pl.ANY)
VMEM = pl.BlockSpec(memory_space=pltpu.VMEM)


def mm(left, right, dims=((1,), (0,))):
    return lax.dot_general(left, right, (dims, ((), ())), preferred_element_type=F32)


def swap_pairs(values, axis, by=1):
    count = lax.axis_size(axis)
    return lax.ppermute(values, axis, [(i, i ^ by) for i in range(count)])


def rope_tables(places):
    half_width = HD // 2
    frequency = jnp.power(10000.0, -2.0 * jnp.arange(half_width).astype(F32) / HD)
    angles = places.astype(F32)[:, None] * frequency[None, :]
    return jnp.cos(angles)[:, None, :], jnp.sin(angles)[:, None, :]


def rotate(values, cosine, sines):
    half_width = HD // 2
    first, second = values[..., :half_width], values[..., half_width:]
    return jnp.concatenate(
        [first * cosine - second * sines, second * cosine + first * sines], axis=-1
    )


def core_rows(rows, core):
    quarter = rows.shape[0] // 4
    low = lax.dynamic_slice_in_dim(rows, core * quarter, quarter, 0)
    high = lax.dynamic_slice_in_dim(rows, (3 - core) * quarter, quarter, 0)
    return jnp.concatenate([low, high], axis=0)


def join_halves(first, second):
    quarter = first.shape[0] // 2
    return jnp.concatenate(
        [first[:quarter], second[:quarter], second[quarter:], first[quarter:]], axis=0
    )


def chip_groups():
    return [[0, 2], [1, 3]]


def gather_blocks(base):
    return lax.all_gather(base, "gx", axis=0)


def chosen(pair, layer):
    return jnp.where(lax.axis_index("section") == layer, *pair)


def fused():
    return lax.axis_size("gx") == 4 and lax.axis_size("gy") == 4


def tall(w):
    return w.reshape(-1, w.shape[-1])


def side(w):
    return jnp.concatenate([w[i] for i in range(w.shape[0])], axis=1)


def cut(w, low, high):
    return w[:, :, low:high]


def core_columns(wide, core):
    rows, width = wide.shape
    parts = wide.reshape(rows, 2, 2, width // 4)
    return lax.dynamic_index_in_dim(parts, core, 2, keepdims=False).reshape(rows, width // 2)


def both_cores(mine):
    return jnp.concatenate([mine, swap_pairs(mine, "gx")], axis=0)


def both_columns(wide):
    core = lax.axis_index("gx") % 2
    kept, sent = core_columns(wide, core), core_columns(wide, 1 - core)
    return jnp.concatenate([kept, swap_pairs(sent, "gx")], axis=0)


def shard_product(wide, other, tall_out):
    turn = ((0,), (0,))
    if fused():
        wide, other = both_columns(wide), both_cores(other)
    return (mm(wide, other, turn) if tall_out else mm(other, wide, turn)).astype(BF)


def shard_sum(product, tall_out):
    dimension = 0 if tall_out else 1
    groups = chip_groups() if fused() else None
    return lax.psum_scatter(
        product, "gx", scatter_dimension=dimension, tiled=True, axis_index_groups=groups
    )


def line_kernel(
    kind, masked, low, high, deps, gathers, layer,
    gain_ref, resid_ref, valid_ref, h_ref, square_ref, *rest,
):
    forward = kind in ("out", "mlp")
    wide = kind in ("mlp", "mlp_back")
    if kind == "mlp":
        lhs_refs = []
    elif kind == "mlp_back":
        lhs_refs, rest = rest[:3], rest[3:]
    else:
        lhs_refs, rest = rest[:1], rest[1:]
    w_count = 3 if wide else 1
    w_refs, rest = rest[:w_count], rest[w_count + deps :]
    base_refs, rest = rest[: 2 * gathers], rest[2 * gathers :]
    out_ref, gacc_ref, rest = rest[0], rest[1], rest[2:]
    if kind == "mlp":
        normed_ref, ms_ref, gate_ref, up_ref, hidden_ref = rest[:5]
        rest = rest[5:]
    elif kind == "mlp_back":
        d_gate_ref, d_up_ref = rest[:2]
        rest = rest[2:]
    block_refs, rest = rest[:gathers], rest[gathers:]
    w_alls, rest = rest[:w_count], rest[w_count:]
    (
        part, from_end, from_mid, pair,
        w_sem, up_send, up_recv, mid_send, mid_recv, fin_send, fin_recv,
    ) = rest[:11]
    if gathers:
        own_sem, far_send, far_recv, near_send, near_recv = rest[11:]
    shard = lax.axis_index("gx")
    far, near = shard ^ 2, shard ^ 1
    rows, width = resid_ref.shape
    columns = width // 4
    count = rows // CHUNK
    z = lax.axis_index("gy")
    middle = (z == 1) | (z == 2)
    end_of = jnp.where(z == 1, 0, 3)
    mid_of = jnp.where(z == 0, 1, 2)
    across = 3 - z

    loads = []
    for w in range(w_count):
        for j in range(4):
            source = w_refs[w].at[j] if wide else w_refs[w].at[j, :, low:high]
            split = wide and w < 2
            target = w_alls[w].at[j * columns : (j + 1) * columns, :] if split else w_alls[w].at[j]
            loads.append(pltpu.make_async_copy(source, target, w_sem.at[4 * w + j]))
    for load in loads:
        load.start()

    barrier = pltpu.get_barrier_semaphore()
    beside = 0
    if gathers:
        beside = 2
        for peer in (far, near):
            pl.semaphore_signal(barrier, inc=1, device_id={"gx": peer}, device_id_type=MESH)

    @pl.when(middle)
    def _():
        pl.semaphore_signal(barrier, inc=1, device_id={"gy": end_of}, device_id_type=MESH)
        pl.semaphore_signal(barrier, inc=1, device_id={"gy": across}, device_id_type=MESH)
        pl.semaphore_wait(barrier, 2 + beside)

    @pl.when(jnp.logical_not(middle))
    def _():
        pl.semaphore_signal(barrier, inc=1, device_id={"gy": mid_of}, device_id_type=MESH)
        pl.semaphore_wait(barrier, 1 + beside)

    def own_copy(k, source):
        return pltpu.make_async_copy(source, block_refs[k].at[shard], own_sem.at[k])

    def far_copy(k, source):
        return pltpu.make_async_remote_copy(
            src_ref=source, dst_ref=block_refs[k].at[shard], send_sem=far_send.at[k],
            recv_sem=far_recv.at[k], device_id={"gx": far}, device_id_type=MESH,
        )

    def near_copy(k, source):
        return pltpu.make_async_remote_copy(
            src_ref=source, dst_ref=block_refs[k].at[shard], send_sem=near_send.at[2 * k],
            recv_sem=near_recv.at[2 * k], device_id={"gx": near}, device_id_type=MESH,
        )

    def pass_copy(k):
        return pltpu.make_async_remote_copy(
            src_ref=block_refs[k].at[far], dst_ref=block_refs[k].at[far],
            send_sem=near_send.at[2 * k + 1], recv_sem=near_recv.at[2 * k + 1],
            device_id={"gx": near}, device_id_type=MESH,
        )

    def gather_start(k):
        at_home = lax.axis_index("section") == layer
        for ref, holds in zip(base_refs[2 * k : 2 * k + 2], (at_home, jnp.logical_not(at_home))):

            @pl.when(holds)
            def _():
                far_copy(k, ref).start()
                near_copy(k, ref).start()
                own_copy(k, ref).start()

    def gather_pass(k):
        far_copy(k, base_refs[2 * k]).wait_recv()
        pass_copy(k).start()
        if k + 1 < gathers:
            gather_start(k + 1)

    if gathers:
        gather_start(0)

    if not forward:
        gacc_ref[...] = jnp.zeros_like(gacc_ref)
    for load in loads:
        load.wait()

    def at(ref, i):
        return ref.at[pl.ds(pl.multiple_of(i * CHUNK, CHUNK), CHUNK), :]

    def up_copy(i):
        return pltpu.make_async_remote_copy(
            src_ref=at(part, i), dst_ref=at(from_end, i), send_sem=up_send.at[i],
            recv_sem=up_recv.at[i], device_id={"gy": mid_of}, device_id_type=MESH,
        )

    def mid_copy(i):
        return pltpu.make_async_remote_copy(
            src_ref=at(pair, i), dst_ref=at(from_mid, i), send_sem=mid_send.at[i],
            recv_sem=mid_recv.at[i], device_id={"gy": across}, device_id_type=MESH,
        )

    def fin_copy(i):
        return pltpu.make_async_remote_copy(
            src_ref=at(out_ref, i), dst_ref=at(out_ref, i), send_sem=fin_send.at[i],
            recv_sem=fin_recv.at[i], device_id={"gy": end_of}, device_id_type=MESH,
        )

    def dot(left, right, transposed=False):
        dims = (((1,), (1 if transposed else 0,)), ((), ()))
        return lax.dot_general(left, right, dims, preferred_element_type=F32)

    def spans(extent):
        return [(x, min(x + 512, extent)) for x in range(0, extent, 512)]

    half = rows // STEPS
    if wide:
        w_gate, w_up, w_down = w_alls

    def product(step, carry):
        here = pl.ds(pl.multiple_of(step * half, half), half)
        if kind == "mlp":
            values = resid_ref[here, :].astype(F32)
            square = jnp.mean(values * values, axis=1, keepdims=True)
            ms_ref[here, :] = square
            normed_ref[here, :] = (values * lax.rsqrt(square + EPS) * gain_ref[...]).astype(BF)
            for x0, x1 in spans(w_gate.shape[1]):
                gate = dot(normed_ref[here, :], w_gate[:, x0:x1])
                up = dot(normed_ref[here, :], w_up[:, x0:x1])
                gate_ref[here, x0:x1] = gate.astype(BF)
                up_ref[here, x0:x1] = up.astype(BF)
                hidden_ref[here, x0:x1] = (gate * jax.nn.sigmoid(gate) * up).astype(BF)
        if kind == "mlp_back":
            dm_ref, saved_gate, saved_up = lhs_refs
            for x0, x1 in spans(w_gate.shape[1]):
                d_hidden = sum(
                    dot(dm_ref[here, j * columns : (j + 1) * columns], w_down[j, x0:x1, :], True)
                    for j in range(4)
                )
                gate = saved_gate[here, x0:x1].astype(F32)
                up = saved_up[here, x0:x1].astype(F32)
                sigmoid = jax.nn.sigmoid(gate)
                d_up_ref[here, x0:x1] = (d_hidden * (gate * sigmoid)).astype(BF)
                d_gate_ref[here, x0:x1] = (
                    d_hidden * up * sigmoid * (1.0 + gate * (1.0 - sigmoid))
                ).astype(BF)
        for j in range(4):
            span = slice(j * columns, (j + 1) * columns)
            if kind == "out":
                value = dot(lhs_refs[0][here, :], w_alls[0][j])
            elif kind == "mlp":
                value = dot(hidden_ref[here, :], w_down[j])
            elif kind == "mlp_back":
                value = dot(d_gate_ref[here, :], w_gate[span, :], True)
                value += dot(d_up_ref[here, :], w_up[span, :], True)
            else:
                value = dot(lhs_refs[0][here, :], w_alls[0][j], True)
            part[here, span] = value.astype(BF)

        @pl.when(jnp.logical_not(middle))
        def _():
            def send(i, inner):
                up_copy(step * (count // STEPS) + i).start()
                return inner

            lax.fori_loop(0, count // STEPS, send, 0)

        return carry

    lax.fori_loop(0, STEPS, product, 0)

    def finish(i):
        mid_copy(i).wait_recv()
        here = pl.ds(pl.multiple_of(i * CHUNK, CHUNK), CHUNK)
        total = pair[here, :].astype(F32) + from_mid[here, :].astype(F32)
        resid = resid_ref[here, :].astype(F32)
        if forward:
            result = resid + total
            if masked:
                result = result * valid_ref[here, :]
        else:
            values = h_ref[here, :].astype(F32)
            scaled = total * gain_ref[...]
            ratio = lax.rsqrt(square_ref[here, :] + EPS)
            mean_term = jnp.sum(scaled * values, axis=1, keepdims=True) * (1.0 / width)
            result = resid + ratio * scaled - values * (ratio * ratio * ratio) * mean_term
            gains = total * values * ratio
            gacc_ref[...] += jnp.sum(gains.reshape(CHUNK // 8, 8, width), axis=0)
        out_ref[here, :] = result.astype(BF)
        fin_copy(i).start()

    def pass_on(i):
        for k in range(gathers - 1):

            @pl.when(i == (k + 1) * count // gathers)
            def _():
                gather_pass(k)

    @pl.when(middle)
    def _():
        def step(i, carry):
            up_copy(i).wait_recv()
            here = pl.ds(pl.multiple_of(i * CHUNK, CHUNK), CHUNK)
            pair[here, :] = (part[here, :].astype(F32) + from_end[here, :].astype(F32)).astype(BF)
            mid_copy(i).start()

            @pl.when(i >= 1)
            def _():
                finish(i - 1)

            pass_on(i)
            return carry

        lax.fori_loop(0, count, step, 0)
        finish(count - 1)

        def drain(i, carry):
            mid_copy(i).wait_send()
            fin_copy(i).wait_send()
            return carry

        lax.fori_loop(0, count, drain, 0)

    @pl.when(jnp.logical_not(middle))
    def _():
        def drain(i, carry):
            up_copy(i).wait_send()
            fin_copy(i).wait_recv()
            pass_on(i)
            return carry

        lax.fori_loop(0, count, drain, 0)

    if gathers:
        gather_pass(gathers - 1)
    for k in range(gathers):
        own_copy(k, base_refs[2 * k]).wait()
        far_copy(k, base_refs[2 * k]).wait_send()
        near_copy(k, base_refs[2 * k]).wait()
        pass_copy(k).wait()


def line_sum(kind, ident, resid, weights, lhs=(), gain=None, valid=None, back=None, low=0, high=0, deps=(), bases=(), layer=0):
    rows, width = resid.shape
    one = jnp.ones((rows, 1), F32)
    h, square = back if back is not None else (jnp.zeros((16, 128), BF), jnp.zeros((8, 1), F32))
    gain = jnp.zeros((width,), F32) if gain is None else gain
    wide = kind in ("mlp", "mlp_back")
    hidden = weights[0].shape[2] if wide else 0
    w_scratch = []
    for i, w in enumerate(weights):
        _, depth, across = w.shape
        if wide and i < 2:
            w_scratch.append(pltpu.VMEM((width, across), BF))
        else:
            w_scratch.append(pltpu.VMEM((4, depth, across if wide else high - low), BF))
    outs = [((rows, width), BF), ((8, width), F32)]
    if kind == "mlp":
        outs += [((rows, width), BF), ((rows, 1), F32)] + [((rows, hidden), BF)] * 3
    elif kind == "mlp_back":
        outs += [((rows, hidden), BF)] * 2
    blocks = [((4,) + base[0].shape, BF) for base in bases]
    pairs = [x for base in bases for x in base]
    depth = 3 * hidden if wide else lhs[0].shape[1]
    count = rows // CHUNK
    dma = pltpu.SemaphoreType.DMA
    return pl.pallas_call(
        functools.partial(
            line_kernel, kind, valid is not None, low, high, len(deps), len(bases), layer
        ),
        out_shape=tuple(jax.ShapeDtypeStruct(*o) for o in outs + blocks),
        in_specs=[VMEM] * (5 + len(lhs)) + [ANY] * (len(weights) + len(deps) + len(pairs)),
        out_specs=tuple([VMEM] * len(outs) + [ANY] * len(blocks)),
        scratch_shapes=w_scratch
        + [pltpu.VMEM((rows, width), BF)] * 4
        + [dma((4 * len(weights),))]
        + [dma((count,))] * 6
        + [dma((n * len(bases),)) for n in (1, 1, 1, 2, 2) if bases],
        compiler_params=pltpu.CompilerParams(
            collective_id=ident, has_side_effects=True, vmem_limit_bytes=VMEM_LIMIT
        ),
        cost_estimate=pl.CostEstimate(
            flops=2 * rows * depth * width, bytes_accessed=200 * 1024 * 1024, transcendentals=0
        ),
        name="line_" + kind,
    )(gain[None], resid, one if valid is None else valid, h, square, *lhs, *weights, *deps, *pairs)


def plain_sum(total):
    return lax.psum(total.astype(BF), "gy").astype(F32)


def normed(h, gain):
    values = h.astype(F32)
    square = jnp.mean(values * values, axis=1, keepdims=True)
    return square, (values * lax.rsqrt(square + EPS) * gain).astype(BF)


def norm_back(d_normed, h, square, gain):
    values = h.astype(F32)
    ratio = lax.rsqrt(square + EPS)
    scaled = d_normed * gain
    mean_term = jnp.mean(scaled * values, axis=1, keepdims=True)
    grad = ratio * scaled - values * (ratio * ratio * ratio) * mean_term
    return grad, jnp.sum(d_normed * values * ratio, axis=0)


def probabilities(q_rot, k_all, allowed):
    scores = jnp.einsum("ihd,jd->hij", q_rot, k_all, preferred_element_type=F32) * HD ** (-0.5)
    scores = jnp.where(allowed[None], scores, -1e30)
    exponent = jnp.exp(scores - jnp.max(scores, axis=-1, keepdims=True))
    return exponent / jnp.sum(exponent, axis=-1, keepdims=True)


def attention_forward(h, gain, w_attn, cosine, sines, allowed, ident, bases, layer, deps=()):
    rows, width = h.shape
    all_width = w_attn.shape[-1]
    qkv_width = all_width - width // lax.axis_size("gx")
    q_width = qkv_width - 2 * HD
    square, n1 = normed(h, gain)
    qkv = mm(n1, tall(cut(w_attn, 0, qkv_width)))
    q_rot = rotate(qkv[:, :q_width].reshape(rows, -1, HD), cosine, sines).astype(BF)
    k_rot = rotate(qkv[:, None, q_width : q_width + HD], cosine, sines)[:, 0].astype(BF)
    kv = jnp.concatenate([k_rot, qkv[:, q_width + HD :].astype(BF)], axis=1)
    kv_all = jnp.concatenate([kv, swap_pairs(kv, "gx")], axis=0)
    k_all, v_all = kv_all[:, :HD], kv_all[:, HD:]
    probs = probabilities(q_rot, k_all, allowed).astype(BF)
    heads = jnp.einsum("hij,jd->ihd", probs, v_all, preferred_element_type=F32)
    heads = heads.reshape(rows, -1).astype(BF)
    if fused():
        h1, _, *blocks = line_sum(
            "out", ident, h, [w_attn], (heads,), low=qkv_width, high=all_width,
            deps=deps, bases=bases, layer=layer,
        )
    else:
        total = plain_sum(mm(heads, side(cut(w_attn, qkv_width, all_width))))
        h1 = (h.astype(F32) + total).astype(BF)
        blocks = [gather_blocks(chosen(x, layer)) for x in bases]
    return h1, square, blocks, (h, square, n1, q_rot, k_all, v_all, heads)


def mlp_forward(h1, gain, weights, valid, ident, bases=(), layer=0):
    if fused():
        result, _, n2, square, gate, up, hidden, *blocks = line_sum(
            "mlp", ident, h1, weights, gain=gain, valid=valid, bases=bases, layer=layer
        )
    else:
        square, n2 = normed(h1, gain)
        gate = mm(n2, tall(weights[0]))
        up = mm(n2, tall(weights[1]))
        hidden = (gate * jax.nn.sigmoid(gate) * up).astype(BF)
        gate, up = gate.astype(BF), up.astype(BF)
        result = h1.astype(F32) + plain_sum(mm(hidden, side(weights[2])))
        result = (result * valid).astype(BF)
        blocks = [gather_blocks(chosen(x, layer)) for x in bases]
    return result, square, blocks, (h1, square, n2, gate, up, hidden)


def mlp_backward(dm, gain, weights, saved, ident, deps=()):
    h1, square, n2, gate, up, hidden = saved
    if fused():
        e1, gains, d_gate, d_up = line_sum(
            "mlp_back", ident, dm, weights, (dm, gate, up), gain=gain, back=(h1, square), deps=deps
        )
        return e1, jnp.sum(gains, axis=0), d_gate, d_up
    gate, up = gate.astype(F32), up.astype(F32)
    d_hidden = mm(dm, side(weights[2]), ((1,), (1,)))
    sigmoid = jax.nn.sigmoid(gate)
    d_gate = (d_hidden * up * sigmoid * (1.0 + gate * (1.0 - sigmoid))).astype(BF)
    d_up = (d_hidden * (gate * sigmoid)).astype(BF)
    total = mm(d_gate, tall(weights[0]), ((1,), (1,))) + mm(d_up, tall(weights[1]), ((1,), (1,)))
    grad, gains = norm_back(plain_sum(total), h1, square, gain)
    return (dm.astype(F32) + grad).astype(BF), gains, d_gate, d_up


def attention_backward(e1, w_attn, cosine, sines, allowed, saved):
    h, square, n1, q_rot, k_all, v_all, heads = saved
    rows, width = h.shape
    all_width = w_attn.shape[-1]
    qkv_width = all_width - width // lax.axis_size("gx")
    w_o = side(cut(w_attn, qkv_width, all_width))
    d_heads = mm(e1, w_o, ((1,), (1,))).astype(BF).reshape(q_rot.shape)
    probs = probabilities(q_rot, k_all, allowed)
    d_probs = jnp.einsum("ihd,jd->hij", d_heads, v_all, preferred_element_type=F32)
    delta = jnp.sum(d_probs * probs, axis=-1, keepdims=True)
    d_scores = (probs * (d_probs - delta)).astype(BF)
    scaling = HD ** (-0.5)
    dq = jnp.einsum("hij,jd->ihd", d_scores, k_all, preferred_element_type=F32) * scaling
    dk = jnp.einsum("hij,ihd->jd", d_scores, q_rot, preferred_element_type=F32) * scaling
    dv = jnp.einsum("hij,ihd->jd", probs.astype(BF), d_heads, preferred_element_type=F32)
    dkv = jnp.concatenate([dk, dv], axis=1)
    dkv = dkv[:rows] + swap_pairs(dkv[rows:], "gx")
    dq = rotate(dq, cosine, -sines).reshape(rows, -1)
    dk = rotate(dkv[:, None, :HD], cosine, -sines)[:, 0]
    return jnp.concatenate([dq, dk, dkv[:, HD:]], axis=1).astype(BF)


def attention_end(d_qkv, e1, w_attn, gain, saved, ident, deps=()):
    h, square = saved[:2]
    qkv_width = d_qkv.shape[1]
    if fused():
        grad, gains = line_sum(
            "back", ident, e1, [w_attn], (d_qkv,), gain=gain, back=(h, square),
            low=0, high=qkv_width, deps=deps,
        )
        return grad, jnp.sum(gains, axis=0)
    total = plain_sum(mm(d_qkv, tall(cut(w_attn, 0, qkv_width)), ((1,), (1,))))
    grad, gains = norm_back(total, h, square, gain)
    return (e1.astype(F32) + grad).astype(BF), gains


def on_device(
    hidden_in, out_grad, lengths, dealing, attn_gain, w_query, w_key, w_value, w_out,
    mlp_gain, w_gate, w_up, w_down,
):
    shards = lax.axis_size("gx")
    shard = lax.axis_index("gx")
    section = lax.axis_index("section")
    column = lax.axis_index("gy")
    core = shard % 2
    sequence = (shard // 2) * 2 + section
    span, width = hidden_in.shape
    half = span // 2
    seq_length = lax.dynamic_index_in_dim(lengths, sequence, keepdims=False)

    both = jnp.concatenate([hidden_in, out_grad], axis=1)
    mine = core_rows(both, core)
    theirs = swap_pairs(core_rows(both, 1 - core), "gx")
    mine = jnp.where(core == section, mine, theirs)
    wide = lax.all_gather(mine.reshape(half, 2, width), "gy", axis=2, tiled=True)
    h, d_out = wide[:, 0], wide[:, 1]

    kv_head = column * (w_query.shape[2] // HD) // (QH // KVH)
    attn_own = jnp.concatenate(
        [
            w_query[0],
            lax.dynamic_slice_in_dim(w_key[0], kv_head * HD, HD, 1),
            lax.dynamic_slice_in_dim(w_value[0], kv_head * HD, HD, 1),
            w_out[0],
        ],
        axis=1,
    )
    own = (attn_own, w_gate[0], w_up[0], w_down[0])
    gains_both = lax.all_gather(jnp.stack([attn_gain[0], mlp_gain[0]]), ("section", "gx"), axis=0)
    gains_both = gains_both.reshape(LAYERS, shards, 2, -1).transpose(0, 2, 1, 3)
    gains_both = gains_both.reshape(LAYERS, 2, -1).astype(F32)
    first = [(array, lax.ppermute(array, "section", [(0, 1)])) for array in own]
    second = [(array, lax.ppermute(array, "section", [(1, 0)])) for array in own]

    here = core_rows(jnp.arange(span), core)
    there = core_rows(jnp.arange(span), 1 - core)
    keys_at = jnp.concatenate([here, there])
    allowed = (keys_at[None, :] <= here[:, None]) & (keys_at[None, :] < seq_length)
    valid = (here < seq_length)[:, None].astype(F32)
    cosine, sines = rope_tables(here)

    rope = (cosine, sines, allowed)
    gains0, gains1 = gains_both[0], gains_both[1]
    attn0, gate0 = gather_blocks(chosen(first[0], 0)), gather_blocks(chosen(first[1], 0))
    h1, square_a, blocks, saved_a0 = attention_forward(
        h, gains0[0], attn0, *rope, 0, first[2:], 0, (gate0,)
    )
    mlp0 = [gate0] + blocks
    h, square_m, (attn1, gate1), saved_m0 = mlp_forward(
        h1, gains0[1], mlp0, valid, 1, second[:2], 1
    )
    outputs, squares = [h], [square_a, square_m]
    h1, square_a, blocks, saved_a1 = attention_forward(
        h, gains1[0], attn1, *rope, 2, second[2:], 1
    )
    mlp1 = [gate1] + blocks
    h, square_m, _, saved_m1 = mlp_forward(h1, gains1[1], mlp1, valid, 3)
    outputs.append(h)
    squares = jnp.concatenate(squares + [square_a, square_m], axis=1)
    rms = (jnp.sqrt(squares + EPS) * valid).T
    statistics = [rms[:2], rms[2:]]
    outputs = [lax.dynamic_slice_in_dim(x, column * width, width, 1) for x in outputs]

    def to_section(per_layer):
        kept = jnp.where(section == 0, per_layer[0], per_layer[1])
        sent = swap_pairs(jnp.where(section == 0, per_layer[1], per_layer[0]), "section")
        return kept, sent

    kept, sent = to_section(outputs)
    by_section = jnp.stack([jnp.where(section == 0, kept, sent), jnp.where(section == 0, sent, kept)])
    everything = lax.all_gather(by_section, "gx", axis=0)
    stat_kept, stat_sent = to_section(statistics)
    stat_both = jnp.stack(
        [jnp.where(section == 0, stat_kept, stat_sent), jnp.where(section == 0, stat_sent, stat_kept)]
    )
    every_stat = lax.all_gather(stat_both, "gx", axis=0)
    owner = jnp.sum(jnp.where(dealing == shard, jnp.arange(shards), 0))
    halves = lax.dynamic_slice(
        everything, ((owner // 2) * 2, owner % 2, 0, 0), (2, 1, half, width)
    )
    layer_out = join_halves(halves[0, 0], halves[1, 0])
    stat_halves = lax.dynamic_slice(every_stat, ((owner // 2) * 2, owner % 2, 0, 0), (2, 1, 2, half))
    stats_out = join_halves(stat_halves[0, 0].T, stat_halves[1, 0].T).T

    tall_out = (True, True, False, True, False)
    dm = (d_out.astype(F32) * valid).astype(BF)
    e1, gain_m1, dg, du = mlp_backward(dm, gains1[1], mlp1, saved_m1, 4)
    n2, hidden, n1, heads = saved_m1[2], saved_m1[5], saved_a1[2], saved_a1[6]
    products1 = [shard_product(*p) for p in ((n2, dg, True), (n2, du, True), (dm, hidden, False))]
    d_qkv = attention_backward(e1, attn1, *rope, saved_a1)
    grad1, gain_a1 = attention_end(
        d_qkv, e1, attn1, gains1[0], saved_a1, 5, products1 if fused() else ()
    )
    products1 += [shard_product(n1, d_qkv, True), shard_product(e1, heads, False)]
    local1 = [shard_sum(*p) for p in zip(products1, tall_out)]

    dm = (grad1.astype(F32) * valid).astype(BF)
    deps = products1[3:] + local1[:2]
    e1, gain_m0, dg, du = mlp_backward(dm, gains0[1], mlp0, saved_m0, 6, deps)
    n2, hidden, n1, heads = saved_m0[2], saved_m0[5], saved_a0[2], saved_a0[6]
    products0 = [shard_product(*p) for p in ((n2, dg, True), (n2, du, True), (dm, hidden, False))]
    d_qkv = attention_backward(e1, attn0, *rope, saved_a0)
    products0 += [shard_product(n1, d_qkv, True), shard_product(e1, heads, False)]
    local0 = [shard_sum(*p) for p in zip(products0, tall_out)]
    grad0, gain_a0 = attention_end(
        d_qkv, e1, attn0, gains0[0], saved_a0, 7, products0 + local1[2:]
    )
    gain_sums = [jnp.stack([gain_a0, gain_m0]), jnp.stack([gain_a1, gain_m1])]
    input_grads = [lax.dynamic_slice_in_dim(x, column * width, width, 1) for x in (grad0, grad1)]
    received0 = [lax.ppermute(g, "section", [(1, 0)]) for g in local0]
    received1 = [lax.ppermute(g, "section", [(0, 1)]) for g in local1]
    totals = [
        jnp.where(section == 0, a0.astype(F32) + r0.astype(F32), a1.astype(F32) + r1.astype(F32))
        for a0, r0, a1, r1 in zip(local0, received0, local1, received1)
    ]
    s_gate, s_up, s_down, s_attn, s_out = totals
    q_width = w_query.shape[2]
    kv_width = w_key.shape[2]

    def spread(part):
        blank = jnp.zeros((part.shape[0], kv_width), F32)
        return lax.dynamic_update_slice_in_dim(blank, part, kv_head * HD, 1)

    kv_sum = lax.psum(
        jnp.stack([spread(s_attn[:, q_width : q_width + HD]), spread(s_attn[:, q_width + HD : q_width + 2 * HD])]).astype(BF),
        "gy",
    ).astype(F32)
    gains = jnp.stack(gain_sums)
    if fused():
        gains = lax.psum(gains, ("section", "gx", "gy")) * 0.5
    else:
        gains = lax.psum(gains, ("section", "gx"))
    gains = lax.dynamic_index_in_dim(gains, section, 0, keepdims=False)
    part = attn_gain.shape[1]
    gains = lax.dynamic_slice_in_dim(gains, shard * part, part, 1)

    kept, sent = to_section(input_grads)
    keep = jnp.where(core == section, kept, sent)
    give = swap_pairs(jnp.where(core == section, sent, kept), "gx")
    back_home = join_halves(jnp.where(core == 0, keep, give), jnp.where(core == 0, give, keep))
    return (
        layer_out[None],
        stats_out[None],
        back_home[None],
        gains[None, 0],
        s_attn[None, :, :q_width],
        kv_sum[None, 0],
        kv_sum[None, 1],
        s_out[None],
        gains[None, 1],
        s_gate[None],
        s_up[None],
        s_down[None],
    )


def solution(mesh):
    rows_cols = P("section", "gx", "gy")
    cols_rows = P("section", "gy", "gx")
    rows_only = P("section", "gx", None)
    gain = P("section", "gx")
    return jax.shard_map(
        on_device,
        mesh=mesh,
        in_specs=(
            P("gx", "gy"), P("gx", "gy"), P(), P(), gain, rows_cols, rows_only, rows_only,
            cols_rows, gain, rows_cols, rows_cols, cols_rows,
        ),
        out_specs=(
            rows_cols, P("section", None, "gx"), rows_cols, gain, rows_cols, rows_only, rows_only,
            cols_rows, gain, rows_cols, rows_cols, cols_rows,
        ),
        check_vma=False,
    )
```

```python
import functools

import jax
import jax.numpy as jnp
from jax import lax
from jax.experimental import pallas as pl
from jax.experimental.pallas import tpu as pltpu
from jax.sharding import PartitionSpec as P

QH = 32
KVH = 4
HD = 64
LAYERS = 2
EPS = 1e-05
BF = jnp.bfloat16
F32 = jnp.float32
MESH = pl.DeviceIdType.MESH
CHUNK = 32
STEPS = 2
VMEM_LIMIT = 56 * 1024 * 1024
ANY = pl.BlockSpec(memory_space=pl.ANY)
VMEM = pl.BlockSpec(memory_space=pltpu.VMEM)


def mm(left, right, dims=((1,), (0,))):
    return lax.dot_general(left, right, (dims, ((), ())), preferred_element_type=F32)


def swap_pairs(values, axis, by=1):
    count = lax.axis_size(axis)
    return lax.ppermute(values, axis, [(i, i ^ by) for i in range(count)])


def rope_tables(places):
    half_width = HD // 2
    frequency = jnp.power(10000.0, -2.0 * jnp.arange(half_width).astype(F32) / HD)
    angles = frequency[:, None] * places.astype(F32)[None, :]
    return jnp.cos(angles), jnp.sin(angles)


def core_rows(rows, core):
    quarter = rows.shape[0] // 4
    low = lax.dynamic_slice_in_dim(rows, core * quarter, quarter, 0)
    high = lax.dynamic_slice_in_dim(rows, (3 - core) * quarter, quarter, 0)
    return jnp.concatenate([low, high], axis=0)


def join_halves(first, second):
    quarter = first.shape[0] // 2
    return jnp.concatenate(
        [first[:quarter], second[:quarter], second[quarter:], first[quarter:]], axis=0
    )


def chip_groups():
    return [[0, 2], [1, 3]]


def gather_blocks(base):
    return lax.all_gather(base, "gx", axis=0)


def chosen(pair, layer):
    return jnp.where(lax.axis_index("section") == layer, *pair)


def fused():
    return lax.axis_size("gx") == 4 and lax.axis_size("gy") == 4


def tall(w):
    return w.reshape(-1, w.shape[-1])


def side(w):
    return jnp.concatenate([w[i] for i in range(w.shape[0])], axis=1)


def cut(w, low, high):
    return w[:, :, low:high]


def shard_sum(product):
    return lax.psum_scatter(product, "gx", scatter_dimension=0, tiled=True)


def chip_sum(product):
    product = product.reshape(-1, product.shape[-1])
    return lax.psum_scatter(
        product, "gx", scatter_dimension=0, tiled=True, axis_index_groups=[[0, 2], [1, 3]]
    )


def chip_sum_permuted(product):
    y = lax.axis_index("gx") // 2
    kept = lax.dynamic_index_in_dim(product, y, 0, keepdims=False)
    sent = lax.dynamic_index_in_dim(product, 1 - y, 0, keepdims=False)
    return (kept.astype(F32) + swap_pairs(sent, "gx", 2).astype(F32)).astype(BF)


def rope_down(values, cosine, sines):
    half_width = HD // 2
    first, second = values[:half_width], values[half_width:]
    return jnp.concatenate(
        [first * cosine - second * sines, second * cosine + first * sines], axis=0
    )


def fill_bias(bias_ref, key_ref, query_ref, length_ref):
    keys = key_ref[...]
    allowed = (keys <= query_ref[...]) & (keys < length_ref[...])
    bias_ref[...] = jnp.where(allowed, 0.0, -1e30)


def dot_to(left, right, dims):
    return lax.dot_general(left, right, (dims, ((), ())), preferred_element_type=F32)


def attend_kernel(
    q_ref, k_ref, vt_ref, cos_ref, sin_ref, key_ref, query_ref, length_ref,
    heads_ref, rot_ref, lse_ref, bias_ref, out_ref,
):
    fill_bias(bias_ref, key_ref, query_ref, length_ref)

    def head(h, carry):
        here = pl.ds(pl.multiple_of(h * HD, HD), HD)
        rotated = rope_down(q_ref[here, :], cos_ref[...], sin_ref[...]).astype(BF)
        rot_ref[here, :] = rotated
        scaled = (rotated.astype(F32) * HD ** (-0.5)).astype(BF)
        scores = dot_to(k_ref[...], scaled, ((1,), (0,))) + bias_ref[...]
        top = jnp.max(scores, axis=0, keepdims=True)
        exponent = jnp.exp(scores - top)
        total = jnp.sum(exponent, axis=0, keepdims=True)
        probs = (exponent * (1.0 / total)).astype(BF)
        out_ref[here, :] = dot_to(vt_ref[...], probs, ((1,), (0,)))
        lse_ref[pl.ds(h, 1), :] = top + jnp.log(total)
        return carry

    lax.fori_loop(0, q_ref.shape[0] // HD, head, 0)
    heads_ref[...] = out_ref[...].T.astype(BF)


def attend_back_kernel(
    rot_ref, k_ref, kt_ref, v_ref, d_ref, lse_ref, cos_ref, sin_ref, key_ref, query_ref, length_ref,
    dq_ref, dk_ref, dv_ref, bias_ref, out_ref,
):
    fill_bias(bias_ref, key_ref, query_ref, length_ref)
    dk_ref[...] = jnp.zeros_like(dk_ref)
    dv_ref[...] = jnp.zeros_like(dv_ref)
    scaling = HD ** (-0.5)

    def head(h, carry):
        here = pl.ds(pl.multiple_of(h * HD, HD), HD)
        scaled = (rot_ref[here, :].astype(F32) * scaling).astype(BF)
        scores = dot_to(k_ref[...], scaled, ((1,), (0,))) + bias_ref[...]
        probs = jnp.exp(scores - lse_ref[pl.ds(h, 1), :])
        d_probs = dot_to(v_ref[...], d_ref[here, :], ((1,), (0,)))
        delta = jnp.sum(probs * d_probs, axis=0, keepdims=True)
        d_scores = (probs * (d_probs - delta)).astype(BF)
        dk_ref[...] += dot_to(d_scores, scaled, ((1,), (1,)))
        dv_ref[...] += dot_to(probs.astype(BF), d_ref[here, :], ((1,), (1,)))
        dq = dot_to(kt_ref[...], d_scores, ((1,), (0,))) * scaling
        out_ref[here, :] = rope_down(dq, cos_ref[...], -sin_ref[...])
        return carry

    lax.fori_loop(0, rot_ref.shape[0] // HD, head, 0)
    dq_ref[...] = out_ref[...].T.astype(BF)


def attend(q_down, k_all, v_all, tables):
    cosine, sines, keys_at, places, length = tables
    width, rows = q_down.shape
    return pl.pallas_call(
        attend_kernel,
        out_shape=(
            jax.ShapeDtypeStruct((rows, width), BF),
            jax.ShapeDtypeStruct((width, rows), BF),
            jax.ShapeDtypeStruct((width // HD, rows), F32),
        ),
        in_specs=[VMEM] * 8,
        out_specs=(VMEM,) * 3,
        scratch_shapes=[pltpu.VMEM((k_all.shape[0], rows), F32), pltpu.VMEM((width, rows), F32)],
        compiler_params=pltpu.CompilerParams(vmem_limit_bytes=VMEM_LIMIT),
        cost_estimate=pl.CostEstimate(
            flops=16 * width * rows * k_all.shape[0], bytes_accessed=60_000_000, transcendentals=0
        ),
        name="attend",
    )(q_down, k_all, v_all.T, cosine, sines, keys_at[:, None], places[None], length)


def attend_back(rotated, k_all, v_all, d_down, lse, tables):
    cosine, sines, keys_at, places, length = tables
    width, rows = rotated.shape
    return pl.pallas_call(
        attend_back_kernel,
        out_shape=(
            jax.ShapeDtypeStruct((rows, width), BF),
            jax.ShapeDtypeStruct(k_all.shape, F32),
            jax.ShapeDtypeStruct(k_all.shape, F32),
        ),
        in_specs=[VMEM] * 11,
        out_specs=(VMEM,) * 3,
        scratch_shapes=[pltpu.VMEM((k_all.shape[0], rows), F32), pltpu.VMEM((width, rows), F32)],
        compiler_params=pltpu.CompilerParams(vmem_limit_bytes=VMEM_LIMIT),
        cost_estimate=pl.CostEstimate(
            flops=40 * width * rows * k_all.shape[0], bytes_accessed=80_000_000, transcendentals=0
        ),
        name="attend_back",
    )(
        rotated, k_all, k_all.T, v_all, d_down, lse, cosine, sines,
        keys_at[:, None], places[None], length,
    )


def line_kernel(
    kind, masked, low, high, deps, gathers, layer,
    gain_ref, resid_ref, valid_ref, h_ref, square_ref, *rest,
):
    forward = kind in ("out", "mlp")
    wide = kind in ("mlp", "mlp_back")
    if kind == "mlp":
        lhs_refs = []
    elif kind == "mlp_back":
        lhs_refs, rest = rest[:4], rest[4:]
    else:
        lhs_refs, rest = rest[:1], rest[1:]
    w_count = 3 if wide else 1
    w_refs, rest = rest[:w_count], rest[w_count + deps :]
    base_refs, rest = rest[: 2 * gathers], rest[2 * gathers :]
    out_ref, rest = rest[0], rest[1:]
    if kind == "mlp":
        normed_ref, ms_ref, gate_ref, up_ref, hidden_ref = rest[:5]
        rest = rest[5:]
    elif kind == "mlp_back":
        product_refs, rest = rest[:3], rest[3:]
    block_refs, rest = rest[:gathers], rest[gathers:]
    w_alls, rest = rest[:w_count], rest[w_count:]
    (
        part, from_end, from_mid, pair,
        w_sem, up_send, up_recv, mid_send, mid_recv, fin_send, fin_recv,
    ) = rest[:11]
    if gathers:
        own_sem, far_send, far_recv, near_send, near_recv = rest[11:]
    if kind == "mlp_back":
        (
            d_gate_ref, d_up_ref, far_normed, far_dm, far_hidden, far_d_gate, far_d_up, stage,
            give_sem, take_sem, stage_sem,
        ) = rest[11:]
    shard = lax.axis_index("gx")
    far, near = shard ^ 2, shard ^ 1
    rows, width = resid_ref.shape
    columns = width // 4
    count = rows // CHUNK
    z = lax.axis_index("gy")
    middle = (z == 1) | (z == 2)
    end_of = jnp.where(z == 1, 0, 3)
    mid_of = jnp.where(z == 0, 1, 2)
    across = 3 - z

    loads = []
    for w in range(w_count):
        for j in range(4):
            source = w_refs[w].at[j] if wide else w_refs[w].at[j, :, low:high]
            split = wide and w < 2
            target = w_alls[w].at[j * columns : (j + 1) * columns, :] if split else w_alls[w].at[j]
            loads.append(pltpu.make_async_copy(source, target, w_sem.at[4 * w + j]))
    for load in loads:
        load.start()

    barrier = pltpu.get_barrier_semaphore()
    peers = [far, near] if gathers else [near] if kind == "mlp_back" else []
    beside = len(peers)
    if peers:
        for peer in peers:
            pl.semaphore_signal(barrier, inc=1, device_id={"gx": peer}, device_id_type=MESH)

    @pl.when(middle)
    def _():
        pl.semaphore_signal(barrier, inc=1, device_id={"gy": end_of}, device_id_type=MESH)
        pl.semaphore_signal(barrier, inc=1, device_id={"gy": across}, device_id_type=MESH)
        pl.semaphore_wait(barrier, 2 + beside)

    @pl.when(jnp.logical_not(middle))
    def _():
        pl.semaphore_signal(barrier, inc=1, device_id={"gy": mid_of}, device_id_type=MESH)
        pl.semaphore_wait(barrier, 1 + beside)

    def own_copy(k, source):
        return pltpu.make_async_copy(source, block_refs[k].at[shard], own_sem.at[k])

    def far_copy(k, source):
        return pltpu.make_async_remote_copy(
            src_ref=source, dst_ref=block_refs[k].at[shard], send_sem=far_send.at[k],
            recv_sem=far_recv.at[k], device_id={"gx": far}, device_id_type=MESH,
        )

    def near_copy(k, source):
        return pltpu.make_async_remote_copy(
            src_ref=source, dst_ref=block_refs[k].at[shard], send_sem=near_send.at[2 * k],
            recv_sem=near_recv.at[2 * k], device_id={"gx": near}, device_id_type=MESH,
        )

    def pass_copy(k):
        return pltpu.make_async_remote_copy(
            src_ref=block_refs[k].at[far], dst_ref=block_refs[k].at[far],
            send_sem=near_send.at[2 * k + 1], recv_sem=near_recv.at[2 * k + 1],
            device_id={"gx": near}, device_id_type=MESH,
        )

    def gather_start(k):
        at_home = lax.axis_index("section") == layer
        for ref, holds in zip(base_refs[2 * k : 2 * k + 2], (at_home, jnp.logical_not(at_home))):

            @pl.when(holds)
            def _():
                far_copy(k, ref).start()
                near_copy(k, ref).start()
                own_copy(k, ref).start()

    def gather_pass(k):
        far_copy(k, base_refs[2 * k]).wait_recv()
        pass_copy(k).start()

    for k in range(gathers):
        gather_start(k)

    half = rows // STEPS
    core = lax.rem(shard, 2)

    def give(slot, source, target):
        return pltpu.make_async_remote_copy(
            src_ref=source, dst_ref=target, send_sem=give_sem.at[slot],
            recv_sem=take_sem.at[slot], device_id={"gx": near}, device_id_type=MESH,
        )

    def chip_columns(ref, y, of):
        return ref.at[:, pl.ds(pl.multiple_of((2 * y + of) * columns, columns), columns)]

    def step_rows(ref, step):
        return ref.at[pl.ds(pl.multiple_of(step * half, half), half), :]

    if kind == "mlp_back":
        saved_gate, saved_up, saved_normed, saved_hidden = lhs_refs
        early = [give(0, saved_hidden, far_hidden)]
        for y in range(2):
            early.append(give(1 + y, chip_columns(resid_ref, y, 1 - core), far_dm.at[y]))
        for y in range(2):
            early.append(give(3 + y, chip_columns(saved_normed, y, 1 - core), far_normed.at[y]))
        for copy in early:
            copy.start()

    def give_step(step):
        return [
            give(5 + step, step_rows(d_gate_ref, step), step_rows(far_d_gate, step)),
            give(5 + STEPS + step, step_rows(d_up_ref, step), step_rows(far_d_up, step)),
        ]

    for load in loads:
        load.wait()

    def at(ref, i):
        return ref.at[pl.ds(pl.multiple_of(i * CHUNK, CHUNK), CHUNK), :]

    def up_copy(i):
        return pltpu.make_async_remote_copy(
            src_ref=at(part, i), dst_ref=at(from_end, i), send_sem=up_send.at[i],
            recv_sem=up_recv.at[i], device_id={"gy": mid_of}, device_id_type=MESH,
        )

    def mid_copy(i):
        return pltpu.make_async_remote_copy(
            src_ref=at(pair, i), dst_ref=at(from_mid, i), send_sem=mid_send.at[i],
            recv_sem=mid_recv.at[i], device_id={"gy": across}, device_id_type=MESH,
        )

    def fin_copy(i):
        return pltpu.make_async_remote_copy(
            src_ref=at(out_ref, i), dst_ref=at(out_ref, i), send_sem=fin_send.at[i],
            recv_sem=fin_recv.at[i], device_id={"gy": end_of}, device_id_type=MESH,
        )

    def dot(left, right, transposed=False):
        dims = (((1,), (1 if transposed else 0,)), ((), ()))
        return lax.dot_general(left, right, dims, preferred_element_type=F32)

    def spans(extent):
        return [(x, min(x + 512, extent)) for x in range(0, extent, 512)]

    if wide:
        w_gate, w_up, w_down = w_alls

    def product(step, carry):
        here = pl.ds(pl.multiple_of(step * half, half), half)
        if kind == "mlp":
            values = resid_ref[here, :].astype(F32)
            square = jnp.mean(values * values, axis=1, keepdims=True)
            ms_ref[here, :] = square
            normed_ref[here, :] = (values * lax.rsqrt(square + EPS) * gain_ref[...]).astype(BF)
            for x0, x1 in spans(w_gate.shape[1]):
                gate = dot(normed_ref[here, :], w_gate[:, x0:x1])
                up = dot(normed_ref[here, :], w_up[:, x0:x1])
                gate_ref[here, x0:x1] = gate.astype(BF)
                up_ref[here, x0:x1] = up.astype(BF)
                hidden_ref[here, x0:x1] = (gate * jax.nn.sigmoid(gate) * up).astype(BF)
        if kind == "mlp_back":
            for x0, x1 in spans(w_gate.shape[1]):
                d_hidden = sum(
                    dot(resid_ref[here, j * columns : (j + 1) * columns], w_down[j, x0:x1, :], True)
                    for j in range(4)
                )
                gate = saved_gate[here, x0:x1].astype(F32)
                up = saved_up[here, x0:x1].astype(F32)
                sigmoid = jax.nn.sigmoid(gate)
                d_up_ref[here, x0:x1] = (d_hidden * (gate * sigmoid)).astype(BF)
                d_gate_ref[here, x0:x1] = (
                    d_hidden * up * sigmoid * (1.0 + gate * (1.0 - sigmoid))
                ).astype(BF)
            for copy in give_step(step):
                copy.start()
        for j in range(4):
            span = slice(j * columns, (j + 1) * columns)
            if kind == "out":
                value = dot(lhs_refs[0][here, :], w_alls[0][j])
            elif kind == "mlp":
                value = dot(hidden_ref[here, :], w_down[j])
            elif kind == "mlp_back":
                value = dot(d_gate_ref[here, :], w_gate[span, :], True)
                value += dot(d_up_ref[here, :], w_up[span, :], True)
            else:
                value = dot(lhs_refs[0][here, :], w_alls[0][j], True)
            part[here, span] = value.astype(BF)

        @pl.when(jnp.logical_not(middle))
        def _():
            def send(i, inner):
                up_copy(step * (count // STEPS) + i).start()
                return inner

            lax.fori_loop(0, count // STEPS, send, 0)

        return carry

    lax.fori_loop(0, STEPS, product, 0)

    def finish(i):
        mid_copy(i).wait_recv()
        here = pl.ds(pl.multiple_of(i * CHUNK, CHUNK), CHUNK)
        total = pair[here, :].astype(F32) + from_mid[here, :].astype(F32)
        resid = resid_ref[here, :].astype(F32)
        if forward:
            result = resid + total
            if masked:
                result = result * valid_ref[here, :]
        else:
            values = h_ref[here, :].astype(F32)
            scaled = total * gain_ref[...]
            ratio = lax.rsqrt(square_ref[here, :] + EPS)
            mean_term = jnp.sum(scaled * values, axis=1, keepdims=True) * (1.0 / width)
            result = resid + ratio * scaled - values * (ratio * ratio * ratio) * mean_term
        out_ref[here, :] = result.astype(BF)
        fin_copy(i).start()

    tile = columns // 2

    def stage_copy(number, sub, slot):
        target = product_refs[number].at[sub // 2, pl.ds(pl.multiple_of(sub % 2 * tile, tile), tile), :]
        return pltpu.make_async_copy(stage.at[slot], target, stage_sem.at[slot])

    def gradient_tile(number, sub):
        slot = sub % 2
        left, far_left, right, far_right = (
            (resid_ref, far_dm, saved_hidden, far_hidden),
            (saved_normed, far_normed, d_gate_ref, far_d_gate),
            (saved_normed, far_normed, d_up_ref, far_d_up),
        )[number]

        @pl.when(sub == 0)
        def _():
            waits = [early[:3], early[3:] + give_all[:STEPS], give_all[STEPS:]][number]
            for copy in waits:
                copy.wait_recv()

        @pl.when((sub >= 2) | (number > 0))
        def _():
            stage_copy(number, sub, slot).wait()

        start = (sub // 2 * 2 + core) * columns + sub % 2 * tile
        mine = left[:, pl.ds(pl.multiple_of(start, tile), tile)]
        theirs = far_left[sub // 2, :, pl.ds(pl.multiple_of(sub % 2 * tile, tile), tile)]
        value = dot_to(mine, right[...], ((0,), (0,))) + dot_to(theirs, far_right[...], ((0,), (0,)))
        stage[slot] = value.astype(BF)
        stage_copy(number, sub, slot).start()

    if kind == "mlp_back":
        give_all = [x for pair in zip(*(give_step(n) for n in range(STEPS))) for x in pair]

    def beside_step(i):
        pass_on(i)
        if kind == "mlp_back":
            for number in range(3):
                first = 3 + 4 * number

                @pl.when((i >= first) & (i < first + 4))
                def _():
                    gradient_tile(number, i - first)

    def pass_on(i):
        for k in range(gathers - 1):

            @pl.when(i == (k + 1) * count // gathers)
            def _():
                gather_pass(k)

    @pl.when(middle)
    def _():
        def step(i, carry):
            up_copy(i).wait_recv()
            here = pl.ds(pl.multiple_of(i * CHUNK, CHUNK), CHUNK)
            pair[here, :] = (part[here, :].astype(F32) + from_end[here, :].astype(F32)).astype(BF)
            mid_copy(i).start()

            @pl.when(i >= 1)
            def _():
                finish(i - 1)

            beside_step(i)
            return carry

        lax.fori_loop(0, count, step, 0)
        finish(count - 1)

        def drain(i, carry):
            mid_copy(i).wait_send()
            fin_copy(i).wait_send()
            return carry

        lax.fori_loop(0, count, drain, 0)

    @pl.when(jnp.logical_not(middle))
    def _():
        def drain(i, carry):
            up_copy(i).wait_send()
            fin_copy(i).wait_recv()
            beside_step(i)
            return carry

        lax.fori_loop(0, count, drain, 0)

    if kind == "mlp_back":
        for slot in range(2):
            stage_copy(2, 2 + slot, slot).wait()
        for copy in early + give_all:
            copy.wait_send()
    if gathers:
        gather_pass(gathers - 1)
    for k in range(gathers):
        own_copy(k, base_refs[2 * k]).wait()
        far_copy(k, base_refs[2 * k]).wait_send()
        near_copy(k, base_refs[2 * k]).wait()
        pass_copy(k).wait()


def line_sum(kind, ident, resid, weights, lhs=(), gain=None, valid=None, back=None, low=0, high=0, deps=(), bases=(), layer=0):
    rows, width = resid.shape
    one = jnp.ones((rows, 1), F32)
    h, square = back if back is not None else (jnp.zeros((16, 128), BF), jnp.zeros((8, 1), F32))
    gain = jnp.zeros((width,), F32) if gain is None else gain
    wide = kind in ("mlp", "mlp_back")
    hidden = weights[0].shape[2] if wide else 0
    w_scratch = []
    for i, w in enumerate(weights):
        _, depth, across = w.shape
        if wide and i < 2:
            w_scratch.append(pltpu.VMEM((width, across), BF))
        else:
            w_scratch.append(pltpu.VMEM((4, depth, across if wide else high - low), BF))
    outs, products, beside = [((rows, width), BF)], [], []
    if kind == "mlp":
        outs += [((rows, width), BF), ((rows, 1), F32)] + [((rows, hidden), BF)] * 3
    elif kind == "mlp_back":
        products = [((2, width // 4, hidden), BF)] * 3
        half_block = pltpu.VMEM((2, rows, width // 4), BF)
        beside = [pltpu.VMEM((rows, hidden), BF)] * 2 + [half_block] * 2
        beside += [pltpu.VMEM((rows, hidden), BF)] * 3 + [pltpu.VMEM((2, width // 8, hidden), BF)]
        beside += [pltpu.SemaphoreType.DMA((n,)) for n in (5 + 2 * STEPS, 5 + 2 * STEPS, 2)]
    blocks = [((4,) + base[0].shape, BF) for base in bases]
    pairs = [x for base in bases for x in base]
    depth = 3 * hidden if wide else lhs[0].shape[1]
    count = rows // CHUNK
    dma = pltpu.SemaphoreType.DMA
    return pl.pallas_call(
        functools.partial(
            line_kernel, kind, valid is not None, low, high, len(deps), len(bases), layer
        ),
        out_shape=tuple(jax.ShapeDtypeStruct(*o) for o in outs + products + blocks),
        in_specs=[VMEM] * (5 + len(lhs)) + [ANY] * (len(weights) + len(deps) + len(pairs)),
        out_specs=tuple([VMEM] * len(outs) + [ANY] * len(products + blocks)),
        scratch_shapes=w_scratch
        + [pltpu.VMEM((rows, width), BF)] * 4
        + [dma((4 * len(weights),))]
        + [dma((count,))] * 6
        + [dma((n * len(bases),)) for n in (1, 1, 1, 2, 2) if bases]
        + beside,
        compiler_params=pltpu.CompilerParams(
            collective_id=ident, has_side_effects=True, vmem_limit_bytes=VMEM_LIMIT
        ),
        cost_estimate=pl.CostEstimate(
            flops=2 * rows * depth * width, bytes_accessed=200 * 1024 * 1024, transcendentals=0
        ),
        name="line_" + kind,
    )(gain[None], resid, one if valid is None else valid, h, square, *lhs, *weights, *deps, *pairs)


def plain_sum(total):
    return lax.psum(total.astype(BF), "gy").astype(F32)


def normed(h, gain):
    values = h.astype(F32)
    square = jnp.mean(values * values, axis=1, keepdims=True)
    return square, (values * lax.rsqrt(square + EPS) * gain).astype(BF)


def norm_back(d_normed, h, square, gain):
    values = h.astype(F32)
    ratio = lax.rsqrt(square + EPS)
    scaled = d_normed * gain
    mean_term = jnp.mean(scaled * values, axis=1, keepdims=True)
    return ratio * scaled - values * (ratio * ratio * ratio) * mean_term


def attention_forward(h, gain, w_attn, low, tables, ident, bases, layer, deps=()):
    rows, width = h.shape
    high = low + width // lax.axis_size("gx")
    q_width = low - 2 * HD
    cosine, sines = tables[:2]
    square, n1 = normed(h, gain)
    q_down = mm(tall(cut(w_attn, 0, q_width)), n1, ((0,), (1,)))
    kv = mm(n1, tall(cut(w_attn, q_width, low)))
    k_rot = rope_down(kv[:, :HD].T, cosine, sines).T.astype(BF)
    kv = jnp.concatenate([k_rot, kv[:, HD:].astype(BF)], axis=1)
    kv_all = jnp.concatenate([kv, swap_pairs(kv, "gx")], axis=0)
    k_all, v_all = kv_all[:, :HD], kv_all[:, HD:]
    heads, rotated, lse = attend(q_down, k_all, v_all, tables)
    if fused():
        h1, *blocks = line_sum(
            "out", ident, h, [w_attn], (heads,), low=low, high=high,
            deps=deps, bases=bases, layer=layer,
        )
    else:
        h1 = (h.astype(F32) + plain_sum(mm(heads, side(cut(w_attn, low, high))))).astype(BF)
        blocks = [gather_blocks(chosen(x, layer)) for x in bases]
    return h1, square, blocks, (h, square, n1, rotated, lse, k_all, v_all, heads)


def mlp_forward(h1, gain, weights, valid, ident, bases=(), layer=0):
    if fused():
        result, n2, square, gate, up, hidden, *blocks = line_sum(
            "mlp", ident, h1, weights, gain=gain, valid=valid, bases=bases, layer=layer
        )
    else:
        square, n2 = normed(h1, gain)
        gate = mm(n2, tall(weights[0]))
        up = mm(n2, tall(weights[1]))
        hidden = (gate * jax.nn.sigmoid(gate) * up).astype(BF)
        gate, up = gate.astype(BF), up.astype(BF)
        result = h1.astype(F32) + plain_sum(mm(hidden, side(weights[2])))
        result = (result * valid).astype(BF)
        blocks = [gather_blocks(chosen(x, layer)) for x in bases]
    return result, square, blocks, (h1, square, n2, gate, up, hidden)


def mlp_backward(dm, gain, weights, saved, ident, deps=()):
    h1, square, n2, gate, up, hidden = saved
    if fused():
        e1, *products = line_sum(
            "mlp_back", ident, dm, weights, (gate, up, n2, hidden), gain=gain,
            back=(h1, square), deps=deps,
        )
        return e1, products
    gate, up = gate.astype(F32), up.astype(F32)
    d_hidden = mm(dm, side(weights[2]), ((1,), (1,)))
    sigmoid = jax.nn.sigmoid(gate)
    d_gate = (d_hidden * up * sigmoid * (1.0 + gate * (1.0 - sigmoid))).astype(BF)
    d_up = (d_hidden * (gate * sigmoid)).astype(BF)
    total = mm(d_gate, tall(weights[0]), ((1,), (1,))) + mm(d_up, tall(weights[1]), ((1,), (1,)))
    e1 = (dm.astype(F32) + norm_back(plain_sum(total), h1, square, gain)).astype(BF)
    turn = ((0,), (0,))
    products = [mm(dm, hidden, turn), mm(n2, d_gate, turn), mm(n2, d_up, turn)]
    return e1, [p.astype(BF) for p in products]


def attention_backward(e1, w_attn, low, tables, saved):
    h, square, n1, rotated, lse, k_all, v_all, heads = saved
    rows, width = h.shape
    cosine, sines = tables[:2]
    w_o = side(cut(w_attn, low, low + width // lax.axis_size("gx")))
    d_down = mm(w_o, e1, ((1,), (1,))).astype(BF)
    dq, dk, dv = attend_back(rotated, k_all, v_all, d_down, lse, tables)
    dkv = jnp.concatenate([dk, dv], axis=1)
    dkv = dkv[:rows] + swap_pairs(dkv[rows:], "gx")
    dk = rope_down(dkv[:, :HD].T, cosine, -sines).T
    d_qkv = jnp.concatenate([dq, dk.astype(BF), dkv[:, HD:].astype(BF)], axis=1)
    turn = ((0,), (0,))
    return d_qkv, [mm(n1, d_qkv, turn).astype(BF), mm(e1, heads, turn).astype(BF)]


def attention_end(d_qkv, e1, w_attn, gain, saved, ident, deps=()):
    h, square = saved[:2]
    qkv_width = d_qkv.shape[1]
    if fused():
        return line_sum(
            "back", ident, e1, [w_attn], (d_qkv,), gain=gain, back=(h, square),
            low=0, high=qkv_width, deps=deps,
        )[0]
    total = plain_sum(mm(d_qkv, tall(cut(w_attn, 0, qkv_width)), ((1,), (1,))))
    return (e1.astype(F32) + norm_back(total, h, square, gain)).astype(BF)


def on_device(
    hidden_in, out_grad, lengths, dealing, attn_gain, w_query, w_key, w_value, w_out,
    mlp_gain, w_gate, w_up, w_down,
):
    shards = lax.axis_size("gx")
    shard = lax.axis_index("gx")
    section = lax.axis_index("section")
    column = lax.axis_index("gy")
    core = shard % 2
    sequence = (shard // 2) * 2 + section
    span, width = hidden_in.shape
    half = span // 2
    seq_length = lax.dynamic_index_in_dim(lengths, sequence, keepdims=False)

    both = jnp.concatenate([hidden_in, out_grad], axis=1)
    mine = core_rows(both, core)
    theirs = swap_pairs(core_rows(both, 1 - core), "gx")
    mine = jnp.where(core == section, mine, theirs)
    wide = lax.all_gather(mine.reshape(half, 2, width), "gy", axis=2, tiled=True)
    h, d_out = wide[:, 0], wide[:, 1]

    kv_head = column * (w_query.shape[2] // HD) // (QH // KVH)
    low = w_query.shape[2] + 2 * HD
    both_gains = jnp.stack([attn_gain[0], mlp_gain[0]], axis=1)
    attn_own = jnp.concatenate(
        [
            w_query[0],
            lax.dynamic_slice_in_dim(w_key[0], kv_head * HD, HD, 1),
            lax.dynamic_slice_in_dim(w_value[0], kv_head * HD, HD, 1),
            w_out[0],
            jnp.pad(both_gains, ((0, 0), (0, 126))),
        ],
        axis=1,
    )
    own = (attn_own, w_gate[0], w_up[0], w_down[0])
    first = [(array, lax.ppermute(array, "section", [(0, 1)])) for array in own]
    second = [(array, lax.ppermute(array, "section", [(1, 0)])) for array in own]

    def gains_of(w_attn):
        pair = w_attn[:, :, w_attn.shape[2] - 128 : w_attn.shape[2] - 126]
        return pair.reshape(-1, 2).T.astype(F32)

    here = core_rows(jnp.arange(span), core)
    there = core_rows(jnp.arange(span), 1 - core)
    keys_at = jnp.concatenate([here, there])
    valid = (here < seq_length)[:, None].astype(F32)
    tables = (*rope_tables(here), keys_at, here, seq_length.reshape(1, 1))

    attn0, gate0 = gather_blocks(chosen(first[0], 0)), gather_blocks(chosen(first[1], 0))
    gains0 = gains_of(attn0)
    h1, square_a, blocks, saved_a0 = attention_forward(
        h, gains0[0], attn0, low, tables, 0, first[2:], 0, (gate0,)
    )
    mlp0 = [gate0] + blocks
    h, square_m, (attn1, gate1), saved_m0 = mlp_forward(
        h1, gains0[1], mlp0, valid, 1, second[:2], 1
    )
    gains1 = gains_of(attn1)
    outputs, squares = [h], [square_a, square_m]
    h1, square_a, blocks, saved_a1 = attention_forward(
        h, gains1[0], attn1, low, tables, 2, second[2:], 1
    )
    mlp1 = [gate1] + blocks
    h, square_m, _, saved_m1 = mlp_forward(h1, gains1[1], mlp1, valid, 3)
    outputs.append(h)
    squares = jnp.concatenate(squares + [square_a, square_m], axis=1)
    rms = (jnp.sqrt(squares + EPS) * valid).T
    statistics = [rms[:2], rms[2:]]
    outputs = [lax.dynamic_slice_in_dim(x, column * width, width, 1) for x in outputs]

    def to_section(per_layer):
        kept = jnp.where(section == 0, per_layer[0], per_layer[1])
        sent = swap_pairs(jnp.where(section == 0, per_layer[1], per_layer[0]), "section")
        return kept, sent

    kept, sent = to_section(outputs)
    by_section = jnp.stack([jnp.where(section == 0, kept, sent), jnp.where(section == 0, sent, kept)])
    everything = lax.all_gather(by_section, "gx", axis=0)
    stat_kept, stat_sent = to_section(statistics)
    stat_both = jnp.stack(
        [jnp.where(section == 0, stat_kept, stat_sent), jnp.where(section == 0, stat_sent, stat_kept)]
    )
    every_stat = lax.all_gather(stat_both, "gx", axis=0)
    owner = jnp.sum(jnp.where(dealing == shard, jnp.arange(shards), 0))
    halves = lax.dynamic_slice(
        everything, ((owner // 2) * 2, owner % 2, 0, 0), (2, 1, half, width)
    )
    layer_out = join_halves(halves[0, 0], halves[1, 0])
    stat_halves = lax.dynamic_slice(every_stat, ((owner // 2) * 2, owner % 2, 0, 0), (2, 1, 2, half))
    stats_out = join_halves(stat_halves[0, 0].T, stat_halves[1, 0].T).T

    dm = (d_out.astype(F32) * valid).astype(BF)
    e1, products = mlp_backward(dm, gains1[1], mlp1, saved_m1, 4)
    local1 = [chip_sum(p) if fused() else shard_sum(p) for p in products]
    d_qkv, products = attention_backward(e1, attn1, low, tables, saved_a1)
    local1 += [shard_sum(p) for p in products]
    grad1 = attention_end(d_qkv, e1, attn1, gains1[0], saved_a1, 5, products)

    dm = (grad1.astype(F32) * valid).astype(BF)
    e1, products = mlp_backward(dm, gains0[1], mlp0, saved_m0, 6, local1[:2])
    local0 = [chip_sum_permuted(p) if fused() else shard_sum(p) for p in products]
    d_qkv, products = attention_backward(e1, attn0, low, tables, saved_a0)
    local0 += [shard_sum(p) for p in products]
    grad0 = attention_end(d_qkv, e1, attn0, gains0[0], saved_a0, 7, products + local1[2:])

    input_grads = [lax.dynamic_slice_in_dim(x, column * width, width, 1) for x in (grad0, grad1)]
    received0 = [lax.ppermute(g, "section", [(1, 0)]) for g in local0]
    received1 = [lax.ppermute(g, "section", [(0, 1)]) for g in local1]
    totals = [
        jnp.where(section == 0, a0.astype(F32) + r0.astype(F32), a1.astype(F32) + r1.astype(F32))
        for a0, r0, a1, r1 in zip(local0, received0, local1, received1)
    ]
    s_down, s_gate, s_up, s_attn, s_out = totals
    q_width = w_query.shape[2]

    attn_sum = jnp.sum(s_attn * attn_own[:, :low].astype(F32), axis=1)
    mlp_sum = jnp.sum(s_gate * w_gate[0].astype(F32) + s_up * w_up[0].astype(F32), axis=1)
    sums = jnp.pad(jnp.stack([attn_sum, mlp_sum], axis=1), ((0, 0), (0, 126)))
    spread = jnp.concatenate([s_attn[:, q_width:], sums], axis=1).astype(BF)
    spread = lax.all_gather(spread, "gy", axis=0).astype(F32)
    gains = jnp.sum(spread[:, :, 2 * HD : 2 * HD + 2], axis=0).T / both_gains.astype(F32).T
    kv_sum = spread[:, :, : 2 * HD].reshape(KVH, -1, *spread.shape[1:2], 2, HD).sum(axis=1)
    kv_sum = kv_sum.transpose(2, 1, 0, 3).reshape(2, spread.shape[1], KVH * HD)

    kept, sent = to_section(input_grads)
    keep = jnp.where(core == section, kept, sent)
    give = swap_pairs(jnp.where(core == section, sent, kept), "gx")
    back_home = join_halves(jnp.where(core == 0, keep, give), jnp.where(core == 0, give, keep))
    return (
        layer_out[None],
        stats_out[None],
        back_home[None],
        gains[None, 0],
        s_attn[None, :, :q_width],
        kv_sum[None, 0],
        kv_sum[None, 1],
        s_out.T[None],
        gains[None, 1],
        s_gate[None],
        s_up[None],
        s_down.T[None],
    )


def solution(mesh):
    rows_cols = P("section", "gx", "gy")
    cols_rows = P("section", "gy", "gx")
    rows_only = P("section", "gx", None)
    gain = P("section", "gx")
    return jax.shard_map(
        on_device,
        mesh=mesh,
        in_specs=(
            P("gx", "gy"), P("gx", "gy"), P(), P(), gain, rows_cols, rows_only, rows_only,
            cols_rows, gain, rows_cols, rows_cols, cols_rows,
        ),
        out_specs=(
            rows_cols, P("section", None, "gx"), rows_cols, gain, rows_cols, rows_only, rows_only,
            cols_rows, gain, rows_cols, rows_cols, cols_rows,
        ),
        check_vma=False,
    )
```

```python
import functools

import jax
import jax.numpy as jnp
from jax import lax
from jax.experimental import pallas as pl
from jax.experimental.pallas import tpu as pltpu
from jax.sharding import PartitionSpec as P

QH = 32
KVH = 4
HD = 64
LAYERS = 2
EPS = 1e-05
BF = jnp.bfloat16
F32 = jnp.float32
MESH = pl.DeviceIdType.MESH
CHUNK = 16
STEPS = 2
VMEM_LIMIT = 56 * 1024 * 1024
ANY = pl.BlockSpec(memory_space=pl.ANY)
VMEM = pl.BlockSpec(memory_space=pltpu.VMEM)


def mm(left, right, dims=((1,), (0,))):
    return lax.dot_general(left, right, (dims, ((), ())), preferred_element_type=F32)


def swap_pairs(values, axis, by=1):
    count = lax.axis_size(axis)
    return lax.ppermute(values, axis, [(i, i ^ by) for i in range(count)])


def rope_tables(places):
    half_width = HD // 2
    frequency = jnp.power(10000.0, -2.0 * jnp.arange(half_width).astype(F32) / HD)
    angles = frequency[:, None] * places.astype(F32)[None, :]
    return jnp.cos(angles), jnp.sin(angles)


def core_rows(rows, core):
    quarter = rows.shape[0] // 4
    low = lax.dynamic_slice_in_dim(rows, core * quarter, quarter, 0)
    high = lax.dynamic_slice_in_dim(rows, (3 - core) * quarter, quarter, 0)
    return jnp.concatenate([low, high], axis=0)


def join_halves(first, second):
    quarter = first.shape[0] // 2
    return jnp.concatenate(
        [first[:quarter], second[:quarter], second[quarter:], first[quarter:]], axis=0
    )


def chip_groups():
    return [[0, 2], [1, 3]]


def gather_blocks(base):
    return lax.all_gather(base, "gx", axis=0)


def chosen(pair, layer):
    return jnp.where(lax.axis_index("section") == layer, *pair)


def fused():
    return lax.axis_size("gx") == 4 and lax.axis_size("gy") == 4


def tall(w):
    return w.reshape(-1, w.shape[-1])


def side(w):
    return jnp.concatenate([w[i] for i in range(w.shape[0])], axis=1)


def cut(w, low, high):
    return w[:, :, low:high]


def shard_sum(product):
    return lax.psum_scatter(product, "gx", scatter_dimension=0, tiled=True)


def chip_sum(product):
    product = product.reshape(-1, product.shape[-1])
    return lax.psum_scatter(
        product, "gx", scatter_dimension=0, tiled=True, axis_index_groups=[[0, 2], [1, 3]]
    )


def rope_down(values, cosine, sines):
    half_width = HD // 2
    first, second = values[:half_width], values[half_width:]
    return jnp.concatenate(
        [first * cosine - second * sines, second * cosine + first * sines], axis=0
    )


def fill_bias(bias_ref, key_ref, query_ref, length_ref):
    keys = key_ref[...]
    allowed = (keys <= query_ref[...]) & (keys < length_ref[...])
    bias_ref[...] = jnp.where(allowed, 0.0, -1e30)


def dot_to(left, right, dims):
    return lax.dot_general(left, right, (dims, ((), ())), preferred_element_type=F32)


def attend_kernel(
    q_ref, k_ref, vt_ref, cos_ref, sin_ref, key_ref, query_ref, length_ref,
    heads_ref, rot_ref, lse_ref, bias_ref, out_ref,
):
    fill_bias(bias_ref, key_ref, query_ref, length_ref)

    def head(h, carry):
        here = pl.ds(pl.multiple_of(h * HD, HD), HD)
        rotated = rope_down(q_ref[here, :], cos_ref[...], sin_ref[...]).astype(BF)
        rot_ref[here, :] = rotated
        scaled = (rotated.astype(F32) * HD ** (-0.5)).astype(BF)
        scores = dot_to(k_ref[...], scaled, ((1,), (0,))) + bias_ref[...]
        top = jnp.max(scores, axis=0, keepdims=True)
        exponent = jnp.exp(scores - top)
        total = jnp.sum(exponent, axis=0, keepdims=True)
        probs = (exponent * (1.0 / total)).astype(BF)
        out_ref[here, :] = dot_to(vt_ref[...], probs, ((1,), (0,)))
        lse_ref[pl.ds(h, 1), :] = top + jnp.log(total)
        return carry

    lax.fori_loop(0, q_ref.shape[0] // HD, head, 0)
    heads_ref[...] = out_ref[...].T.astype(BF)


def attend_back_kernel(
    rot_ref, k_ref, kt_ref, v_ref, d_ref, lse_ref, cos_ref, sin_ref, key_ref, query_ref, length_ref,
    dq_ref, dk_ref, dv_ref, bias_ref, out_ref,
):
    fill_bias(bias_ref, key_ref, query_ref, length_ref)
    dk_ref[...] = jnp.zeros_like(dk_ref)
    dv_ref[...] = jnp.zeros_like(dv_ref)
    scaling = HD ** (-0.5)

    def head(h, carry):
        here = pl.ds(pl.multiple_of(h * HD, HD), HD)
        scaled = (rot_ref[here, :].astype(F32) * scaling).astype(BF)
        scores = dot_to(k_ref[...], scaled, ((1,), (0,))) + bias_ref[...]
        probs = jnp.exp(scores - lse_ref[pl.ds(h, 1), :])
        d_probs = dot_to(v_ref[...], d_ref[here, :], ((1,), (0,)))
        delta = jnp.sum(probs * d_probs, axis=0, keepdims=True)
        d_scores = (probs * (d_probs - delta)).astype(BF)
        dk_ref[...] += dot_to(d_scores, scaled, ((1,), (1,)))
        dv_ref[...] += dot_to(probs.astype(BF), d_ref[here, :], ((1,), (1,)))
        dq = dot_to(kt_ref[...], d_scores, ((1,), (0,))) * scaling
        out_ref[here, :] = rope_down(dq, cos_ref[...], -sin_ref[...])
        return carry

    lax.fori_loop(0, rot_ref.shape[0] // HD, head, 0)
    dq_ref[...] = out_ref[...].T.astype(BF)


def attend(q_down, k_all, v_all, tables):
    cosine, sines, keys_at, places, length = tables
    width, rows = q_down.shape
    return pl.pallas_call(
        attend_kernel,
        out_shape=(
            jax.ShapeDtypeStruct((rows, width), BF),
            jax.ShapeDtypeStruct((width, rows), BF),
            jax.ShapeDtypeStruct((width // HD, rows), F32),
        ),
        in_specs=[VMEM] * 8,
        out_specs=(VMEM,) * 3,
        scratch_shapes=[pltpu.VMEM((k_all.shape[0], rows), F32), pltpu.VMEM((width, rows), F32)],
        compiler_params=pltpu.CompilerParams(vmem_limit_bytes=VMEM_LIMIT),
        cost_estimate=pl.CostEstimate(
            flops=16 * width * rows * k_all.shape[0], bytes_accessed=60_000_000, transcendentals=0
        ),
        name="attend",
    )(q_down, k_all, v_all.T, cosine, sines, keys_at[:, None], places[None], length)


def attend_back(rotated, k_all, v_all, d_down, lse, tables):
    cosine, sines, keys_at, places, length = tables
    width, rows = rotated.shape
    return pl.pallas_call(
        attend_back_kernel,
        out_shape=(
            jax.ShapeDtypeStruct((rows, width), BF),
            jax.ShapeDtypeStruct(k_all.shape, F32),
            jax.ShapeDtypeStruct(k_all.shape, F32),
        ),
        in_specs=[VMEM] * 11,
        out_specs=(VMEM,) * 3,
        scratch_shapes=[pltpu.VMEM((k_all.shape[0], rows), F32), pltpu.VMEM((width, rows), F32)],
        compiler_params=pltpu.CompilerParams(vmem_limit_bytes=VMEM_LIMIT),
        cost_estimate=pl.CostEstimate(
            flops=40 * width * rows * k_all.shape[0], bytes_accessed=80_000_000, transcendentals=0
        ),
        name="attend_back",
    )(
        rotated, k_all, k_all.T, v_all, d_down, lse, cosine, sines,
        keys_at[:, None], places[None], length,
    )


def line_kernel(
    kind, masked, low, high, deps, gathers, layer, exchange,
    gain_ref, resid_ref, valid_ref, h_ref, square_ref, *rest,
):
    forward = kind in ("out", "mlp")
    wide = kind in ("mlp", "mlp_back")
    if kind == "mlp":
        lhs_refs = []
    elif kind == "mlp_back":
        lhs_refs, rest = rest[:4], rest[4:]
    else:
        lhs_refs, rest = rest[:1], rest[1:]
    w_count = 3 if wide else 1
    w_refs, rest = rest[:w_count], rest[w_count + deps :]
    base_refs, rest = rest[: 2 * gathers], rest[2 * gathers :]
    out_ref, rest = rest[0], rest[1:]
    if kind == "mlp":
        normed_ref, ms_ref, gate_ref, up_ref, hidden_ref = rest[:5]
        rest = rest[5:]
    elif kind == "mlp_back":
        product_refs, rest = rest[:3], rest[3:]
        arrived_refs, rest = rest[:exchange], rest[exchange:]
    block_refs, rest = rest[:gathers], rest[gathers:]
    w_alls, rest = rest[:w_count], rest[w_count:]
    (
        part, from_end, from_mid, pair,
        w_sem, up_send, up_recv, mid_send, mid_recv, fin_send, fin_recv,
    ) = rest[:11]
    if gathers:
        own_sem, far_send, far_recv, near_send, near_recv, cross_send, cross_recv = rest[11:]
    if kind == "mlp_back":
        (
            d_gate_ref, d_up_ref, far_normed, far_dm, far_hidden, far_d_gate, far_d_up, stage,
            give_sem, take_sem, stage_sem,
        ) = rest[11:22]
    if exchange:
        y_send, y_recv = rest[22:]
    shard = lax.axis_index("gx")
    far, near = shard ^ 2, shard ^ 1
    rows, width = resid_ref.shape
    columns = width // 4
    count = rows // CHUNK
    z = lax.axis_index("gy")
    middle = (z == 1) | (z == 2)
    end_of = jnp.where(z == 1, 0, 3)
    mid_of = jnp.where(z == 0, 1, 2)
    across = 3 - z

    loads = []
    for w in range(w_count):
        for j in range(4):
            source = w_refs[w].at[j] if wide else w_refs[w].at[j, :, low:high]
            split = wide and w < 2
            target = w_alls[w].at[j * columns : (j + 1) * columns, :] if split else w_alls[w].at[j]
            loads.append(pltpu.make_async_copy(source, target, w_sem.at[4 * w + j]))
    for load in loads:
        load.start()

    barrier = pltpu.get_barrier_semaphore()
    peers = []
    if gathers:
        peers = [{"gx": far}, {"gx": near}, {"section": 1 - lax.axis_index("section")}]
    elif kind == "mlp_back":
        peers = [{"gx": near}] + [{"gx": far}] * (exchange > 0)
    beside = len(peers)
    for peer in peers:
        pl.semaphore_signal(barrier, inc=1, device_id=peer, device_id_type=MESH)

    @pl.when(middle)
    def _():
        pl.semaphore_signal(barrier, inc=1, device_id={"gy": end_of}, device_id_type=MESH)
        pl.semaphore_signal(barrier, inc=1, device_id={"gy": across}, device_id_type=MESH)
        pl.semaphore_wait(barrier, 2 + beside)

    @pl.when(jnp.logical_not(middle))
    def _():
        pl.semaphore_signal(barrier, inc=1, device_id={"gy": mid_of}, device_id_type=MESH)
        pl.semaphore_wait(barrier, 1 + beside)

    section = lax.axis_index("section")
    x_peer = {"section": 1 - section}

    def half_of(ref, k, which):
        size = base_refs[2 * k].shape[0] // 2
        return ref.at[pl.ds(pl.multiple_of(which * size, 16), size), :]

    def own_copy(k, source):
        return pltpu.make_async_copy(source, block_refs[k].at[shard], own_sem.at[k])

    def far_copy(k, source):
        return pltpu.make_async_remote_copy(
            src_ref=half_of(source, k, section),
            dst_ref=half_of(block_refs[k].at[shard], k, section),
            send_sem=far_send.at[k], recv_sem=far_recv.at[k],
            device_id={"gx": far}, device_id_type=MESH,
        )

    def near_copy(k, source):
        return pltpu.make_async_remote_copy(
            src_ref=source, dst_ref=block_refs[k].at[shard], send_sem=near_send.at[3 * k],
            recv_sem=near_recv.at[3 * k], device_id={"gx": near}, device_id_type=MESH,
        )

    def cross_copy(k):
        rows_here = half_of(block_refs[k].at[far], k, section)
        return pltpu.make_async_remote_copy(
            src_ref=rows_here, dst_ref=rows_here, send_sem=cross_send.at[k],
            recv_sem=cross_recv.at[k], device_id=x_peer, device_id_type=MESH,
        )

    def pass_copy(k, late):
        rows_here = half_of(block_refs[k].at[far], k, 1 - section if late else section)
        return pltpu.make_async_remote_copy(
            src_ref=rows_here, dst_ref=rows_here, send_sem=near_send.at[3 * k + 1 + late],
            recv_sem=near_recv.at[3 * k + 1 + late], device_id={"gx": near}, device_id_type=MESH,
        )

    at_home = section == layer

    def from_base(k, starts):
        for ref, holds in zip(base_refs[2 * k : 2 * k + 2], (at_home, jnp.logical_not(at_home))):

            @pl.when(holds)
            def _():
                for make in starts:
                    make(k, ref).start()

    def gather_middle(k):
        far_copy(k, base_refs[2 * k]).wait_recv()
        cross_copy(k).start()
        pass_copy(k, 0).start()
        if k + 1 < gathers:
            from_base(k + 1, [far_copy])

    def gather_late(k):
        cross_copy(k).wait_recv()
        pass_copy(k, 1).start()

    if gathers:
        from_base(0, [far_copy])
    for k in range(gathers):
        from_base(k, [near_copy, own_copy])

    half = rows // STEPS
    core = lax.rem(shard, 2)

    def give(slot, source, target):
        return pltpu.make_async_remote_copy(
            src_ref=source, dst_ref=target, send_sem=give_sem.at[slot],
            recv_sem=take_sem.at[slot], device_id={"gx": near}, device_id_type=MESH,
        )

    def chip_columns(ref, y, of):
        return ref.at[:, pl.ds(pl.multiple_of((2 * y + of) * columns, columns), columns)]

    def step_rows(ref, step):
        return ref.at[pl.ds(pl.multiple_of(step * half, half), half), :]

    if kind == "mlp_back":
        saved_gate, saved_up, saved_normed, saved_hidden = lhs_refs
        early = [give(0, saved_hidden, far_hidden)]
        for y in range(2):
            early.append(give(1 + y, chip_columns(resid_ref, y, 1 - core), far_dm.at[y]))
        for y in range(2):
            early.append(give(3 + y, chip_columns(saved_normed, y, 1 - core), far_normed.at[y]))
        for copy in early:
            copy.start()

    def give_step(step):
        return [
            give(5 + step, step_rows(d_gate_ref, step), step_rows(far_d_gate, step)),
            give(5 + STEPS + step, step_rows(d_up_ref, step), step_rows(far_d_up, step)),
        ]

    for load in loads:
        load.wait()

    def at(ref, i):
        return ref.at[pl.ds(pl.multiple_of(i * CHUNK, CHUNK), CHUNK), :]

    def up_copy(i):
        return pltpu.make_async_remote_copy(
            src_ref=at(part, i), dst_ref=at(from_end, i), send_sem=up_send.at[i],
            recv_sem=up_recv.at[i], device_id={"gy": mid_of}, device_id_type=MESH,
        )

    def mid_copy(i):
        return pltpu.make_async_remote_copy(
            src_ref=at(pair, i), dst_ref=at(from_mid, i), send_sem=mid_send.at[i],
            recv_sem=mid_recv.at[i], device_id={"gy": across}, device_id_type=MESH,
        )

    def fin_copy(i):
        return pltpu.make_async_remote_copy(
            src_ref=at(out_ref, i), dst_ref=at(out_ref, i), send_sem=fin_send.at[i],
            recv_sem=fin_recv.at[i], device_id={"gy": end_of}, device_id_type=MESH,
        )

    def dot(left, right, transposed=False):
        dims = (((1,), (1 if transposed else 0,)), ((), ()))
        return lax.dot_general(left, right, dims, preferred_element_type=F32)

    def spans(extent):
        return [(x, min(x + 512, extent)) for x in range(0, extent, 512)]

    if wide:
        w_gate, w_up, w_down = w_alls

    def product(step, carry):
        here = pl.ds(pl.multiple_of(step * half, half), half)
        if kind == "mlp":
            values = resid_ref[here, :].astype(F32)
            square = jnp.mean(values * values, axis=1, keepdims=True)
            ms_ref[here, :] = square
            normed_ref[here, :] = (values * lax.rsqrt(square + EPS) * gain_ref[...]).astype(BF)
            for x0, x1 in spans(w_gate.shape[1]):
                gate = dot(normed_ref[here, :], w_gate[:, x0:x1])
                up = dot(normed_ref[here, :], w_up[:, x0:x1])
                gate_ref[here, x0:x1] = gate.astype(BF)
                up_ref[here, x0:x1] = up.astype(BF)
                hidden_ref[here, x0:x1] = (gate * jax.nn.sigmoid(gate) * up).astype(BF)
        if kind == "mlp_back":
            for x0, x1 in spans(w_gate.shape[1]):
                d_hidden = sum(
                    dot(resid_ref[here, j * columns : (j + 1) * columns], w_down[j, x0:x1, :], True)
                    for j in range(4)
                )
                gate = saved_gate[here, x0:x1].astype(F32)
                up = saved_up[here, x0:x1].astype(F32)
                sigmoid = jax.nn.sigmoid(gate)
                d_up_ref[here, x0:x1] = (d_hidden * (gate * sigmoid)).astype(BF)
                d_gate_ref[here, x0:x1] = (
                    d_hidden * up * sigmoid * (1.0 + gate * (1.0 - sigmoid))
                ).astype(BF)
            for copy in give_step(step):
                copy.start()
        for j in range(4):
            span = slice(j * columns, (j + 1) * columns)
            if kind == "out":
                value = dot(lhs_refs[0][here, :], w_alls[0][j])
            elif kind == "mlp":
                value = dot(hidden_ref[here, :], w_down[j])
            elif kind == "mlp_back":
                value = dot(d_gate_ref[here, :], w_gate[span, :], True)
                value += dot(d_up_ref[here, :], w_up[span, :], True)
            else:
                value = dot(lhs_refs[0][here, :], w_alls[0][j], True)
            part[here, span] = value.astype(BF)

        @pl.when(jnp.logical_not(middle))
        def _():
            def send(i, inner):
                up_copy(step * (count // STEPS) + i).start()
                return inner

            lax.fori_loop(0, count // STEPS, send, 0)

        return carry

    lax.fori_loop(0, STEPS, product, 0)

    def finish(i):
        mid_copy(i).wait_recv()
        here = pl.ds(pl.multiple_of(i * CHUNK, CHUNK), CHUNK)
        total = pair[here, :].astype(F32) + from_mid[here, :].astype(F32)
        resid = resid_ref[here, :].astype(F32)
        if forward:
            result = resid + total
            if masked:
                result = result * valid_ref[here, :]
        else:
            values = h_ref[here, :].astype(F32)
            scaled = total * gain_ref[...]
            ratio = lax.rsqrt(square_ref[here, :] + EPS)
            mean_term = jnp.sum(scaled * values, axis=1, keepdims=True) * (1.0 / width)
            result = resid + ratio * scaled - values * (ratio * ratio * ratio) * mean_term
        out_ref[here, :] = result.astype(BF)
        fin_copy(i).start()

    tile = columns // 2

    def tile_rows(sub):
        return pl.ds(pl.multiple_of(sub % 2 * tile, tile), tile)

    def stage_copy(number, sub, slot):
        target = product_refs[number].at[sub // 2, tile_rows(sub), :]
        return pltpu.make_async_copy(stage.at[slot], target, stage_sem.at[slot])

    def y_copy(number, sub, slot):
        return pltpu.make_async_remote_copy(
            src_ref=stage.at[slot], dst_ref=arrived_refs[number].at[tile_rows(sub), :],
            send_sem=y_send.at[2 * number + slot], recv_sem=y_recv.at[2 * number + slot],
            device_id={"gx": far}, device_id_type=MESH,
        )

    def gradient_tile(number, sub):
        slot = sub % 2
        left, far_left, right, far_right = (
            (resid_ref, far_dm, saved_hidden, far_hidden),
            (saved_normed, far_normed, d_gate_ref, far_d_gate),
            (saved_normed, far_normed, d_up_ref, far_d_up),
        )[number]

        @pl.when(sub == 0)
        def _():
            waits = [early[:3], early[3:] + give_all[:STEPS], give_all[STEPS:]][number]
            for copy in waits:
                copy.wait_recv()

        @pl.when(sub >= 2)
        def _():
            if number < exchange:
                y_copy(number, sub, slot).wait_send()
            else:
                stage_copy(number, sub, slot).wait()

        if number > 0:

            @pl.when(sub < 2)
            def _():
                stage_copy(number, sub, slot).wait()

        y = sub // 2
        if number < exchange:
            y = jnp.where(sub < 2, 1 - lax.div(shard, 2), lax.div(shard, 2))
        start = (y * 2 + core) * columns + sub % 2 * tile
        mine = left[:, pl.ds(pl.multiple_of(start, tile), tile)]
        theirs = far_left[y, :, tile_rows(sub)]
        value = dot_to(mine, right[...], ((0,), (0,))) + dot_to(theirs, far_right[...], ((0,), (0,)))
        stage[slot] = value.astype(BF)
        if number < exchange:

            @pl.when(sub < 2)
            def _():
                y_copy(number, sub, slot).start()

            @pl.when(sub >= 2)
            def _():
                stage_copy(number, sub - 2, slot).start()

        else:
            stage_copy(number, sub, slot).start()

    if kind == "mlp_back":
        give_all = [x for pair in zip(*(give_step(n) for n in range(STEPS))) for x in pair]

    def beside_step(i):
        pass_on(i)
        if kind == "mlp_back":
            for number in range(3):
                first = 3 + 4 * number

                @pl.when((i >= 2 * first) & (i < 2 * first + 8) & (i % 2 == 0))
                def _():
                    gradient_tile(number, i // 2 - first)

    def pass_on(i):
        if gathers == 2:

            @pl.when(i == count * 6 // 16)
            def _():
                gather_middle(0)

            @pl.when(i == count * 12 // 16)
            def _():
                gather_late(0)
                gather_middle(1)

    @pl.when(middle)
    def _():
        def step(i, carry):
            up_copy(i).wait_recv()
            here = pl.ds(pl.multiple_of(i * CHUNK, CHUNK), CHUNK)
            pair[here, :] = (part[here, :].astype(F32) + from_end[here, :].astype(F32)).astype(BF)
            mid_copy(i).start()

            @pl.when(i >= 1)
            def _():
                finish(i - 1)

            beside_step(i)
            return carry

        lax.fori_loop(0, count, step, 0)
        finish(count - 1)

        def drain(i, carry):
            mid_copy(i).wait_send()
            fin_copy(i).wait_send()
            return carry

        lax.fori_loop(0, count, drain, 0)

    @pl.when(jnp.logical_not(middle))
    def _():
        def drain(i, carry):
            up_copy(i).wait_send()
            fin_copy(i).wait_recv()
            beside_step(i)
            return carry

        lax.fori_loop(0, count, drain, 0)

    if kind == "mlp_back":
        for slot in range(2):
            stage_copy(2, 2 + slot, slot).wait()
        for copy in early + give_all:
            copy.wait_send()
        for number in range(exchange):
            for slot in range(2):
                y_copy(number, slot, slot).wait_recv()
    if gathers:
        gather_late(1)
    for k in range(gathers):
        own_copy(k, base_refs[2 * k]).wait()
        far_copy(k, base_refs[2 * k]).wait_send()
        near_copy(k, base_refs[2 * k]).wait()
        cross_copy(k).wait_send()
        pass_copy(k, 0).wait()
        pass_copy(k, 1).wait()


def line_sum(kind, ident, resid, weights, lhs=(), gain=None, valid=None, back=None, low=0, high=0, deps=(), bases=(), layer=0, exchange=0):
    rows, width = resid.shape
    one = jnp.ones((rows, 1), F32)
    h, square = back if back is not None else (jnp.zeros((16, 128), BF), jnp.zeros((8, 1), F32))
    gain = jnp.zeros((width,), F32) if gain is None else gain
    wide = kind in ("mlp", "mlp_back")
    hidden = weights[0].shape[2] if wide else 0
    w_scratch = []
    for i, w in enumerate(weights):
        _, depth, across = w.shape
        if wide and i < 2:
            w_scratch.append(pltpu.VMEM((width, across), BF))
        else:
            w_scratch.append(pltpu.VMEM((4, depth, across if wide else high - low), BF))
    outs, products, beside = [((rows, width), BF)], [], []
    if kind == "mlp":
        outs += [((rows, width), BF), ((rows, 1), F32)] + [((rows, hidden), BF)] * 3
    elif kind == "mlp_back":
        products = [((1 if n < exchange else 2, width // 4, hidden), BF) for n in range(3)]
        products += [((width // 4, hidden), BF)] * exchange
        half_block = pltpu.VMEM((2, rows, width // 4), BF)
        beside = [pltpu.VMEM((rows, hidden), BF)] * 2 + [half_block] * 2
        beside += [pltpu.VMEM((rows, hidden), BF)] * 3 + [pltpu.VMEM((2, width // 8, hidden), BF)]
        beside += [pltpu.SemaphoreType.DMA((n,)) for n in (5 + 2 * STEPS, 5 + 2 * STEPS, 2)]
        beside += [pltpu.SemaphoreType.DMA((2 * exchange,))] * 2 * (exchange > 0)
    blocks = [((4,) + base[0].shape, BF) for base in bases]
    pairs = [x for base in bases for x in base]
    depth = 3 * hidden if wide else lhs[0].shape[1]
    count = rows // CHUNK
    dma = pltpu.SemaphoreType.DMA
    return pl.pallas_call(
        functools.partial(
            line_kernel, kind, valid is not None, low, high, len(deps), len(bases), layer, exchange
        ),
        out_shape=tuple(jax.ShapeDtypeStruct(*o) for o in outs + products + blocks),
        in_specs=[VMEM] * (5 + len(lhs)) + [ANY] * (len(weights) + len(deps) + len(pairs)),
        out_specs=tuple([VMEM] * len(outs) + [ANY] * len(products + blocks)),
        scratch_shapes=w_scratch
        + [pltpu.VMEM((rows, width), BF)] * 4
        + [dma((4 * len(weights),))]
        + [dma((count,))] * 6
        + [dma((n * len(bases),)) for n in (1, 1, 1, 3, 3, 1, 1) if bases]
        + beside,
        compiler_params=pltpu.CompilerParams(
            collective_id=ident, has_side_effects=True, vmem_limit_bytes=VMEM_LIMIT
        ),
        cost_estimate=pl.CostEstimate(
            flops=2 * rows * depth * width, bytes_accessed=200 * 1024 * 1024, transcendentals=0
        ),
        name="line_" + kind,
    )(gain[None], resid, one if valid is None else valid, h, square, *lhs, *weights, *deps, *pairs)


def plain_sum(total):
    return lax.psum(total.astype(BF), "gy").astype(F32)


def normed(h, gain):
    values = h.astype(F32)
    square = jnp.mean(values * values, axis=1, keepdims=True)
    return square, (values * lax.rsqrt(square + EPS) * gain).astype(BF)


def norm_back(d_normed, h, square, gain):
    values = h.astype(F32)
    ratio = lax.rsqrt(square + EPS)
    scaled = d_normed * gain
    mean_term = jnp.mean(scaled * values, axis=1, keepdims=True)
    return ratio * scaled - values * (ratio * ratio * ratio) * mean_term


def attention_forward(h, gain, w_attn, low, tables, ident, bases, layer, deps=()):
    rows, width = h.shape
    high = low + width // lax.axis_size("gx")
    q_width = low - 2 * HD
    cosine, sines = tables[:2]
    square, n1 = normed(h, gain)
    q_down = mm(tall(cut(w_attn, 0, q_width)), n1, ((0,), (1,)))
    kv = mm(n1, tall(cut(w_attn, q_width, low)))
    k_rot = rope_down(kv[:, :HD].T, cosine, sines).T.astype(BF)
    kv = jnp.concatenate([k_rot, kv[:, HD:].astype(BF)], axis=1)
    kv_all = jnp.concatenate([kv, swap_pairs(kv, "gx")], axis=0)
    k_all, v_all = kv_all[:, :HD], kv_all[:, HD:]
    heads, rotated, lse = attend(q_down, k_all, v_all, tables)
    if fused():
        h1, *blocks = line_sum(
            "out", ident, h, [w_attn], (heads,), low=low, high=high,
            deps=deps, bases=bases, layer=layer,
        )
    else:
        h1 = (h.astype(F32) + plain_sum(mm(heads, side(cut(w_attn, low, high))))).astype(BF)
        blocks = [gather_blocks(chosen(x, layer)) for x in bases]
    return h1, square, blocks, (h, square, n1, rotated, lse, k_all, v_all, heads)


def mlp_forward(h1, gain, weights, valid, ident, bases=(), layer=0):
    if fused():
        result, n2, square, gate, up, hidden, *blocks = line_sum(
            "mlp", ident, h1, weights, gain=gain, valid=valid, bases=bases, layer=layer
        )
    else:
        square, n2 = normed(h1, gain)
        gate = mm(n2, tall(weights[0]))
        up = mm(n2, tall(weights[1]))
        hidden = (gate * jax.nn.sigmoid(gate) * up).astype(BF)
        gate, up = gate.astype(BF), up.astype(BF)
        result = h1.astype(F32) + plain_sum(mm(hidden, side(weights[2])))
        result = (result * valid).astype(BF)
        blocks = [gather_blocks(chosen(x, layer)) for x in bases]
    return result, square, blocks, (h1, square, n2, gate, up, hidden)


def mlp_backward(dm, gain, weights, saved, ident, deps=(), exchange=0):
    h1, square, n2, gate, up, hidden = saved
    if fused():
        e1, *products = line_sum(
            "mlp_back", ident, dm, weights, (gate, up, n2, hidden), gain=gain,
            back=(h1, square), deps=deps, exchange=exchange,
        )
        return e1, products
    gate, up = gate.astype(F32), up.astype(F32)
    d_hidden = mm(dm, side(weights[2]), ((1,), (1,)))
    sigmoid = jax.nn.sigmoid(gate)
    d_gate = (d_hidden * up * sigmoid * (1.0 + gate * (1.0 - sigmoid))).astype(BF)
    d_up = (d_hidden * (gate * sigmoid)).astype(BF)
    total = mm(d_gate, tall(weights[0]), ((1,), (1,))) + mm(d_up, tall(weights[1]), ((1,), (1,)))
    e1 = (dm.astype(F32) + norm_back(plain_sum(total), h1, square, gain)).astype(BF)
    turn = ((0,), (0,))
    products = [mm(dm, hidden, turn), mm(n2, d_gate, turn), mm(n2, d_up, turn)]
    return e1, [p.astype(BF) for p in products]


def attention_backward(e1, w_attn, low, tables, saved):
    h, square, n1, rotated, lse, k_all, v_all, heads = saved
    rows, width = h.shape
    cosine, sines = tables[:2]
    w_o = side(cut(w_attn, low, low + width // lax.axis_size("gx")))
    d_down = mm(w_o, e1, ((1,), (1,))).astype(BF)
    dq, dk, dv = attend_back(rotated, k_all, v_all, d_down, lse, tables)
    dkv = jnp.concatenate([dk, dv], axis=1)
    dkv = dkv[:rows] + swap_pairs(dkv[rows:], "gx")
    dk = rope_down(dkv[:, :HD].T, cosine, -sines).T
    d_qkv = jnp.concatenate([dq, dk.astype(BF), dkv[:, HD:].astype(BF)], axis=1)
    turn = ((0,), (0,))
    products = [mm(n1, d_qkv, turn).astype(BF), mm(e1, heads, turn).astype(BF)]
    return d_qkv, jnp.concatenate(products, axis=1)


def attention_end(d_qkv, e1, w_attn, gain, saved, ident, deps=()):
    h, square = saved[:2]
    qkv_width = d_qkv.shape[1]
    if fused():
        return line_sum(
            "back", ident, e1, [w_attn], (d_qkv,), gain=gain, back=(h, square),
            low=0, high=qkv_width, deps=deps,
        )[0]
    total = plain_sum(mm(d_qkv, tall(cut(w_attn, 0, qkv_width)), ((1,), (1,))))
    return (e1.astype(F32) + norm_back(total, h, square, gain)).astype(BF)


def on_device(
    hidden_in, out_grad, lengths, dealing, attn_gain, w_query, w_key, w_value, w_out,
    mlp_gain, w_gate, w_up, w_down,
):
    shards = lax.axis_size("gx")
    shard = lax.axis_index("gx")
    section = lax.axis_index("section")
    column = lax.axis_index("gy")
    core = shard % 2
    sequence = (shard // 2) * 2 + section
    span, width = hidden_in.shape
    half = span // 2
    seq_length = lax.dynamic_index_in_dim(lengths, sequence, keepdims=False)

    both = jnp.concatenate([hidden_in, out_grad], axis=1)
    mine = core_rows(both, core)
    theirs = swap_pairs(core_rows(both, 1 - core), "gx")
    mine = jnp.where(core == section, mine, theirs)
    h = lax.all_gather(mine[:, :width], "gy", axis=1, tiled=True)

    kv_head = column * (w_query.shape[2] // HD) // (QH // KVH)
    low = w_query.shape[2] + 2 * HD
    both_gains = jnp.stack([attn_gain[0], mlp_gain[0]], axis=1)
    attn_own = jnp.concatenate(
        [
            w_query[0],
            lax.dynamic_slice_in_dim(w_key[0], kv_head * HD, HD, 1),
            lax.dynamic_slice_in_dim(w_value[0], kv_head * HD, HD, 1),
            w_out[0],
            jnp.pad(both_gains, ((0, 0), (0, 126))),
        ],
        axis=1,
    )
    own = (attn_own, w_gate[0], w_up[0], w_down[0])
    first = [(array, lax.ppermute(array, "section", [(0, 1)])) for array in own]
    second = [(array, lax.ppermute(array, "section", [(1, 0)])) for array in own]

    def gains_of(w_attn):
        pair = w_attn[:, :, w_attn.shape[2] - 128 : w_attn.shape[2] - 126]
        return pair.reshape(-1, 2).T.astype(F32)

    here = core_rows(jnp.arange(span), core)
    there = core_rows(jnp.arange(span), 1 - core)
    keys_at = jnp.concatenate([here, there])
    valid = (here < seq_length)[:, None].astype(F32)
    tables = (*rope_tables(here), keys_at, here, seq_length.reshape(1, 1))

    attn0, gate0 = gather_blocks(chosen(first[0], 0)), gather_blocks(chosen(first[1], 0))
    gains0 = gains_of(attn0)
    h1, square_a, blocks, saved_a0 = attention_forward(
        h, gains0[0], attn0, low, tables, 0, first[2:], 0, (gate0,)
    )
    mlp0 = [gate0] + blocks
    h, square_m, (attn1, gate1), saved_m0 = mlp_forward(
        h1, gains0[1], mlp0, valid, 1, second[:2], 1
    )
    gains1 = gains_of(attn1)
    outputs, squares = [h], [square_a, square_m]
    d_mine = mine[:, width:] + h[:1, :1] * 0
    d_out = lax.all_gather(d_mine, "gy", axis=1, tiled=True)
    h1, square_a, blocks, saved_a1 = attention_forward(
        h, gains1[0], attn1, low, tables, 2, second[2:], 1
    )
    mlp1 = [gate1] + blocks
    h, square_m, _, saved_m1 = mlp_forward(h1, gains1[1], mlp1, valid, 3)
    outputs.append(h)
    squares = jnp.concatenate(squares + [square_a, square_m], axis=1)
    rms = (jnp.sqrt(squares + EPS) * valid).T
    statistics = [rms[:2], rms[2:]]
    outputs = [lax.dynamic_slice_in_dim(x, column * width, width, 1) for x in outputs]

    def to_section(per_layer):
        kept = jnp.where(section == 0, per_layer[0], per_layer[1])
        sent = swap_pairs(jnp.where(section == 0, per_layer[1], per_layer[0]), "section")
        return kept, sent

    kept, sent = to_section(outputs)
    by_section = jnp.stack([jnp.where(section == 0, kept, sent), jnp.where(section == 0, sent, kept)])
    everything = lax.all_gather(by_section, "gx", axis=0)
    stat_kept, stat_sent = to_section(statistics)
    stat_both = jnp.stack(
        [jnp.where(section == 0, stat_kept, stat_sent), jnp.where(section == 0, stat_sent, stat_kept)]
    )
    every_stat = lax.all_gather(stat_both, "gx", axis=0)
    owner = jnp.sum(jnp.where(dealing == shard, jnp.arange(shards), 0))
    halves = lax.dynamic_slice(
        everything, ((owner // 2) * 2, owner % 2, 0, 0), (2, 1, half, width)
    )
    layer_out = join_halves(halves[0, 0], halves[1, 0])
    stat_halves = lax.dynamic_slice(every_stat, ((owner // 2) * 2, owner % 2, 0, 0), (2, 1, 2, half))
    stats_out = join_halves(stat_halves[0, 0].T, stat_halves[1, 0].T).T

    dm = (d_out.astype(F32) * valid).astype(BF)
    e1, products = mlp_backward(dm, gains1[1], mlp1, saved_m1, 4)
    products = [p + everything[0, 0, :1, :1] * 0 for p in products]
    local1 = [chip_sum(p) if fused() else shard_sum(p) for p in products]
    d_qkv, products = attention_backward(e1, attn1, low, tables, saved_a1)
    local1.append(shard_sum(products))
    grad1 = attention_end(d_qkv, e1, attn1, gains1[0], saved_a1, 5, (products,))

    received1 = [lax.ppermute(g, "section", [(0, 1)]) for g in local1]

    dm = (grad1.astype(F32) * valid).astype(BF)
    e1, products = mlp_backward(dm, gains0[1], mlp0, saved_m0, 6, local1[:2], 1)
    if fused():
        down, gate, up, arrived = products
        local0 = [(down[0].astype(F32) + arrived.astype(F32)).astype(BF)]
        local0 += [chip_sum(gate), chip_sum(up)]
    else:
        local0 = [shard_sum(p) for p in products]
    d_qkv, products = attention_backward(e1, attn0, low, tables, saved_a0)
    local0.append(shard_sum(products))
    grad0 = attention_end(d_qkv, e1, attn0, gains0[0], saved_a0, 7, [products] + received1[:2] + local1[2:])

    input_grads = [lax.dynamic_slice_in_dim(x, column * width, width, 1) for x in (grad0, grad1)]
    received0 = [lax.ppermute(g, "section", [(1, 0)]) for g in local0]
    totals = [
        jnp.where(section == 0, a0.astype(F32) + r0.astype(F32), a1.astype(F32) + r1.astype(F32))
        for a0, r0, a1, r1 in zip(local0, received0, local1, received1)
    ]
    s_down, s_gate, s_up, s_attn = totals
    s_out = s_attn[:, low:]
    q_width = w_query.shape[2]

    attn_sum = jnp.sum(s_attn[:, :low] * attn_own[:, :low].astype(F32), axis=1)
    mlp_sum = jnp.sum(s_gate * w_gate[0].astype(F32) + s_up * w_up[0].astype(F32), axis=1)
    sums = jnp.pad(jnp.stack([attn_sum, mlp_sum], axis=1), ((0, 0), (0, 126)))
    spread = jnp.concatenate([s_attn[:, q_width:low], sums], axis=1).astype(BF)
    spread = lax.all_gather(spread, "gy", axis=0).astype(F32)
    gains = jnp.sum(spread[:, :, 2 * HD : 2 * HD + 2], axis=0).T / both_gains.astype(F32).T
    kv_sum = spread[:, :, : 2 * HD].reshape(KVH, -1, *spread.shape[1:2], 2, HD).sum(axis=1)
    kv_sum = kv_sum.transpose(2, 1, 0, 3).reshape(2, spread.shape[1], KVH * HD)

    kept, sent = to_section(input_grads)
    keep = jnp.where(core == section, kept, sent)
    give = swap_pairs(jnp.where(core == section, sent, kept), "gx")
    back_home = join_halves(jnp.where(core == 0, keep, give), jnp.where(core == 0, give, keep))
    return (
        layer_out[None],
        stats_out[None],
        back_home[None],
        gains[None, 0],
        s_attn[None, :, :q_width],
        kv_sum[None, 0],
        kv_sum[None, 1],
        s_out.T[None],
        gains[None, 1],
        s_gate[None],
        s_up[None],
        s_down.T[None],
    )


def solution(mesh):
    rows_cols = P("section", "gx", "gy")
    cols_rows = P("section", "gy", "gx")
    rows_only = P("section", "gx", None)
    gain = P("section", "gx")
    return jax.shard_map(
        on_device,
        mesh=mesh,
        in_specs=(
            P("gx", "gy"), P("gx", "gy"), P(), P(), gain, rows_cols, rows_only, rows_only,
            cols_rows, gain, rows_cols, rows_cols, cols_rows,
        ),
        out_specs=(
            rows_cols, P("section", None, "gx"), rows_cols, gain, rows_cols, rows_only, rows_only,
            cols_rows, gain, rows_cols, rows_cols, cols_rows,
        ),
        check_vma=False,
    )
```

```python
import functools

import jax
import jax.numpy as jnp
from jax import lax
from jax.experimental import pallas as pl
from jax.experimental.pallas import tpu as pltpu
from jax.sharding import PartitionSpec as P

QH = 32
KVH = 4
HD = 64
LAYERS = 2
EPS = 1e-05
BF = jnp.bfloat16
F32 = jnp.float32
MESH = pl.DeviceIdType.MESH
CHUNK = 32
STEPS = 2
VMEM_LIMIT = 56 * 1024 * 1024
ANY = pl.BlockSpec(memory_space=pl.ANY)
VMEM = pl.BlockSpec(memory_space=pltpu.VMEM)


def mm(left, right, dims=((1,), (0,))):
    return lax.dot_general(left, right, (dims, ((), ())), preferred_element_type=F32)


def swap_pairs(values, axis, by=1):
    count = lax.axis_size(axis)
    return lax.ppermute(values, axis, [(i, i ^ by) for i in range(count)])


def rope_tables(places):
    half_width = HD // 2
    frequency = jnp.power(10000.0, -2.0 * jnp.arange(half_width).astype(F32) / HD)
    angles = frequency[:, None] * places.astype(F32)[None, :]
    return jnp.cos(angles), jnp.sin(angles)


def core_rows(rows, core):
    quarter = rows.shape[0] // 4
    low = lax.dynamic_slice_in_dim(rows, core * quarter, quarter, 0)
    high = lax.dynamic_slice_in_dim(rows, (3 - core) * quarter, quarter, 0)
    return jnp.concatenate([low, high], axis=0)


def join_halves(first, second):
    quarter = first.shape[0] // 2
    return jnp.concatenate(
        [first[:quarter], second[:quarter], second[quarter:], first[quarter:]], axis=0
    )


def chip_groups():
    return [[0, 2], [1, 3]]


def gather_blocks(base):
    return lax.all_gather(base, "gx", axis=0)


def chosen(pair, layer):
    return jnp.where(lax.axis_index("section") == layer, *pair)


def fused():
    return lax.axis_size("gx") == 4 and lax.axis_size("gy") == 4


def tall(w):
    return w.reshape(-1, w.shape[-1])


def side(w):
    return jnp.concatenate([w[i] for i in range(w.shape[0])], axis=1)


def cut(w, low, high):
    return w[:, :, low:high]


def shard_sum(product):
    return lax.psum_scatter(product, "gx", scatter_dimension=0, tiled=True)


def chip_sum(product):
    product = product.reshape(-1, product.shape[-1])
    return lax.psum_scatter(
        product, "gx", scatter_dimension=0, tiled=True, axis_index_groups=[[0, 2], [1, 3]]
    )


def rope_down(values, cosine, sines):
    half_width = HD // 2
    first, second = values[:half_width], values[half_width:]
    return jnp.concatenate(
        [first * cosine - second * sines, second * cosine + first * sines], axis=0
    )


def fill_bias(bias_ref, key_ref, query_ref, length_ref):
    keys = key_ref[...]
    allowed = (keys <= query_ref[...]) & (keys < length_ref[...])
    bias_ref[...] = jnp.where(allowed, 0.0, -1e30)


def dot_to(left, right, dims):
    return lax.dot_general(left, right, (dims, ((), ())), preferred_element_type=F32)


def attend_kernel(
    q_ref, k_ref, vt_ref, cos_ref, sin_ref, key_ref, query_ref, length_ref,
    heads_ref, rot_ref, lse_ref, bias_ref, out_ref,
):
    fill_bias(bias_ref, key_ref, query_ref, length_ref)

    def head(h, carry):
        here = pl.ds(pl.multiple_of(h * HD, HD), HD)
        rotated = rope_down(q_ref[here, :], cos_ref[...], sin_ref[...]).astype(BF)
        rot_ref[here, :] = rotated
        scaled = (rotated.astype(F32) * HD ** (-0.5)).astype(BF)
        scores = dot_to(k_ref[...], scaled, ((1,), (0,))) + bias_ref[...]
        top = jnp.max(scores, axis=0, keepdims=True)
        exponent = jnp.exp(scores - top)
        total = jnp.sum(exponent, axis=0, keepdims=True)
        probs = (exponent * (1.0 / total)).astype(BF)
        out_ref[here, :] = dot_to(vt_ref[...], probs, ((1,), (0,)))
        lse_ref[pl.ds(h, 1), :] = top + jnp.log(total)
        return carry

    lax.fori_loop(0, q_ref.shape[0] // HD, head, 0)
    heads_ref[...] = out_ref[...].T.astype(BF)


def attend_back_kernel(
    rot_ref, k_ref, kt_ref, v_ref, d_ref, lse_ref, cos_ref, sin_ref, key_ref, query_ref, length_ref,
    dq_ref, dk_ref, dv_ref, bias_ref, out_ref,
):
    fill_bias(bias_ref, key_ref, query_ref, length_ref)
    dk_ref[...] = jnp.zeros_like(dk_ref)
    dv_ref[...] = jnp.zeros_like(dv_ref)
    scaling = HD ** (-0.5)

    def head(h, carry):
        here = pl.ds(pl.multiple_of(h * HD, HD), HD)
        scaled = (rot_ref[here, :].astype(F32) * scaling).astype(BF)
        scores = dot_to(k_ref[...], scaled, ((1,), (0,))) + bias_ref[...]
        probs = jnp.exp(scores - lse_ref[pl.ds(h, 1), :])
        d_probs = dot_to(v_ref[...], d_ref[here, :], ((1,), (0,)))
        delta = jnp.sum(probs * d_probs, axis=0, keepdims=True)
        d_scores = (probs * (d_probs - delta)).astype(BF)
        dk_ref[...] += dot_to(d_scores, scaled, ((1,), (1,)))
        dv_ref[...] += dot_to(probs.astype(BF), d_ref[here, :], ((1,), (1,)))
        dq = dot_to(kt_ref[...], d_scores, ((1,), (0,))) * scaling
        out_ref[here, :] = rope_down(dq, cos_ref[...], -sin_ref[...])
        return carry

    lax.fori_loop(0, rot_ref.shape[0] // HD, head, 0)
    dq_ref[...] = out_ref[...].T.astype(BF)


def attend(q_down, k_all, v_all, tables):
    cosine, sines, keys_at, places, length = tables
    width, rows = q_down.shape
    return pl.pallas_call(
        attend_kernel,
        out_shape=(
            jax.ShapeDtypeStruct((rows, width), BF),
            jax.ShapeDtypeStruct((width, rows), BF),
            jax.ShapeDtypeStruct((width // HD, rows), F32),
        ),
        in_specs=[VMEM] * 8,
        out_specs=(VMEM,) * 3,
        scratch_shapes=[pltpu.VMEM((k_all.shape[0], rows), F32), pltpu.VMEM((width, rows), F32)],
        compiler_params=pltpu.CompilerParams(vmem_limit_bytes=VMEM_LIMIT),
        cost_estimate=pl.CostEstimate(
            flops=16 * width * rows * k_all.shape[0], bytes_accessed=60_000_000, transcendentals=0
        ),
        name="attend",
    )(q_down, k_all, v_all.T, cosine, sines, keys_at[:, None], places[None], length)


def attend_back(rotated, k_all, v_all, d_down, lse, tables):
    cosine, sines, keys_at, places, length = tables
    width, rows = rotated.shape
    return pl.pallas_call(
        attend_back_kernel,
        out_shape=(
            jax.ShapeDtypeStruct((rows, width), BF),
            jax.ShapeDtypeStruct(k_all.shape, F32),
            jax.ShapeDtypeStruct(k_all.shape, F32),
        ),
        in_specs=[VMEM] * 11,
        out_specs=(VMEM,) * 3,
        scratch_shapes=[pltpu.VMEM((k_all.shape[0], rows), F32), pltpu.VMEM((width, rows), F32)],
        compiler_params=pltpu.CompilerParams(vmem_limit_bytes=VMEM_LIMIT),
        cost_estimate=pl.CostEstimate(
            flops=40 * width * rows * k_all.shape[0], bytes_accessed=80_000_000, transcendentals=0
        ),
        name="attend_back",
    )(
        rotated, k_all, k_all.T, v_all, d_down, lse, cosine, sines,
        keys_at[:, None], places[None], length,
    )


def line_kernel(
    kind, masked, low, high, deps, gathers, layer, exchange,
    gain_ref, resid_ref, valid_ref, h_ref, square_ref, *rest,
):
    forward = kind in ("out", "mlp")
    wide = kind in ("mlp", "mlp_back")
    if kind == "mlp":
        lhs_refs = []
    elif kind == "mlp_back":
        lhs_refs, rest = rest[:4], rest[4:]
    else:
        lhs_refs, rest = rest[:1], rest[1:]
    w_count = 3 if wide else 1
    w_refs, rest = rest[:w_count], rest[w_count + deps :]
    base_refs, rest = rest[: 2 * gathers], rest[2 * gathers :]
    out_ref, rest = rest[0], rest[1:]
    if kind == "mlp":
        normed_ref, ms_ref, gate_ref, up_ref, hidden_ref = rest[:5]
        rest = rest[5:]
    elif kind == "mlp_back":
        product_refs, rest = rest[:3], rest[3:]
        arrived_refs, rest = rest[:exchange], rest[exchange:]
    block_refs, rest = rest[:gathers], rest[gathers:]
    w_alls, rest = rest[:w_count], rest[w_count:]
    (
        part, from_end, from_mid, pair,
        w_sem, up_send, up_recv, mid_send, mid_recv, fin_send, fin_recv,
    ) = rest[:11]
    if gathers:
        own_sem, far_send, far_recv, near_send, near_recv, cross_send, cross_recv = rest[11:]
    if kind == "mlp_back":
        (
            d_gate_ref, d_up_ref, far_normed, far_dm, far_hidden, far_d_gate, far_d_up, stage,
            give_sem, take_sem, stage_sem,
        ) = rest[11:22]
    if exchange:
        y_stage, y_send, y_recv = rest[22:]
    shard = lax.axis_index("gx")
    far, near = shard ^ 2, shard ^ 1
    rows, width = resid_ref.shape
    columns = width // 4
    count = rows // CHUNK
    z = lax.axis_index("gy")
    middle = (z == 1) | (z == 2)
    end_of = jnp.where(z == 1, 0, 3)
    mid_of = jnp.where(z == 0, 1, 2)
    across = 3 - z

    loads = []
    for w in range(w_count):
        for j in range(4):
            source = w_refs[w].at[j] if wide else w_refs[w].at[j, :, low:high]
            split = wide and w < 2
            target = w_alls[w].at[j * columns : (j + 1) * columns, :] if split else w_alls[w].at[j]
            loads.append(pltpu.make_async_copy(source, target, w_sem.at[4 * w + j]))
    for load in loads:
        load.start()

    barrier = pltpu.get_barrier_semaphore()
    peers = []
    if gathers:
        peers = [{"gx": far}, {"gx": near}, {"section": 1 - lax.axis_index("section")}]
    elif kind == "mlp_back":
        peers = [{"gx": near}] + [{"gx": far}] * (exchange > 0)
    beside = len(peers)
    for peer in peers:
        pl.semaphore_signal(barrier, inc=1, device_id=peer, device_id_type=MESH)

    @pl.when(middle)
    def _():
        pl.semaphore_signal(barrier, inc=1, device_id={"gy": end_of}, device_id_type=MESH)
        pl.semaphore_signal(barrier, inc=1, device_id={"gy": across}, device_id_type=MESH)
        pl.semaphore_wait(barrier, 2 + beside)

    @pl.when(jnp.logical_not(middle))
    def _():
        pl.semaphore_signal(barrier, inc=1, device_id={"gy": mid_of}, device_id_type=MESH)
        pl.semaphore_wait(barrier, 1 + beside)

    section = lax.axis_index("section")
    x_peer = {"section": 1 - section}

    def half_of(ref, k, which):
        size = base_refs[2 * k].shape[0] // 2
        return ref.at[pl.ds(pl.multiple_of(which * size, 16), size), :]

    def own_copy(k, source):
        return pltpu.make_async_copy(source, block_refs[k].at[shard], own_sem.at[k])

    def far_copy(k, source):
        return pltpu.make_async_remote_copy(
            src_ref=half_of(source, k, section),
            dst_ref=half_of(block_refs[k].at[shard], k, section),
            send_sem=far_send.at[k], recv_sem=far_recv.at[k],
            device_id={"gx": far}, device_id_type=MESH,
        )

    def near_copy(k, source):
        return pltpu.make_async_remote_copy(
            src_ref=source, dst_ref=block_refs[k].at[shard], send_sem=near_send.at[3 * k],
            recv_sem=near_recv.at[3 * k], device_id={"gx": near}, device_id_type=MESH,
        )

    def cross_copy(k):
        rows_here = half_of(block_refs[k].at[far], k, section)
        return pltpu.make_async_remote_copy(
            src_ref=rows_here, dst_ref=rows_here, send_sem=cross_send.at[k],
            recv_sem=cross_recv.at[k], device_id=x_peer, device_id_type=MESH,
        )

    def pass_copy(k, late):
        rows_here = half_of(block_refs[k].at[far], k, 1 - section if late else section)
        return pltpu.make_async_remote_copy(
            src_ref=rows_here, dst_ref=rows_here, send_sem=near_send.at[3 * k + 1 + late],
            recv_sem=near_recv.at[3 * k + 1 + late], device_id={"gx": near}, device_id_type=MESH,
        )

    at_home = section == layer

    def from_base(k, starts):
        for ref, holds in zip(base_refs[2 * k : 2 * k + 2], (at_home, jnp.logical_not(at_home))):

            @pl.when(holds)
            def _():
                for make in starts:
                    make(k, ref).start()

    def gather_middle(k):
        far_copy(k, base_refs[2 * k]).wait_recv()
        cross_copy(k).start()
        pass_copy(k, 0).start()
        if k + 1 < gathers:
            from_base(k + 1, [far_copy])

    def gather_late(k):
        cross_copy(k).wait_recv()
        pass_copy(k, 1).start()

    if gathers:
        from_base(0, [far_copy])
    for k in range(gathers):
        from_base(k, [near_copy, own_copy])

    half = rows // STEPS
    core = lax.rem(shard, 2)

    def give(slot, source, target):
        return pltpu.make_async_remote_copy(
            src_ref=source, dst_ref=target, send_sem=give_sem.at[slot],
            recv_sem=take_sem.at[slot], device_id={"gx": near}, device_id_type=MESH,
        )

    def chip_columns(ref, y, of):
        return ref.at[:, pl.ds(pl.multiple_of((2 * y + of) * columns, columns), columns)]

    def step_rows(ref, step):
        return ref.at[pl.ds(pl.multiple_of(step * half, half), half), :]

    if kind == "mlp_back":
        saved_gate, saved_up, saved_normed, saved_hidden = lhs_refs
        early = [give(0, saved_hidden, far_hidden)]
        for y in range(2):
            early.append(give(1 + y, chip_columns(resid_ref, y, 1 - core), far_dm.at[y]))
        for y in range(2):
            early.append(give(3 + y, chip_columns(saved_normed, y, 1 - core), far_normed.at[y]))
        for copy in early:
            copy.start()

    def give_step(step):
        return [
            give(5 + step, step_rows(d_gate_ref, step), step_rows(far_d_gate, step)),
            give(5 + STEPS + step, step_rows(d_up_ref, step), step_rows(far_d_up, step)),
        ]

    for load in loads:
        load.wait()

    def at(ref, i):
        return ref.at[pl.ds(pl.multiple_of(i * CHUNK, CHUNK), CHUNK), :]

    def up_copy(i):
        return pltpu.make_async_remote_copy(
            src_ref=at(part, i), dst_ref=at(from_end, i), send_sem=up_send.at[i],
            recv_sem=up_recv.at[i], device_id={"gy": mid_of}, device_id_type=MESH,
        )

    def mid_copy(i):
        return pltpu.make_async_remote_copy(
            src_ref=at(pair, i), dst_ref=at(from_mid, i), send_sem=mid_send.at[i],
            recv_sem=mid_recv.at[i], device_id={"gy": across}, device_id_type=MESH,
        )

    def fin_copy(i):
        return pltpu.make_async_remote_copy(
            src_ref=at(out_ref, i), dst_ref=at(out_ref, i), send_sem=fin_send.at[i],
            recv_sem=fin_recv.at[i], device_id={"gy": end_of}, device_id_type=MESH,
        )

    def dot(left, right, transposed=False):
        dims = (((1,), (1 if transposed else 0,)), ((), ()))
        return lax.dot_general(left, right, dims, preferred_element_type=F32)

    def spans(extent):
        return [(x, min(x + 512, extent)) for x in range(0, extent, 512)]

    if wide:
        w_gate, w_up, w_down = w_alls

    def product(step, carry):
        here = pl.ds(pl.multiple_of(step * half, half), half)
        if kind == "mlp":
            values = resid_ref[here, :].astype(F32)
            square = jnp.mean(values * values, axis=1, keepdims=True)
            ms_ref[here, :] = square
            normed_ref[here, :] = (values * lax.rsqrt(square + EPS) * gain_ref[...]).astype(BF)
            for x0, x1 in spans(w_gate.shape[1]):
                gate = dot(normed_ref[here, :], w_gate[:, x0:x1])
                up = dot(normed_ref[here, :], w_up[:, x0:x1])
                gate_ref[here, x0:x1] = gate.astype(BF)
                up_ref[here, x0:x1] = up.astype(BF)
                hidden_ref[here, x0:x1] = (gate * jax.nn.sigmoid(gate) * up).astype(BF)
        if kind == "mlp_back":
            for x0, x1 in spans(w_gate.shape[1]):
                d_hidden = sum(
                    dot(resid_ref[here, j * columns : (j + 1) * columns], w_down[j, x0:x1, :], True)
                    for j in range(4)
                )
                gate = saved_gate[here, x0:x1].astype(F32)
                up = saved_up[here, x0:x1].astype(F32)
                sigmoid = jax.nn.sigmoid(gate)
                d_up_ref[here, x0:x1] = (d_hidden * (gate * sigmoid)).astype(BF)
                d_gate_ref[here, x0:x1] = (
                    d_hidden * up * sigmoid * (1.0 + gate * (1.0 - sigmoid))
                ).astype(BF)
            for copy in give_step(step):
                copy.start()
        for j in range(4):
            span = slice(j * columns, (j + 1) * columns)
            if kind == "out":
                value = dot(lhs_refs[0][here, :], w_alls[0][j])
            elif kind == "mlp":
                value = dot(hidden_ref[here, :], w_down[j])
            elif kind == "mlp_back":
                value = dot(d_gate_ref[here, :], w_gate[span, :], True)
                value += dot(d_up_ref[here, :], w_up[span, :], True)
            else:
                value = dot(lhs_refs[0][here, :], w_alls[0][j], True)
            part[here, span] = value.astype(BF)

        @pl.when(jnp.logical_not(middle))
        def _():
            def send(i, inner):
                up_copy(step * (count // STEPS) + i).start()
                return inner

            lax.fori_loop(0, count // STEPS, send, 0)

        return carry

    lax.fori_loop(0, STEPS, product, 0)

    def finish(i):
        mid_copy(i).wait_recv()
        here = pl.ds(pl.multiple_of(i * CHUNK, CHUNK), CHUNK)
        total = pair[here, :].astype(F32) + from_mid[here, :].astype(F32)
        resid = resid_ref[here, :].astype(F32)
        if forward:
            result = resid + total
            if masked:
                result = result * valid_ref[here, :]
        else:
            values = h_ref[here, :].astype(F32)
            scaled = total * gain_ref[...]
            ratio = lax.rsqrt(square_ref[here, :] + EPS)
            mean_term = jnp.sum(scaled * values, axis=1, keepdims=True) * (1.0 / width)
            result = resid + ratio * scaled - values * (ratio * ratio * ratio) * mean_term
        out_ref[here, :] = result.astype(BF)
        fin_copy(i).start()

    tile = columns // 2

    def tile_rows(sub):
        return pl.ds(pl.multiple_of(sub % 2 * tile, tile), tile)

    def stage_copy(number, sub, slot):
        target = product_refs[number].at[sub // 2, tile_rows(sub), :]
        return pltpu.make_async_copy(stage.at[slot], target, stage_sem.at[slot])

    def y_copy(number, sub, slot):
        return pltpu.make_async_remote_copy(
            src_ref=y_stage.at[2 * number + slot], dst_ref=arrived_refs[number].at[tile_rows(sub), :],
            send_sem=y_send.at[2 * number + slot], recv_sem=y_recv.at[2 * number + slot],
            device_id={"gx": far}, device_id_type=MESH,
        )

    def gradient_tile(number, sub):
        slot = sub % 2
        left, far_left, right, far_right = (
            (resid_ref, far_dm, saved_hidden, far_hidden),
            (saved_normed, far_normed, d_gate_ref, far_d_gate),
            (saved_normed, far_normed, d_up_ref, far_d_up),
        )[number]

        @pl.when(sub == 0)
        def _():
            waits = [early[:3], early[3:] + give_all[:STEPS], give_all[STEPS:]][number]
            for copy in waits:
                copy.wait_recv()

        if number >= exchange:

            @pl.when((sub >= 2) | (number > 0))
            def _():
                stage_copy(number, sub, slot).wait()

        elif number > 0:

            @pl.when(sub >= 2)
            def _():
                stage_copy(number, sub - 2, slot).wait()

        y = sub // 2
        if number < exchange:
            y = jnp.where(sub < 2, 1 - lax.div(shard, 2), lax.div(shard, 2))
        start = (y * 2 + core) * columns + sub % 2 * tile
        mine = left[:, pl.ds(pl.multiple_of(start, tile), tile)]
        theirs = far_left[y, :, tile_rows(sub)]
        value = dot_to(mine, right[...], ((0,), (0,))) + dot_to(theirs, far_right[...], ((0,), (0,)))
        if number < exchange:

            @pl.when(sub < 2)
            def _():
                y_stage[2 * number + slot] = value.astype(BF)
                y_copy(number, sub, slot).start()

            @pl.when(sub >= 2)
            def _():
                stage[slot] = value.astype(BF)
                stage_copy(number, sub - 2, slot).start()

        else:
            stage[slot] = value.astype(BF)
            stage_copy(number, sub, slot).start()

    if kind == "mlp_back":
        give_all = [x for pair in zip(*(give_step(n) for n in range(STEPS))) for x in pair]

    def beside_step(i):
        pass_on(i)
        if kind == "mlp_back":
            for number in range(3):
                first = 3 + 4 * number

                @pl.when((i >= first) & (i < first + 4))
                def _():
                    gradient_tile(number, i - first)

    def pass_on(i):
        if gathers == 2:

            @pl.when(i == count * 6 // 16)
            def _():
                gather_middle(0)

            @pl.when(i == count * 12 // 16)
            def _():
                gather_late(0)
                gather_middle(1)

    @pl.when(middle)
    def _():
        def step(i, carry):
            up_copy(i).wait_recv()
            here = pl.ds(pl.multiple_of(i * CHUNK, CHUNK), CHUNK)
            pair[here, :] = (part[here, :].astype(F32) + from_end[here, :].astype(F32)).astype(BF)
            mid_copy(i).start()

            @pl.when(i >= 1)
            def _():
                finish(i - 1)

            beside_step(i)
            return carry

        lax.fori_loop(0, count, step, 0)
        finish(count - 1)

        def drain(i, carry):
            mid_copy(i).wait_send()
            fin_copy(i).wait_send()
            return carry

        lax.fori_loop(0, count, drain, 0)

    @pl.when(jnp.logical_not(middle))
    def _():
        def drain(i, carry):
            up_copy(i).wait_send()
            fin_copy(i).wait_recv()
            beside_step(i)
            return carry

        lax.fori_loop(0, count, drain, 0)

    if kind == "mlp_back":
        for slot in range(2):
            stage_copy(2, 2 + slot, slot).wait()
        for copy in early + give_all:
            copy.wait_send()
        for number in range(exchange):
            for slot in range(2):
                y_copy(number, slot, slot).wait()
    if gathers:
        gather_late(1)
    for k in range(gathers):
        own_copy(k, base_refs[2 * k]).wait()
        far_copy(k, base_refs[2 * k]).wait_send()
        near_copy(k, base_refs[2 * k]).wait()
        cross_copy(k).wait_send()
        pass_copy(k, 0).wait()
        pass_copy(k, 1).wait()


def line_sum(kind, ident, resid, weights, lhs=(), gain=None, valid=None, back=None, low=0, high=0, deps=(), bases=(), layer=0, exchange=0):
    rows, width = resid.shape
    one = jnp.ones((rows, 1), F32)
    h, square = back if back is not None else (jnp.zeros((16, 128), BF), jnp.zeros((8, 1), F32))
    gain = jnp.zeros((width,), F32) if gain is None else gain
    wide = kind in ("mlp", "mlp_back")
    hidden = weights[0].shape[2] if wide else 0
    w_scratch = []
    for i, w in enumerate(weights):
        _, depth, across = w.shape
        if wide and i < 2:
            w_scratch.append(pltpu.VMEM((width, across), BF))
        else:
            w_scratch.append(pltpu.VMEM((4, depth, across if wide else high - low), BF))
    outs, products, beside = [((rows, width), BF)], [], []
    if kind == "mlp":
        outs += [((rows, width), BF), ((rows, 1), F32)] + [((rows, hidden), BF)] * 3
    elif kind == "mlp_back":
        products = [((1 if n < exchange else 2, width // 4, hidden), BF) for n in range(3)]
        products += [((width // 4, hidden), BF)] * exchange
        half_block = pltpu.VMEM((2, rows, width // 4), BF)
        beside = [pltpu.VMEM((rows, hidden), BF)] * 2 + [half_block] * 2
        beside += [pltpu.VMEM((rows, hidden), BF)] * 3 + [pltpu.VMEM((2, width // 8, hidden), BF)]
        beside += [pltpu.SemaphoreType.DMA((n,)) for n in (5 + 2 * STEPS, 5 + 2 * STEPS, 2)]
        if exchange:
            beside += [pltpu.VMEM((2 * exchange, width // 8, hidden), BF)]
            beside += [pltpu.SemaphoreType.DMA((2 * exchange,))] * 2
    blocks = [((4,) + base[0].shape, BF) for base in bases]
    pairs = [x for base in bases for x in base]
    depth = 3 * hidden if wide else lhs[0].shape[1]
    count = rows // CHUNK
    dma = pltpu.SemaphoreType.DMA
    return pl.pallas_call(
        functools.partial(
            line_kernel, kind, valid is not None, low, high, len(deps), len(bases), layer, exchange
        ),
        out_shape=tuple(jax.ShapeDtypeStruct(*o) for o in outs + products + blocks),
        in_specs=[VMEM] * (5 + len(lhs)) + [ANY] * (len(weights) + len(deps) + len(pairs)),
        out_specs=tuple([VMEM] * len(outs) + [ANY] * len(products + blocks)),
        scratch_shapes=w_scratch
        + [pltpu.VMEM((rows, width), BF)] * 4
        + [dma((4 * len(weights),))]
        + [dma((count,))] * 6
        + [dma((n * len(bases),)) for n in (1, 1, 1, 3, 3, 1, 1) if bases]
        + beside,
        compiler_params=pltpu.CompilerParams(
            collective_id=ident, has_side_effects=True, vmem_limit_bytes=VMEM_LIMIT
        ),
        cost_estimate=pl.CostEstimate(
            flops=2 * rows * depth * width, bytes_accessed=200 * 1024 * 1024, transcendentals=0
        ),
        name="line_" + kind,
    )(gain[None], resid, one if valid is None else valid, h, square, *lhs, *weights, *deps, *pairs)


def plain_sum(total):
    return lax.psum(total.astype(BF), "gy").astype(F32)


def normed(h, gain):
    values = h.astype(F32)
    square = jnp.mean(values * values, axis=1, keepdims=True)
    return square, (values * lax.rsqrt(square + EPS) * gain).astype(BF)


def norm_back(d_normed, h, square, gain):
    values = h.astype(F32)
    ratio = lax.rsqrt(square + EPS)
    scaled = d_normed * gain
    mean_term = jnp.mean(scaled * values, axis=1, keepdims=True)
    return ratio * scaled - values * (ratio * ratio * ratio) * mean_term


def attention_forward(h, gain, w_attn, low, tables, ident, bases, layer, deps=()):
    rows, width = h.shape
    high = low + width // lax.axis_size("gx")
    q_width = low - 2 * HD
    cosine, sines = tables[:2]
    square, n1 = normed(h, gain)
    q_down = mm(tall(cut(w_attn, 0, q_width)), n1, ((0,), (1,)))
    kv = mm(n1, tall(cut(w_attn, q_width, low)))
    k_rot = rope_down(kv[:, :HD].T, cosine, sines).T.astype(BF)
    kv = jnp.concatenate([k_rot, kv[:, HD:].astype(BF)], axis=1)
    kv_all = jnp.concatenate([kv, swap_pairs(kv, "gx")], axis=0)
    k_all, v_all = kv_all[:, :HD], kv_all[:, HD:]
    heads, rotated, lse = attend(q_down, k_all, v_all, tables)
    if fused():
        h1, *blocks = line_sum(
            "out", ident, h, [w_attn], (heads,), low=low, high=high,
            deps=deps, bases=bases, layer=layer,
        )
    else:
        h1 = (h.astype(F32) + plain_sum(mm(heads, side(cut(w_attn, low, high))))).astype(BF)
        blocks = [gather_blocks(chosen(x, layer)) for x in bases]
    return h1, square, blocks, (h, square, n1, rotated, lse, k_all, v_all, heads)


def mlp_forward(h1, gain, weights, valid, ident, bases=(), layer=0):
    if fused():
        result, n2, square, gate, up, hidden, *blocks = line_sum(
            "mlp", ident, h1, weights, gain=gain, valid=valid, bases=bases, layer=layer
        )
    else:
        square, n2 = normed(h1, gain)
        gate = mm(n2, tall(weights[0]))
        up = mm(n2, tall(weights[1]))
        hidden = (gate * jax.nn.sigmoid(gate) * up).astype(BF)
        gate, up = gate.astype(BF), up.astype(BF)
        result = h1.astype(F32) + plain_sum(mm(hidden, side(weights[2])))
        result = (result * valid).astype(BF)
        blocks = [gather_blocks(chosen(x, layer)) for x in bases]
    return result, square, blocks, (h1, square, n2, gate, up, hidden)


def mlp_backward(dm, gain, weights, saved, ident, deps=(), exchange=2):
    h1, square, n2, gate, up, hidden = saved
    if fused():
        e1, *products = line_sum(
            "mlp_back", ident, dm, weights, (gate, up, n2, hidden), gain=gain,
            back=(h1, square), deps=deps, exchange=exchange,
        )
        return e1, products
    gate, up = gate.astype(F32), up.astype(F32)
    d_hidden = mm(dm, side(weights[2]), ((1,), (1,)))
    sigmoid = jax.nn.sigmoid(gate)
    d_gate = (d_hidden * up * sigmoid * (1.0 + gate * (1.0 - sigmoid))).astype(BF)
    d_up = (d_hidden * (gate * sigmoid)).astype(BF)
    total = mm(d_gate, tall(weights[0]), ((1,), (1,))) + mm(d_up, tall(weights[1]), ((1,), (1,)))
    e1 = (dm.astype(F32) + norm_back(plain_sum(total), h1, square, gain)).astype(BF)
    turn = ((0,), (0,))
    products = [mm(dm, hidden, turn), mm(n2, d_gate, turn), mm(n2, d_up, turn)]
    return e1, [p.astype(BF) for p in products]


def mlp_sums(products):
    if not fused():
        return [shard_sum(p) for p in products]
    down, gate, up, *arrived = products
    sums = [(x[0].astype(F32) + y.astype(F32)).astype(BF) for x, y in zip((down, gate), arrived)]
    return sums + [chip_sum(up)]


def attention_backward(e1, w_attn, low, tables, saved):
    h, square, n1, rotated, lse, k_all, v_all, heads = saved
    rows, width = h.shape
    cosine, sines = tables[:2]
    w_o = side(cut(w_attn, low, low + width // lax.axis_size("gx")))
    d_down = mm(w_o, e1, ((1,), (1,))).astype(BF)
    dq, dk, dv = attend_back(rotated, k_all, v_all, d_down, lse, tables)
    dkv = jnp.concatenate([dk, dv], axis=1)
    dkv = dkv[:rows] + swap_pairs(dkv[rows:], "gx")
    dk = rope_down(dkv[:, :HD].T, cosine, -sines).T
    d_qkv = jnp.concatenate([dq, dk.astype(BF), dkv[:, HD:].astype(BF)], axis=1)
    turn = ((0,), (0,))
    products = [mm(n1, d_qkv, turn).astype(BF), mm(e1, heads, turn).astype(BF)]
    return d_qkv, jnp.concatenate(products, axis=1)


def attention_end(d_qkv, e1, w_attn, gain, saved, ident, deps=()):
    h, square = saved[:2]
    qkv_width = d_qkv.shape[1]
    if fused():
        return line_sum(
            "back", ident, e1, [w_attn], (d_qkv,), gain=gain, back=(h, square),
            low=0, high=qkv_width, deps=deps,
        )[0]
    total = plain_sum(mm(d_qkv, tall(cut(w_attn, 0, qkv_width)), ((1,), (1,))))
    return (e1.astype(F32) + norm_back(total, h, square, gain)).astype(BF)


def on_device(
    hidden_in, out_grad, lengths, dealing, attn_gain, w_query, w_key, w_value, w_out,
    mlp_gain, w_gate, w_up, w_down,
):
    shards = lax.axis_size("gx")
    shard = lax.axis_index("gx")
    section = lax.axis_index("section")
    column = lax.axis_index("gy")
    core = shard % 2
    sequence = (shard // 2) * 2 + section
    span, width = hidden_in.shape
    half = span // 2
    seq_length = lax.dynamic_index_in_dim(lengths, sequence, keepdims=False)

    both = jnp.concatenate([hidden_in, out_grad], axis=1)
    mine = core_rows(both, core)
    theirs = swap_pairs(core_rows(both, 1 - core), "gx")
    mine = jnp.where(core == section, mine, theirs)
    h = lax.all_gather(mine[:, :width], "gy", axis=1, tiled=True)

    kv_head = column * (w_query.shape[2] // HD) // (QH // KVH)
    low = w_query.shape[2] + 2 * HD
    both_gains = jnp.stack([attn_gain[0], mlp_gain[0]], axis=1)
    attn_own = jnp.concatenate(
        [
            w_query[0],
            lax.dynamic_slice_in_dim(w_key[0], kv_head * HD, HD, 1),
            lax.dynamic_slice_in_dim(w_value[0], kv_head * HD, HD, 1),
            w_out[0],
            jnp.pad(both_gains, ((0, 0), (0, 126))),
        ],
        axis=1,
    )
    own = (attn_own, w_gate[0], w_up[0], w_down[0])
    first = [(array, lax.ppermute(array, "section", [(0, 1)])) for array in own]
    second = [(array, lax.ppermute(array, "section", [(1, 0)])) for array in own]

    def gains_of(w_attn):
        pair = w_attn[:, :, w_attn.shape[2] - 128 : w_attn.shape[2] - 126]
        return pair.reshape(-1, 2).T.astype(F32)

    here = core_rows(jnp.arange(span), core)
    there = core_rows(jnp.arange(span), 1 - core)
    keys_at = jnp.concatenate([here, there])
    valid = (here < seq_length)[:, None].astype(F32)
    tables = (*rope_tables(here), keys_at, here, seq_length.reshape(1, 1))

    attn0, gate0 = gather_blocks(chosen(first[0], 0)), gather_blocks(chosen(first[1], 0))
    gains0 = gains_of(attn0)
    h1, square_a, blocks, saved_a0 = attention_forward(
        h, gains0[0], attn0, low, tables, 0, first[2:], 0, (gate0,)
    )
    mlp0 = [gate0] + blocks
    h, square_m, (attn1, gate1), saved_m0 = mlp_forward(
        h1, gains0[1], mlp0, valid, 1, second[:2], 1
    )
    gains1 = gains_of(attn1)
    outputs, squares = [h], [square_a, square_m]
    d_mine = mine[:, width:] + h[:1, :1] * 0
    d_out = lax.all_gather(d_mine, "gy", axis=1, tiled=True)
    h1, square_a, blocks, saved_a1 = attention_forward(
        h, gains1[0], attn1, low, tables, 2, second[2:], 1
    )
    mlp1 = [gate1] + blocks
    h, square_m, _, saved_m1 = mlp_forward(h1, gains1[1], mlp1, valid, 3)
    outputs.append(h)
    squares = jnp.concatenate(squares + [square_a, square_m], axis=1)
    rms = (jnp.sqrt(squares + EPS) * valid).T
    statistics = [rms[:2], rms[2:]]
    outputs = [lax.dynamic_slice_in_dim(x, column * width, width, 1) for x in outputs]

    def to_section(per_layer):
        kept = jnp.where(section == 0, per_layer[0], per_layer[1])
        sent = swap_pairs(jnp.where(section == 0, per_layer[1], per_layer[0]), "section")
        return kept, sent

    kept, sent = to_section(outputs)
    by_section = jnp.stack([jnp.where(section == 0, kept, sent), jnp.where(section == 0, sent, kept)])
    everything = lax.all_gather(by_section, "gx", axis=0)
    stat_kept, stat_sent = to_section(statistics)
    stat_both = jnp.stack(
        [jnp.where(section == 0, stat_kept, stat_sent), jnp.where(section == 0, stat_sent, stat_kept)]
    )
    every_stat = lax.all_gather(stat_both, "gx", axis=0)
    owner = jnp.sum(jnp.where(dealing == shard, jnp.arange(shards), 0))
    halves = lax.dynamic_slice(
        everything, ((owner // 2) * 2, owner % 2, 0, 0), (2, 1, half, width)
    )
    layer_out = join_halves(halves[0, 0], halves[1, 0])
    stat_halves = lax.dynamic_slice(every_stat, ((owner // 2) * 2, owner % 2, 0, 0), (2, 1, 2, half))
    stats_out = join_halves(stat_halves[0, 0].T, stat_halves[1, 0].T).T

    dm = (d_out.astype(F32) * valid).astype(BF)
    e1, products = mlp_backward(dm, gains1[1], mlp1, saved_m1, 4)
    local1 = mlp_sums(products)
    d_qkv, products = attention_backward(e1, attn1, low, tables, saved_a1)
    local1.append(shard_sum(products))
    grad1 = attention_end(d_qkv, e1, attn1, gains1[0], saved_a1, 5, (products,))

    dm = (grad1.astype(F32) * valid).astype(BF)
    e1, products = mlp_backward(dm, gains0[1], mlp0, saved_m0, 6, local1[:3] + [everything])
    local0 = mlp_sums(products)
    d_qkv, products = attention_backward(e1, attn0, low, tables, saved_a0)
    local0.append(shard_sum(products))
    grad0 = attention_end(d_qkv, e1, attn0, gains0[0], saved_a0, 7, [products, local1[3]] + local0[:2])

    input_grads = [lax.dynamic_slice_in_dim(x, column * width, width, 1) for x in (grad0, grad1)]
    received1 = [lax.ppermute(g, "section", [(0, 1)]) for g in local1]
    received0 = [lax.ppermute(g, "section", [(1, 0)]) for g in local0]
    totals = [
        jnp.where(section == 0, a0.astype(F32) + r0.astype(F32), a1.astype(F32) + r1.astype(F32))
        for a0, r0, a1, r1 in zip(local0, received0, local1, received1)
    ]
    s_down, s_gate, s_up, s_attn = totals
    s_out = s_attn[:, low:]
    q_width = w_query.shape[2]

    attn_sum = jnp.sum(s_attn[:, :low] * attn_own[:, :low].astype(F32), axis=1)
    mlp_sum = jnp.sum(s_gate * w_gate[0].astype(F32) + s_up * w_up[0].astype(F32), axis=1)
    sums = jnp.pad(jnp.stack([attn_sum, mlp_sum], axis=1), ((0, 0), (0, 126)))
    spread = jnp.concatenate([s_attn[:, q_width:low], sums], axis=1).astype(BF)
    spread = lax.all_gather(spread, "gy", axis=0).astype(F32)
    gains = jnp.sum(spread[:, :, 2 * HD : 2 * HD + 2], axis=0).T / both_gains.astype(F32).T
    kv_sum = spread[:, :, : 2 * HD].reshape(KVH, -1, *spread.shape[1:2], 2, HD).sum(axis=1)
    kv_sum = kv_sum.transpose(2, 1, 0, 3).reshape(2, spread.shape[1], KVH * HD)

    kept, sent = to_section(input_grads)
    keep = jnp.where(core == section, kept, sent)
    give = swap_pairs(jnp.where(core == section, sent, kept), "gx")
    back_home = join_halves(jnp.where(core == 0, keep, give), jnp.where(core == 0, give, keep))
    return (
        layer_out[None],
        stats_out[None],
        back_home[None],
        gains[None, 0],
        s_attn[None, :, :q_width],
        kv_sum[None, 0],
        kv_sum[None, 1],
        s_out.T[None],
        gains[None, 1],
        s_gate[None],
        s_up[None],
        s_down.T[None],
    )


def solution(mesh):
    rows_cols = P("section", "gx", "gy")
    cols_rows = P("section", "gy", "gx")
    rows_only = P("section", "gx", None)
    gain = P("section", "gx")
    return jax.shard_map(
        on_device,
        mesh=mesh,
        in_specs=(
            P("gx", "gy"), P("gx", "gy"), P(), P(), gain, rows_cols, rows_only, rows_only,
            cols_rows, gain, rows_cols, rows_cols, cols_rows,
        ),
        out_specs=(
            rows_cols, P("section", None, "gx"), rows_cols, gain, rows_cols, rows_only, rows_only,
            cols_rows, gain, rows_cols, rows_cols, cols_rows,
        ),
        check_vma=False,
    )
```

```python
import functools

import jax
import jax.numpy as jnp
from jax import lax
from jax.experimental import pallas as pl
from jax.experimental.pallas import tpu as pltpu
from jax.sharding import PartitionSpec as P

QH = 32
KVH = 4
HD = 64
LAYERS = 2
EPS = 1e-05
BF = jnp.bfloat16
F32 = jnp.float32
MESH = pl.DeviceIdType.MESH
CHUNK = 32
STEPS = 2
VMEM_LIMIT = 56 * 1024 * 1024
ANY = pl.BlockSpec(memory_space=pl.ANY)
VMEM = pl.BlockSpec(memory_space=pltpu.VMEM)


def mm(left, right, dims=((1,), (0,))):
    return lax.dot_general(left, right, (dims, ((), ())), preferred_element_type=F32)


def swap_pairs(values, axis, by=1):
    count = lax.axis_size(axis)
    return lax.ppermute(values, axis, [(i, i ^ by) for i in range(count)])


def rope_tables(places):
    half_width = HD // 2
    frequency = jnp.power(10000.0, -2.0 * jnp.arange(half_width).astype(F32) / HD)
    angles = frequency[:, None] * places.astype(F32)[None, :]
    return jnp.cos(angles), jnp.sin(angles)


def core_rows(rows, core):
    quarter = rows.shape[0] // 4
    low = lax.dynamic_slice_in_dim(rows, core * quarter, quarter, 0)
    high = lax.dynamic_slice_in_dim(rows, (3 - core) * quarter, quarter, 0)
    return jnp.concatenate([low, high], axis=0)


def join_halves(first, second):
    quarter = first.shape[0] // 2
    return jnp.concatenate(
        [first[:quarter], second[:quarter], second[quarter:], first[quarter:]], axis=0
    )


def chip_groups():
    return [[0, 2], [1, 3]]


def gather_blocks(base):
    return lax.all_gather(base, "gx", axis=0)


def chosen(pair, layer):
    return jnp.where(lax.axis_index("section") == layer, *pair)


def fused():
    return lax.axis_size("gx") == 4 and lax.axis_size("gy") == 4


def tall(w):
    return w.reshape(-1, w.shape[-1])


def side(w):
    return jnp.concatenate([w[i] for i in range(w.shape[0])], axis=1)


def cut(w, low, high):
    return w[:, :, low:high]


def shard_sum(product):
    return lax.psum_scatter(product, "gx", scatter_dimension=0, tiled=True)


def chip_sum(product):
    product = product.reshape(-1, product.shape[-1])
    return lax.psum_scatter(
        product, "gx", scatter_dimension=0, tiled=True, axis_index_groups=[[0, 2], [1, 3]]
    )


def rope_down(values, cosine, sines):
    half_width = HD // 2
    first, second = values[:half_width], values[half_width:]
    return jnp.concatenate(
        [first * cosine - second * sines, second * cosine + first * sines], axis=0
    )


def fill_bias(bias_ref, key_ref, query_ref, length_ref):
    keys = key_ref[...]
    allowed = (keys <= query_ref[...]) & (keys < length_ref[...])
    bias_ref[...] = jnp.where(allowed, 0.0, -1e30)


def dot_to(left, right, dims):
    return lax.dot_general(left, right, (dims, ((), ())), preferred_element_type=F32)


def attend_kernel(
    q_ref, k_ref, vt_ref, cos_ref, sin_ref, key_ref, query_ref, length_ref,
    heads_ref, rot_ref, lse_ref, bias_ref, out_ref,
):
    fill_bias(bias_ref, key_ref, query_ref, length_ref)

    def head(h, carry):
        here = pl.ds(pl.multiple_of(h * HD, HD), HD)
        rotated = rope_down(q_ref[here, :], cos_ref[...], sin_ref[...]).astype(BF)
        rot_ref[here, :] = rotated
        scaled = (rotated.astype(F32) * HD ** (-0.5)).astype(BF)
        scores = dot_to(k_ref[...], scaled, ((1,), (0,))) + bias_ref[...]
        top = jnp.max(scores, axis=0, keepdims=True)
        exponent = jnp.exp(scores - top)
        total = jnp.sum(exponent, axis=0, keepdims=True)
        probs = (exponent * (1.0 / total)).astype(BF)
        out_ref[here, :] = dot_to(vt_ref[...], probs, ((1,), (0,)))
        lse_ref[pl.ds(h, 1), :] = top + jnp.log(total)
        return carry

    lax.fori_loop(0, q_ref.shape[0] // HD, head, 0)
    heads_ref[...] = out_ref[...].T.astype(BF)


def attend_back_kernel(
    rot_ref, k_ref, kt_ref, v_ref, d_ref, lse_ref, cos_ref, sin_ref, key_ref, query_ref, length_ref,
    dq_ref, dk_ref, dv_ref, bias_ref, out_ref,
):
    fill_bias(bias_ref, key_ref, query_ref, length_ref)
    dk_ref[...] = jnp.zeros_like(dk_ref)
    dv_ref[...] = jnp.zeros_like(dv_ref)
    scaling = HD ** (-0.5)

    def head(h, carry):
        here = pl.ds(pl.multiple_of(h * HD, HD), HD)
        scaled = (rot_ref[here, :].astype(F32) * scaling).astype(BF)
        scores = dot_to(k_ref[...], scaled, ((1,), (0,))) + bias_ref[...]
        probs = jnp.exp(scores - lse_ref[pl.ds(h, 1), :])
        d_probs = dot_to(v_ref[...], d_ref[here, :], ((1,), (0,)))
        delta = jnp.sum(probs * d_probs, axis=0, keepdims=True)
        d_scores = (probs * (d_probs - delta)).astype(BF)
        dk_ref[...] += dot_to(d_scores, scaled, ((1,), (1,)))
        dv_ref[...] += dot_to(probs.astype(BF), d_ref[here, :], ((1,), (1,)))
        dq = dot_to(kt_ref[...], d_scores, ((1,), (0,))) * scaling
        out_ref[here, :] = rope_down(dq, cos_ref[...], -sin_ref[...])
        return carry

    lax.fori_loop(0, rot_ref.shape[0] // HD, head, 0)
    dq_ref[...] = out_ref[...].T.astype(BF)


def attend(q_down, k_all, v_all, tables):
    cosine, sines, keys_at, places, length = tables
    width, rows = q_down.shape
    return pl.pallas_call(
        attend_kernel,
        out_shape=(
            jax.ShapeDtypeStruct((rows, width), BF),
            jax.ShapeDtypeStruct((width, rows), BF),
            jax.ShapeDtypeStruct((width // HD, rows), F32),
        ),
        in_specs=[VMEM] * 8,
        out_specs=(VMEM,) * 3,
        scratch_shapes=[pltpu.VMEM((k_all.shape[0], rows), F32), pltpu.VMEM((width, rows), F32)],
        compiler_params=pltpu.CompilerParams(vmem_limit_bytes=VMEM_LIMIT),
        cost_estimate=pl.CostEstimate(
            flops=16 * width * rows * k_all.shape[0], bytes_accessed=60_000_000, transcendentals=0
        ),
        name="attend",
    )(q_down, k_all, v_all.T, cosine, sines, keys_at[:, None], places[None], length)


def attend_back(rotated, k_all, v_all, d_down, lse, tables):
    cosine, sines, keys_at, places, length = tables
    width, rows = rotated.shape
    return pl.pallas_call(
        attend_back_kernel,
        out_shape=(
            jax.ShapeDtypeStruct((rows, width), BF),
            jax.ShapeDtypeStruct(k_all.shape, F32),
            jax.ShapeDtypeStruct(k_all.shape, F32),
        ),
        in_specs=[VMEM] * 11,
        out_specs=(VMEM,) * 3,
        scratch_shapes=[pltpu.VMEM((k_all.shape[0], rows), F32), pltpu.VMEM((width, rows), F32)],
        compiler_params=pltpu.CompilerParams(vmem_limit_bytes=VMEM_LIMIT),
        cost_estimate=pl.CostEstimate(
            flops=40 * width * rows * k_all.shape[0], bytes_accessed=80_000_000, transcendentals=0
        ),
        name="attend_back",
    )(
        rotated, k_all, k_all.T, v_all, d_down, lse, cosine, sines,
        keys_at[:, None], places[None], length,
    )


def line_kernel(
    kind, masked, low, high, deps, gathers, layer, exchange,
    gain_ref, resid_ref, valid_ref, h_ref, square_ref, *rest,
):
    forward = kind in ("out", "mlp")
    wide = kind in ("mlp", "mlp_back")
    if kind == "mlp":
        lhs_refs = []
    elif kind == "mlp_back":
        lhs_refs, rest = rest[:4], rest[4:]
    else:
        lhs_refs, rest = rest[:1], rest[1:]
    w_count = 3 if wide else 1
    w_refs, rest = rest[:w_count], rest[w_count + deps :]
    base_refs, rest = rest[: 2 * gathers], rest[2 * gathers :]
    out_ref, rest = rest[0], rest[1:]
    if kind == "mlp":
        normed_ref, ms_ref, gate_ref, up_ref, hidden_ref = rest[:5]
        rest = rest[5:]
    elif kind == "mlp_back":
        product_refs, rest = rest[:3], rest[3:]
        arrived_refs, rest = rest[:exchange], rest[exchange:]
    block_refs, rest = rest[:gathers], rest[gathers:]
    w_alls, rest = rest[:w_count], rest[w_count:]
    (
        part, from_end, from_mid, pair,
        w_sem, up_send, up_recv, mid_send, mid_recv, fin_send, fin_recv,
    ) = rest[:11]
    if gathers:
        far_send, far_recv, near_send, near_recv, cross_send, cross_recv = rest[11:]
    if kind == "mlp_back":
        (
            d_gate_ref, d_up_ref, far_normed, far_dm, far_hidden, far_d_gate, far_d_up, stage,
            give_sem, take_sem, stage_sem,
        ) = rest[11:22]
    if exchange:
        y_stage, y_send, y_recv = rest[22:]
    shard = lax.axis_index("gx")
    far, near = shard ^ 2, shard ^ 1
    rows, width = resid_ref.shape
    columns = width // 4
    count = rows // CHUNK
    z = lax.axis_index("gy")
    middle = (z == 1) | (z == 2)
    end_of = jnp.where(z == 1, 0, 3)
    mid_of = jnp.where(z == 0, 1, 2)
    across = 3 - z

    loads, downs = [], []
    if wide:
        hidden_width = w_alls[0].shape[1]
        for x0 in range(0, hidden_width, 512):
            x1 = min(x0 + 512, hidden_width)
            for w in range(2):
                for j in range(4):
                    source = w_refs[w].at[j, :, x0:x1]
                    target = w_alls[w].at[j * columns : (j + 1) * columns, x0:x1]
                    loads.append(pltpu.make_async_copy(source, target, w_sem.at[len(loads)]))
        downs = [
            pltpu.make_async_copy(w_refs[2].at[j], w_alls[2].at[j], w_sem.at[len(loads) + j])
            for j in range(4)
        ]
    else:
        loads = [
            pltpu.make_async_copy(w_refs[0].at[j, :, low:high], w_alls[0].at[j], w_sem.at[j])
            for j in range(4)
        ]
    order = downs + loads if kind == "mlp_back" else loads + downs
    for load in order:
        load.start()

    barrier = pltpu.get_barrier_semaphore()
    peers = []
    if gathers:
        peers = [{"gx": far}, {"gx": near}, {"section": 1 - lax.axis_index("section")}]
    elif kind == "mlp_back":
        peers = [{"gx": near}] + [{"gx": far}] * (exchange > 0)
    beside = len(peers)
    for peer in peers:
        pl.semaphore_signal(barrier, inc=1, device_id=peer, device_id_type=MESH)

    @pl.when(middle)
    def _():
        pl.semaphore_signal(barrier, inc=1, device_id={"gy": end_of}, device_id_type=MESH)
        pl.semaphore_signal(barrier, inc=1, device_id={"gy": across}, device_id_type=MESH)
        pl.semaphore_wait(barrier, 2 + beside)

    @pl.when(jnp.logical_not(middle))
    def _():
        pl.semaphore_signal(barrier, inc=1, device_id={"gy": mid_of}, device_id_type=MESH)
        pl.semaphore_wait(barrier, 1 + beside)

    section = lax.axis_index("section")
    x_peer = {"section": 1 - section}

    def half_of(ref, k, which):
        size = base_refs[2 * k].shape[0] // 2
        return ref.at[pl.ds(pl.multiple_of(which * size, 16), size), :]

    def far_copy(k, source):
        return pltpu.make_async_remote_copy(
            src_ref=half_of(source, k, section),
            dst_ref=half_of(block_refs[k].at[shard], k, section),
            send_sem=far_send.at[k], recv_sem=far_recv.at[k],
            device_id={"gx": far}, device_id_type=MESH,
        )

    def near_copy(k, source):
        return pltpu.make_async_remote_copy(
            src_ref=source, dst_ref=block_refs[k].at[shard], send_sem=near_send.at[3 * k],
            recv_sem=near_recv.at[3 * k], device_id={"gx": near}, device_id_type=MESH,
        )

    def cross_copy(k):
        rows_here = half_of(block_refs[k].at[far], k, section)
        return pltpu.make_async_remote_copy(
            src_ref=rows_here, dst_ref=rows_here, send_sem=cross_send.at[k],
            recv_sem=cross_recv.at[k], device_id=x_peer, device_id_type=MESH,
        )

    def pass_copy(k, late):
        rows_here = half_of(block_refs[k].at[far], k, 1 - section if late else section)
        return pltpu.make_async_remote_copy(
            src_ref=rows_here, dst_ref=rows_here, send_sem=near_send.at[3 * k + 1 + late],
            recv_sem=near_recv.at[3 * k + 1 + late], device_id={"gx": near}, device_id_type=MESH,
        )

    at_home = section == layer

    def from_base(k, starts):
        for ref, holds in zip(base_refs[2 * k : 2 * k + 2], (at_home, jnp.logical_not(at_home))):

            @pl.when(holds)
            def _():
                for make in starts:
                    make(k, ref).start()

    def gather_middle(k):
        far_copy(k, base_refs[2 * k]).wait_recv()
        cross_copy(k).start()
        pass_copy(k, 0).start()
        if k + 1 < gathers:
            from_base(k + 1, [far_copy])

    def gather_late(k):
        cross_copy(k).wait_recv()
        pass_copy(k, 1).start()

    if gathers:
        from_base(0, [far_copy])
    for k in range(gathers):
        from_base(k, [near_copy])

    half = rows // STEPS
    core = lax.rem(shard, 2)

    def give(slot, source, target):
        return pltpu.make_async_remote_copy(
            src_ref=source, dst_ref=target, send_sem=give_sem.at[slot],
            recv_sem=take_sem.at[slot], device_id={"gx": near}, device_id_type=MESH,
        )

    def chip_columns(ref, y, of):
        return ref.at[:, pl.ds(pl.multiple_of((2 * y + of) * columns, columns), columns)]

    def step_rows(ref, step):
        return ref.at[pl.ds(pl.multiple_of(step * half, half), half), :]

    if kind == "mlp_back":
        saved_gate, saved_up, saved_normed, saved_hidden = lhs_refs
        early = [give(0, saved_hidden, far_hidden)]
        for y in range(2):
            early.append(give(1 + y, chip_columns(resid_ref, y, 1 - core), far_dm.at[y]))
        for y in range(2):
            early.append(give(3 + y, chip_columns(saved_normed, y, 1 - core), far_normed.at[y]))
        for copy in early:
            copy.start()

    def give_step(step):
        return [
            give(5 + step, step_rows(d_gate_ref, step), step_rows(far_d_gate, step)),
            give(5 + STEPS + step, step_rows(d_up_ref, step), step_rows(far_d_up, step)),
        ]

    if not wide:
        for load in loads:
            load.wait()

    def at_first(step, copies):
        @pl.when(step == 0)
        def _():
            for copy in copies:
                copy.wait()

    def at(ref, i):
        return ref.at[pl.ds(pl.multiple_of(i * CHUNK, CHUNK), CHUNK), :]

    def up_copy(i):
        return pltpu.make_async_remote_copy(
            src_ref=at(part, i), dst_ref=at(from_end, i), send_sem=up_send.at[i],
            recv_sem=up_recv.at[i], device_id={"gy": mid_of}, device_id_type=MESH,
        )

    def mid_copy(i):
        return pltpu.make_async_remote_copy(
            src_ref=at(pair, i), dst_ref=at(from_mid, i), send_sem=mid_send.at[i],
            recv_sem=mid_recv.at[i], device_id={"gy": across}, device_id_type=MESH,
        )

    def fin_copy(i):
        return pltpu.make_async_remote_copy(
            src_ref=at(out_ref, i), dst_ref=at(out_ref, i), send_sem=fin_send.at[i],
            recv_sem=fin_recv.at[i], device_id={"gy": end_of}, device_id_type=MESH,
        )

    def dot(left, right, transposed=False):
        dims = (((1,), (1 if transposed else 0,)), ((), ()))
        return lax.dot_general(left, right, dims, preferred_element_type=F32)

    def spans(extent):
        return [(x, min(x + 512, extent)) for x in range(0, extent, 512)]

    if wide:
        w_gate, w_up, w_down = w_alls

    def product(step, carry):
        here = pl.ds(pl.multiple_of(step * half, half), half)
        if kind == "mlp":
            values = resid_ref[here, :].astype(F32)
            square = jnp.mean(values * values, axis=1, keepdims=True)
            ms_ref[here, :] = square
            normed_ref[here, :] = (values * lax.rsqrt(square + EPS) * gain_ref[...]).astype(BF)
            for n, (x0, x1) in enumerate(spans(w_gate.shape[1])):
                at_first(step, loads[8 * n : 8 * n + 8])
                gate = dot(normed_ref[here, :], w_gate[:, x0:x1])
                up = dot(normed_ref[here, :], w_up[:, x0:x1])
                gate_ref[here, x0:x1] = gate.astype(BF)
                up_ref[here, x0:x1] = up.astype(BF)
                hidden_ref[here, x0:x1] = (gate * jax.nn.sigmoid(gate) * up).astype(BF)
        if kind == "mlp_back":
            at_first(step, downs)
            for x0, x1 in spans(w_gate.shape[1]):
                d_hidden = sum(
                    dot(resid_ref[here, j * columns : (j + 1) * columns], w_down[j, x0:x1, :], True)
                    for j in range(4)
                )
                gate = saved_gate[here, x0:x1].astype(F32)
                up = saved_up[here, x0:x1].astype(F32)
                sigmoid = jax.nn.sigmoid(gate)
                d_up_ref[here, x0:x1] = (d_hidden * (gate * sigmoid)).astype(BF)
                d_gate_ref[here, x0:x1] = (
                    d_hidden * up * sigmoid * (1.0 + gate * (1.0 - sigmoid))
                ).astype(BF)
            for copy in give_step(step):
                copy.start()
        if wide:
            at_first(step, downs if kind == "mlp" else loads)
        for j in range(4):
            span = slice(j * columns, (j + 1) * columns)
            if kind == "out":
                value = dot(lhs_refs[0][here, :], w_alls[0][j])
            elif kind == "mlp":
                value = dot(hidden_ref[here, :], w_down[j])
            elif kind == "mlp_back":
                value = dot(d_gate_ref[here, :], w_gate[span, :], True)
                value += dot(d_up_ref[here, :], w_up[span, :], True)
            else:
                value = dot(lhs_refs[0][here, :], w_alls[0][j], True)
            part[here, span] = value.astype(BF)

        @pl.when(jnp.logical_not(middle))
        def _():
            def send(i, inner):
                up_copy(step * (count // STEPS) + i).start()
                return inner

            lax.fori_loop(0, count // STEPS, send, 0)

        return carry

    lax.fori_loop(0, STEPS, product, 0)

    def finish(i):
        mid_copy(i).wait_recv()
        here = pl.ds(pl.multiple_of(i * CHUNK, CHUNK), CHUNK)
        total = pair[here, :].astype(F32) + from_mid[here, :].astype(F32)
        resid = resid_ref[here, :].astype(F32)
        if forward:
            result = resid + total
            if masked:
                result = result * valid_ref[here, :]
        else:
            values = h_ref[here, :].astype(F32)
            scaled = total * gain_ref[...]
            ratio = lax.rsqrt(square_ref[here, :] + EPS)
            mean_term = jnp.sum(scaled * values, axis=1, keepdims=True) * (1.0 / width)
            result = resid + ratio * scaled - values * (ratio * ratio * ratio) * mean_term
        out_ref[here, :] = result.astype(BF)
        fin_copy(i).start()

    tile = columns // 2

    def tile_rows(sub):
        return pl.ds(pl.multiple_of(sub % 2 * tile, tile), tile)

    def stage_copy(number, sub, slot):
        target = product_refs[number].at[sub // 2, tile_rows(sub), :]
        return pltpu.make_async_copy(stage.at[slot], target, stage_sem.at[slot])

    def y_copy(number, sub, slot):
        return pltpu.make_async_remote_copy(
            src_ref=y_stage.at[2 * number + slot], dst_ref=arrived_refs[number].at[tile_rows(sub), :],
            send_sem=y_send.at[2 * number + slot], recv_sem=y_recv.at[2 * number + slot],
            device_id={"gx": far}, device_id_type=MESH,
        )

    def gradient_tile(number, sub):
        slot = sub % 2
        left, far_left, right, far_right = (
            (resid_ref, far_dm, saved_hidden, far_hidden),
            (saved_normed, far_normed, d_gate_ref, far_d_gate),
            (saved_normed, far_normed, d_up_ref, far_d_up),
        )[number]

        @pl.when(sub == 0)
        def _():
            waits = [early[:3], early[3:] + give_all[:STEPS], give_all[STEPS:]][number]
            for copy in waits:
                copy.wait_recv()

        if number >= exchange:

            @pl.when((sub >= 2) | (number > 0))
            def _():
                stage_copy(number, sub, slot).wait()

        elif number > 0:

            @pl.when(sub >= 2)
            def _():
                stage_copy(number, sub - 2, slot).wait()

        y = sub // 2
        if number < exchange:
            y = jnp.where(sub < 2, 1 - lax.div(shard, 2), lax.div(shard, 2))
        start = (y * 2 + core) * columns + sub % 2 * tile
        mine = left[:, pl.ds(pl.multiple_of(start, tile), tile)]
        theirs = far_left[y, :, tile_rows(sub)]
        value = dot_to(mine, right[...], ((0,), (0,))) + dot_to(theirs, far_right[...], ((0,), (0,)))
        if number < exchange:

            @pl.when(sub < 2)
            def _():
                y_stage[2 * number + slot] = value.astype(BF)
                y_copy(number, sub, slot).start()

            @pl.when(sub >= 2)
            def _():
                stage[slot] = value.astype(BF)
                stage_copy(number, sub - 2, slot).start()

        else:
            stage[slot] = value.astype(BF)
            stage_copy(number, sub, slot).start()

    if kind == "mlp_back":
        give_all = [x for pair in zip(*(give_step(n) for n in range(STEPS))) for x in pair]

    def beside_step(i):
        pass_on(i)
        if kind == "mlp_back":
            for number in range(3):
                first = 3 + 4 * number

                @pl.when((i >= first) & (i < first + 4))
                def _():
                    gradient_tile(number, i - first)

    def pass_on(i):
        if gathers == 2:

            @pl.when(i == count * 6 // 16)
            def _():
                gather_middle(0)

            @pl.when(i == count * 12 // 16)
            def _():
                gather_late(0)
                gather_middle(1)

    @pl.when(middle)
    def _():
        def step(i, carry):
            up_copy(i).wait_recv()
            here = pl.ds(pl.multiple_of(i * CHUNK, CHUNK), CHUNK)
            pair[here, :] = (part[here, :].astype(F32) + from_end[here, :].astype(F32)).astype(BF)
            mid_copy(i).start()

            @pl.when(i >= 1)
            def _():
                finish(i - 1)

            beside_step(i)
            return carry

        lax.fori_loop(0, count, step, 0)
        finish(count - 1)

        def drain(i, carry):
            mid_copy(i).wait_send()
            fin_copy(i).wait_send()
            return carry

        lax.fori_loop(0, count, drain, 0)

    @pl.when(jnp.logical_not(middle))
    def _():
        def drain(i, carry):
            up_copy(i).wait_send()
            fin_copy(i).wait_recv()
            beside_step(i)
            return carry

        lax.fori_loop(0, count, drain, 0)

    if kind == "mlp_back":
        for slot in range(2):
            stage_copy(2, 2 + slot, slot).wait()
        for copy in early + give_all:
            copy.wait_send()
        for number in range(exchange):
            for slot in range(2):
                y_copy(number, slot, slot).wait()
    if gathers:
        gather_late(1)
    for k in range(gathers):
        far_copy(k, base_refs[2 * k]).wait_send()
        near_copy(k, base_refs[2 * k]).wait()
        cross_copy(k).wait_send()
        pass_copy(k, 0).wait()
        pass_copy(k, 1).wait()


def line_sum(kind, ident, resid, weights, lhs=(), gain=None, valid=None, back=None, low=0, high=0, deps=(), bases=(), layer=0, exchange=0):
    rows, width = resid.shape
    one = jnp.ones((rows, 1), F32)
    h, square = back if back is not None else (jnp.zeros((16, 128), BF), jnp.zeros((8, 1), F32))
    gain = jnp.zeros((width,), F32) if gain is None else gain
    wide = kind in ("mlp", "mlp_back")
    hidden = weights[0].shape[2] if wide else 0
    w_scratch = []
    for i, w in enumerate(weights):
        _, depth, across = w.shape
        if wide and i < 2:
            w_scratch.append(pltpu.VMEM((width, across), BF))
        else:
            w_scratch.append(pltpu.VMEM((4, depth, across if wide else high - low), BF))
    outs, products, beside = [((rows, width), BF)], [], []
    if kind == "mlp":
        outs += [((rows, width), BF), ((rows, 1), F32)] + [((rows, hidden), BF)] * 3
    elif kind == "mlp_back":
        products = [((1 if n < exchange else 2, width // 4, hidden), BF) for n in range(3)]
        products += [((width // 4, hidden), BF)] * exchange
        half_block = pltpu.VMEM((2, rows, width // 4), BF)
        beside = [pltpu.VMEM((rows, hidden), BF)] * 2 + [half_block] * 2
        beside += [pltpu.VMEM((rows, hidden), BF)] * 3 + [pltpu.VMEM((2, width // 8, hidden), BF)]
        beside += [pltpu.SemaphoreType.DMA((n,)) for n in (5 + 2 * STEPS, 5 + 2 * STEPS, 2)]
        if exchange:
            beside += [pltpu.VMEM((2 * exchange, width // 8, hidden), BF)]
            beside += [pltpu.SemaphoreType.DMA((2 * exchange,))] * 2
    blocks = [((4,) + base[0].shape, BF) for base in bases]
    pairs = [x for base in bases for x in base]
    depth = 3 * hidden if wide else lhs[0].shape[1]
    count = rows // CHUNK
    dma = pltpu.SemaphoreType.DMA
    results = pl.pallas_call(
        functools.partial(
            line_kernel, kind, valid is not None, low, high, len(deps), len(bases), layer, exchange
        ),
        out_shape=tuple(jax.ShapeDtypeStruct(*o) for o in outs + products + blocks),
        in_specs=[VMEM] * (5 + len(lhs)) + [ANY] * (len(weights) + len(deps) + len(pairs)),
        out_specs=tuple([VMEM] * len(outs) + [ANY] * len(products + blocks)),
        scratch_shapes=w_scratch
        + [pltpu.VMEM((rows, width), BF)] * 4
        + [dma((8 * -(-hidden // 512) + 4,))]
        + [dma((count,))] * 6
        + [dma((n * len(bases),)) for n in (1, 1, 3, 3, 1, 1) if bases]
        + beside,
        compiler_params=pltpu.CompilerParams(
            collective_id=ident, has_side_effects=True, vmem_limit_bytes=VMEM_LIMIT
        ),
        cost_estimate=pl.CostEstimate(
            flops=2 * rows * depth * width, bytes_accessed=200 * 1024 * 1024, transcendentals=0
        ),
        name="line_" + kind,
    )(gain[None], resid, one if valid is None else valid, h, square, *lhs, *weights, *deps, *pairs)
    if not bases:
        return results
    kept = len(results) - len(bases)
    shard = lax.axis_index("gx")
    whole = [
        lax.dynamic_update_index_in_dim(w, chosen(base, layer), shard, 0)
        for w, base in zip(results[kept:], bases)
    ]
    return (*results[:kept], *whole)


def plain_sum(total):
    return lax.psum(total.astype(BF), "gy").astype(F32)


def normed(h, gain):
    values = h.astype(F32)
    square = jnp.mean(values * values, axis=1, keepdims=True)
    return square, (values * lax.rsqrt(square + EPS) * gain).astype(BF)


def norm_back(d_normed, h, square, gain):
    values = h.astype(F32)
    ratio = lax.rsqrt(square + EPS)
    scaled = d_normed * gain
    mean_term = jnp.mean(scaled * values, axis=1, keepdims=True)
    return ratio * scaled - values * (ratio * ratio * ratio) * mean_term


def attention_forward(h, gain, w_attn, low, tables, ident, bases, layer, deps=()):
    rows, width = h.shape
    high = low + width // lax.axis_size("gx")
    q_width = low - 2 * HD
    cosine, sines = tables[:2]
    square, n1 = normed(h, gain)
    q_down = mm(tall(cut(w_attn, 0, q_width)), n1, ((0,), (1,)))
    kv = mm(n1, tall(cut(w_attn, q_width, low)))
    k_rot = rope_down(kv[:, :HD].T, cosine, sines).T.astype(BF)
    kv = jnp.concatenate([k_rot, kv[:, HD:].astype(BF)], axis=1)
    kv_all = jnp.concatenate([kv, swap_pairs(kv, "gx")], axis=0)
    k_all, v_all = kv_all[:, :HD], kv_all[:, HD:]
    heads, rotated, lse = attend(q_down, k_all, v_all, tables)
    if fused():
        h1, *blocks = line_sum(
            "out", ident, h, [w_attn], (heads,), low=low, high=high,
            deps=deps, bases=bases, layer=layer,
        )
    else:
        h1 = (h.astype(F32) + plain_sum(mm(heads, side(cut(w_attn, low, high))))).astype(BF)
        blocks = [gather_blocks(chosen(x, layer)) for x in bases]
    return h1, square, blocks, (h, square, n1, rotated, lse, k_all, v_all, heads)


def mlp_forward(h1, gain, weights, valid, ident, bases=(), layer=0):
    if fused():
        result, n2, square, gate, up, hidden, *blocks = line_sum(
            "mlp", ident, h1, weights, gain=gain, valid=valid, bases=bases, layer=layer
        )
    else:
        square, n2 = normed(h1, gain)
        gate = mm(n2, tall(weights[0]))
        up = mm(n2, tall(weights[1]))
        hidden = (gate * jax.nn.sigmoid(gate) * up).astype(BF)
        gate, up = gate.astype(BF), up.astype(BF)
        result = h1.astype(F32) + plain_sum(mm(hidden, side(weights[2])))
        result = (result * valid).astype(BF)
        blocks = [gather_blocks(chosen(x, layer)) for x in bases]
    return result, square, blocks, (h1, square, n2, gate, up, hidden)


def mlp_backward(dm, gain, weights, saved, ident, deps=(), exchange=1):
    h1, square, n2, gate, up, hidden = saved
    if fused():
        e1, *products = line_sum(
            "mlp_back", ident, dm, weights, (gate, up, n2, hidden), gain=gain,
            back=(h1, square), deps=deps, exchange=exchange,
        )
        return e1, products
    gate, up = gate.astype(F32), up.astype(F32)
    d_hidden = mm(dm, side(weights[2]), ((1,), (1,)))
    sigmoid = jax.nn.sigmoid(gate)
    d_gate = (d_hidden * up * sigmoid * (1.0 + gate * (1.0 - sigmoid))).astype(BF)
    d_up = (d_hidden * (gate * sigmoid)).astype(BF)
    total = mm(d_gate, tall(weights[0]), ((1,), (1,))) + mm(d_up, tall(weights[1]), ((1,), (1,)))
    e1 = (dm.astype(F32) + norm_back(plain_sum(total), h1, square, gain)).astype(BF)
    turn = ((0,), (0,))
    products = [mm(dm, hidden, turn), mm(n2, d_gate, turn), mm(n2, d_up, turn)]
    return e1, [p.astype(BF) for p in products]


def mlp_sums(products):
    if not fused():
        return [shard_sum(p) for p in products]
    down, gate, up, arrived = products
    first = (down[0].astype(F32) + arrived.astype(F32)).astype(BF)
    return [first, chip_sum(gate), chip_sum(up)]


def attention_backward(e1, w_attn, low, tables, saved):
    h, square, n1, rotated, lse, k_all, v_all, heads = saved
    rows, width = h.shape
    cosine, sines = tables[:2]
    w_o = side(cut(w_attn, low, low + width // lax.axis_size("gx")))
    d_down = mm(w_o, e1, ((1,), (1,))).astype(BF)
    dq, dk, dv = attend_back(rotated, k_all, v_all, d_down, lse, tables)
    dkv = jnp.concatenate([dk, dv], axis=1)
    dkv = dkv[:rows] + swap_pairs(dkv[rows:], "gx")
    dk = rope_down(dkv[:, :HD].T, cosine, -sines).T
    d_qkv = jnp.concatenate([dq, dk.astype(BF), dkv[:, HD:].astype(BF)], axis=1)
    turn = ((0,), (0,))
    products = [mm(n1, d_qkv, turn).astype(BF), mm(e1, heads, turn).astype(BF)]
    return d_qkv, jnp.concatenate(products, axis=1)


def attention_end(d_qkv, e1, w_attn, gain, saved, ident, deps=()):
    h, square = saved[:2]
    qkv_width = d_qkv.shape[1]
    if fused():
        return line_sum(
            "back", ident, e1, [w_attn], (d_qkv,), gain=gain, back=(h, square),
            low=0, high=qkv_width, deps=deps,
        )[0]
    total = plain_sum(mm(d_qkv, tall(cut(w_attn, 0, qkv_width)), ((1,), (1,))))
    return (e1.astype(F32) + norm_back(total, h, square, gain)).astype(BF)


def on_device(
    hidden_in, out_grad, lengths, dealing, attn_gain, w_query, w_key, w_value, w_out,
    mlp_gain, w_gate, w_up, w_down,
):
    shards = lax.axis_size("gx")
    shard = lax.axis_index("gx")
    section = lax.axis_index("section")
    column = lax.axis_index("gy")
    core = shard % 2
    sequence = (shard // 2) * 2 + section
    span, width = hidden_in.shape
    half = span // 2
    seq_length = lax.dynamic_index_in_dim(lengths, sequence, keepdims=False)

    both = jnp.concatenate([hidden_in, out_grad], axis=1)
    mine = core_rows(both, core)
    theirs = swap_pairs(core_rows(both, 1 - core), "gx")
    mine = jnp.where(core == section, mine, theirs)
    h = lax.all_gather(mine[:, :width], "gy", axis=1, tiled=True)

    kv_head = column * (w_query.shape[2] // HD) // (QH // KVH)
    low = w_query.shape[2] + 2 * HD
    both_gains = jnp.stack([attn_gain[0], mlp_gain[0]], axis=1)
    attn_own = jnp.concatenate(
        [
            w_query[0],
            lax.dynamic_slice_in_dim(w_key[0], kv_head * HD, HD, 1),
            lax.dynamic_slice_in_dim(w_value[0], kv_head * HD, HD, 1),
            w_out[0],
            jnp.pad(both_gains, ((0, 0), (0, 126))),
        ],
        axis=1,
    )
    own = (attn_own, w_gate[0], w_up[0], w_down[0])
    first = [(array, lax.ppermute(array, "section", [(0, 1)])) for array in own]
    second = [(array, lax.ppermute(array, "section", [(1, 0)])) for array in own]

    def gains_of(w_attn):
        pair = w_attn[:, :, w_attn.shape[2] - 128 : w_attn.shape[2] - 126]
        return pair.reshape(-1, 2).T.astype(F32)

    here = core_rows(jnp.arange(span), core)
    there = core_rows(jnp.arange(span), 1 - core)
    keys_at = jnp.concatenate([here, there])
    valid = (here < seq_length)[:, None].astype(F32)
    tables = (*rope_tables(here), keys_at, here, seq_length.reshape(1, 1))

    attn0, gate0 = gather_blocks(chosen(first[0], 0)), gather_blocks(chosen(first[1], 0))
    gains0 = gains_of(attn0)
    h1, square_a, blocks, saved_a0 = attention_forward(
        h, gains0[0], attn0, low, tables, 0, first[2:], 0, (gate0,)
    )
    mlp0 = [gate0] + blocks
    h, square_m, (attn1, gate1), saved_m0 = mlp_forward(
        h1, gains0[1], mlp0, valid, 1, second[:2], 1
    )
    gains1 = gains_of(attn1)
    outputs, squares = [h], [square_a, square_m]
    d_mine = mine[:, width:] + h[:1, :1] * 0
    d_out = lax.all_gather(d_mine, "gy", axis=1, tiled=True)
    h1, square_a, blocks, saved_a1 = attention_forward(
        h, gains1[0], attn1, low, tables, 2, second[2:], 1
    )
    mlp1 = [gate1] + blocks
    h, square_m, _, saved_m1 = mlp_forward(h1, gains1[1], mlp1, valid, 3)
    outputs.append(h)
    squares = jnp.concatenate(squares + [square_a, square_m], axis=1)
    rms = (jnp.sqrt(squares + EPS) * valid).T
    statistics = [rms[:2], rms[2:]]
    outputs = [lax.dynamic_slice_in_dim(x, column * width, width, 1) for x in outputs]

    def to_section(per_layer):
        kept = jnp.where(section == 0, per_layer[0], per_layer[1])
        sent = swap_pairs(jnp.where(section == 0, per_layer[1], per_layer[0]), "section")
        return kept, sent

    dm = (d_out.astype(F32) * valid).astype(BF)
    e1, products = mlp_backward(dm, gains1[1], mlp1, saved_m1, 4)
    local1 = mlp_sums(products)

    both = []
    for output, stat in zip(outputs, statistics):
        high = stat.astype(BF)
        rest = (stat - high.astype(F32)).astype(BF)
        parts = jnp.concatenate([high, rest], axis=0).reshape(-1, width)
        parts = jnp.pad(parts, ((0, -parts.shape[0] % 16), (0, 0)))
        both.append(jnp.concatenate([output + e1[:1, :1] * 0, parts], axis=0))
    kept, sent = to_section(both)
    by_section = jnp.stack([jnp.where(section == 0, kept, sent), jnp.where(section == 0, sent, kept)])
    everything = lax.all_gather(by_section, "gx", axis=0)
    owner = jnp.sum(jnp.where(dealing == shard, jnp.arange(shards), 0))
    halves = lax.dynamic_slice(
        everything, ((owner // 2) * 2, owner % 2, 0, 0), (2, 1) + everything.shape[2:]
    )[:, 0]
    layer_out = join_halves(halves[0, :half], halves[1, :half])
    stat_rows = 4 * half // width
    parts = halves[:, half : half + stat_rows].astype(F32).reshape(2, 4, half)
    stat_halves = parts[:, :2] + parts[:, 2:]
    stats_out = join_halves(stat_halves[0].T, stat_halves[1].T).T
    d_qkv, products = attention_backward(e1, attn1, low, tables, saved_a1)
    local1.append(shard_sum(products))
    grad1 = attention_end(d_qkv, e1, attn1, gains1[0], saved_a1, 5, (products,))

    dm = (grad1.astype(F32) * valid).astype(BF)
    e1, products = mlp_backward(dm, gains0[1], mlp0, saved_m0, 6, local1[:2] + local1[3:])
    local0 = mlp_sums(products)
    d_qkv, products = attention_backward(e1, attn0, low, tables, saved_a0)
    local0.append(shard_sum(products))
    grad0 = attention_end(d_qkv, e1, attn0, gains0[0], saved_a0, 7, [products, local1[2], everything, local0[0]])

    input_grads = [lax.dynamic_slice_in_dim(x, column * width, width, 1) for x in (grad0, grad1)]
    received1 = [lax.ppermute(g, "section", [(0, 1)]) for g in local1]
    received0 = [lax.ppermute(g, "section", [(1, 0)]) for g in local0]
    totals = [
        jnp.where(section == 0, a0.astype(F32) + r0.astype(F32), a1.astype(F32) + r1.astype(F32))
        for a0, r0, a1, r1 in zip(local0, received0, local1, received1)
    ]
    s_down, s_gate, s_up, s_attn = totals
    s_out = s_attn[:, low:]
    q_width = w_query.shape[2]

    attn_sum = jnp.sum(s_attn[:, :low] * attn_own[:, :low].astype(F32), axis=1)
    mlp_sum = jnp.sum(s_gate * w_gate[0].astype(F32) + s_up * w_up[0].astype(F32), axis=1)
    sums = jnp.pad(jnp.stack([attn_sum, mlp_sum], axis=1), ((0, 0), (0, 126)))
    spread = jnp.concatenate([s_attn[:, q_width:low], sums], axis=1).astype(BF)
    spread = lax.all_gather(spread, "gy", axis=0).astype(F32)
    gains = jnp.sum(spread[:, :, 2 * HD : 2 * HD + 2], axis=0).T / both_gains.astype(F32).T
    kv_sum = spread[:, :, : 2 * HD].reshape(KVH, -1, *spread.shape[1:2], 2, HD).sum(axis=1)
    kv_sum = kv_sum.transpose(2, 1, 0, 3).reshape(2, spread.shape[1], KVH * HD)

    kept, sent = to_section(input_grads)
    keep = jnp.where(core == section, kept, sent)
    give = swap_pairs(jnp.where(core == section, sent, kept), "gx")
    back_home = join_halves(jnp.where(core == 0, keep, give), jnp.where(core == 0, give, keep))
    return (
        layer_out[None],
        stats_out[None],
        back_home[None],
        gains[None, 0],
        s_attn[None, :, :q_width],
        kv_sum[None, 0],
        kv_sum[None, 1],
        s_out.T[None],
        gains[None, 1],
        s_gate[None],
        s_up[None],
        s_down.T[None],
    )


def solution(mesh):
    rows_cols = P("section", "gx", "gy")
    cols_rows = P("section", "gy", "gx")
    rows_only = P("section", "gx", None)
    gain = P("section", "gx")
    return jax.shard_map(
        on_device,
        mesh=mesh,
        in_specs=(
            P("gx", "gy"), P("gx", "gy"), P(), P(), gain, rows_cols, rows_only, rows_only,
            cols_rows, gain, rows_cols, rows_cols, cols_rows,
        ),
        out_specs=(
            rows_cols, P("section", None, "gx"), rows_cols, gain, rows_cols, rows_only, rows_only,
            cols_rows, gain, rows_cols, rows_cols, cols_rows,
        ),
        check_vma=False,
    )
```

```python
import functools

import jax
import jax.numpy as jnp
from jax import lax
from jax.experimental import pallas as pl
from jax.experimental.pallas import tpu as pltpu
from jax.sharding import PartitionSpec as P

QH = 32
KVH = 4
HD = 64
LAYERS = 2
EPS = 1e-05
BF = jnp.bfloat16
F32 = jnp.float32
MESH = pl.DeviceIdType.MESH
CHUNK = 32
STEPS = 2
VMEM_LIMIT = 56 * 1024 * 1024
ANY = pl.BlockSpec(memory_space=pl.ANY)
VMEM = pl.BlockSpec(memory_space=pltpu.VMEM)


def mm(left, right, dims=((1,), (0,))):
    return lax.dot_general(left, right, (dims, ((), ())), preferred_element_type=F32)


def swap_pairs(values, axis, by=1):
    count = lax.axis_size(axis)
    return lax.ppermute(values, axis, [(i, i ^ by) for i in range(count)])


def rope_tables(places):
    half_width = HD // 2
    frequency = jnp.power(10000.0, -2.0 * jnp.arange(half_width).astype(F32) / HD)
    angles = frequency[:, None] * places.astype(F32)[None, :]
    return jnp.cos(angles), jnp.sin(angles)


def core_rows(rows, core):
    quarter = rows.shape[0] // 4
    low = lax.dynamic_slice_in_dim(rows, core * quarter, quarter, 0)
    high = lax.dynamic_slice_in_dim(rows, (3 - core) * quarter, quarter, 0)
    return jnp.concatenate([low, high], axis=0)


def join_halves(first, second):
    quarter = first.shape[0] // 2
    return jnp.concatenate(
        [first[:quarter], second[:quarter], second[quarter:], first[quarter:]], axis=0
    )


def chip_groups():
    return [[0, 2], [1, 3]]


def gather_blocks(base):
    return lax.all_gather(base, "gx", axis=0)


def chosen(pair, layer):
    return jnp.where(lax.axis_index("section") == layer, *pair)


def with_own(stack, pair, layer):
    shard = lax.axis_index("gx")
    return lax.dynamic_update_index_in_dim(stack, chosen(pair, layer), shard, 0)


def fused():
    return lax.axis_size("gx") == 4 and lax.axis_size("gy") == 4


def tall(w):
    return w.reshape(-1, w.shape[-1])


def side(w):
    return jnp.concatenate([w[i] for i in range(w.shape[0])], axis=1)


def cut(w, low, high):
    return w[:, :, low:high]


def shard_sum(product):
    return lax.psum_scatter(product, "gx", scatter_dimension=0, tiled=True)


def chip_sum(product):
    product = product.reshape(-1, product.shape[-1])
    return lax.psum_scatter(
        product, "gx", scatter_dimension=0, tiled=True, axis_index_groups=[[0, 2], [1, 3]]
    )


def rope_down(values, cosine, sines):
    half_width = HD // 2
    first, second = values[:half_width], values[half_width:]
    return jnp.concatenate(
        [first * cosine - second * sines, second * cosine + first * sines], axis=0
    )


def fill_bias(bias_ref, key_ref, query_ref, length_ref):
    keys = key_ref[...]
    allowed = (keys <= query_ref[...]) & (keys < length_ref[...])
    bias_ref[...] = jnp.where(allowed, 0.0, -1e30)


def dot_to(left, right, dims):
    return lax.dot_general(left, right, (dims, ((), ())), preferred_element_type=F32)


def attend_kernel(
    q_ref, k_ref, vt_ref, cos_ref, sin_ref, key_ref, query_ref, length_ref,
    heads_ref, rot_ref, lse_ref, bias_ref, out_ref,
):
    fill_bias(bias_ref, key_ref, query_ref, length_ref)

    def head(h, carry):
        here = pl.ds(pl.multiple_of(h * HD, HD), HD)
        rotated = rope_down(q_ref[here, :], cos_ref[...], sin_ref[...]).astype(BF)
        rot_ref[here, :] = rotated
        scaled = (rotated.astype(F32) * HD ** (-0.5)).astype(BF)
        scores = dot_to(k_ref[...], scaled, ((1,), (0,))) + bias_ref[...]
        top = jnp.max(scores, axis=0, keepdims=True)
        exponent = jnp.exp(scores - top)
        total = jnp.sum(exponent, axis=0, keepdims=True)
        probs = (exponent * (1.0 / total)).astype(BF)
        out_ref[here, :] = dot_to(vt_ref[...], probs, ((1,), (0,)))
        lse_ref[pl.ds(h, 1), :] = top + jnp.log(total)
        return carry

    lax.fori_loop(0, q_ref.shape[0] // HD, head, 0)
    heads_ref[...] = out_ref[...].T.astype(BF)


def attend_back_kernel(
    rot_ref, k_ref, kt_ref, v_ref, d_ref, lse_ref, cos_ref, sin_ref, key_ref, query_ref, length_ref,
    dq_ref, dk_ref, dv_ref, bias_ref, out_ref,
):
    fill_bias(bias_ref, key_ref, query_ref, length_ref)
    dk_ref[...] = jnp.zeros_like(dk_ref)
    dv_ref[...] = jnp.zeros_like(dv_ref)
    scaling = HD ** (-0.5)

    def head(h, carry):
        here = pl.ds(pl.multiple_of(h * HD, HD), HD)
        scaled = (rot_ref[here, :].astype(F32) * scaling).astype(BF)
        scores = dot_to(k_ref[...], scaled, ((1,), (0,))) + bias_ref[...]
        probs = jnp.exp(scores - lse_ref[pl.ds(h, 1), :])
        d_probs = dot_to(v_ref[...], d_ref[here, :], ((1,), (0,)))
        delta = jnp.sum(probs * d_probs, axis=0, keepdims=True)
        d_scores = (probs * (d_probs - delta)).astype(BF)
        dk_ref[...] += dot_to(d_scores, scaled, ((1,), (1,)))
        dv_ref[...] += dot_to(probs.astype(BF), d_ref[here, :], ((1,), (1,)))
        dq = dot_to(kt_ref[...], d_scores, ((1,), (0,))) * scaling
        out_ref[here, :] = rope_down(dq, cos_ref[...], -sin_ref[...])
        return carry

    lax.fori_loop(0, rot_ref.shape[0] // HD, head, 0)
    dq_ref[...] = out_ref[...].T.astype(BF)


def attend(q_down, k_all, v_all, tables):
    cosine, sines, keys_at, places, length = tables
    width, rows = q_down.shape
    return pl.pallas_call(
        attend_kernel,
        out_shape=(
            jax.ShapeDtypeStruct((rows, width), BF),
            jax.ShapeDtypeStruct((width, rows), BF),
            jax.ShapeDtypeStruct((width // HD, rows), F32),
        ),
        in_specs=[VMEM] * 8,
        out_specs=(VMEM,) * 3,
        scratch_shapes=[pltpu.VMEM((k_all.shape[0], rows), F32), pltpu.VMEM((width, rows), F32)],
        compiler_params=pltpu.CompilerParams(vmem_limit_bytes=VMEM_LIMIT),
        cost_estimate=pl.CostEstimate(
            flops=16 * width * rows * k_all.shape[0], bytes_accessed=60_000_000, transcendentals=0
        ),
        name="attend",
    )(q_down, k_all, v_all.T, cosine, sines, keys_at[:, None], places[None], length)


def attend_back(rotated, k_all, v_all, d_down, lse, tables):
    cosine, sines, keys_at, places, length = tables
    width, rows = rotated.shape
    return pl.pallas_call(
        attend_back_kernel,
        out_shape=(
            jax.ShapeDtypeStruct((rows, width), BF),
            jax.ShapeDtypeStruct(k_all.shape, F32),
            jax.ShapeDtypeStruct(k_all.shape, F32),
        ),
        in_specs=[VMEM] * 11,
        out_specs=(VMEM,) * 3,
        scratch_shapes=[pltpu.VMEM((k_all.shape[0], rows), F32), pltpu.VMEM((width, rows), F32)],
        compiler_params=pltpu.CompilerParams(vmem_limit_bytes=VMEM_LIMIT),
        cost_estimate=pl.CostEstimate(
            flops=40 * width * rows * k_all.shape[0], bytes_accessed=80_000_000, transcendentals=0
        ),
        name="attend_back",
    )(
        rotated, k_all, k_all.T, v_all, d_down, lse, cosine, sines,
        keys_at[:, None], places[None], length,
    )


def line_kernel(
    kind, masked, low, high, deps, gathers, layer, exchange, triples, w_layer, crosses,
    gain_ref, resid_ref, valid_ref, h_ref, square_ref, *rest,
):
    forward = kind in ("out", "mlp")
    wide = kind in ("mlp", "mlp_back")
    if kind == "mlp":
        lhs_refs = []
    elif kind == "mlp_back":
        lhs_refs, rest = rest[:4], rest[4:]
    else:
        lhs_refs, rest = rest[:1], rest[1:]
    w_count = 3 if wide else 1
    w_refs = []
    for triple in triples:
        w_refs.append(rest[: 3 if triple else 1])
        rest = rest[3 if triple else 1 :]
    rest = rest[deps:]
    base_refs, rest = rest[: 2 * gathers], rest[2 * gathers :]
    cross_refs, rest = rest[: len(crosses)], rest[len(crosses) :]
    out_ref, rest = rest[0], rest[1:]
    if kind == "mlp":
        normed_ref, ms_ref, gate_ref, up_ref, hidden_ref = rest[:5]
        rest = rest[5:]
    elif kind == "mlp_back":
        product_refs, rest = rest[:3], rest[3:]
        arrived_refs, rest = rest[:exchange], rest[exchange:]
    block_refs, rest = rest[:gathers], rest[gathers:]
    crossed_refs, rest = rest[: len(crosses)], rest[len(crosses) :]
    if crosses:
        x_send, x_recv = rest[-2:]
        rest = rest[:-2]
    w_alls, rest = rest[:w_count], rest[w_count:]
    (
        part, from_end, from_mid, pair,
        w_sem, up_send, up_recv, mid_send, mid_recv, fin_send, fin_recv,
    ) = rest[:11]
    if gathers:
        far_send, far_recv, near_send, near_recv, cross_send, cross_recv = rest[11:]
    if kind == "mlp_back":
        (
            d_gate_ref, d_up_ref, far_normed, far_dm, far_hidden, far_d_gate, far_d_up, stage,
            give_sem, take_sem, stage_sem,
        ) = rest[11:22]
    if exchange:
        y_stage, y_send, y_recv = rest[22:]
    shard = lax.axis_index("gx")
    far, near = shard ^ 2, shard ^ 1
    section = lax.axis_index("section")
    rows, width = resid_ref.shape
    columns = width // 4
    count = rows // CHUNK
    z = lax.axis_index("gy")
    middle = (z == 1) | (z == 2)
    end_of = jnp.where(z == 1, 0, 3)
    mid_of = jnp.where(z == 0, 1, 2)
    across = 3 - z

    def loading(w, j, cut_of, target, slot):
        whole = w_refs[w]
        copies = [(None, pltpu.make_async_copy(cut_of(whole[0].at[j]), target, w_sem.at[slot]))]
        if triples[w]:
            home = section == w_layer
            copies = [(shard != j, copies[0][1])]
            for ref, holds in zip(whole[1:], (home, jnp.logical_not(home))):
                copy = pltpu.make_async_copy(cut_of(ref), target, w_sem.at[slot])
                copies.append(((shard == j) & holds, copy))
        return copies

    loads, downs = [], []
    if wide:
        hidden_width = w_alls[0].shape[1]
        for x0 in range(0, hidden_width, 512):
            x1 = min(x0 + 512, hidden_width)
            for w in range(2):
                for j in range(4):
                    target = w_alls[w].at[j * columns : (j + 1) * columns, x0:x1]
                    loads.append(loading(w, j, lambda ref: ref.at[:, x0:x1], target, len(loads)))
        for j in range(4):
            downs.append(loading(2, j, lambda ref: ref, w_alls[2].at[j], len(loads) + j))
    else:
        for j in range(4):
            loads.append(loading(0, j, lambda ref: ref.at[:, low:high], w_alls[0].at[j], j))
    for load in downs + loads if kind == "mlp_back" else loads + downs:
        for holds, copy in load:
            if holds is None:
                copy.start()
            else:
                pl.when(holds)(copy.start)
    loads, downs = [x[0][1] for x in loads], [x[0][1] for x in downs]

    barrier = pltpu.get_barrier_semaphore()
    peers = []
    if gathers:
        peers = [{"gx": far}, {"gx": near}, {"section": 1 - section}]
    elif kind == "mlp_back":
        peers = [{"gx": near}] + [{"gx": far}] * (exchange > 0)
    if crosses:
        assert not gathers
        peers.append({"section": 1 - section})
    beside = len(peers)
    for peer in peers:
        pl.semaphore_signal(barrier, inc=1, device_id=peer, device_id_type=MESH)

    @pl.when(middle)
    def _():
        pl.semaphore_signal(barrier, inc=1, device_id={"gy": end_of}, device_id_type=MESH)
        pl.semaphore_signal(barrier, inc=1, device_id={"gy": across}, device_id_type=MESH)
        pl.semaphore_wait(barrier, 2 + beside)

    @pl.when(jnp.logical_not(middle))
    def _():
        pl.semaphore_signal(barrier, inc=1, device_id={"gy": mid_of}, device_id_type=MESH)
        pl.semaphore_wait(barrier, 1 + beside)

    x_peer = {"section": 1 - section}

    def x_copy(k):
        return pltpu.make_async_remote_copy(
            src_ref=cross_refs[k], dst_ref=crossed_refs[k], send_sem=x_send.at[k],
            recv_sem=x_recv.at[k], device_id=x_peer, device_id_type=MESH,
        )

    def x_sends(k):
        return section != crosses[k] if crosses[k] < 2 else section >= 0

    def x_takes(k):
        return section == crosses[k] if crosses[k] < 2 else section >= 0

    for k in range(len(crosses)):
        pl.when(x_sends(k))(lambda k=k: x_copy(k).start())

    def half_of(ref, k, which):
        size = base_refs[2 * k].shape[0] // 2
        return ref.at[pl.ds(pl.multiple_of(which * size, 16), size), :]

    def far_copy(k, source):
        return pltpu.make_async_remote_copy(
            src_ref=half_of(source, k, section),
            dst_ref=half_of(block_refs[k].at[shard], k, section),
            send_sem=far_send.at[k], recv_sem=far_recv.at[k],
            device_id={"gx": far}, device_id_type=MESH,
        )

    def near_copy(k, source):
        return pltpu.make_async_remote_copy(
            src_ref=source, dst_ref=block_refs[k].at[shard], send_sem=near_send.at[3 * k],
            recv_sem=near_recv.at[3 * k], device_id={"gx": near}, device_id_type=MESH,
        )

    def cross_copy(k):
        rows_here = half_of(block_refs[k].at[far], k, section)
        return pltpu.make_async_remote_copy(
            src_ref=rows_here, dst_ref=rows_here, send_sem=cross_send.at[k],
            recv_sem=cross_recv.at[k], device_id=x_peer, device_id_type=MESH,
        )

    def pass_copy(k, late):
        rows_here = half_of(block_refs[k].at[far], k, 1 - section if late else section)
        return pltpu.make_async_remote_copy(
            src_ref=rows_here, dst_ref=rows_here, send_sem=near_send.at[3 * k + 1 + late],
            recv_sem=near_recv.at[3 * k + 1 + late], device_id={"gx": near}, device_id_type=MESH,
        )

    at_home = section == layer

    def from_base(k, starts):
        for ref, holds in zip(base_refs[2 * k : 2 * k + 2], (at_home, jnp.logical_not(at_home))):

            @pl.when(holds)
            def _():
                for make in starts:
                    make(k, ref).start()

    def gather_middle(k):
        far_copy(k, base_refs[2 * k]).wait_recv()
        cross_copy(k).start()
        pass_copy(k, 0).start()

    def gather_late(k):
        cross_copy(k).wait_recv()
        pass_copy(k, 1).start()

    if gathers:
        from_base(0, [far_copy])
    for k in range(gathers):
        from_base(k, [near_copy])

    half = rows // STEPS
    core = lax.rem(shard, 2)

    def give(slot, source, target):
        return pltpu.make_async_remote_copy(
            src_ref=source, dst_ref=target, send_sem=give_sem.at[slot],
            recv_sem=take_sem.at[slot], device_id={"gx": near}, device_id_type=MESH,
        )

    def chip_columns(ref, y, of):
        return ref.at[:, pl.ds(pl.multiple_of((2 * y + of) * columns, columns), columns)]

    def step_rows(ref, step):
        return ref.at[pl.ds(pl.multiple_of(step * half, half), half), :]

    if kind == "mlp_back":
        saved_gate, saved_up, saved_normed, saved_hidden = lhs_refs
        early = [give(0, saved_hidden, far_hidden)]
        for y in range(2):
            early.append(give(1 + y, chip_columns(resid_ref, y, 1 - core), far_dm.at[y]))
        for y in range(2):
            early.append(give(3 + y, chip_columns(saved_normed, y, 1 - core), far_normed.at[y]))
        for copy in early:
            copy.start()

    def give_step(step):
        return [
            give(5 + step, step_rows(d_gate_ref, step), step_rows(far_d_gate, step)),
            give(5 + STEPS + step, step_rows(d_up_ref, step), step_rows(far_d_up, step)),
        ]

    if not wide:
        for load in loads:
            load.wait()

    def at_first(step, copies):
        @pl.when(step == 0)
        def _():
            for copy in copies:
                copy.wait()

    def rows_at(ref, i):
        return ref.at[pl.ds(pl.multiple_of(i * CHUNK, CHUNK), CHUNK), :]

    def up_copy(i):
        return pltpu.make_async_remote_copy(
            src_ref=rows_at(part, i), dst_ref=rows_at(from_end, i), send_sem=up_send.at[i],
            recv_sem=up_recv.at[i], device_id={"gy": mid_of}, device_id_type=MESH,
        )

    def mid_copy(i):
        return pltpu.make_async_remote_copy(
            src_ref=rows_at(pair, i), dst_ref=rows_at(from_mid, i), send_sem=mid_send.at[i],
            recv_sem=mid_recv.at[i], device_id={"gy": across}, device_id_type=MESH,
        )

    def fin_copy(i):
        return pltpu.make_async_remote_copy(
            src_ref=rows_at(out_ref, i), dst_ref=rows_at(out_ref, i), send_sem=fin_send.at[i],
            recv_sem=fin_recv.at[i], device_id={"gy": end_of}, device_id_type=MESH,
        )

    def dot(left, right, transposed=False):
        dims = (((1,), (1 if transposed else 0,)), ((), ()))
        return lax.dot_general(left, right, dims, preferred_element_type=F32)

    def spans(extent):
        return [(x, min(x + 512, extent)) for x in range(0, extent, 512)]

    if wide:
        w_gate, w_up, w_down = w_alls

    def product(step, carry):
        here = pl.ds(pl.multiple_of(step * half, half), half)
        if kind == "mlp":
            values = resid_ref[here, :].astype(F32)
            square = jnp.mean(values * values, axis=1, keepdims=True)
            ms_ref[here, :] = square
            normed_ref[here, :] = (values * lax.rsqrt(square + EPS) * gain_ref[...]).astype(BF)
            for n, (x0, x1) in enumerate(spans(w_gate.shape[1])):
                at_first(step, loads[8 * n : 8 * n + 8])
                gate = dot(normed_ref[here, :], w_gate[:, x0:x1])
                up = dot(normed_ref[here, :], w_up[:, x0:x1])
                gate_ref[here, x0:x1] = gate.astype(BF)
                up_ref[here, x0:x1] = up.astype(BF)
                hidden_ref[here, x0:x1] = (gate * jax.nn.sigmoid(gate) * up).astype(BF)
        if kind == "mlp_back":
            at_first(step, downs)
            for x0, x1 in spans(w_gate.shape[1]):
                d_hidden = sum(
                    dot(resid_ref[here, j * columns : (j + 1) * columns], w_down[j, x0:x1, :], True)
                    for j in range(4)
                )
                gate = saved_gate[here, x0:x1].astype(F32)
                up = saved_up[here, x0:x1].astype(F32)
                sigmoid = jax.nn.sigmoid(gate)
                d_up_ref[here, x0:x1] = (d_hidden * (gate * sigmoid)).astype(BF)
                d_gate_ref[here, x0:x1] = (
                    d_hidden * up * sigmoid * (1.0 + gate * (1.0 - sigmoid))
                ).astype(BF)
            for copy in give_step(step):
                copy.start()
        if wide:
            at_first(step, downs if kind == "mlp" else loads)
        for j in range(4):
            span = slice(j * columns, (j + 1) * columns)
            if kind == "out":
                value = dot(lhs_refs[0][here, :], w_alls[0][j])
            elif kind == "mlp":
                value = dot(hidden_ref[here, :], w_down[j])
            elif kind == "mlp_back":
                value = dot(d_gate_ref[here, :], w_gate[span, :], True)
                value += dot(d_up_ref[here, :], w_up[span, :], True)
            else:
                value = dot(lhs_refs[0][here, :], w_alls[0][j], True)
            part[here, span] = value.astype(BF)

        @pl.when(jnp.logical_not(middle))
        def _():
            def send(i, inner):
                up_copy(step * (count // STEPS) + i).start()
                return inner

            lax.fori_loop(0, count // STEPS, send, 0)

        return carry

    lax.fori_loop(0, STEPS, product, 0)

    def finish(i):
        mid_copy(i).wait_recv()
        here = pl.ds(pl.multiple_of(i * CHUNK, CHUNK), CHUNK)
        total = pair[here, :].astype(F32) + from_mid[here, :].astype(F32)
        resid = resid_ref[here, :].astype(F32)
        if forward:
            result = resid + total
            if masked:
                result = result * valid_ref[here, :]
        else:
            values = h_ref[here, :].astype(F32)
            scaled = total * gain_ref[...]
            ratio = lax.rsqrt(square_ref[here, :] + EPS)
            mean_term = jnp.sum(scaled * values, axis=1, keepdims=True) * (1.0 / width)
            result = resid + ratio * scaled - values * (ratio * ratio * ratio) * mean_term
        out_ref[here, :] = result.astype(BF)
        fin_copy(i).start()

    tile = columns // 2

    def tile_rows(sub):
        return pl.ds(pl.multiple_of(sub % 2 * tile, tile), tile)

    def stage_copy(number, sub, slot):
        target = product_refs[number].at[sub // 2, tile_rows(sub), :]
        return pltpu.make_async_copy(stage.at[slot], target, stage_sem.at[slot])

    def y_copy(number, sub, slot):
        return pltpu.make_async_remote_copy(
            src_ref=y_stage.at[2 * number + slot], dst_ref=arrived_refs[number].at[tile_rows(sub), :],
            send_sem=y_send.at[2 * number + slot], recv_sem=y_recv.at[2 * number + slot],
            device_id={"gx": far}, device_id_type=MESH,
        )

    def gradient_tile(number, sub):
        slot = sub % 2
        left, far_left, right, far_right = (
            (resid_ref, far_dm, saved_hidden, far_hidden),
            (saved_normed, far_normed, d_gate_ref, far_d_gate),
            (saved_normed, far_normed, d_up_ref, far_d_up),
        )[number]

        @pl.when(sub == 0)
        def _():
            waits = [early[:3], early[3:] + give_all[:STEPS], give_all[STEPS:]][number]
            for copy in waits:
                copy.wait_recv()

        if number >= exchange:

            @pl.when((sub >= 2) | (number > 0))
            def _():
                stage_copy(number, sub, slot).wait()

        elif number > 0:

            @pl.when(sub >= 2)
            def _():
                stage_copy(number, sub - 2, slot).wait()

        y = sub // 2
        if number < exchange:
            y = jnp.where(sub < 2, 1 - lax.div(shard, 2), lax.div(shard, 2))
        start = (y * 2 + core) * columns + sub % 2 * tile
        mine = left[:, pl.ds(pl.multiple_of(start, tile), tile)]
        theirs = far_left[y, :, tile_rows(sub)]
        value = dot_to(mine, right[...], ((0,), (0,))) + dot_to(theirs, far_right[...], ((0,), (0,)))
        if number < exchange:

            @pl.when(sub < 2)
            def _():
                y_stage[2 * number + slot] = value.astype(BF)
                y_copy(number, sub, slot).start()

            @pl.when(sub >= 2)
            def _():
                stage[slot] = value.astype(BF)
                stage_copy(number, sub - 2, slot).start()

        else:
            stage[slot] = value.astype(BF)
            stage_copy(number, sub, slot).start()

    if kind == "mlp_back":
        give_all = [x for pair in zip(*(give_step(n) for n in range(STEPS))) for x in pair]

    def beside_step(i):
        pass_on(i)
        if kind == "mlp_back":
            for number in range(3):
                first = 3 + 4 * number

                @pl.when((i >= first) & (i < first + 4))
                def _():
                    gradient_tile(number, i - first)

    def pass_on(i):
        if gathers == 2:
            at(2, i, lambda: from_base(1, [far_copy]))
            at(6, i, lambda: gather_middle(0))
            at(10, i, lambda: gather_middle(1))
            at(11, i, lambda: gather_late(0))
            at(15, i, lambda: gather_late(1))

    def at(sixteenth, i, action):
        pl.when(i == count * sixteenth // 16)(action)

    @pl.when(middle)
    def _():
        def step(i, carry):
            up_copy(i).wait_recv()
            here = pl.ds(pl.multiple_of(i * CHUNK, CHUNK), CHUNK)
            pair[here, :] = (part[here, :].astype(F32) + from_end[here, :].astype(F32)).astype(BF)
            mid_copy(i).start()

            @pl.when(i >= 1)
            def _():
                finish(i - 1)

            beside_step(i)
            return carry

        lax.fori_loop(0, count, step, 0)
        finish(count - 1)

        def drain(i, carry):
            mid_copy(i).wait_send()
            fin_copy(i).wait_send()
            return carry

        lax.fori_loop(0, count, drain, 0)

    @pl.when(jnp.logical_not(middle))
    def _():
        def drain(i, carry):
            up_copy(i).wait_send()
            fin_copy(i).wait_recv()
            beside_step(i)
            return carry

        lax.fori_loop(0, count, drain, 0)

    if kind == "mlp_back":
        for slot in range(2):
            stage_copy(2, 2 + slot, slot).wait()
        for copy in early + give_all:
            copy.wait_send()
        for number in range(exchange):
            for slot in range(2):
                y_copy(number, slot, slot).wait()
    for k in range(len(crosses)):
        pl.when(x_sends(k))(lambda k=k: x_copy(k).wait_send())
        pl.when(x_takes(k))(lambda k=k: x_copy(k).wait_recv())
    for k in range(gathers):
        far_copy(k, base_refs[2 * k]).wait_send()
        near_copy(k, base_refs[2 * k]).wait()
        cross_copy(k).wait_send()
        pass_copy(k, 0).wait()
        pass_copy(k, 1).wait()


def line_sum(kind, ident, resid, weights, lhs=(), gain=None, valid=None, back=None, low=0, high=0, deps=(), bases=(), layer=0, exchange=0, w_layer=0, crosses=()):
    rows, width = resid.shape
    one = jnp.ones((rows, 1), F32)
    h, square = back if back is not None else (jnp.zeros((16, 128), BF), jnp.zeros((8, 1), F32))
    gain = jnp.zeros((width,), F32) if gain is None else gain
    wide = kind in ("mlp", "mlp_back")
    hidden = 0
    if wide:
        hidden = (weights[2][0] if isinstance(weights[2], tuple) else weights[2]).shape[1]
    w_scratch = []
    triples = [isinstance(w, tuple) for w in weights]
    w_flat = [x for w in weights for x in (w if isinstance(w, tuple) else (w,))]
    for i, w in enumerate(weights):
        _, depth, across = (w[0] if isinstance(w, tuple) else w).shape
        if wide and i < 2:
            w_scratch.append(pltpu.VMEM((width, across), BF))
        else:
            w_scratch.append(pltpu.VMEM((4, depth, across if wide else high - low), BF))
    outs, products, beside = [((rows, width), BF)], [], []
    if kind == "mlp":
        outs += [((rows, width), BF), ((rows, 1), F32)] + [((rows, hidden), BF)] * 3
    elif kind == "mlp_back":
        products = [((1 if n < exchange else 2, width // 4, hidden), BF) for n in range(3)]
        products += [((width // 4, hidden), BF)] * exchange
        half_block = pltpu.VMEM((2, rows, width // 4), BF)
        beside = [pltpu.VMEM((rows, hidden), BF)] * 2 + [half_block] * 2
        beside += [pltpu.VMEM((rows, hidden), BF)] * 3 + [pltpu.VMEM((2, width // 8, hidden), BF)]
        beside += [pltpu.SemaphoreType.DMA((n,)) for n in (5 + 2 * STEPS, 5 + 2 * STEPS, 2)]
        if exchange:
            beside += [pltpu.VMEM((2 * exchange, width // 8, hidden), BF)]
            beside += [pltpu.SemaphoreType.DMA((2 * exchange,))] * 2
    blocks = [((4,) + base[0].shape, BF) for base in bases]
    pairs = [x for base in bases for x in base]
    crossed = [(x[0].shape, BF) for x in crosses]
    depth = 3 * hidden if wide else lhs[0].shape[1]
    count = rows // CHUNK
    dma = pltpu.SemaphoreType.DMA
    return pl.pallas_call(
        functools.partial(
            line_kernel, kind, valid is not None, low, high, len(deps), len(bases), layer, exchange,
            triples, w_layer, [x[1] for x in crosses],
        ),
        out_shape=tuple(jax.ShapeDtypeStruct(*o) for o in outs + products + blocks + crossed),
        in_specs=[VMEM] * (5 + len(lhs)) + [ANY] * (len(w_flat) + len(deps) + len(pairs) + len(crosses)),
        out_specs=tuple([VMEM] * len(outs) + [ANY] * len(products + blocks + crossed)),
        scratch_shapes=w_scratch
        + [pltpu.VMEM((rows, width), BF)] * 4
        + [dma((8 * -(-hidden // 512) + 4,))]
        + [dma((count,))] * 6
        + [dma((n * len(bases),)) for n in (1, 1, 3, 3, 1, 1) if bases]
        + beside
        + [dma((len(crosses),))] * 2 * bool(crosses),
        compiler_params=pltpu.CompilerParams(
            collective_id=ident, has_side_effects=True, vmem_limit_bytes=VMEM_LIMIT
        ),
        cost_estimate=pl.CostEstimate(
            flops=2 * rows * depth * width, bytes_accessed=200 * 1024 * 1024, transcendentals=0
        ),
        name="line_" + kind,
    )(
        gain[None], resid, one if valid is None else valid, h, square, *lhs, *w_flat, *deps, *pairs,
        *(x[0] for x in crosses),
    )


def plain_sum(total):
    return lax.psum(total.astype(BF), "gy").astype(F32)


def normed(h, gain):
    values = h.astype(F32)
    square = jnp.mean(values * values, axis=1, keepdims=True)
    return square, (values * lax.rsqrt(square + EPS) * gain).astype(BF)


def norm_back(d_normed, h, square, gain):
    values = h.astype(F32)
    ratio = lax.rsqrt(square + EPS)
    scaled = d_normed * gain
    mean_term = jnp.mean(scaled * values, axis=1, keepdims=True)
    return ratio * scaled - values * (ratio * ratio * ratio) * mean_term


def attention_forward(h, gain, w_attn, low, tables, ident, bases, layer, deps=()):
    rows, width = h.shape
    high = low + width // lax.axis_size("gx")
    q_width = low - 2 * HD
    cosine, sines = tables[:2]
    square, n1 = normed(h, gain)
    q_down = mm(tall(cut(w_attn, 0, q_width)), n1, ((0,), (1,)))
    kv = mm(n1, tall(cut(w_attn, q_width, low)))
    k_rot = rope_down(kv[:, :HD].T, cosine, sines).T.astype(BF)
    kv = jnp.concatenate([k_rot, kv[:, HD:].astype(BF)], axis=1)
    kv_all = jnp.concatenate([kv, swap_pairs(kv, "gx")], axis=0)
    k_all, v_all = kv_all[:, :HD], kv_all[:, HD:]
    heads, rotated, lse = attend(q_down, k_all, v_all, tables)
    if fused():
        h1, *stacks = line_sum(
            "out", ident, h, [w_attn], (heads,), low=low, high=high,
            deps=deps, bases=bases, layer=layer,
        )
        blocks = [(x, *pair) for x, pair in zip(stacks, bases)]
    else:
        h1 = (h.astype(F32) + plain_sum(mm(heads, side(cut(w_attn, low, high))))).astype(BF)
        blocks = [gather_blocks(chosen(x, layer)) for x in bases]
    return h1, square, blocks, (h, square, n1, rotated, lse, k_all, v_all, heads)


def mlp_forward(h1, gain, weights, valid, ident, bases=(), layer=0, w_layer=0):
    if fused():
        result, n2, square, gate, up, hidden, *stacks = line_sum(
            "mlp", ident, h1, weights, gain=gain, valid=valid, bases=bases, layer=layer,
            w_layer=w_layer,
        )
        blocks = [(x, *pair) for x, pair in zip(stacks, bases)]
    else:
        square, n2 = normed(h1, gain)
        gate = mm(n2, tall(weights[0]))
        up = mm(n2, tall(weights[1]))
        hidden = (gate * jax.nn.sigmoid(gate) * up).astype(BF)
        gate, up = gate.astype(BF), up.astype(BF)
        result = h1.astype(F32) + plain_sum(mm(hidden, side(weights[2])))
        result = (result * valid).astype(BF)
        blocks = [gather_blocks(chosen(x, layer)) for x in bases]
    return result, square, blocks, (h1, square, n2, gate, up, hidden)


def mlp_backward(dm, gain, weights, saved, ident, w_layer, crosses=(), deps=(), exchange=1):
    h1, square, n2, gate, up, hidden = saved
    if fused():
        e1, *products = line_sum(
            "mlp_back", ident, dm, weights, (gate, up, n2, hidden), gain=gain,
            back=(h1, square), exchange=exchange, w_layer=w_layer, crosses=crosses, deps=deps,
        )
        return e1, products[:4], products[4:]
    gate, up = gate.astype(F32), up.astype(F32)
    d_hidden = mm(dm, side(weights[2]), ((1,), (1,)))
    sigmoid = jax.nn.sigmoid(gate)
    d_gate = (d_hidden * up * sigmoid * (1.0 + gate * (1.0 - sigmoid))).astype(BF)
    d_up = (d_hidden * (gate * sigmoid)).astype(BF)
    total = mm(d_gate, tall(weights[0]), ((1,), (1,))) + mm(d_up, tall(weights[1]), ((1,), (1,)))
    e1 = (dm.astype(F32) + norm_back(plain_sum(total), h1, square, gain)).astype(BF)
    turn = ((0,), (0,))
    products = [mm(dm, hidden, turn), mm(n2, d_gate, turn), mm(n2, d_up, turn)]
    return e1, [p.astype(BF) for p in products], crossing(crosses)


def crossing(crosses):
    pairs = ([(1, 0)], [(0, 1)], [(0, 1), (1, 0)])
    return [lax.ppermute(x, "section", pairs[way]) for x, way in crosses]


def mlp_sums(products):
    if not fused():
        return [shard_sum(p) for p in products]
    down, gate, up, arrived = products
    first = (down[0].astype(F32) + arrived.astype(F32)).astype(BF)
    return [first, chip_sum(gate), chip_sum(up)]


def attention_backward(e1, w_attn, low, tables, saved):
    h, square, n1, rotated, lse, k_all, v_all, heads = saved
    rows, width = h.shape
    cosine, sines = tables[:2]
    w_o = side(cut(w_attn, low, low + width // lax.axis_size("gx")))
    d_down = mm(w_o, e1, ((1,), (1,))).astype(BF)
    dq, dk, dv = attend_back(rotated, k_all, v_all, d_down, lse, tables)
    dkv = jnp.concatenate([dk, dv], axis=1)
    dkv = dkv[:rows] + swap_pairs(dkv[rows:], "gx")
    dk = rope_down(dkv[:, :HD].T, cosine, -sines).T
    d_qkv = jnp.concatenate([dq, dk.astype(BF), dkv[:, HD:].astype(BF)], axis=1)
    turn = ((0,), (0,))
    products = [mm(n1, d_qkv, turn).astype(BF), mm(e1, heads, turn).astype(BF)]
    return d_qkv, jnp.concatenate(products, axis=1)


def attention_end(d_qkv, e1, w_attn, gain, saved, ident, deps, crosses):
    h, square = saved[:2]
    qkv_width = d_qkv.shape[1]
    if fused():
        grad, *crossed = line_sum(
            "back", ident, e1, [w_attn], (d_qkv,), gain=gain, back=(h, square),
            low=0, high=qkv_width, deps=deps, crosses=crosses,
        )
        return grad, crossed
    total = plain_sum(mm(d_qkv, tall(cut(w_attn, 0, qkv_width)), ((1,), (1,))))
    grad = (e1.astype(F32) + norm_back(total, h, square, gain)).astype(BF)
    return grad, crossing(crosses)


def on_device(
    hidden_in, out_grad, lengths, dealing, attn_gain, w_query, w_key, w_value, w_out,
    mlp_gain, w_gate, w_up, w_down,
):
    shards = lax.axis_size("gx")
    shard = lax.axis_index("gx")
    section = lax.axis_index("section")
    column = lax.axis_index("gy")
    core = shard % 2
    sequence = (shard // 2) * 2 + section
    span, width = hidden_in.shape
    half = span // 2
    seq_length = lax.dynamic_index_in_dim(lengths, sequence, keepdims=False)

    both = jnp.concatenate([hidden_in, out_grad], axis=1)
    mine = core_rows(both, core)
    theirs = swap_pairs(core_rows(both, 1 - core), "gx")
    mine = jnp.where(core == section, mine, theirs)
    h = lax.all_gather(mine[:, :width], "gy", axis=1, tiled=True)

    kv_head = column * (w_query.shape[2] // HD) // (QH // KVH)
    low = w_query.shape[2] + 2 * HD
    both_gains = jnp.stack([attn_gain[0], mlp_gain[0]], axis=1)
    attn_own = jnp.concatenate(
        [
            w_query[0],
            lax.dynamic_slice_in_dim(w_key[0], kv_head * HD, HD, 1),
            lax.dynamic_slice_in_dim(w_value[0], kv_head * HD, HD, 1),
            w_out[0],
            jnp.pad(both_gains, ((0, 0), (0, 126))),
        ],
        axis=1,
    )
    own = (attn_own, w_gate[0], w_up[0], w_down[0])
    first = [(array, lax.ppermute(array, "section", [(0, 1)])) for array in own]
    second = [(array, lax.ppermute(array, "section", [(1, 0)])) for array in own]

    def gains_of(w_attn):
        pair = w_attn[:, :, w_attn.shape[2] - 128 : w_attn.shape[2] - 126]
        return pair.reshape(-1, 2).T.astype(F32)

    here = core_rows(jnp.arange(span), core)
    there = core_rows(jnp.arange(span), 1 - core)
    keys_at = jnp.concatenate([here, there])
    valid = (here < seq_length)[:, None].astype(F32)
    tables = (*rope_tables(here), keys_at, here, seq_length.reshape(1, 1))

    attn0, gate0 = gather_blocks(chosen(first[0], 0)), gather_blocks(chosen(first[1], 0))
    gains0 = gains_of(attn0)
    h1, square_a, blocks, saved_a0 = attention_forward(
        h, gains0[0], attn0, low, tables, 0, first[2:], 0, (gate0,)
    )
    mlp0 = [gate0] + blocks
    h, square_m, (attn1, gate1), saved_m0 = mlp_forward(
        h1, gains0[1], mlp0, valid, 1, second[:2], 1
    )
    if fused():
        attn1 = with_own(attn1[0], second[0], 1)
    gains1 = gains_of(attn1)
    outputs, squares = [h], [square_a, square_m]
    d_mine = mine[:, width:] + h[:1, :1] * 0
    d_out = lax.all_gather(d_mine, "gy", axis=1, tiled=True)
    h1, square_a, blocks, saved_a1 = attention_forward(
        h, gains1[0], attn1, low, tables, 2, second[2:], 1
    )
    mlp1 = [gate1] + blocks
    h, square_m, _, saved_m1 = mlp_forward(h1, gains1[1], mlp1, valid, 3, w_layer=1)
    outputs.append(h)
    squares = jnp.concatenate(squares + [square_a, square_m], axis=1)
    rms = (jnp.sqrt(squares + EPS) * valid).T
    statistics = [rms[:2], rms[2:]]
    outputs = [lax.dynamic_slice_in_dim(x, column * width, width, 1) for x in outputs]

    def to_section(per_layer):
        kept = jnp.where(section == 0, per_layer[0], per_layer[1])
        sent = swap_pairs(jnp.where(section == 0, per_layer[1], per_layer[0]), "section")
        return kept, sent

    dm = (d_out.astype(F32) * valid).astype(BF)
    e1, products, _ = mlp_backward(dm, gains1[1], mlp1, saved_m1, 4, 1)
    local1 = mlp_sums(products)

    both = []
    for output, stat in zip(outputs, statistics):
        high = stat.astype(BF)
        rest = (stat - high.astype(F32)).astype(BF)
        parts = jnp.concatenate([high, rest], axis=0).reshape(-1, width)
        parts = jnp.pad(parts, ((0, -parts.shape[0] % 16), (0, 0)))
        both.append(jnp.concatenate([output + e1[:1, :1] * 0, parts], axis=0))
    kept = jnp.where(section == 0, both[0], both[1])
    sent = jnp.where(section == 0, both[1], both[0])

    d_qkv, products = attention_backward(e1, attn1, low, tables, saved_a1)
    local1.append(shard_sum(products))
    crosses = [(sent, 2), (local1[0], 1)]
    grad1, (sent, down1) = attention_end(
        d_qkv, e1, attn1, gains1[0], saved_a1, 5, (products,), crosses
    )
    by_section = jnp.stack([jnp.where(section == 0, kept, sent), jnp.where(section == 0, sent, kept)])
    everything = lax.all_gather(by_section, "gx", axis=0)
    owner = jnp.sum(jnp.where(dealing == shard, jnp.arange(shards), 0))
    halves = lax.dynamic_slice(
        everything, ((owner // 2) * 2, owner % 2, 0, 0), (2, 1) + everything.shape[2:]
    )[:, 0]
    layer_out = join_halves(halves[0, :half], halves[1, :half])
    stat_rows = 4 * half // width
    parts = halves[:, half : half + stat_rows].astype(F32).reshape(2, 4, half)
    stat_halves = parts[:, :2] + parts[:, 2:]
    stats_out = join_halves(stat_halves[0].T, stat_halves[1].T).T

    dm = (grad1.astype(F32) * valid).astype(BF)
    crosses = [(local1[1], 1), (local1[3], 1)]
    e1, products, (gate1, attn_sum1) = mlp_backward(
        dm, gains0[1], mlp0, saved_m0, 6, 0, crosses, local1[2:3]
    )
    local0 = mlp_sums(products)
    d_qkv, products = attention_backward(e1, attn0, low, tables, saved_a0)
    local0.append(shard_sum(products))
    crosses = [(local1[2], 1), (local0[0], 0), (local0[1], 0)]
    grad0, (up1, down0, gate0) = attention_end(
        d_qkv, e1, attn0, gains0[0], saved_a0, 7, (products, everything), crosses
    )

    input_grads = [lax.dynamic_slice_in_dim(x, column * width, width, 1) for x in (grad0, grad1)]
    local0[2] = local0[2] + grad0[:1, :1] * 0
    received0 = [down0, gate0] + crossing([(x, 0) for x in local0[2:]])
    received1 = [down1, gate1, up1, attn_sum1]
    totals = [
        jnp.where(section == 0, a0.astype(F32) + r0.astype(F32), a1.astype(F32) + r1.astype(F32))
        for a0, r0, a1, r1 in zip(local0, received0, local1, received1)
    ]
    s_down, s_gate, s_up, s_attn = totals
    s_out = s_attn[:, low:]
    q_width = w_query.shape[2]

    attn_sum = jnp.sum(s_attn[:, :low] * attn_own[:, :low].astype(F32), axis=1)
    mlp_sum = jnp.sum(s_gate * w_gate[0].astype(F32) + s_up * w_up[0].astype(F32), axis=1)
    sums = jnp.pad(jnp.stack([attn_sum, mlp_sum], axis=1), ((0, 0), (0, 126)))
    spread = jnp.concatenate([s_attn[:, q_width:low], sums], axis=1).astype(BF)
    spread = lax.all_gather(spread, "gy", axis=0).astype(F32)
    gains = jnp.sum(spread[:, :, 2 * HD : 2 * HD + 2], axis=0).T / both_gains.astype(F32).T
    kv_sum = spread[:, :, : 2 * HD].reshape(KVH, -1, *spread.shape[1:2], 2, HD).sum(axis=1)
    kv_sum = kv_sum.transpose(2, 1, 0, 3).reshape(2, spread.shape[1], KVH * HD)

    kept, sent = to_section(input_grads)
    keep = jnp.where(core == section, kept, sent)
    give = swap_pairs(jnp.where(core == section, sent, kept), "gx")
    back_home = join_halves(jnp.where(core == 0, keep, give), jnp.where(core == 0, give, keep))
    return (
        layer_out[None],
        stats_out[None],
        back_home[None],
        gains[None, 0],
        s_attn[None, :, :q_width],
        kv_sum[None, 0],
        kv_sum[None, 1],
        s_out.T[None],
        gains[None, 1],
        s_gate[None],
        s_up[None],
        s_down.T[None],
    )


def solution(mesh):
    rows_cols = P("section", "gx", "gy")
    cols_rows = P("section", "gy", "gx")
    rows_only = P("section", "gx", None)
    gain = P("section", "gx")
    return jax.shard_map(
        on_device,
        mesh=mesh,
        in_specs=(
            P("gx", "gy"), P("gx", "gy"), P(), P(), gain, rows_cols, rows_only, rows_only,
            cols_rows, gain, rows_cols, rows_cols, cols_rows,
        ),
        out_specs=(
            rows_cols, P("section", None, "gx"), rows_cols, gain, rows_cols, rows_only, rows_only,
            cols_rows, gain, rows_cols, rows_cols, cols_rows,
        ),
        check_vma=False,
    )
```

```python
import functools

import jax
import jax.numpy as jnp
from jax import lax
from jax.experimental import pallas as pl
from jax.experimental.pallas import tpu as pltpu
from jax.sharding import PartitionSpec as P

QH = 32
KVH = 4
HD = 64
LAYERS = 2
EPS = 1e-05
BF = jnp.bfloat16
F32 = jnp.float32
MESH = pl.DeviceIdType.MESH
CHUNK = 32
STEPS = 2
VMEM_LIMIT = 56 * 1024 * 1024
ANY = pl.BlockSpec(memory_space=pl.ANY)
VMEM = pl.BlockSpec(memory_space=pltpu.VMEM)


def mm(left, right, dims=((1,), (0,))):
    return lax.dot_general(left, right, (dims, ((), ())), preferred_element_type=F32)


def swap_pairs(values, axis, by=1):
    count = lax.axis_size(axis)
    return lax.ppermute(values, axis, [(i, i ^ by) for i in range(count)])


def rope_tables(places):
    half_width = HD // 2
    frequency = jnp.power(10000.0, -2.0 * jnp.arange(half_width).astype(F32) / HD)
    angles = frequency[:, None] * places.astype(F32)[None, :]
    return jnp.cos(angles), jnp.sin(angles)


def core_rows(rows, core):
    quarter = rows.shape[0] // 4
    low = lax.dynamic_slice_in_dim(rows, core * quarter, quarter, 0)
    high = lax.dynamic_slice_in_dim(rows, (3 - core) * quarter, quarter, 0)
    return jnp.concatenate([low, high], axis=0)


def join_halves(first, second):
    quarter = first.shape[0] // 2
    return jnp.concatenate(
        [first[:quarter], second[:quarter], second[quarter:], first[quarter:]], axis=0
    )


def chip_groups():
    return [[0, 2], [1, 3]]


def gather_blocks(base):
    return lax.all_gather(base, "gx", axis=0)


def chosen(pair, layer):
    return jnp.where(lax.axis_index("section") == layer, *pair)


def with_own(stack, pair, layer):
    shard = lax.axis_index("gx")
    return lax.dynamic_update_index_in_dim(stack, chosen(pair, layer), shard, 0)


def fused():
    return lax.axis_size("gx") == 4 and lax.axis_size("gy") == 4


def tall(w):
    return w.reshape(-1, w.shape[-1])


def side(w):
    return jnp.concatenate([w[i] for i in range(w.shape[0])], axis=1)


def cut(w, low, high):
    return w[:, :, low:high]


def shard_sum(product):
    return lax.psum_scatter(product, "gx", scatter_dimension=0, tiled=True)


def chip_sum(product):
    product = product.reshape(-1, product.shape[-1])
    return lax.psum_scatter(
        product, "gx", scatter_dimension=0, tiled=True, axis_index_groups=[[0, 2], [1, 3]]
    )


def rope_down(values, cosine, sines):
    half_width = HD // 2
    first, second = values[:half_width], values[half_width:]
    return jnp.concatenate(
        [first * cosine - second * sines, second * cosine + first * sines], axis=0
    )


def fill_bias(bias_ref, key_ref, query_ref, length_ref):
    keys = key_ref[...]
    allowed = (keys <= query_ref[...]) & (keys < length_ref[...])
    bias_ref[...] = jnp.where(allowed, 0.0, -1e30)


def dot_to(left, right, dims):
    return lax.dot_general(left, right, (dims, ((), ())), preferred_element_type=F32)


def attend_kernel(
    q_ref, k_ref, vt_ref, cos_ref, sin_ref, key_ref, query_ref, length_ref,
    heads_ref, rot_ref, lse_ref, bias_ref, out_ref,
):
    fill_bias(bias_ref, key_ref, query_ref, length_ref)

    def head(h, carry):
        here = pl.ds(pl.multiple_of(h * HD, HD), HD)
        rotated = rope_down(q_ref[here, :], cos_ref[...], sin_ref[...]).astype(BF)
        rot_ref[here, :] = rotated
        scaled = (rotated.astype(F32) * HD ** (-0.5)).astype(BF)
        scores = dot_to(k_ref[...], scaled, ((1,), (0,))) + bias_ref[...]
        top = jnp.max(scores, axis=0, keepdims=True)
        exponent = jnp.exp(scores - top)
        total = jnp.sum(exponent, axis=0, keepdims=True)
        probs = (exponent * (1.0 / total)).astype(BF)
        out_ref[here, :] = dot_to(vt_ref[...], probs, ((1,), (0,)))
        lse_ref[pl.ds(h, 1), :] = top + jnp.log(total)
        return carry

    lax.fori_loop(0, q_ref.shape[0] // HD, head, 0)
    heads_ref[...] = out_ref[...].T.astype(BF)


def attend_back_kernel(
    rot_ref, k_ref, kt_ref, v_ref, d_ref, lse_ref, cos_ref, sin_ref, key_ref, query_ref, length_ref,
    dq_ref, dk_ref, dv_ref, bias_ref, out_ref,
):
    fill_bias(bias_ref, key_ref, query_ref, length_ref)
    dk_ref[...] = jnp.zeros_like(dk_ref)
    dv_ref[...] = jnp.zeros_like(dv_ref)
    scaling = HD ** (-0.5)

    def head(h, carry):
        here = pl.ds(pl.multiple_of(h * HD, HD), HD)
        scaled = (rot_ref[here, :].astype(F32) * scaling).astype(BF)
        scores = dot_to(k_ref[...], scaled, ((1,), (0,))) + bias_ref[...]
        probs = jnp.exp(scores - lse_ref[pl.ds(h, 1), :])
        d_probs = dot_to(v_ref[...], d_ref[here, :], ((1,), (0,)))
        delta = jnp.sum(probs * d_probs, axis=0, keepdims=True)
        d_scores = (probs * (d_probs - delta)).astype(BF)
        dk_ref[...] += dot_to(d_scores, scaled, ((1,), (1,)))
        dv_ref[...] += dot_to(probs.astype(BF), d_ref[here, :], ((1,), (1,)))
        dq = dot_to(kt_ref[...], d_scores, ((1,), (0,))) * scaling
        out_ref[here, :] = rope_down(dq, cos_ref[...], -sin_ref[...])
        return carry

    lax.fori_loop(0, rot_ref.shape[0] // HD, head, 0)
    dq_ref[...] = out_ref[...].T.astype(BF)


def attend(q_down, k_all, v_all, tables):
    cosine, sines, keys_at, places, length = tables
    width, rows = q_down.shape
    return pl.pallas_call(
        attend_kernel,
        out_shape=(
            jax.ShapeDtypeStruct((rows, width), BF),
            jax.ShapeDtypeStruct((width, rows), BF),
            jax.ShapeDtypeStruct((width // HD, rows), F32),
        ),
        in_specs=[VMEM] * 8,
        out_specs=(VMEM,) * 3,
        scratch_shapes=[pltpu.VMEM((k_all.shape[0], rows), F32), pltpu.VMEM((width, rows), F32)],
        compiler_params=pltpu.CompilerParams(vmem_limit_bytes=VMEM_LIMIT),
        cost_estimate=pl.CostEstimate(
            flops=16 * width * rows * k_all.shape[0], bytes_accessed=60_000_000, transcendentals=0
        ),
        name="attend",
    )(q_down, k_all, v_all.T, cosine, sines, keys_at[:, None], places[None], length)


def attend_back(rotated, k_all, v_all, d_down, lse, tables):
    cosine, sines, keys_at, places, length = tables
    width, rows = rotated.shape
    return pl.pallas_call(
        attend_back_kernel,
        out_shape=(
            jax.ShapeDtypeStruct((rows, width), BF),
            jax.ShapeDtypeStruct(k_all.shape, F32),
            jax.ShapeDtypeStruct(k_all.shape, F32),
        ),
        in_specs=[VMEM] * 11,
        out_specs=(VMEM,) * 3,
        scratch_shapes=[pltpu.VMEM((k_all.shape[0], rows), F32), pltpu.VMEM((width, rows), F32)],
        compiler_params=pltpu.CompilerParams(vmem_limit_bytes=VMEM_LIMIT),
        cost_estimate=pl.CostEstimate(
            flops=40 * width * rows * k_all.shape[0], bytes_accessed=80_000_000, transcendentals=0
        ),
        name="attend_back",
    )(
        rotated, k_all, k_all.T, v_all, d_down, lse, cosine, sines,
        keys_at[:, None], places[None], length,
    )


def start_pieces(source, target, send_sem, recv_sem, device_id, pieces=4):
    rows = source.shape[0]
    size = -(-rows // (16 * pieces)) * 16
    for low in range(0, rows, size):
        here = pl.ds(low, min(size, rows - low))
        pltpu.make_async_remote_copy(
            src_ref=source.at[here], dst_ref=target.at[here], send_sem=send_sem,
            recv_sem=recv_sem, device_id=device_id, device_id_type=MESH,
        ).start()


class Bulk:
    def __init__(self, source, target, send_sem, recv_sem, device_id):
        self.parts = (source, target, send_sem, recv_sem, device_id)
        self.make = lambda: pltpu.make_async_remote_copy(
            src_ref=source, dst_ref=target, send_sem=send_sem, recv_sem=recv_sem,
            device_id=device_id, device_id_type=MESH,
        )

    def start(self):
        start_pieces(*self.parts)

    def wait(self):
        self.make().wait()

    def wait_send(self):
        self.make().wait_send()

    def wait_recv(self):
        self.make().wait_recv()


def line_kernel(
    kind, masked, low, high, deps, gathers, layer, exchange, triples, w_layer, crosses,
    gain_ref, resid_ref, valid_ref, h_ref, square_ref, *rest,
):
    forward = kind in ("out", "mlp")
    wide = kind in ("mlp", "mlp_back")
    if kind == "mlp":
        lhs_refs = []
    elif kind == "mlp_back":
        lhs_refs, rest = rest[:4], rest[4:]
    else:
        lhs_refs, rest = rest[:1], rest[1:]
    w_count = 3 if wide else 1
    w_refs = []
    for triple in triples:
        w_refs.append(rest[: 3 if triple else 1])
        rest = rest[3 if triple else 1 :]
    rest = rest[deps:]
    base_refs, rest = rest[: 2 * gathers], rest[2 * gathers :]
    cross_refs, rest = rest[: len(crosses)], rest[len(crosses) :]
    out_ref, rest = rest[0], rest[1:]
    if kind == "mlp":
        normed_ref, ms_ref, gate_ref, up_ref, hidden_ref = rest[:5]
        rest = rest[5:]
    elif kind == "mlp_back":
        product_refs, rest = rest[:3], rest[3:]
        arrived_refs, rest = rest[:exchange], rest[exchange:]
    block_refs, rest = rest[:gathers], rest[gathers:]
    crossed_refs, rest = rest[: len(crosses)], rest[len(crosses) :]
    if crosses:
        x_send, x_recv = rest[-2:]
        rest = rest[:-2]
    w_alls, rest = rest[:w_count], rest[w_count:]
    (
        part, from_end, from_mid, pair,
        w_sem, up_send, up_recv, mid_send, mid_recv, fin_send, fin_recv,
    ) = rest[:11]
    if gathers:
        far_send, far_recv, near_send, near_recv, cross_send, cross_recv = rest[11:]
    if kind == "mlp_back":
        (
            d_gate_ref, d_up_ref, far_normed, far_dm, far_hidden, far_d_gate, far_d_up, stage,
            give_sem, take_sem, stage_sem,
        ) = rest[11:22]
    if exchange:
        y_stage, y_send, y_recv = rest[22:]
    shard = lax.axis_index("gx")
    far, near = shard ^ 2, shard ^ 1
    section = lax.axis_index("section")
    rows, width = resid_ref.shape
    columns = width // 4
    count = rows // CHUNK
    z = lax.axis_index("gy")
    middle = (z == 1) | (z == 2)
    end_of = jnp.where(z == 1, 0, 3)
    mid_of = jnp.where(z == 0, 1, 2)
    across = 3 - z

    def loading(w, j, cut_of, target, slot):
        whole = w_refs[w]
        copies = [(None, pltpu.make_async_copy(cut_of(whole[0].at[j]), target, w_sem.at[slot]))]
        if triples[w]:
            home = section == w_layer
            copies = [(shard != j, copies[0][1])]
            for ref, holds in zip(whole[1:], (home, jnp.logical_not(home))):
                copy = pltpu.make_async_copy(cut_of(ref), target, w_sem.at[slot])
                copies.append(((shard == j) & holds, copy))
        return copies

    loads, downs = [], []
    if wide:
        hidden_width = w_alls[0].shape[1]
        for x0 in range(0, hidden_width, 512):
            x1 = min(x0 + 512, hidden_width)
            for w in range(2):
                for j in range(4):
                    target = w_alls[w].at[j * columns : (j + 1) * columns, x0:x1]
                    loads.append(loading(w, j, lambda ref: ref.at[:, x0:x1], target, len(loads)))
        for j in range(4):
            downs.append(loading(2, j, lambda ref: ref, w_alls[2].at[j], len(loads) + j))
    else:
        for j in range(4):
            loads.append(loading(0, j, lambda ref: ref.at[:, low:high], w_alls[0].at[j], j))
    for load in downs + loads if kind == "mlp_back" else loads + downs:
        for holds, copy in load:
            if holds is None:
                copy.start()
            else:
                pl.when(holds)(copy.start)
    loads, downs = [x[0][1] for x in loads], [x[0][1] for x in downs]

    barrier = pltpu.get_barrier_semaphore()
    peers = []
    if gathers:
        peers = [{"gx": far}, {"gx": near}, {"section": 1 - section}]
    elif kind == "mlp_back":
        peers = [{"gx": near}] + [{"gx": far}] * (exchange > 0)
    if crosses:
        assert not gathers
        peers.append({"section": 1 - section})
    beside = len(peers)
    for peer in peers:
        pl.semaphore_signal(barrier, inc=1, device_id=peer, device_id_type=MESH)

    @pl.when(middle)
    def _():
        pl.semaphore_signal(barrier, inc=1, device_id={"gy": end_of}, device_id_type=MESH)
        pl.semaphore_signal(barrier, inc=1, device_id={"gy": across}, device_id_type=MESH)
        pl.semaphore_wait(barrier, 2 + beside)

    @pl.when(jnp.logical_not(middle))
    def _():
        pl.semaphore_signal(barrier, inc=1, device_id={"gy": mid_of}, device_id_type=MESH)
        pl.semaphore_wait(barrier, 1 + beside)

    x_peer = {"section": 1 - section}

    def x_copy(k):
        return Bulk(cross_refs[k], crossed_refs[k], x_send.at[k], x_recv.at[k], x_peer)

    def x_sends(k):
        return section != crosses[k] if crosses[k] < 2 else section >= 0

    def x_takes(k):
        return section == crosses[k] if crosses[k] < 2 else section >= 0

    for k in range(len(crosses)):
        pl.when(x_sends(k))(lambda k=k: x_copy(k).start())

    def half_of(ref, k, which):
        size = base_refs[2 * k].shape[0] // 2
        return ref.at[pl.ds(pl.multiple_of(which * size, 16), size), :]

    def far_copy(k, source):
        return Bulk(
            half_of(source, k, section), half_of(block_refs[k].at[shard], k, section),
            far_send.at[k], far_recv.at[k], {"gx": far},
        )

    def near_copy(k, source):
        return Bulk(
            source, block_refs[k].at[shard], near_send.at[3 * k], near_recv.at[3 * k], {"gx": near}
        )

    def cross_copy(k):
        rows_here = half_of(block_refs[k].at[far], k, section)
        return Bulk(rows_here, rows_here, cross_send.at[k], cross_recv.at[k], x_peer)

    def pass_copy(k, late):
        rows_here = half_of(block_refs[k].at[far], k, 1 - section if late else section)
        slot = 3 * k + 1 + late
        return Bulk(rows_here, rows_here, near_send.at[slot], near_recv.at[slot], {"gx": near})

    at_home = section == layer

    def from_base(k, starts):
        for ref, holds in zip(base_refs[2 * k : 2 * k + 2], (at_home, jnp.logical_not(at_home))):

            @pl.when(holds)
            def _():
                for make in starts:
                    make(k, ref).start()

    def gather_middle(k):
        far_copy(k, base_refs[2 * k]).wait_recv()
        cross_copy(k).start()
        pass_copy(k, 0).start()

    def gather_late(k):
        cross_copy(k).wait_recv()
        pass_copy(k, 1).start()

    if gathers:
        from_base(0, [far_copy])
    for k in range(gathers):
        from_base(k, [near_copy])

    half = rows // STEPS
    core = lax.rem(shard, 2)

    def give(slot, source, target):
        return pltpu.make_async_remote_copy(
            src_ref=source, dst_ref=target, send_sem=give_sem.at[slot],
            recv_sem=take_sem.at[slot], device_id={"gx": near}, device_id_type=MESH,
        )

    def chip_columns(ref, y, of):
        return ref.at[:, pl.ds(pl.multiple_of((2 * y + of) * columns, columns), columns)]

    def step_rows(ref, step):
        return ref.at[pl.ds(pl.multiple_of(step * half, half), half), :]

    if kind == "mlp_back":
        saved_gate, saved_up, saved_normed, saved_hidden = lhs_refs
        early = [give(0, saved_hidden, far_hidden)]
        for y in range(2):
            early.append(give(1 + y, chip_columns(resid_ref, y, 1 - core), far_dm.at[y]))
        for y in range(2):
            early.append(give(3 + y, chip_columns(saved_normed, y, 1 - core), far_normed.at[y]))
        for copy in early:
            copy.start()

    def give_step(step):
        return [
            give(5 + step, step_rows(d_gate_ref, step), step_rows(far_d_gate, step)),
            give(5 + STEPS + step, step_rows(d_up_ref, step), step_rows(far_d_up, step)),
        ]

    if not wide:
        for load in loads:
            load.wait()

    def at_first(step, copies):
        @pl.when(step == 0)
        def _():
            for copy in copies:
                copy.wait()

    def rows_at(ref, i):
        return ref.at[pl.ds(pl.multiple_of(i * CHUNK, CHUNK), CHUNK), :]

    def up_copy(i):
        return pltpu.make_async_remote_copy(
            src_ref=rows_at(part, i), dst_ref=rows_at(from_end, i), send_sem=up_send.at[i],
            recv_sem=up_recv.at[i], device_id={"gy": mid_of}, device_id_type=MESH,
        )

    def mid_copy(i):
        return pltpu.make_async_remote_copy(
            src_ref=rows_at(pair, i), dst_ref=rows_at(from_mid, i), send_sem=mid_send.at[i],
            recv_sem=mid_recv.at[i], device_id={"gy": across}, device_id_type=MESH,
        )

    def fin_copy(i):
        return pltpu.make_async_remote_copy(
            src_ref=rows_at(out_ref, i), dst_ref=rows_at(out_ref, i), send_sem=fin_send.at[i],
            recv_sem=fin_recv.at[i], device_id={"gy": end_of}, device_id_type=MESH,
        )

    def dot(left, right, transposed=False):
        dims = (((1,), (1 if transposed else 0,)), ((), ()))
        return lax.dot_general(left, right, dims, preferred_element_type=F32)

    def spans(extent):
        return [(x, min(x + 512, extent)) for x in range(0, extent, 512)]

    if wide:
        w_gate, w_up, w_down = w_alls

    def product(step, carry):
        here = pl.ds(pl.multiple_of(step * half, half), half)
        if kind == "mlp":
            values = resid_ref[here, :].astype(F32)
            square = jnp.mean(values * values, axis=1, keepdims=True)
            ms_ref[here, :] = square
            normed_ref[here, :] = (values * lax.rsqrt(square + EPS) * gain_ref[...]).astype(BF)
            for n, (x0, x1) in enumerate(spans(w_gate.shape[1])):
                at_first(step, loads[8 * n : 8 * n + 8])
                gate = dot(normed_ref[here, :], w_gate[:, x0:x1])
                up = dot(normed_ref[here, :], w_up[:, x0:x1])
                gate_ref[here, x0:x1] = gate.astype(BF)
                up_ref[here, x0:x1] = up.astype(BF)
                hidden_ref[here, x0:x1] = (gate * jax.nn.sigmoid(gate) * up).astype(BF)
        if kind == "mlp_back":
            at_first(step, downs)
            for x0, x1 in spans(w_gate.shape[1]):
                d_hidden = sum(
                    dot(resid_ref[here, j * columns : (j + 1) * columns], w_down[j, x0:x1, :], True)
                    for j in range(4)
                )
                gate = saved_gate[here, x0:x1].astype(F32)
                up = saved_up[here, x0:x1].astype(F32)
                sigmoid = jax.nn.sigmoid(gate)
                d_up_ref[here, x0:x1] = (d_hidden * (gate * sigmoid)).astype(BF)
                d_gate_ref[here, x0:x1] = (
                    d_hidden * up * sigmoid * (1.0 + gate * (1.0 - sigmoid))
                ).astype(BF)
            for copy in give_step(step):
                copy.start()
        if wide:
            at_first(step, downs if kind == "mlp" else loads)
        for j in range(4):
            span = slice(j * columns, (j + 1) * columns)
            if kind == "out":
                value = dot(lhs_refs[0][here, :], w_alls[0][j])
            elif kind == "mlp":
                value = dot(hidden_ref[here, :], w_down[j])
            elif kind == "mlp_back":
                value = dot(d_gate_ref[here, :], w_gate[span, :], True)
                value += dot(d_up_ref[here, :], w_up[span, :], True)
            else:
                value = dot(lhs_refs[0][here, :], w_alls[0][j], True)
            part[here, span] = value.astype(BF)

        @pl.when(jnp.logical_not(middle))
        def _():
            def send(i, inner):
                up_copy(step * (count // STEPS) + i).start()
                return inner

            lax.fori_loop(0, count // STEPS, send, 0)

        return carry

    lax.fori_loop(0, STEPS, product, 0)

    def finish(i):
        mid_copy(i).wait_recv()
        here = pl.ds(pl.multiple_of(i * CHUNK, CHUNK), CHUNK)
        total = pair[here, :].astype(F32) + from_mid[here, :].astype(F32)
        resid = resid_ref[here, :].astype(F32)
        if forward:
            result = resid + total
            if masked:
                result = result * valid_ref[here, :]
        else:
            values = h_ref[here, :].astype(F32)
            scaled = total * gain_ref[...]
            ratio = lax.rsqrt(square_ref[here, :] + EPS)
            mean_term = jnp.sum(scaled * values, axis=1, keepdims=True) * (1.0 / width)
            result = resid + ratio * scaled - values * (ratio * ratio * ratio) * mean_term
        out_ref[here, :] = result.astype(BF)
        fin_copy(i).start()

    tile = columns // 2

    def tile_rows(sub):
        return pl.ds(pl.multiple_of(sub % 2 * tile, tile), tile)

    def stage_copy(number, sub, slot):
        target = product_refs[number].at[sub // 2, tile_rows(sub), :]
        return pltpu.make_async_copy(stage.at[slot], target, stage_sem.at[slot])

    def y_copy(number, sub, slot):
        return Bulk(
            y_stage.at[2 * number + slot], arrived_refs[number].at[tile_rows(sub), :],
            y_send.at[2 * number + slot], y_recv.at[2 * number + slot], {"gx": far},
        )

    def gradient_tile(number, sub):
        slot = sub % 2
        left, far_left, right, far_right = (
            (resid_ref, far_dm, saved_hidden, far_hidden),
            (saved_normed, far_normed, d_gate_ref, far_d_gate),
            (saved_normed, far_normed, d_up_ref, far_d_up),
        )[number]

        @pl.when(sub == 0)
        def _():
            waits = [early[:3], early[3:] + give_all[:STEPS], give_all[STEPS:]][number]
            for copy in waits:
                copy.wait_recv()

        if number >= exchange:

            @pl.when((sub >= 2) | (number > 0))
            def _():
                stage_copy(number, sub, slot).wait()

        elif number > 0:

            @pl.when(sub >= 2)
            def _():
                stage_copy(number, sub - 2, slot).wait()

        y = sub // 2
        if number < exchange:
            y = jnp.where(sub < 2, 1 - lax.div(shard, 2), lax.div(shard, 2))
        start = (y * 2 + core) * columns + sub % 2 * tile
        mine = left[:, pl.ds(pl.multiple_of(start, tile), tile)]
        theirs = far_left[y, :, tile_rows(sub)]
        value = dot_to(mine, right[...], ((0,), (0,))) + dot_to(theirs, far_right[...], ((0,), (0,)))
        if number < exchange:

            @pl.when(sub < 2)
            def _():
                y_stage[2 * number + slot] = value.astype(BF)
                y_copy(number, sub, slot).start()

            @pl.when(sub >= 2)
            def _():
                stage[slot] = value.astype(BF)
                stage_copy(number, sub - 2, slot).start()

        else:
            stage[slot] = value.astype(BF)
            stage_copy(number, sub, slot).start()

    if kind == "mlp_back":
        give_all = [x for pair in zip(*(give_step(n) for n in range(STEPS))) for x in pair]

    def beside_step(i):
        pass_on(i)
        if kind == "mlp_back":
            for number in range(3):
                first = 3 + 4 * number

                @pl.when((i >= first) & (i < first + 4))
                def _():
                    gradient_tile(number, i - first)

    def pass_on(i):
        if gathers == 2:
            at(2, i, lambda: from_base(1, [far_copy]))
            at(6, i, lambda: gather_middle(0))
            at(10, i, lambda: gather_middle(1))
            at(11, i, lambda: gather_late(0))
            at(15, i, lambda: gather_late(1))

    def at(sixteenth, i, action):
        pl.when(i == count * sixteenth // 16)(action)

    @pl.when(middle)
    def _():
        def step(i, carry):
            up_copy(i).wait_recv()
            here = pl.ds(pl.multiple_of(i * CHUNK, CHUNK), CHUNK)
            pair[here, :] = (part[here, :].astype(F32) + from_end[here, :].astype(F32)).astype(BF)
            mid_copy(i).start()

            @pl.when(i >= 1)
            def _():
                finish(i - 1)

            beside_step(i)
            return carry

        lax.fori_loop(0, count, step, 0)
        finish(count - 1)

        def drain(i, carry):
            mid_copy(i).wait_send()
            fin_copy(i).wait_send()
            return carry

        lax.fori_loop(0, count, drain, 0)

    @pl.when(jnp.logical_not(middle))
    def _():
        def drain(i, carry):
            up_copy(i).wait_send()
            fin_copy(i).wait_recv()
            beside_step(i)
            return carry

        lax.fori_loop(0, count, drain, 0)

    if kind == "mlp_back":
        for slot in range(2):
            stage_copy(2, 2 + slot, slot).wait()
        for copy in early + give_all:
            copy.wait_send()
        for number in range(exchange):
            for slot in range(2):
                y_copy(number, slot, slot).wait()
    for k in range(len(crosses)):
        pl.when(x_sends(k))(lambda k=k: x_copy(k).wait_send())
        pl.when(x_takes(k))(lambda k=k: x_copy(k).wait_recv())
    for k in range(gathers):
        far_copy(k, base_refs[2 * k]).wait_send()
        near_copy(k, base_refs[2 * k]).wait()
        cross_copy(k).wait_send()
        pass_copy(k, 0).wait()
        pass_copy(k, 1).wait()


def line_sum(kind, ident, resid, weights, lhs=(), gain=None, valid=None, back=None, low=0, high=0, deps=(), bases=(), layer=0, exchange=0, w_layer=0, crosses=()):
    rows, width = resid.shape
    one = jnp.ones((rows, 1), F32)
    h, square = back if back is not None else (jnp.zeros((16, 128), BF), jnp.zeros((8, 1), F32))
    gain = jnp.zeros((width,), F32) if gain is None else gain
    wide = kind in ("mlp", "mlp_back")
    hidden = 0
    if wide:
        hidden = (weights[2][0] if isinstance(weights[2], tuple) else weights[2]).shape[1]
    w_scratch = []
    triples = [isinstance(w, tuple) for w in weights]
    w_flat = [x for w in weights for x in (w if isinstance(w, tuple) else (w,))]
    for i, w in enumerate(weights):
        _, depth, across = (w[0] if isinstance(w, tuple) else w).shape
        if wide and i < 2:
            w_scratch.append(pltpu.VMEM((width, across), BF))
        else:
            w_scratch.append(pltpu.VMEM((4, depth, across if wide else high - low), BF))
    outs, products, beside = [((rows, width), BF)], [], []
    if kind == "mlp":
        outs += [((rows, width), BF), ((rows, 1), F32)] + [((rows, hidden), BF)] * 3
    elif kind == "mlp_back":
        products = [((1 if n < exchange else 2, width // 4, hidden), BF) for n in range(3)]
        products += [((width // 4, hidden), BF)] * exchange
        half_block = pltpu.VMEM((2, rows, width // 4), BF)
        beside = [pltpu.VMEM((rows, hidden), BF)] * 2 + [half_block] * 2
        beside += [pltpu.VMEM((rows, hidden), BF)] * 3 + [pltpu.VMEM((2, width // 8, hidden), BF)]
        beside += [pltpu.SemaphoreType.DMA((n,)) for n in (5 + 2 * STEPS, 5 + 2 * STEPS, 2)]
        if exchange:
            beside += [pltpu.VMEM((2 * exchange, width // 8, hidden), BF)]
            beside += [pltpu.SemaphoreType.DMA((2 * exchange,))] * 2
    blocks = [((4,) + base[0].shape, BF) for base in bases]
    pairs = [x for base in bases for x in base]
    crossed = [(x[0].shape, BF) for x in crosses]
    depth = 3 * hidden if wide else lhs[0].shape[1]
    count = rows // CHUNK
    dma = pltpu.SemaphoreType.DMA
    return pl.pallas_call(
        functools.partial(
            line_kernel, kind, valid is not None, low, high, len(deps), len(bases), layer, exchange,
            triples, w_layer, [x[1] for x in crosses],
        ),
        out_shape=tuple(jax.ShapeDtypeStruct(*o) for o in outs + products + blocks + crossed),
        in_specs=[VMEM] * (5 + len(lhs)) + [ANY] * (len(w_flat) + len(deps) + len(pairs) + len(crosses)),
        out_specs=tuple([VMEM] * len(outs) + [ANY] * len(products + blocks + crossed)),
        scratch_shapes=w_scratch
        + [pltpu.VMEM((rows, width), BF)] * 4
        + [dma((8 * -(-hidden // 512) + 4,))]
        + [dma((count,))] * 6
        + [dma((n * len(bases),)) for n in (1, 1, 3, 3, 1, 1) if bases]
        + beside
        + [dma((len(crosses),))] * 2 * bool(crosses),
        compiler_params=pltpu.CompilerParams(
            collective_id=ident, has_side_effects=True, vmem_limit_bytes=VMEM_LIMIT
        ),
        cost_estimate=pl.CostEstimate(
            flops=2 * rows * depth * width, bytes_accessed=200 * 1024 * 1024, transcendentals=0
        ),
        name="line_" + kind,
    )(
        gain[None], resid, one if valid is None else valid, h, square, *lhs, *w_flat, *deps, *pairs,
        *(x[0] for x in crosses),
    )


def plain_sum(total):
    return lax.psum(total.astype(BF), "gy").astype(F32)


def normed(h, gain):
    values = h.astype(F32)
    square = jnp.mean(values * values, axis=1, keepdims=True)
    return square, (values * lax.rsqrt(square + EPS) * gain).astype(BF)


def norm_back(d_normed, h, square, gain):
    values = h.astype(F32)
    ratio = lax.rsqrt(square + EPS)
    scaled = d_normed * gain
    mean_term = jnp.mean(scaled * values, axis=1, keepdims=True)
    return ratio * scaled - values * (ratio * ratio * ratio) * mean_term


def attention_forward(h, gain, w_attn, low, tables, ident, bases, layer, deps=()):
    rows, width = h.shape
    high = low + width // lax.axis_size("gx")
    q_width = low - 2 * HD
    cosine, sines = tables[:2]
    square, n1 = normed(h, gain)
    q_down = mm(tall(cut(w_attn, 0, q_width)), n1, ((0,), (1,)))
    kv = mm(n1, tall(cut(w_attn, q_width, low)))
    k_rot = rope_down(kv[:, :HD].T, cosine, sines).T.astype(BF)
    kv = jnp.concatenate([k_rot, kv[:, HD:].astype(BF)], axis=1)
    kv_all = jnp.concatenate([kv, swap_pairs(kv, "gx")], axis=0)
    k_all, v_all = kv_all[:, :HD], kv_all[:, HD:]
    heads, rotated, lse = attend(q_down, k_all, v_all, tables)
    if fused():
        h1, *stacks = line_sum(
            "out", ident, h, [w_attn], (heads,), low=low, high=high,
            deps=deps, bases=bases, layer=layer,
        )
        blocks = [(x, *pair) for x, pair in zip(stacks, bases)]
    else:
        h1 = (h.astype(F32) + plain_sum(mm(heads, side(cut(w_attn, low, high))))).astype(BF)
        blocks = [gather_blocks(chosen(x, layer)) for x in bases]
    return h1, square, blocks, (h, square, n1, rotated, lse, k_all, v_all, heads)


def mlp_forward(h1, gain, weights, valid, ident, bases=(), layer=0, w_layer=0):
    if fused():
        result, n2, square, gate, up, hidden, *stacks = line_sum(
            "mlp", ident, h1, weights, gain=gain, valid=valid, bases=bases, layer=layer,
            w_layer=w_layer,
        )
        blocks = [(x, *pair) for x, pair in zip(stacks, bases)]
    else:
        square, n2 = normed(h1, gain)
        gate = mm(n2, tall(weights[0]))
        up = mm(n2, tall(weights[1]))
        hidden = (gate * jax.nn.sigmoid(gate) * up).astype(BF)
        gate, up = gate.astype(BF), up.astype(BF)
        result = h1.astype(F32) + plain_sum(mm(hidden, side(weights[2])))
        result = (result * valid).astype(BF)
        blocks = [gather_blocks(chosen(x, layer)) for x in bases]
    return result, square, blocks, (h1, square, n2, gate, up, hidden)


def mlp_backward(dm, gain, weights, saved, ident, w_layer, crosses=(), deps=(), exchange=2):
    h1, square, n2, gate, up, hidden = saved
    if fused():
        e1, *products = line_sum(
            "mlp_back", ident, dm, weights, (gate, up, n2, hidden), gain=gain,
            back=(h1, square), exchange=exchange, w_layer=w_layer, crosses=crosses, deps=deps,
        )
        return e1, products[: 3 + exchange], products[3 + exchange :]
    gate, up = gate.astype(F32), up.astype(F32)
    d_hidden = mm(dm, side(weights[2]), ((1,), (1,)))
    sigmoid = jax.nn.sigmoid(gate)
    d_gate = (d_hidden * up * sigmoid * (1.0 + gate * (1.0 - sigmoid))).astype(BF)
    d_up = (d_hidden * (gate * sigmoid)).astype(BF)
    total = mm(d_gate, tall(weights[0]), ((1,), (1,))) + mm(d_up, tall(weights[1]), ((1,), (1,)))
    e1 = (dm.astype(F32) + norm_back(plain_sum(total), h1, square, gain)).astype(BF)
    turn = ((0,), (0,))
    products = [mm(dm, hidden, turn), mm(n2, d_gate, turn), mm(n2, d_up, turn)]
    return e1, [p.astype(BF) for p in products], crossing(crosses)


def crossing(crosses):
    pairs = ([(1, 0)], [(0, 1)], [(0, 1), (1, 0)])
    return [lax.ppermute(x, "section", pairs[way]) for x, way in crosses]


def mlp_sums(products):
    if not fused():
        return [shard_sum(p) for p in products]
    down, gate, up, *arrived = products
    sums = [(x[0].astype(F32) + y.astype(F32)).astype(BF) for x, y in zip((down, gate), arrived)]
    return sums + [chip_sum(up)]


def attention_backward(e1, w_attn, low, tables, saved):
    h, square, n1, rotated, lse, k_all, v_all, heads = saved
    rows, width = h.shape
    cosine, sines = tables[:2]
    w_o = side(cut(w_attn, low, low + width // lax.axis_size("gx")))
    d_down = mm(w_o, e1, ((1,), (1,))).astype(BF)
    dq, dk, dv = attend_back(rotated, k_all, v_all, d_down, lse, tables)
    dkv = jnp.concatenate([dk, dv], axis=1)
    dkv = dkv[:rows] + swap_pairs(dkv[rows:], "gx")
    dk = rope_down(dkv[:, :HD].T, cosine, -sines).T
    d_qkv = jnp.concatenate([dq, dk.astype(BF), dkv[:, HD:].astype(BF)], axis=1)
    turn = ((0,), (0,))
    products = [mm(n1, d_qkv, turn).astype(BF), mm(e1, heads, turn).astype(BF)]
    return d_qkv, jnp.concatenate(products, axis=1)


def attention_end(d_qkv, e1, w_attn, gain, saved, ident, deps, crosses):
    h, square = saved[:2]
    qkv_width = d_qkv.shape[1]
    if fused():
        grad, *crossed = line_sum(
            "back", ident, e1, [w_attn], (d_qkv,), gain=gain, back=(h, square),
            low=0, high=qkv_width, deps=deps, crosses=crosses,
        )
        return grad, crossed
    total = plain_sum(mm(d_qkv, tall(cut(w_attn, 0, qkv_width)), ((1,), (1,))))
    grad = (e1.astype(F32) + norm_back(total, h, square, gain)).astype(BF)
    return grad, crossing(crosses)


def on_device(
    hidden_in, out_grad, lengths, dealing, attn_gain, w_query, w_key, w_value, w_out,
    mlp_gain, w_gate, w_up, w_down,
):
    shards = lax.axis_size("gx")
    shard = lax.axis_index("gx")
    section = lax.axis_index("section")
    column = lax.axis_index("gy")
    core = shard % 2
    sequence = (shard // 2) * 2 + section
    span, width = hidden_in.shape
    half = span // 2
    seq_length = lax.dynamic_index_in_dim(lengths, sequence, keepdims=False)

    both = jnp.concatenate([hidden_in, out_grad], axis=1)
    mine = core_rows(both, core)
    theirs = swap_pairs(core_rows(both, 1 - core), "gx")
    mine = jnp.where(core == section, mine, theirs)
    h = lax.all_gather(mine[:, :width], "gy", axis=1, tiled=True)

    kv_head = column * (w_query.shape[2] // HD) // (QH // KVH)
    low = w_query.shape[2] + 2 * HD
    both_gains = jnp.stack([attn_gain[0], mlp_gain[0]], axis=1)
    attn_own = jnp.concatenate(
        [
            w_query[0],
            lax.dynamic_slice_in_dim(w_key[0], kv_head * HD, HD, 1),
            lax.dynamic_slice_in_dim(w_value[0], kv_head * HD, HD, 1),
            w_out[0],
            jnp.pad(both_gains, ((0, 0), (0, 126))),
        ],
        axis=1,
    )
    own = (attn_own, w_gate[0], w_up[0], w_down[0])
    first = [(array, lax.ppermute(array, "section", [(0, 1)])) for array in own]
    second = [(array, lax.ppermute(array, "section", [(1, 0)])) for array in own]

    def gains_of(w_attn):
        pair = w_attn[:, :, w_attn.shape[2] - 128 : w_attn.shape[2] - 126]
        return pair.reshape(-1, 2).T.astype(F32)

    here = core_rows(jnp.arange(span), core)
    there = core_rows(jnp.arange(span), 1 - core)
    keys_at = jnp.concatenate([here, there])
    valid = (here < seq_length)[:, None].astype(F32)
    tables = (*rope_tables(here), keys_at, here, seq_length.reshape(1, 1))

    attn0, gate0 = gather_blocks(chosen(first[0], 0)), gather_blocks(chosen(first[1], 0))
    gains0 = gains_of(attn0)
    h1, square_a, blocks, saved_a0 = attention_forward(
        h, gains0[0], attn0, low, tables, 0, first[2:], 0, (gate0,)
    )
    mlp0 = [gate0] + blocks
    h, square_m, (attn1, gate1), saved_m0 = mlp_forward(
        h1, gains0[1], mlp0, valid, 1, second[:2], 1
    )
    if fused():
        attn1 = with_own(attn1[0], second[0], 1)
    gains1 = gains_of(attn1)
    outputs, squares = [h], [square_a, square_m]
    d_mine = mine[:, width:] + h[:1, :1] * 0
    d_out = lax.all_gather(d_mine, "gy", axis=1, tiled=True)
    h1, square_a, blocks, saved_a1 = attention_forward(
        h, gains1[0], attn1, low, tables, 2, second[2:], 1
    )
    mlp1 = [gate1] + blocks
    h, square_m, _, saved_m1 = mlp_forward(h1, gains1[1], mlp1, valid, 3, w_layer=1)
    outputs.append(h)
    squares = jnp.concatenate(squares + [square_a, square_m], axis=1)
    rms = (jnp.sqrt(squares + EPS) * valid).T
    statistics = [rms[:2], rms[2:]]
    outputs = [lax.dynamic_slice_in_dim(x, column * width, width, 1) for x in outputs]

    def to_section(per_layer):
        kept = jnp.where(section == 0, per_layer[0], per_layer[1])
        sent = swap_pairs(jnp.where(section == 0, per_layer[1], per_layer[0]), "section")
        return kept, sent

    dm = (d_out.astype(F32) * valid).astype(BF)
    e1, products, _ = mlp_backward(dm, gains1[1], mlp1, saved_m1, 4, 1)
    local1 = mlp_sums(products)

    both = []
    for output, stat in zip(outputs, statistics):
        high = stat.astype(BF)
        rest = (stat - high.astype(F32)).astype(BF)
        parts = jnp.concatenate([high, rest], axis=0).reshape(-1, width)
        parts = jnp.pad(parts, ((0, -parts.shape[0] % 16), (0, 0)))
        both.append(jnp.concatenate([output + e1[:1, :1] * 0, parts], axis=0))
    kept = jnp.where(section == 0, both[0], both[1])
    sent = jnp.where(section == 0, both[1], both[0])

    d_qkv, products = attention_backward(e1, attn1, low, tables, saved_a1)
    local1.append(shard_sum(products))
    crosses = [(sent, 2), (local1[0], 1)]
    grad1, (sent, down1) = attention_end(
        d_qkv, e1, attn1, gains1[0], saved_a1, 5, (products,), crosses
    )
    by_section = jnp.stack([jnp.where(section == 0, kept, sent), jnp.where(section == 0, sent, kept)])
    everything = lax.all_gather(by_section, "gx", axis=0)
    owner = jnp.sum(jnp.where(dealing == shard, jnp.arange(shards), 0))
    halves = lax.dynamic_slice(
        everything, ((owner // 2) * 2, owner % 2, 0, 0), (2, 1) + everything.shape[2:]
    )[:, 0]
    layer_out = join_halves(halves[0, :half], halves[1, :half])
    stat_rows = 4 * half // width
    parts = halves[:, half : half + stat_rows].astype(F32).reshape(2, 4, half)
    stat_halves = parts[:, :2] + parts[:, 2:]
    stats_out = join_halves(stat_halves[0].T, stat_halves[1].T).T

    dm = (grad1.astype(F32) * valid).astype(BF)
    crosses = [(local1[1], 1), (local1[2], 1)]
    e1, products, (gate1, up1) = mlp_backward(dm, gains0[1], mlp0, saved_m0, 6, 0, crosses)
    local0 = mlp_sums(products)
    d_qkv, products = attention_backward(e1, attn0, low, tables, saved_a0)
    local0.append(shard_sum(products))
    crosses = [(local1[3], 1), (local0[0], 0), (local0[1], 0)]
    grad0, (attn_sum1, down0, gate0) = attention_end(
        d_qkv, e1, attn0, gains0[0], saved_a0, 7, (products, everything), crosses
    )

    input_grads = [lax.dynamic_slice_in_dim(x, column * width, width, 1) for x in (grad0, grad1)]
    local0[2] = local0[2] + grad0[:1, :1] * 0
    received0 = [down0, gate0] + crossing([(x, 0) for x in local0[2:]])
    received1 = [down1, gate1, up1, attn_sum1]
    totals = [
        jnp.where(section == 0, a0.astype(F32) + r0.astype(F32), a1.astype(F32) + r1.astype(F32))
        for a0, r0, a1, r1 in zip(local0, received0, local1, received1)
    ]
    s_down, s_gate, s_up, s_attn = totals
    s_out = s_attn[:, low:]
    q_width = w_query.shape[2]

    attn_sum = jnp.sum(s_attn[:, :low] * attn_own[:, :low].astype(F32), axis=1)
    mlp_sum = jnp.sum(s_gate * w_gate[0].astype(F32) + s_up * w_up[0].astype(F32), axis=1)
    sums = jnp.pad(jnp.stack([attn_sum, mlp_sum], axis=1), ((0, 0), (0, 126)))
    spread = jnp.concatenate([s_attn[:, q_width:low], sums], axis=1).astype(BF)
    spread = lax.all_gather(spread, "gy", axis=0).astype(F32)
    gains = jnp.sum(spread[:, :, 2 * HD : 2 * HD + 2], axis=0).T / both_gains.astype(F32).T
    kv_sum = spread[:, :, : 2 * HD].reshape(KVH, -1, *spread.shape[1:2], 2, HD).sum(axis=1)
    kv_sum = kv_sum.transpose(2, 1, 0, 3).reshape(2, spread.shape[1], KVH * HD)

    kept, sent = to_section(input_grads)
    keep = jnp.where(core == section, kept, sent)
    give = swap_pairs(jnp.where(core == section, sent, kept), "gx")
    back_home = join_halves(jnp.where(core == 0, keep, give), jnp.where(core == 0, give, keep))
    return (
        layer_out[None],
        stats_out[None],
        back_home[None],
        gains[None, 0],
        s_attn[None, :, :q_width],
        kv_sum[None, 0],
        kv_sum[None, 1],
        s_out.T[None],
        gains[None, 1],
        s_gate[None],
        s_up[None],
        s_down.T[None],
    )


def solution(mesh):
    rows_cols = P("section", "gx", "gy")
    cols_rows = P("section", "gy", "gx")
    rows_only = P("section", "gx", None)
    gain = P("section", "gx")
    return jax.shard_map(
        on_device,
        mesh=mesh,
        in_specs=(
            P("gx", "gy"), P("gx", "gy"), P(), P(), gain, rows_cols, rows_only, rows_only,
            cols_rows, gain, rows_cols, rows_cols, cols_rows,
        ),
        out_specs=(
            rows_cols, P("section", None, "gx"), rows_cols, gain, rows_cols, rows_only, rows_only,
            cols_rows, gain, rows_cols, rows_cols, cols_rows,
        ),
        check_vma=False,
    )
```

```python
import functools

import jax
import jax.numpy as jnp
from jax import lax
from jax.experimental import pallas as pl
from jax.experimental.pallas import tpu as pltpu
from jax.sharding import PartitionSpec as P

QH = 32
KVH = 4
HD = 64
LAYERS = 2
EPS = 1e-05
BF = jnp.bfloat16
F32 = jnp.float32
MESH = pl.DeviceIdType.MESH
CHUNK = 32
STEPS = 2
GAIN_ROWS = 32
VMEM_LIMIT = 56 * 1024 * 1024
ANY = pl.BlockSpec(memory_space=pl.ANY)
VMEM = pl.BlockSpec(memory_space=pltpu.VMEM)


def mm(left, right, dims=((1,), (0,))):
    return lax.dot_general(left, right, (dims, ((), ())), preferred_element_type=F32)


def swap_pairs(values, axis, by=1):
    count = lax.axis_size(axis)
    return lax.ppermute(values, axis, [(i, i ^ by) for i in range(count)])


def rope_tables(places):
    half_width = HD // 2
    frequency = jnp.power(10000.0, -2.0 * jnp.arange(half_width).astype(F32) / HD)
    angles = frequency[:, None] * places.astype(F32)[None, :]
    return jnp.cos(angles), jnp.sin(angles)


def core_rows(rows, core):
    quarter = rows.shape[0] // 4
    low = lax.dynamic_slice_in_dim(rows, core * quarter, quarter, 0)
    high = lax.dynamic_slice_in_dim(rows, (3 - core) * quarter, quarter, 0)
    return jnp.concatenate([low, high], axis=0)


def join_halves(first, second):
    quarter = first.shape[0] // 2
    return jnp.concatenate(
        [first[:quarter], second[:quarter], second[quarter:], first[quarter:]], axis=0
    )


def chip_groups():
    return [[0, 2], [1, 3]]


def gather_blocks(base):
    return lax.all_gather(base, "gx", axis=0)


def chosen(pair, layer):
    return jnp.where(lax.axis_index("section") == layer, *pair)


def with_own(stack, pair, layer):
    shard = lax.axis_index("gx")
    return lax.dynamic_update_index_in_dim(stack, chosen(pair, layer), shard, 0)


def fused():
    return lax.axis_size("gx") == 4 and lax.axis_size("gy") == 4


def tall(w):
    return w.reshape(-1, w.shape[-1])


def side(w):
    return jnp.concatenate([w[i] for i in range(w.shape[0])], axis=1)


def cut(w, low, high):
    return w[:, :-GAIN_ROWS, low:high]


def shard_sum(product):
    return lax.psum_scatter(product, "gx", scatter_dimension=0, tiled=True)


def chip_sum(product):
    product = product.reshape(-1, product.shape[-1])
    return lax.psum_scatter(
        product, "gx", scatter_dimension=0, tiled=True, axis_index_groups=[[0, 2], [1, 3]]
    )


def rope_down(values, cosine, sines):
    half_width = HD // 2
    first, second = values[:half_width], values[half_width:]
    return jnp.concatenate(
        [first * cosine - second * sines, second * cosine + first * sines], axis=0
    )


def fill_bias(bias_ref, key_ref, query_ref, length_ref):
    keys = key_ref[...]
    allowed = (keys <= query_ref[...]) & (keys < length_ref[...])
    bias_ref[...] = jnp.where(allowed, 0.0, -1e30)


def dot_to(left, right, dims):
    return lax.dot_general(left, right, (dims, ((), ())), preferred_element_type=F32)


def attend_kernel(
    q_ref, k_ref, vt_ref, cos_ref, sin_ref, key_ref, query_ref, length_ref,
    heads_ref, rot_ref, lse_ref, bias_ref, out_ref,
):
    fill_bias(bias_ref, key_ref, query_ref, length_ref)

    def head(h, carry):
        here = pl.ds(pl.multiple_of(h * HD, HD), HD)
        rotated = rope_down(q_ref[here, :], cos_ref[...], sin_ref[...]).astype(BF)
        rot_ref[here, :] = rotated
        scaled = (rotated.astype(F32) * HD ** (-0.5)).astype(BF)
        scores = dot_to(k_ref[...], scaled, ((1,), (0,))) + bias_ref[...]
        top = jnp.max(scores, axis=0, keepdims=True)
        exponent = jnp.exp(scores - top)
        total = jnp.sum(exponent, axis=0, keepdims=True)
        probs = (exponent * (1.0 / total)).astype(BF)
        out_ref[here, :] = dot_to(vt_ref[...], probs, ((1,), (0,)))
        lse_ref[pl.ds(h, 1), :] = top + jnp.log(total)
        return carry

    lax.fori_loop(0, q_ref.shape[0] // HD, head, 0)
    heads_ref[...] = out_ref[...].T.astype(BF)


def attend_back_kernel(
    rot_ref, k_ref, kt_ref, v_ref, d_ref, lse_ref, cos_ref, sin_ref, key_ref, query_ref, length_ref,
    dq_ref, dk_ref, dv_ref, bias_ref, out_ref,
):
    fill_bias(bias_ref, key_ref, query_ref, length_ref)
    dk_ref[...] = jnp.zeros_like(dk_ref)
    dv_ref[...] = jnp.zeros_like(dv_ref)
    scaling = HD ** (-0.5)

    def head(h, carry):
        here = pl.ds(pl.multiple_of(h * HD, HD), HD)
        scaled = (rot_ref[here, :].astype(F32) * scaling).astype(BF)
        scores = dot_to(k_ref[...], scaled, ((1,), (0,))) + bias_ref[...]
        probs = jnp.exp(scores - lse_ref[pl.ds(h, 1), :])
        d_probs = dot_to(v_ref[...], d_ref[here, :], ((1,), (0,)))
        delta = jnp.sum(probs * d_probs, axis=0, keepdims=True)
        d_scores = (probs * (d_probs - delta)).astype(BF)
        dk_ref[...] += dot_to(d_scores, scaled, ((1,), (1,)))
        dv_ref[...] += dot_to(probs.astype(BF), d_ref[here, :], ((1,), (1,)))
        dq = dot_to(kt_ref[...], d_scores, ((1,), (0,))) * scaling
        out_ref[here, :] = rope_down(dq, cos_ref[...], -sin_ref[...])
        return carry

    lax.fori_loop(0, rot_ref.shape[0] // HD, head, 0)
    dq_ref[...] = out_ref[...].T.astype(BF)


def attend(q_down, k_all, v_all, tables):
    cosine, sines, keys_at, places, length = tables
    width, rows = q_down.shape
    return pl.pallas_call(
        attend_kernel,
        out_shape=(
            jax.ShapeDtypeStruct((rows, width), BF),
            jax.ShapeDtypeStruct((width, rows), BF),
            jax.ShapeDtypeStruct((width // HD, rows), F32),
        ),
        in_specs=[VMEM] * 8,
        out_specs=(VMEM,) * 3,
        scratch_shapes=[pltpu.VMEM((k_all.shape[0], rows), F32), pltpu.VMEM((width, rows), F32)],
        compiler_params=pltpu.CompilerParams(vmem_limit_bytes=VMEM_LIMIT),
        cost_estimate=pl.CostEstimate(
            flops=16 * width * rows * k_all.shape[0], bytes_accessed=60_000_000, transcendentals=0
        ),
        name="attend",
    )(q_down, k_all, v_all.T, cosine, sines, keys_at[:, None], places[None], length)


def attend_back(rotated, k_all, v_all, d_down, lse, tables):
    cosine, sines, keys_at, places, length = tables
    width, rows = rotated.shape
    return pl.pallas_call(
        attend_back_kernel,
        out_shape=(
            jax.ShapeDtypeStruct((rows, width), BF),
            jax.ShapeDtypeStruct(k_all.shape, F32),
            jax.ShapeDtypeStruct(k_all.shape, F32),
        ),
        in_specs=[VMEM] * 11,
        out_specs=(VMEM,) * 3,
        scratch_shapes=[pltpu.VMEM((k_all.shape[0], rows), F32), pltpu.VMEM((width, rows), F32)],
        compiler_params=pltpu.CompilerParams(vmem_limit_bytes=VMEM_LIMIT),
        cost_estimate=pl.CostEstimate(
            flops=40 * width * rows * k_all.shape[0], bytes_accessed=80_000_000, transcendentals=0
        ),
        name="attend_back",
    )(
        rotated, k_all, k_all.T, v_all, d_down, lse, cosine, sines,
        keys_at[:, None], places[None], length,
    )


def load_blocks(w_refs, w_layer, low, high, target_of, sem):
    shard, home = lax.axis_index("gx"), lax.axis_index("section") == w_layer
    waits = []
    for j in range(4):

        def copy(ref):
            source = ref.at[: ref.shape[0] - GAIN_ROWS, low:high]
            return pltpu.make_async_copy(source, target_of(j), sem.at[j])

        waits.append(copy(w_refs[0].at[j]))
        if len(w_refs) == 1:
            waits[j].start()
        else:
            pl.when(shard != j)(waits[j].start)
            pl.when((shard == j) & home)(copy(w_refs[1]).start)
            pl.when((shard == j) & jnp.logical_not(home))(copy(w_refs[2]).start)
    return waits


def meet_near():
    near = {"gx": lax.axis_index("gx") ^ 1}
    barrier = pltpu.get_barrier_semaphore()
    pl.semaphore_signal(barrier, inc=1, device_id=near, device_id_type=MESH)
    pl.semaphore_wait(barrier, 1)
    return near


def attend_whole_kernel(
    w_layer, listed,
    h_ref, gain_ref, cos_ref, sin_ref, key_ref, query_ref, length_ref, *rest,
):
    w_refs, rest = rest[:listed], rest[listed:]
    (
        heads_ref, normed_ref, ms_ref, rot_ref, lse_ref, k_ref, kt_ref, v_ref,
        w_all, bias_ref, out_ref, q_ref, vt_ref, kv_mine, kv_far, w_sem, send_sem, recv_sem,
    ) = rest
    rows, width = h_ref.shape
    block = width // 4
    q_width = q_ref.shape[0]
    waits = load_blocks(
        w_refs, w_layer, 0, q_width + 2 * HD, lambda j: w_all.at[j * block : (j + 1) * block], w_sem
    )
    near = meet_near()

    def norm(i, carry):
        here = pl.ds(pl.multiple_of(i * 128, 128), 128)
        values = h_ref[here, :].astype(F32)
        square = jnp.mean(values * values, axis=1, keepdims=True)
        ms_ref[here, :] = square
        normed_ref[here, :] = (values * lax.rsqrt(square + EPS) * gain_ref[...]).astype(BF)
        return carry

    lax.fori_loop(0, rows // 128, norm, 0)
    for wait in waits:
        wait.wait()
    kv = dot_to(normed_ref[...], w_all[:, q_width:], ((1,), (0,))).T
    kv = jnp.concatenate([rope_down(kv[:HD], cos_ref[...], sin_ref[...]), kv[HD:]], axis=0)
    kv_mine[...] = kv.T.astype(BF)
    copy = pltpu.make_async_remote_copy(
        src_ref=kv_mine, dst_ref=kv_far, send_sem=send_sem, recv_sem=recv_sem,
        device_id=near, device_id_type=MESH,
    )
    copy.start()
    q_ref[...] = dot_to(normed_ref[...], w_all[:, :q_width], ((1,), (0,))).T
    fill_bias(bias_ref, key_ref, query_ref, length_ref)
    copy.wait()
    for n, ref in enumerate((kv_mine, kv_far)):
        here = pl.ds(n * rows, rows)
        k_ref[here, :] = ref[:, :HD]
        v_ref[here, :] = ref[:, HD:]
        down = ref[...].astype(F32).T.astype(BF)
        kt_ref[:, here] = down[:HD]
        vt_ref[:, here] = down[HD:]

    def head(h, carry):
        here = pl.ds(pl.multiple_of(h * HD, HD), HD)
        rotated = rope_down(q_ref[here, :], cos_ref[...], sin_ref[...]).astype(BF)
        rot_ref[here, :] = rotated
        scaled = (rotated.astype(F32) * HD ** (-0.5)).astype(BF)
        scores = dot_to(k_ref[...], scaled, ((1,), (0,))) + bias_ref[...]
        top = jnp.max(scores, axis=0, keepdims=True)
        exponent = jnp.exp(scores - top)
        total = jnp.sum(exponent, axis=0, keepdims=True)
        probs = (exponent * (1.0 / total)).astype(BF)
        out_ref[here, :] = dot_to(vt_ref[...], probs, ((1,), (0,)))
        lse_ref[pl.ds(h, 1), :] = top + jnp.log(total)
        return carry

    lax.fori_loop(0, q_width // HD, head, 0)
    heads_ref[...] = out_ref[...].T.astype(BF)


def attend_whole_back_kernel(
    w_layer, listed,
    e1_ref, rot_ref, lse_ref, k_ref, kt_ref, v_ref, cos_ref, sin_ref, key_ref, query_ref,
    length_ref, *rest,
):
    w_refs, rest = rest[:listed], rest[listed:]
    (
        d_qkv_ref, w_all, bias_ref, d_ref, out_ref, dk_ref, dv_ref, dkv_send, dkv_far,
        w_sem, send_sem, recv_sem,
    ) = rest
    rows, width = e1_ref.shape
    block = width // 4
    q_width = rot_ref.shape[0]
    low = q_width + 2 * HD
    waits = load_blocks(w_refs, w_layer, low, low + block, lambda j: w_all.at[j], w_sem)
    near = meet_near()
    fill_bias(bias_ref, key_ref, query_ref, length_ref)
    dk_ref[...] = jnp.zeros_like(dk_ref)
    dv_ref[...] = jnp.zeros_like(dv_ref)
    scaling = HD ** (-0.5)
    for wait in waits:
        wait.wait()
    d_ref[...] = sum(
        dot_to(w_all[j], e1_ref[:, j * block : (j + 1) * block], ((1,), (1,))) for j in range(4)
    ).astype(BF)

    def head(h, carry):
        here = pl.ds(pl.multiple_of(h * HD, HD), HD)
        scaled = (rot_ref[here, :].astype(F32) * scaling).astype(BF)
        scores = dot_to(k_ref[...], scaled, ((1,), (0,))) + bias_ref[...]
        probs = jnp.exp(scores - lse_ref[pl.ds(h, 1), :])
        d_probs = dot_to(v_ref[...], d_ref[here, :], ((1,), (0,)))
        delta = jnp.sum(probs * d_probs, axis=0, keepdims=True)
        d_scores = (probs * (d_probs - delta)).astype(BF)
        dk_ref[...] += dot_to(d_scores, scaled, ((1,), (1,)))
        dv_ref[...] += dot_to(probs.astype(BF), d_ref[here, :], ((1,), (1,)))
        dq = dot_to(kt_ref[...], d_scores, ((1,), (0,))) * scaling
        out_ref[here, :] = rope_down(dq, cos_ref[...], -sin_ref[...])
        return carry

    lax.fori_loop(0, q_width // HD, head, 0)
    dkv_send[:, :HD] = dk_ref[rows:, :]
    dkv_send[:, HD:] = dv_ref[rows:, :]
    copy = pltpu.make_async_remote_copy(
        src_ref=dkv_send, dst_ref=dkv_far, send_sem=send_sem, recv_sem=recv_sem,
        device_id=near, device_id_type=MESH,
    )
    copy.start()
    d_qkv_ref[:, :q_width] = out_ref[...].T.astype(BF)
    copy.wait()
    down = (dkv_far[...].T)
    dk = rope_down(dk_ref[:rows, :].T + down[:HD], cos_ref[...], -sin_ref[...])
    dkv = jnp.concatenate([dk, dv_ref[:rows, :].T + down[HD:]], axis=0)
    d_qkv_ref[:, q_width:] = dkv.T.astype(BF)


def attend_whole(h, gain, w_attn, low, tables, w_layer, ident):
    cosine, sines, keys_at, places, length = tables
    rows, width = h.shape
    keys, q_width = keys_at.shape[0], low - 2 * HD
    w_list = list(w_attn) if isinstance(w_attn, tuple) else [w_attn]
    outs = [
        ((rows, q_width), BF), ((rows, width), BF), ((rows, 1), F32), ((q_width, rows), BF),
        ((q_width // HD, rows), F32), ((keys, HD), BF), ((HD, keys), BF), ((keys, HD), BF),
    ]
    return pl.pallas_call(
        functools.partial(attend_whole_kernel, w_layer, len(w_list)),
        out_shape=tuple(jax.ShapeDtypeStruct(*o) for o in outs),
        in_specs=[VMEM] * 7 + [ANY] * len(w_list),
        out_specs=(VMEM,) * 8,
        scratch_shapes=[
            pltpu.VMEM((width, low), BF),
            pltpu.VMEM((keys, rows), F32),
            pltpu.VMEM((q_width, rows), F32),
            pltpu.VMEM((q_width, rows), F32),
            pltpu.VMEM((HD, keys), BF),
            pltpu.VMEM((rows, 2 * HD), BF),
            pltpu.VMEM((rows, 2 * HD), BF),
            pltpu.SemaphoreType.DMA((4,)),
            pltpu.SemaphoreType.DMA,
            pltpu.SemaphoreType.DMA,
        ],
        compiler_params=pltpu.CompilerParams(
            collective_id=ident, has_side_effects=True, vmem_limit_bytes=VMEM_LIMIT
        ),
        cost_estimate=pl.CostEstimate(
            flops=16 * q_width * rows * keys, bytes_accessed=70_000_000, transcendentals=0
        ),
        name="attend_whole",
    )(h, gain, cosine, sines, keys_at[:, None], places[None], length, *w_list)


def attend_whole_back(e1, rotated, lse, k_all, kt_all, v_all, w_attn, tables, w_layer, ident):
    cosine, sines, keys_at, places, length = tables
    q_width, rows = rotated.shape
    keys, width = keys_at.shape[0], e1.shape[1]
    w_list = list(w_attn) if isinstance(w_attn, tuple) else [w_attn]
    return pl.pallas_call(
        functools.partial(attend_whole_back_kernel, w_layer, len(w_list)),
        out_shape=jax.ShapeDtypeStruct((rows, q_width + 2 * HD), BF),
        in_specs=[VMEM] * 11 + [ANY] * len(w_list),
        out_specs=VMEM,
        scratch_shapes=[
            pltpu.VMEM((4, q_width, width // 4), BF),
            pltpu.VMEM((keys, rows), F32),
            pltpu.VMEM((q_width, rows), BF),
            pltpu.VMEM((q_width, rows), F32),
            pltpu.VMEM((keys, HD), F32),
            pltpu.VMEM((keys, HD), F32),
            pltpu.VMEM((rows, 2 * HD), F32),
            pltpu.VMEM((rows, 2 * HD), F32),
            pltpu.SemaphoreType.DMA((4,)),
            pltpu.SemaphoreType.DMA,
            pltpu.SemaphoreType.DMA,
        ],
        compiler_params=pltpu.CompilerParams(
            collective_id=ident, has_side_effects=True, vmem_limit_bytes=VMEM_LIMIT
        ),
        cost_estimate=pl.CostEstimate(
            flops=40 * q_width * rows * keys, bytes_accessed=90_000_000, transcendentals=0
        ),
        name="attend_whole_back",
    )(
        e1, rotated, lse, k_all, kt_all, v_all, cosine, sines, keys_at[:, None], places[None],
        length, *w_list,
    )


def line_kernel(
    kind, masked, low, high, deps, gathers, layer, exchange, triples, w_layer, crosses, homing,
    gain_ref, resid_ref, valid_ref, h_ref, square_ref, *rest,
):
    forward = kind in ("out", "mlp")
    wide = kind in ("mlp", "mlp_back")
    if kind == "mlp":
        lhs_refs = []
    elif kind == "mlp_back":
        lhs_refs, rest = rest[:4], rest[4:]
    else:
        lhs_refs, rest = rest[:1], rest[1:]
    w_count = 3 if wide else 1
    w_refs = []
    for triple in triples:
        w_refs.append(rest[: 3 if triple else 1])
        rest = rest[3 if triple else 1 :]
    rest = rest[deps:]
    base_refs, rest = rest[: 2 * gathers], rest[2 * gathers :]
    cross_refs, rest = rest[: len(crosses)], rest[len(crosses) :]
    out_ref, rest = rest[0], rest[1:]
    if kind == "mlp":
        normed_ref, ms_ref, gate_ref, up_ref, hidden_ref = rest[:5]
        rest = rest[5:]
    elif kind == "mlp_back":
        product_refs, rest = rest[:3], rest[3:]
        arrived_refs, rest = rest[:exchange], rest[exchange:]
    block_refs, rest = rest[:gathers], rest[gathers:]
    crossed_refs, rest = rest[: len(crosses)], rest[len(crosses) :]
    if homing:
        home_ref, home_send, home_recv = rest[0], *rest[-2:]
        rest = rest[1:-2]
    if crosses:
        x_send, x_recv = rest[-2:]
        rest = rest[:-2]
    w_alls, rest = rest[:w_count], rest[w_count:]
    (
        part, from_end, from_mid, pair,
        w_sem, up_send, up_recv, mid_send, mid_recv, fin_send, fin_recv,
    ) = rest[:11]
    if gathers:
        far_send, far_recv, near_send, near_recv, cross_send, cross_recv = rest[11:]
    if kind == "mlp_back":
        (
            d_gate_ref, d_up_ref, far_normed, far_dm, far_hidden, far_d_gate, far_d_up, stage,
            give_sem, take_sem, stage_sem,
        ) = rest[11:22]
    if exchange:
        y_stage, y_send, y_recv = rest[22:]
    shard = lax.axis_index("gx")
    far, near = shard ^ 2, shard ^ 1
    section = lax.axis_index("section")
    rows, width = resid_ref.shape
    columns = width // 4
    count = rows // CHUNK
    z = lax.axis_index("gy")
    middle = (z == 1) | (z == 2)
    end_of = jnp.where(z == 1, 0, 3)
    mid_of = jnp.where(z == 0, 1, 2)
    across = 3 - z

    def loading(w, j, cut_of, target, slot):
        whole = w_refs[w]
        copies = [(None, pltpu.make_async_copy(cut_of(whole[0].at[j]), target, w_sem.at[slot]))]
        if triples[w]:
            home = section == w_layer
            copies = [(shard != j, copies[0][1])]
            for ref, holds in zip(whole[1:], (home, jnp.logical_not(home))):
                copy = pltpu.make_async_copy(cut_of(ref), target, w_sem.at[slot])
                copies.append(((shard == j) & holds, copy))
        return copies

    loads, downs = [], []
    if wide:
        hidden_width = w_alls[0].shape[1]
        for x0 in range(0, hidden_width, 512):
            x1 = min(x0 + 512, hidden_width)
            for w in range(2):
                for j in range(4):
                    target = w_alls[w].at[j * columns : (j + 1) * columns, x0:x1]
                    loads.append(loading(w, j, lambda ref: ref.at[:, x0:x1], target, len(loads)))
        for j in range(4):
            downs.append(loading(2, j, lambda ref: ref, w_alls[2].at[j], len(loads) + j))
    else:
        for j in range(4):
            cut_of = lambda ref: ref.at[: ref.shape[0] - GAIN_ROWS, low:high]
            loads.append(loading(0, j, cut_of, w_alls[0].at[j], j))
    for load in downs + loads if kind == "mlp_back" else loads + downs:
        for holds, copy in load:
            if holds is None:
                copy.start()
            else:
                pl.when(holds)(copy.start)
    loads, downs = [x[0][1] for x in loads], [x[0][1] for x in downs]

    barrier = pltpu.get_barrier_semaphore()
    peers = []
    if gathers:
        peers = [{"gx": far}, {"gx": near}, {"section": 1 - section}]
    elif kind == "mlp_back":
        peers = [{"gx": near}] + [{"gx": far}] * (exchange > 0)
    if crosses:
        assert not gathers
        peers.append({"section": 1 - section})
    beside = len(peers)
    for peer in peers:
        pl.semaphore_signal(barrier, inc=1, device_id=peer, device_id_type=MESH)

    @pl.when(middle)
    def _():
        pl.semaphore_signal(barrier, inc=1, device_id={"gy": end_of}, device_id_type=MESH)
        pl.semaphore_signal(barrier, inc=1, device_id={"gy": across}, device_id_type=MESH)
        pl.semaphore_wait(barrier, 2 + beside)

    @pl.when(jnp.logical_not(middle))
    def _():
        pl.semaphore_signal(barrier, inc=1, device_id={"gy": mid_of}, device_id_type=MESH)
        pl.semaphore_wait(barrier, 1 + beside)

    x_peer = {"section": 1 - section}

    def x_copy(k):
        return pltpu.make_async_remote_copy(
            src_ref=cross_refs[k], dst_ref=crossed_refs[k], send_sem=x_send.at[k],
            recv_sem=x_recv.at[k], device_id=x_peer, device_id_type=MESH,
        )

    def home_copy(rows_here):
        return pltpu.make_async_remote_copy(
            src_ref=out_ref.at[rows_here, pl.ds(pl.multiple_of(z * columns, columns), columns)],
            dst_ref=home_ref.at[rows_here, :], send_sem=home_send, recv_sem=home_recv,
            device_id=x_peer, device_id_type=MESH,
        )

    def home_start(i):
        if homing:
            here = pl.ds(pl.multiple_of(i * CHUNK, CHUNK), CHUNK)
            pl.when(section != w_layer)(lambda: home_copy(here).start())

    def x_sends(k):
        return section != crosses[k] if crosses[k] < 2 else section >= 0

    def x_takes(k):
        return section == crosses[k] if crosses[k] < 2 else section >= 0

    for k in range(len(crosses)):
        pl.when(x_sends(k))(lambda k=k: x_copy(k).start())

    def half_of(ref, k, which):
        size = base_refs[2 * k].shape[0] // 2
        return ref.at[pl.ds(pl.multiple_of(which * size, 16), size), :]

    def far_copy(k, source):
        return pltpu.make_async_remote_copy(
            src_ref=half_of(source, k, section),
            dst_ref=half_of(block_refs[k].at[shard], k, section),
            send_sem=far_send.at[k], recv_sem=far_recv.at[k],
            device_id={"gx": far}, device_id_type=MESH,
        )

    def near_copy(k, source):
        return pltpu.make_async_remote_copy(
            src_ref=source, dst_ref=block_refs[k].at[shard], send_sem=near_send.at[3 * k],
            recv_sem=near_recv.at[3 * k], device_id={"gx": near}, device_id_type=MESH,
        )

    def cross_copy(k):
        rows_here = half_of(block_refs[k].at[far], k, section)
        return pltpu.make_async_remote_copy(
            src_ref=rows_here, dst_ref=rows_here, send_sem=cross_send.at[k],
            recv_sem=cross_recv.at[k], device_id=x_peer, device_id_type=MESH,
        )

    def pass_copy(k, late):
        rows_here = half_of(block_refs[k].at[far], k, 1 - section if late else section)
        return pltpu.make_async_remote_copy(
            src_ref=rows_here, dst_ref=rows_here, send_sem=near_send.at[3 * k + 1 + late],
            recv_sem=near_recv.at[3 * k + 1 + late], device_id={"gx": near}, device_id_type=MESH,
        )

    at_home = section == layer

    def from_base(k, starts):
        for ref, holds in zip(base_refs[2 * k : 2 * k + 2], (at_home, jnp.logical_not(at_home))):

            @pl.when(holds)
            def _():
                for make in starts:
                    make(k, ref).start()

    def gather_middle(k):
        far_copy(k, base_refs[2 * k]).wait_recv()
        cross_copy(k).start()
        pass_copy(k, 0).start()

    def gather_late(k):
        cross_copy(k).wait_recv()
        pass_copy(k, 1).start()

    if gathers:
        from_base(0, [far_copy])
    for k in range(gathers):
        from_base(k, [near_copy])

    half = rows // STEPS
    core = lax.rem(shard, 2)

    def give(slot, source, target):
        return pltpu.make_async_remote_copy(
            src_ref=source, dst_ref=target, send_sem=give_sem.at[slot],
            recv_sem=take_sem.at[slot], device_id={"gx": near}, device_id_type=MESH,
        )

    def chip_columns(ref, y, of):
        return ref.at[:, pl.ds(pl.multiple_of((2 * y + of) * columns, columns), columns)]

    def step_rows(ref, step):
        return ref.at[pl.ds(pl.multiple_of(step * half, half), half), :]

    if kind == "mlp_back":
        saved_gate, saved_up, saved_normed, saved_hidden = lhs_refs
        early = [give(0, saved_hidden, far_hidden)]
        for y in range(2):
            early.append(give(1 + y, chip_columns(resid_ref, y, 1 - core), far_dm.at[y]))
        for y in range(2):
            early.append(give(3 + y, chip_columns(saved_normed, y, 1 - core), far_normed.at[y]))
        for copy in early:
            copy.start()

    def give_step(step):
        return [
            give(5 + step, step_rows(d_gate_ref, step), step_rows(far_d_gate, step)),
            give(5 + STEPS + step, step_rows(d_up_ref, step), step_rows(far_d_up, step)),
        ]

    if not wide:
        for load in loads:
            load.wait()

    def at_first(step, copies):
        @pl.when(step == 0)
        def _():
            for copy in copies:
                copy.wait()

    def rows_at(ref, i):
        return ref.at[pl.ds(pl.multiple_of(i * CHUNK, CHUNK), CHUNK), :]

    def up_copy(i):
        return pltpu.make_async_remote_copy(
            src_ref=rows_at(part, i), dst_ref=rows_at(from_end, i), send_sem=up_send.at[i],
            recv_sem=up_recv.at[i], device_id={"gy": mid_of}, device_id_type=MESH,
        )

    def mid_copy(i):
        return pltpu.make_async_remote_copy(
            src_ref=rows_at(pair, i), dst_ref=rows_at(from_mid, i), send_sem=mid_send.at[i],
            recv_sem=mid_recv.at[i], device_id={"gy": across}, device_id_type=MESH,
        )

    def fin_copy(i):
        return pltpu.make_async_remote_copy(
            src_ref=rows_at(out_ref, i), dst_ref=rows_at(out_ref, i), send_sem=fin_send.at[i],
            recv_sem=fin_recv.at[i], device_id={"gy": end_of}, device_id_type=MESH,
        )

    def dot(left, right, transposed=False):
        dims = (((1,), (1 if transposed else 0,)), ((), ()))
        return lax.dot_general(left, right, dims, preferred_element_type=F32)

    def spans(extent):
        return [(x, min(x + 512, extent)) for x in range(0, extent, 512)]

    if wide:
        w_gate, w_up, w_down = w_alls

    def product(step, carry):
        here = pl.ds(pl.multiple_of(step * half, half), half)
        if kind == "mlp":
            values = resid_ref[here, :].astype(F32)
            square = jnp.mean(values * values, axis=1, keepdims=True)
            ms_ref[here, :] = square
            normed_ref[here, :] = (values * lax.rsqrt(square + EPS) * gain_ref[...]).astype(BF)
            for n, (x0, x1) in enumerate(spans(w_gate.shape[1])):
                at_first(step, loads[8 * n : 8 * n + 8])
                gate = dot(normed_ref[here, :], w_gate[:, x0:x1])
                up = dot(normed_ref[here, :], w_up[:, x0:x1])
                gate_ref[here, x0:x1] = gate.astype(BF)
                up_ref[here, x0:x1] = up.astype(BF)
                hidden_ref[here, x0:x1] = (gate * jax.nn.sigmoid(gate) * up).astype(BF)
        if kind == "mlp_back":
            at_first(step, downs)
            for x0, x1 in spans(w_gate.shape[1]):
                d_hidden = sum(
                    dot(resid_ref[here, j * columns : (j + 1) * columns], w_down[j, x0:x1, :], True)
                    for j in range(4)
                )
                gate = saved_gate[here, x0:x1].astype(F32)
                up = saved_up[here, x0:x1].astype(F32)
                sigmoid = jax.nn.sigmoid(gate)
                d_up_ref[here, x0:x1] = (d_hidden * (gate * sigmoid)).astype(BF)
                d_gate_ref[here, x0:x1] = (
                    d_hidden * up * sigmoid * (1.0 + gate * (1.0 - sigmoid))
                ).astype(BF)
            for copy in give_step(step):
                copy.start()
        if wide:
            at_first(step, downs if kind == "mlp" else loads)
        for j in range(4):
            span = slice(j * columns, (j + 1) * columns)
            if kind == "out":
                value = dot(lhs_refs[0][here, :], w_alls[0][j])
            elif kind == "mlp":
                value = dot(hidden_ref[here, :], w_down[j])
            elif kind == "mlp_back":
                value = dot(d_gate_ref[here, :], w_gate[span, :], True)
                value += dot(d_up_ref[here, :], w_up[span, :], True)
            else:
                value = dot(lhs_refs[0][here, :], w_alls[0][j], True)
            part[here, span] = value.astype(BF)

        @pl.when(jnp.logical_not(middle))
        def _():
            def send(i, inner):
                up_copy(step * (count // STEPS) + i).start()
                return inner

            lax.fori_loop(0, count // STEPS, send, 0)

        return carry

    lax.fori_loop(0, STEPS, product, 0)

    def finish(i):
        mid_copy(i).wait_recv()
        here = pl.ds(pl.multiple_of(i * CHUNK, CHUNK), CHUNK)
        total = pair[here, :].astype(F32) + from_mid[here, :].astype(F32)
        resid = resid_ref[here, :].astype(F32)
        if forward:
            result = resid + total
            if masked:
                result = result * valid_ref[here, :]
        else:
            values = h_ref[here, :].astype(F32)
            scaled = total * gain_ref[...]
            ratio = lax.rsqrt(square_ref[here, :] + EPS)
            mean_term = jnp.sum(scaled * values, axis=1, keepdims=True) * (1.0 / width)
            result = resid + ratio * scaled - values * (ratio * ratio * ratio) * mean_term
        out_ref[here, :] = result.astype(BF)
        fin_copy(i).start()
        home_start(i)

    tile = columns // 2

    def tile_rows(sub):
        return pl.ds(pl.multiple_of(sub % 2 * tile, tile), tile)

    def stage_copy(number, sub, slot):
        target = product_refs[number].at[sub // 2, tile_rows(sub), :]
        return pltpu.make_async_copy(stage.at[slot], target, stage_sem.at[slot])

    def y_copy(number, sub, slot):
        return pltpu.make_async_remote_copy(
            src_ref=y_stage.at[2 * number + slot], dst_ref=arrived_refs[number].at[tile_rows(sub), :],
            send_sem=y_send.at[2 * number + slot], recv_sem=y_recv.at[2 * number + slot],
            device_id={"gx": far}, device_id_type=MESH,
        )

    def gradient_tile(number, sub):
        slot = sub % 2
        left, far_left, right, far_right = (
            (resid_ref, far_dm, saved_hidden, far_hidden),
            (saved_normed, far_normed, d_gate_ref, far_d_gate),
            (saved_normed, far_normed, d_up_ref, far_d_up),
        )[number]

        @pl.when(sub == 0)
        def _():
            waits = [early[:3], early[3:] + give_all[:STEPS], give_all[STEPS:]][number]
            for copy in waits:
                copy.wait_recv()

        if number >= exchange:

            @pl.when((sub >= 2) | (number > 0))
            def _():
                stage_copy(number, sub, slot).wait()

        elif number > 0:

            @pl.when(sub >= 2)
            def _():
                stage_copy(number, sub - 2, slot).wait()

        y = sub // 2
        if number < exchange:
            y = jnp.where(sub < 2, 1 - lax.div(shard, 2), lax.div(shard, 2))
        start = (y * 2 + core) * columns + sub % 2 * tile
        mine = left[:, pl.ds(pl.multiple_of(start, tile), tile)]
        theirs = far_left[y, :, tile_rows(sub)]
        value = dot_to(mine, right[...], ((0,), (0,))) + dot_to(theirs, far_right[...], ((0,), (0,)))
        if number < exchange:

            @pl.when(sub < 2)
            def _():
                y_stage[2 * number + slot] = value.astype(BF)
                y_copy(number, sub, slot).start()

            @pl.when(sub >= 2)
            def _():
                stage[slot] = value.astype(BF)
                stage_copy(number, sub - 2, slot).start()

        else:
            stage[slot] = value.astype(BF)
            stage_copy(number, sub, slot).start()

    if kind == "mlp_back":
        give_all = [x for pair in zip(*(give_step(n) for n in range(STEPS))) for x in pair]

    def beside_step(i):
        pass_on(i)
        if kind == "mlp_back":
            for number in range(3):
                first = 3 + 4 * number

                @pl.when((i >= first) & (i < first + 4))
                def _():
                    gradient_tile(number, i - first)

    def pass_on(i):
        if gathers == 2:
            at(2, i, lambda: from_base(1, [far_copy]))
            at(6, i, lambda: gather_middle(0))
            at(10, i, lambda: gather_middle(1))
            at(11, i, lambda: gather_late(0))
            at(15, i, lambda: gather_late(1))

    def at(sixteenth, i, action):
        pl.when(i == count * sixteenth // 16)(action)

    @pl.when(middle)
    def _():
        def step(i, carry):
            up_copy(i).wait_recv()
            here = pl.ds(pl.multiple_of(i * CHUNK, CHUNK), CHUNK)
            pair[here, :] = (part[here, :].astype(F32) + from_end[here, :].astype(F32)).astype(BF)
            mid_copy(i).start()

            @pl.when(i >= 1)
            def _():
                finish(i - 1)

            beside_step(i)
            return carry

        lax.fori_loop(0, count, step, 0)
        finish(count - 1)

        def drain(i, carry):
            mid_copy(i).wait_send()
            fin_copy(i).wait_send()
            return carry

        lax.fori_loop(0, count, drain, 0)

    @pl.when(jnp.logical_not(middle))
    def _():
        def drain(i, carry):
            up_copy(i).wait_send()
            fin_copy(i).wait_recv()
            home_start(i)
            beside_step(i)
            return carry

        lax.fori_loop(0, count, drain, 0)

    if kind == "mlp_back":
        for slot in range(2):
            stage_copy(2, 2 + slot, slot).wait()
        for copy in early + give_all:
            copy.wait_send()
        for number in range(exchange):
            for slot in range(2):
                y_copy(number, slot, slot).wait()
    if homing:
        every = pl.ds(0, rows)
        pl.when(section != w_layer)(lambda: home_copy(every).wait_send())
        pl.when(section == w_layer)(lambda: home_copy(every).wait_recv())
    for k in range(len(crosses)):
        pl.when(x_sends(k))(lambda k=k: x_copy(k).wait_send())
        pl.when(x_takes(k))(lambda k=k: x_copy(k).wait_recv())
    for k in range(gathers):
        far_copy(k, base_refs[2 * k]).wait_send()
        near_copy(k, base_refs[2 * k]).wait()
        cross_copy(k).wait_send()
        pass_copy(k, 0).wait()
        pass_copy(k, 1).wait()


def line_sum(kind, ident, resid, weights, lhs=(), gain=None, valid=None, back=None, low=0, high=0, deps=(), bases=(), layer=0, exchange=0, w_layer=0, crosses=(), homing=False):
    rows, width = resid.shape
    one = jnp.ones((rows, 1), F32)
    h, square = back if back is not None else (jnp.zeros((16, 128), BF), jnp.zeros((8, 1), F32))
    gain = jnp.zeros((1, width), F32) if gain is None else gain
    wide = kind in ("mlp", "mlp_back")
    hidden = 0
    if wide:
        hidden = (weights[2][0] if isinstance(weights[2], tuple) else weights[2]).shape[1]
    w_scratch = []
    triples = [isinstance(w, tuple) for w in weights]
    w_flat = [x for w in weights for x in (w if isinstance(w, tuple) else (w,))]
    for i, w in enumerate(weights):
        _, depth, across = (w[0] if isinstance(w, tuple) else w).shape
        if wide and i < 2:
            w_scratch.append(pltpu.VMEM((width, across), BF))
        else:
            shape = (4, depth, across) if wide else (4, depth - GAIN_ROWS, high - low)
            w_scratch.append(pltpu.VMEM(shape, BF))
    outs, products, beside = [((rows, width), BF)], [], []
    if kind == "mlp":
        outs += [((rows, width), BF), ((rows, 1), F32)] + [((rows, hidden), BF)] * 3
    elif kind == "mlp_back":
        products = [((1 if n < exchange else 2, width // 4, hidden), BF) for n in range(3)]
        products += [((width // 4, hidden), BF)] * exchange
        half_block = pltpu.VMEM((2, rows, width // 4), BF)
        beside = [pltpu.VMEM((rows, hidden), BF)] * 2 + [half_block] * 2
        beside += [pltpu.VMEM((rows, hidden), BF)] * 3 + [pltpu.VMEM((2, width // 8, hidden), BF)]
        beside += [pltpu.SemaphoreType.DMA((n,)) for n in (5 + 2 * STEPS, 5 + 2 * STEPS, 2)]
        if exchange:
            beside += [pltpu.VMEM((2 * exchange, width // 8, hidden), BF)]
            beside += [pltpu.SemaphoreType.DMA((2 * exchange,))] * 2
    blocks = [((4,) + base[0].shape, BF) for base in bases]
    pairs = [x for base in bases for x in base]
    crossed = [(x[0].shape, BF) for x in crosses] + [((rows, width // 4), BF)] * homing
    depth = 3 * hidden if wide else lhs[0].shape[1]
    count = rows // CHUNK
    dma = pltpu.SemaphoreType.DMA
    return pl.pallas_call(
        functools.partial(
            line_kernel, kind, valid is not None, low, high, len(deps), len(bases), layer, exchange,
            triples, w_layer, [x[1] for x in crosses], homing,
        ),
        out_shape=tuple(jax.ShapeDtypeStruct(*o) for o in outs + products + blocks + crossed),
        in_specs=[VMEM] * (5 + len(lhs)) + [ANY] * (len(w_flat) + len(deps) + len(pairs) + len(crosses)),
        out_specs=tuple([VMEM] * len(outs) + [ANY] * len(products + blocks + crossed)),
        scratch_shapes=w_scratch
        + [pltpu.VMEM((rows, width), BF)] * 4
        + [dma((8 * -(-hidden // 512) + 4,))]
        + [dma((count,))] * 6
        + [dma((n * len(bases),)) for n in (1, 1, 3, 3, 1, 1) if bases]
        + beside
        + [dma((len(crosses),))] * 2 * bool(crosses)
        + [dma] * 2 * homing,
        compiler_params=pltpu.CompilerParams(
            collective_id=ident, has_side_effects=True, vmem_limit_bytes=VMEM_LIMIT
        ),
        cost_estimate=pl.CostEstimate(
            flops=2 * rows * depth * width, bytes_accessed=200 * 1024 * 1024, transcendentals=0
        ),
        name="line_" + kind,
    )(
        gain, resid, one if valid is None else valid, h, square, *lhs, *w_flat, *deps, *pairs,
        *(x[0] for x in crosses),
    )


def plain_sum(total):
    return lax.psum(total.astype(BF), "gy").astype(F32)


def normed(h, gain):
    values = h.astype(F32)
    square = jnp.mean(values * values, axis=1, keepdims=True)
    return square, (values * lax.rsqrt(square + EPS) * gain).astype(BF)


def norm_back(d_normed, h, square, gain):
    values = h.astype(F32)
    ratio = lax.rsqrt(square + EPS)
    scaled = d_normed * gain
    mean_term = jnp.mean(scaled * values, axis=1, keepdims=True)
    return ratio * scaled - values * (ratio * ratio * ratio) * mean_term


def attention_forward(h, gain, w_attn, low, tables, ident, bases, layer, w_layer, deps=()):
    rows, width = h.shape
    high = low + width // lax.axis_size("gx")
    q_width = low - 2 * HD
    if fused():
        heads, n1, square, rotated, lse, k_all, kt_all, v_all = attend_whole(
            h, gain, w_attn, low, tables, w_layer, ident + 8
        )
        h1, *stacks = line_sum(
            "out", ident, h, [w_attn], (heads,), low=low, high=high,
            deps=deps, bases=bases, layer=layer, w_layer=w_layer,
        )
        blocks = [(x, *pair) for x, pair in zip(stacks, bases)]
    else:
        cosine, sines = tables[:2]
        square, n1 = normed(h, gain)
        q_down = mm(tall(cut(w_attn, 0, q_width)), n1, ((0,), (1,)))
        kv = mm(n1, tall(cut(w_attn, q_width, low)))
        k_rot = rope_down(kv[:, :HD].T, cosine, sines).T.astype(BF)
        kv = jnp.concatenate([k_rot, kv[:, HD:].astype(BF)], axis=1)
        kv_all = jnp.concatenate([kv, swap_pairs(kv, "gx")], axis=0)
        k_all, v_all = kv_all[:, :HD], kv_all[:, HD:]
        kt_all = k_all.T
        heads, rotated, lse = attend(q_down, k_all, v_all, tables)
        h1 = (h.astype(F32) + plain_sum(mm(heads, side(cut(w_attn, low, high))))).astype(BF)
        blocks = [gather_blocks(chosen(x, layer)) for x in bases]
    return h1, square, blocks, (h, square, n1, rotated, lse, k_all, kt_all, v_all, heads)


def mlp_forward(h1, gain, weights, valid, ident, bases=(), layer=0, w_layer=0):
    if fused():
        result, n2, square, gate, up, hidden, *stacks = line_sum(
            "mlp", ident, h1, weights, gain=gain, valid=valid, bases=bases, layer=layer,
            w_layer=w_layer,
        )
        blocks = [(x, *pair) for x, pair in zip(stacks, bases)]
    else:
        square, n2 = normed(h1, gain)
        gate = mm(n2, tall(weights[0]))
        up = mm(n2, tall(weights[1]))
        hidden = (gate * jax.nn.sigmoid(gate) * up).astype(BF)
        gate, up = gate.astype(BF), up.astype(BF)
        result = h1.astype(F32) + plain_sum(mm(hidden, side(weights[2])))
        result = (result * valid).astype(BF)
        blocks = [gather_blocks(chosen(x, layer)) for x in bases]
    return result, square, blocks, (h1, square, n2, gate, up, hidden)


def mlp_backward(dm, gain, weights, saved, ident, w_layer, crosses=(), deps=(), exchange=1):
    h1, square, n2, gate, up, hidden = saved
    if fused():
        e1, *products = line_sum(
            "mlp_back", ident, dm, weights, (gate, up, n2, hidden), gain=gain,
            back=(h1, square), exchange=exchange, w_layer=w_layer, crosses=crosses, deps=deps,
        )
        return e1, products[:4], products[4:]
    gate, up = gate.astype(F32), up.astype(F32)
    d_hidden = mm(dm, side(weights[2]), ((1,), (1,)))
    sigmoid = jax.nn.sigmoid(gate)
    d_gate = (d_hidden * up * sigmoid * (1.0 + gate * (1.0 - sigmoid))).astype(BF)
    d_up = (d_hidden * (gate * sigmoid)).astype(BF)
    total = mm(d_gate, tall(weights[0]), ((1,), (1,))) + mm(d_up, tall(weights[1]), ((1,), (1,)))
    e1 = (dm.astype(F32) + norm_back(plain_sum(total), h1, square, gain)).astype(BF)
    turn = ((0,), (0,))
    products = [mm(dm, hidden, turn), mm(n2, d_gate, turn), mm(n2, d_up, turn)]
    return e1, [p.astype(BF) for p in products], crossing(crosses)


def crossing(crosses):
    pairs = ([(1, 0)], [(0, 1)], [(0, 1), (1, 0)])
    return [lax.ppermute(x, "section", pairs[way]) for x, way in crosses]


def mlp_sums(products):
    if not fused():
        return [shard_sum(p) for p in products]
    down, gate, up, arrived = products
    first = (down[0].astype(F32) + arrived.astype(F32)).astype(BF)
    return [first, chip_sum(gate), chip_sum(up)]


def attention_backward(e1, w_attn, low, tables, saved, w_layer, ident):
    h, square, n1, rotated, lse, k_all, kt_all, v_all, heads = saved
    rows, width = h.shape
    if fused():
        d_qkv = attend_whole_back(
            e1, rotated, lse, k_all, kt_all, v_all, w_attn, tables, w_layer, ident
        )
    else:
        cosine, sines = tables[:2]
        w_o = side(cut(w_attn, low, low + width // lax.axis_size("gx")))
        d_down = mm(w_o, e1, ((1,), (1,))).astype(BF)
        dq, dk, dv = attend_back(rotated, k_all, v_all, d_down, lse, tables)
        dkv = jnp.concatenate([dk, dv], axis=1)
        dkv = dkv[:rows] + swap_pairs(dkv[rows:], "gx")
        dk = rope_down(dkv[:, :HD].T, cosine, -sines).T
        d_qkv = jnp.concatenate([dq, dk.astype(BF), dkv[:, HD:].astype(BF)], axis=1)
    turn = ((0,), (0,))
    products = [mm(n1, d_qkv, turn).astype(BF), mm(e1, heads, turn).astype(BF)]
    return d_qkv, jnp.concatenate(products, axis=1)


def attention_end(d_qkv, e1, w_attn, gain, saved, ident, w_layer, deps, crosses):
    h, square = saved[:2]
    qkv_width = d_qkv.shape[1]
    if fused():
        grad, *crossed = line_sum(
            "back", ident, e1, [w_attn], (d_qkv,), gain=gain, back=(h, square),
            low=0, high=qkv_width, deps=deps, crosses=crosses, w_layer=w_layer, homing=True,
        )
        return grad, crossed[-1], crossed[:-1]
    total = plain_sum(mm(d_qkv, tall(cut(w_attn, 0, qkv_width)), ((1,), (1,))))
    grad = (e1.astype(F32) + norm_back(total, h, square, gain)).astype(BF)
    width = grad.shape[1] // lax.axis_size("gy")
    part = lax.dynamic_slice_in_dim(grad, lax.axis_index("gy") * width, width, 1)
    home, *crossed = crossing([(part, w_layer), *crosses])
    return grad, home, crossed


def on_device(
    hidden_in, out_grad, lengths, dealing, attn_gain, w_query, w_key, w_value, w_out,
    mlp_gain, w_gate, w_up, w_down,
):
    shards = lax.axis_size("gx")
    shard = lax.axis_index("gx")
    section = lax.axis_index("section")
    column = lax.axis_index("gy")
    core = shard % 2
    sequence = (shard // 2) * 2 + section
    span, width = hidden_in.shape
    half = span // 2
    seq_length = lax.dynamic_index_in_dim(lengths, sequence, keepdims=False)

    both = jnp.concatenate([hidden_in, out_grad], axis=1)
    mine = core_rows(both, core)
    theirs = swap_pairs(core_rows(both, 1 - core), "gx")
    mine = jnp.where(core == section, mine, theirs)
    h = lax.all_gather(mine[:, :width], "gy", axis=1, tiled=True)

    kv_head = column * (w_query.shape[2] // HD) // (QH // KVH)
    low = w_query.shape[2] + 2 * HD
    both_gains = jnp.stack([attn_gain[0], mlp_gain[0]])
    block_rows = both_gains.shape[1]
    attn_own = jnp.concatenate(
        [
            w_query[0],
            lax.dynamic_slice_in_dim(w_key[0], kv_head * HD, HD, 1),
            lax.dynamic_slice_in_dim(w_value[0], kv_head * HD, HD, 1),
            w_out[0],
        ],
        axis=1,
    )
    gain_rows = jnp.pad(both_gains, ((0, GAIN_ROWS - 2), (0, attn_own.shape[1] - block_rows)))
    attn_own = jnp.concatenate([attn_own, gain_rows], axis=0)
    own = (attn_own, w_gate[0], w_up[0], w_down[0])
    first = [(array, lax.ppermute(array, "section", [(0, 1)])) for array in own]
    second = [(array, lax.ppermute(array, "section", [(1, 0)])) for array in own]

    def gains_of(w_attn, pair):
        cut_of = lambda w: w[..., block_rows : block_rows + 2, :block_rows]
        rows = cut_of(w_attn[0] if isinstance(w_attn, tuple) else w_attn)
        if isinstance(w_attn, tuple):
            rows = with_own(rows, [cut_of(x) for x in pair], 1)
        return rows.transpose(1, 0, 2).reshape(2, 1, -1).astype(F32)

    here = core_rows(jnp.arange(span), core)
    there = core_rows(jnp.arange(span), 1 - core)
    keys_at = jnp.concatenate([here, there])
    valid = (here < seq_length)[:, None].astype(F32)
    tables = (*rope_tables(here), keys_at, here, seq_length.reshape(1, 1))

    attn0, gate0 = gather_blocks(chosen(first[0], 0)), gather_blocks(chosen(first[1], 0))
    gains0 = gains_of(attn0, first[0])
    h1, square_a, blocks, saved_a0 = attention_forward(
        h, gains0[0], attn0, low, tables, 0, first[2:], 0, 0, (gate0,)
    )
    mlp0 = [gate0] + blocks
    h, square_m, (attn1, gate1), saved_m0 = mlp_forward(
        h1, gains0[1], mlp0, valid, 1, second[:2], 1
    )
    gains1 = gains_of(attn1, second[0])
    outputs, squares = [h], [square_a, square_m]
    d_mine = mine[:, width:] + h[:1, :1] * 0
    d_out = lax.all_gather(d_mine, "gy", axis=1, tiled=True)
    h1, square_a, blocks, saved_a1 = attention_forward(
        h, gains1[0], attn1, low, tables, 2, second[2:], 1, 1
    )
    mlp1 = [gate1] + blocks
    h, square_m, _, saved_m1 = mlp_forward(h1, gains1[1], mlp1, valid, 3, w_layer=1)
    outputs.append(h)
    squares = jnp.concatenate(squares + [square_a, square_m], axis=1)
    rms = (jnp.sqrt(squares + EPS) * valid).T
    statistics = [rms[:2], rms[2:]]
    outputs = [lax.dynamic_slice_in_dim(x, column * width, width, 1) for x in outputs]

    dm = (d_out.astype(F32) * valid).astype(BF)
    e1, products, _ = mlp_backward(dm, gains1[1], mlp1, saved_m1, 4, 1)
    local1 = mlp_sums(products)

    both = []
    for output, stat in zip(outputs, statistics):
        high = stat.astype(BF)
        rest = (stat - high.astype(F32)).astype(BF)
        parts = jnp.concatenate([high, rest], axis=0).reshape(-1, width)
        parts = jnp.pad(parts, ((0, -parts.shape[0] % 16), (0, 0)))
        both.append(jnp.concatenate([output + e1[:1, :1] * 0, parts], axis=0))
    kept = jnp.where(section == 0, both[0], both[1])
    sent = jnp.where(section == 0, both[1], both[0])

    d_qkv, products = attention_backward(e1, attn1, low, tables, saved_a1, 1, 9)
    local1.append(shard_sum(products))
    crosses = [(sent, 2), (local1[0], 1)]
    grad1, home1, (sent, down1) = attention_end(
        d_qkv, e1, attn1, gains1[0], saved_a1, 5, 1, (products,), crosses
    )
    by_section = jnp.stack([jnp.where(section == 0, kept, sent), jnp.where(section == 0, sent, kept)])
    everything = lax.all_gather(by_section, "gx", axis=0)
    owner = jnp.sum(jnp.where(dealing == shard, jnp.arange(shards), 0))
    halves = lax.dynamic_slice(
        everything, ((owner // 2) * 2, owner % 2, 0, 0), (2, 1) + everything.shape[2:]
    )[:, 0]
    layer_out = join_halves(halves[0, :half], halves[1, :half])
    stat_rows = 4 * half // width
    parts = halves[:, half : half + stat_rows].astype(F32).reshape(2, 4, half)
    stat_halves = parts[:, :2] + parts[:, 2:]
    stats_out = join_halves(stat_halves[0].T, stat_halves[1].T).T

    dm = (grad1.astype(F32) * valid).astype(BF)
    crosses = [(local1[1], 1), (local1[2], 1)]
    e1, products, (gate1, up1) = mlp_backward(dm, gains0[1], mlp0, saved_m0, 6, 0, crosses)
    local0 = mlp_sums(products)
    d_qkv, products = attention_backward(e1, attn0, low, tables, saved_a0, 0, 11)
    local0.append(shard_sum(products))
    crosses = [(local1[3], 1), (local0[0], 0), (local0[1], 0)]
    grad0, home0, (attn_sum1, down0, gate0) = attention_end(
        d_qkv, e1, attn0, gains0[0], saved_a0, 7, 0, (products, everything), crosses
    )

    input_grads = [lax.dynamic_slice_in_dim(x, column * width, width, 1) for x in (grad0, grad1)]
    local0[2] = local0[2] + grad0[:1, :1] * 0
    received0 = [down0, gate0] + crossing([(x, 0) for x in local0[2:]])
    received1 = [down1, gate1, up1, attn_sum1]
    totals = [
        jnp.where(section == 0, a0.astype(F32) + r0.astype(F32), a1.astype(F32) + r1.astype(F32))
        for a0, r0, a1, r1 in zip(local0, received0, local1, received1)
    ]
    s_down, s_gate, s_up, s_attn = totals
    s_out = s_attn[:, low:]
    q_width = w_query.shape[2]

    attn_sum = jnp.sum(s_attn[:, :low] * attn_own[:block_rows, :low].astype(F32), axis=1)
    mlp_sum = jnp.sum(s_gate * w_gate[0].astype(F32) + s_up * w_up[0].astype(F32), axis=1)
    sums = jnp.pad(jnp.stack([attn_sum, mlp_sum], axis=1), ((0, 0), (0, 126)))
    spread = jnp.concatenate([s_attn[:, q_width:low], sums], axis=1).astype(BF)
    spread = lax.all_gather(spread, "gy", axis=0).astype(F32)
    gains = jnp.sum(spread[:, :, 2 * HD : 2 * HD + 2], axis=0).T / both_gains.astype(F32)
    kv_sum = spread[:, :, : 2 * HD].reshape(KVH, -1, *spread.shape[1:2], 2, HD).sum(axis=1)
    kv_sum = kv_sum.transpose(2, 1, 0, 3).reshape(2, spread.shape[1], KVH * HD)

    kept = jnp.where(section == 0, input_grads[0], input_grads[1])
    sent = jnp.where(section == 0, home0, home1)
    keep = jnp.where(core == section, kept, sent)
    give = swap_pairs(jnp.where(core == section, sent, kept), "gx")
    back_home = join_halves(jnp.where(core == 0, keep, give), jnp.where(core == 0, give, keep))
    return (
        layer_out[None],
        stats_out[None],
        back_home[None],
        gains[None, 0],
        s_attn[None, :, :q_width],
        kv_sum[None, 0],
        kv_sum[None, 1],
        s_out.T[None],
        gains[None, 1],
        s_gate[None],
        s_up[None],
        s_down.T[None],
    )


def solution(mesh):
    rows_cols = P("section", "gx", "gy")
    cols_rows = P("section", "gy", "gx")
    rows_only = P("section", "gx", None)
    gain = P("section", "gx")
    return jax.shard_map(
        on_device,
        mesh=mesh,
        in_specs=(
            P("gx", "gy"), P("gx", "gy"), P(), P(), gain, rows_cols, rows_only, rows_only,
            cols_rows, gain, rows_cols, rows_cols, cols_rows,
        ),
        out_specs=(
            rows_cols, P("section", None, "gx"), rows_cols, gain, rows_cols, rows_only, rows_only,
            cols_rows, gain, rows_cols, rows_cols, cols_rows,
        ),
        check_vma=False,
    )
```

```python
import functools

import jax
import jax.numpy as jnp
from jax import lax
from jax.experimental import pallas as pl
from jax.experimental.pallas import tpu as pltpu
from jax.sharding import PartitionSpec as P

QH = 32
KVH = 4
HD = 64
LAYERS = 2
EPS = 1e-05
BF = jnp.bfloat16
F32 = jnp.float32
MESH = pl.DeviceIdType.MESH
CHUNK = 32
STEPS = 2
GAIN_ROWS = 32
VMEM_LIMIT = 56 * 1024 * 1024
ANY = pl.BlockSpec(memory_space=pl.ANY)
VMEM = pl.BlockSpec(memory_space=pltpu.VMEM)


def mm(left, right, dims=((1,), (0,))):
    return lax.dot_general(left, right, (dims, ((), ())), preferred_element_type=F32)


def swap_pairs(values, axis, by=1):
    count = lax.axis_size(axis)
    return lax.ppermute(values, axis, [(i, i ^ by) for i in range(count)])


def rope_tables(places):
    half_width = HD // 2
    frequency = jnp.power(10000.0, -2.0 * jnp.arange(half_width).astype(F32) / HD)
    angles = frequency[:, None] * places.astype(F32)[None, :]
    return jnp.cos(angles), jnp.sin(angles)


def core_rows(rows, core):
    quarter = rows.shape[0] // 4
    low = lax.dynamic_slice_in_dim(rows, core * quarter, quarter, 0)
    high = lax.dynamic_slice_in_dim(rows, (3 - core) * quarter, quarter, 0)
    return jnp.concatenate([low, high], axis=0)


def join_halves(first, second):
    quarter = first.shape[0] // 2
    return jnp.concatenate(
        [first[:quarter], second[:quarter], second[quarter:], first[quarter:]], axis=0
    )


def chip_groups():
    return [[0, 2], [1, 3]]


def gather_blocks(base):
    return lax.all_gather(base, "gx", axis=0)


def chosen(pair, layer):
    return jnp.where(lax.axis_index("section") == layer, *pair)


def with_own(stack, pair, layer):
    shard = lax.axis_index("gx")
    return lax.dynamic_update_index_in_dim(stack, chosen(pair, layer), shard, 0)


def fused():
    return lax.axis_size("gx") == 4 and lax.axis_size("gy") == 4


def tall(w):
    return w.reshape(-1, w.shape[-1])


def side(w):
    return jnp.concatenate([w[i] for i in range(w.shape[0])], axis=1)


def cut(w, low, high):
    return w[:, :-GAIN_ROWS, low:high]


def shard_sum(product):
    return lax.psum_scatter(product, "gx", scatter_dimension=0, tiled=True)


def chip_sum(product):
    product = product.reshape(-1, product.shape[-1])
    return lax.psum_scatter(
        product, "gx", scatter_dimension=0, tiled=True, axis_index_groups=[[0, 2], [1, 3]]
    )


def rope_down(values, cosine, sines):
    half_width = HD // 2
    first, second = values[:half_width], values[half_width:]
    return jnp.concatenate(
        [first * cosine - second * sines, second * cosine + first * sines], axis=0
    )


def fill_bias(bias_ref, key_ref, query_ref, length_ref):
    keys = key_ref[...]
    allowed = (keys <= query_ref[...]) & (keys < length_ref[...])
    bias_ref[...] = jnp.where(allowed, 0.0, -1e30)


def dot_to(left, right, dims):
    return lax.dot_general(left, right, (dims, ((), ())), preferred_element_type=F32)


def attend_kernel(
    q_ref, k_ref, vt_ref, cos_ref, sin_ref, key_ref, query_ref, length_ref,
    heads_ref, rot_ref, lse_ref, bias_ref, out_ref,
):
    fill_bias(bias_ref, key_ref, query_ref, length_ref)

    def head(h, carry):
        here = pl.ds(pl.multiple_of(h * HD, HD), HD)
        rotated = rope_down(q_ref[here, :], cos_ref[...], sin_ref[...]).astype(BF)
        rot_ref[here, :] = rotated
        scaled = (rotated.astype(F32) * HD ** (-0.5)).astype(BF)
        scores = dot_to(k_ref[...], scaled, ((1,), (0,))) + bias_ref[...]
        top = jnp.max(scores, axis=0, keepdims=True)
        exponent = jnp.exp(scores - top)
        total = jnp.sum(exponent, axis=0, keepdims=True)
        probs = (exponent * (1.0 / total)).astype(BF)
        out_ref[here, :] = dot_to(vt_ref[...], probs, ((1,), (0,)))
        lse_ref[pl.ds(h, 1), :] = top + jnp.log(total)
        return carry

    lax.fori_loop(0, q_ref.shape[0] // HD, head, 0)
    heads_ref[...] = out_ref[...].T.astype(BF)


def attend_back_kernel(
    rot_ref, k_ref, kt_ref, v_ref, d_ref, lse_ref, cos_ref, sin_ref, key_ref, query_ref, length_ref,
    dq_ref, dk_ref, dv_ref, bias_ref, out_ref,
):
    fill_bias(bias_ref, key_ref, query_ref, length_ref)
    dk_ref[...] = jnp.zeros_like(dk_ref)
    dv_ref[...] = jnp.zeros_like(dv_ref)
    scaling = HD ** (-0.5)

    def head(h, carry):
        here = pl.ds(pl.multiple_of(h * HD, HD), HD)
        scaled = (rot_ref[here, :].astype(F32) * scaling).astype(BF)
        scores = dot_to(k_ref[...], scaled, ((1,), (0,))) + bias_ref[...]
        probs = jnp.exp(scores - lse_ref[pl.ds(h, 1), :])
        d_probs = dot_to(v_ref[...], d_ref[here, :], ((1,), (0,)))
        delta = jnp.sum(probs * d_probs, axis=0, keepdims=True)
        d_scores = (probs * (d_probs - delta)).astype(BF)
        dk_ref[...] += dot_to(d_scores, scaled, ((1,), (1,)))
        dv_ref[...] += dot_to(probs.astype(BF), d_ref[here, :], ((1,), (1,)))
        dq = dot_to(kt_ref[...], d_scores, ((1,), (0,))) * scaling
        out_ref[here, :] = rope_down(dq, cos_ref[...], -sin_ref[...])
        return carry

    lax.fori_loop(0, rot_ref.shape[0] // HD, head, 0)
    dq_ref[...] = out_ref[...].T.astype(BF)


def attend(q_down, k_all, v_all, tables):
    cosine, sines, keys_at, places, length = tables
    width, rows = q_down.shape
    return pl.pallas_call(
        attend_kernel,
        out_shape=(
            jax.ShapeDtypeStruct((rows, width), BF),
            jax.ShapeDtypeStruct((width, rows), BF),
            jax.ShapeDtypeStruct((width // HD, rows), F32),
        ),
        in_specs=[VMEM] * 8,
        out_specs=(VMEM,) * 3,
        scratch_shapes=[pltpu.VMEM((k_all.shape[0], rows), F32), pltpu.VMEM((width, rows), F32)],
        compiler_params=pltpu.CompilerParams(vmem_limit_bytes=VMEM_LIMIT),
        cost_estimate=pl.CostEstimate(
            flops=16 * width * rows * k_all.shape[0], bytes_accessed=60_000_000, transcendentals=0
        ),
        name="attend",
    )(q_down, k_all, v_all.T, cosine, sines, keys_at[:, None], places[None], length)


def attend_back(rotated, k_all, v_all, d_down, lse, tables):
    cosine, sines, keys_at, places, length = tables
    width, rows = rotated.shape
    return pl.pallas_call(
        attend_back_kernel,
        out_shape=(
            jax.ShapeDtypeStruct((rows, width), BF),
            jax.ShapeDtypeStruct(k_all.shape, F32),
            jax.ShapeDtypeStruct(k_all.shape, F32),
        ),
        in_specs=[VMEM] * 11,
        out_specs=(VMEM,) * 3,
        scratch_shapes=[pltpu.VMEM((k_all.shape[0], rows), F32), pltpu.VMEM((width, rows), F32)],
        compiler_params=pltpu.CompilerParams(vmem_limit_bytes=VMEM_LIMIT),
        cost_estimate=pl.CostEstimate(
            flops=40 * width * rows * k_all.shape[0], bytes_accessed=80_000_000, transcendentals=0
        ),
        name="attend_back",
    )(
        rotated, k_all, k_all.T, v_all, d_down, lse, cosine, sines,
        keys_at[:, None], places[None], length,
    )


def load_blocks(w_refs, w_layer, low, high, target_of, sem):
    shard, home = lax.axis_index("gx"), lax.axis_index("section") == w_layer
    waits = []
    for j in range(4):

        def copy(ref):
            source = ref.at[: ref.shape[0] - GAIN_ROWS, low:high]
            return pltpu.make_async_copy(source, target_of(j), sem.at[j])

        waits.append(copy(w_refs[0].at[j]))
        if len(w_refs) == 1:
            waits[j].start()
        else:
            pl.when(shard != j)(waits[j].start)
            pl.when((shard == j) & home)(copy(w_refs[1]).start)
            pl.when((shard == j) & jnp.logical_not(home))(copy(w_refs[2]).start)
    return waits


def meet_near(*others):
    near = {"gx": lax.axis_index("gx") ^ 1}
    barrier = pltpu.get_barrier_semaphore()
    for peer in (near, *others):
        pl.semaphore_signal(barrier, inc=1, device_id=peer, device_id_type=MESH)
    pl.semaphore_wait(barrier, 1 + len(others))
    return near


def attend_whole_kernel(
    w_layer, listed,
    h_ref, gain_ref, cos_ref, sin_ref, key_ref, query_ref, length_ref, *rest,
):
    w_refs, rest = rest[:listed], rest[listed:]
    (
        heads_ref, normed_ref, ms_ref, rot_ref, lse_ref, k_ref, kt_ref, v_ref,
        w_all, bias_ref, out_ref, q_ref, vt_ref, kv_mine, kv_far, w_sem, send_sem, recv_sem,
    ) = rest
    rows, width = h_ref.shape
    block = width // 4
    q_width = q_ref.shape[0]
    waits = load_blocks(
        w_refs, w_layer, 0, q_width + 2 * HD, lambda j: w_all.at[j * block : (j + 1) * block], w_sem
    )
    near = meet_near()

    def norm(i, carry):
        here = pl.ds(pl.multiple_of(i * 128, 128), 128)
        values = h_ref[here, :].astype(F32)
        square = jnp.mean(values * values, axis=1, keepdims=True)
        ms_ref[here, :] = square
        normed_ref[here, :] = (values * lax.rsqrt(square + EPS) * gain_ref[...]).astype(BF)
        return carry

    lax.fori_loop(0, rows // 128, norm, 0)
    for wait in waits:
        wait.wait()
    kv = dot_to(normed_ref[...], w_all[:, q_width:], ((1,), (0,))).T
    kv = jnp.concatenate([rope_down(kv[:HD], cos_ref[...], sin_ref[...]), kv[HD:]], axis=0)
    kv_mine[...] = kv.T.astype(BF)
    copy = pltpu.make_async_remote_copy(
        src_ref=kv_mine, dst_ref=kv_far, send_sem=send_sem, recv_sem=recv_sem,
        device_id=near, device_id_type=MESH,
    )
    copy.start()
    q_ref[...] = dot_to(normed_ref[...], w_all[:, :q_width], ((1,), (0,))).T
    fill_bias(bias_ref, key_ref, query_ref, length_ref)
    copy.wait()
    for n, ref in enumerate((kv_mine, kv_far)):
        here = pl.ds(n * rows, rows)
        k_ref[here, :] = ref[:, :HD]
        v_ref[here, :] = ref[:, HD:]
        down = ref[...].astype(F32).T.astype(BF)
        kt_ref[:, here] = down[:HD]
        vt_ref[:, here] = down[HD:]

    def head(h, carry):
        here = pl.ds(pl.multiple_of(h * HD, HD), HD)
        rotated = rope_down(q_ref[here, :], cos_ref[...], sin_ref[...]).astype(BF)
        rot_ref[here, :] = rotated
        scaled = (rotated.astype(F32) * HD ** (-0.5)).astype(BF)
        scores = dot_to(k_ref[...], scaled, ((1,), (0,))) + bias_ref[...]
        top = jnp.max(scores, axis=0, keepdims=True)
        exponent = jnp.exp(scores - top)
        total = jnp.sum(exponent, axis=0, keepdims=True)
        probs = (exponent * (1.0 / total)).astype(BF)
        out_ref[here, :] = dot_to(vt_ref[...], probs, ((1,), (0,)))
        lse_ref[pl.ds(h, 1), :] = top + jnp.log(total)
        return carry

    lax.fori_loop(0, q_width // HD, head, 0)
    heads_ref[...] = out_ref[...].T.astype(BF)


def attend_whole_back_kernel(
    w_layer, listed, crosses,
    e1_ref, rot_ref, lse_ref, k_ref, kt_ref, v_ref, cos_ref, sin_ref, key_ref, query_ref,
    length_ref, *rest,
):
    w_refs, rest = rest[:listed], rest[listed:]
    if crosses:
        source_ref, d_qkv_ref, crossed_ref, *rest, x_send, x_recv = rest
    else:
        d_qkv_ref, *rest = rest
    (
        w_all, bias_ref, d_ref, out_ref, dk_ref, dv_ref, dkv_send, dkv_far,
        w_sem, send_sem, recv_sem,
    ) = rest
    rows, width = e1_ref.shape
    block = width // 4
    q_width = rot_ref.shape[0]
    low = q_width + 2 * HD
    waits = load_blocks(w_refs, w_layer, low, low + block, lambda j: w_all.at[j], w_sem)
    section = lax.axis_index("section")
    x_peer = {"section": 1 - section}
    near = meet_near(x_peer) if crosses else meet_near()

    def x_copy():
        return pltpu.make_async_remote_copy(
            src_ref=source_ref, dst_ref=crossed_ref, send_sem=x_send, recv_sem=x_recv,
            device_id=x_peer, device_id_type=MESH,
        )

    if crosses:
        pl.when(section != w_layer)(lambda: x_copy().start())
    fill_bias(bias_ref, key_ref, query_ref, length_ref)
    dk_ref[...] = jnp.zeros_like(dk_ref)
    dv_ref[...] = jnp.zeros_like(dv_ref)
    scaling = HD ** (-0.5)
    for wait in waits:
        wait.wait()
    d_ref[...] = sum(
        dot_to(w_all[j], e1_ref[:, j * block : (j + 1) * block], ((1,), (1,))) for j in range(4)
    ).astype(BF)

    def head(h, carry):
        here = pl.ds(pl.multiple_of(h * HD, HD), HD)
        scaled = (rot_ref[here, :].astype(F32) * scaling).astype(BF)
        scores = dot_to(k_ref[...], scaled, ((1,), (0,))) + bias_ref[...]
        probs = jnp.exp(scores - lse_ref[pl.ds(h, 1), :])
        d_probs = dot_to(v_ref[...], d_ref[here, :], ((1,), (0,)))
        delta = jnp.sum(probs * d_probs, axis=0, keepdims=True)
        d_scores = (probs * (d_probs - delta)).astype(BF)
        dk_ref[...] += dot_to(d_scores, scaled, ((1,), (1,)))
        dv_ref[...] += dot_to(probs.astype(BF), d_ref[here, :], ((1,), (1,)))
        dq = dot_to(kt_ref[...], d_scores, ((1,), (0,))) * scaling
        out_ref[here, :] = rope_down(dq, cos_ref[...], -sin_ref[...])
        return carry

    lax.fori_loop(0, q_width // HD, head, 0)
    dkv_send[:, :HD] = dk_ref[rows:, :]
    dkv_send[:, HD:] = dv_ref[rows:, :]
    copy = pltpu.make_async_remote_copy(
        src_ref=dkv_send, dst_ref=dkv_far, send_sem=send_sem, recv_sem=recv_sem,
        device_id=near, device_id_type=MESH,
    )
    copy.start()
    d_qkv_ref[:, :q_width] = out_ref[...].T.astype(BF)
    copy.wait()
    down = (dkv_far[...].T)
    dk = rope_down(dk_ref[:rows, :].T + down[:HD], cos_ref[...], -sin_ref[...])
    dkv = jnp.concatenate([dk, dv_ref[:rows, :].T + down[HD:]], axis=0)
    d_qkv_ref[:, q_width:] = dkv.T.astype(BF)
    if crosses:
        pl.when(section != w_layer)(lambda: x_copy().wait_send())
        pl.when(section == w_layer)(lambda: x_copy().wait_recv())


def attend_whole(h, gain, w_attn, low, tables, w_layer, ident):
    cosine, sines, keys_at, places, length = tables
    rows, width = h.shape
    keys, q_width = keys_at.shape[0], low - 2 * HD
    w_list = list(w_attn) if isinstance(w_attn, tuple) else [w_attn]
    outs = [
        ((rows, q_width), BF), ((rows, width), BF), ((rows, 1), F32), ((q_width, rows), BF),
        ((q_width // HD, rows), F32), ((keys, HD), BF), ((HD, keys), BF), ((keys, HD), BF),
    ]
    return pl.pallas_call(
        functools.partial(attend_whole_kernel, w_layer, len(w_list)),
        out_shape=tuple(jax.ShapeDtypeStruct(*o) for o in outs),
        in_specs=[VMEM] * 7 + [ANY] * len(w_list),
        out_specs=(VMEM,) * 8,
        scratch_shapes=[
            pltpu.VMEM((width, low), BF),
            pltpu.VMEM((keys, rows), F32),
            pltpu.VMEM((q_width, rows), F32),
            pltpu.VMEM((q_width, rows), F32),
            pltpu.VMEM((HD, keys), BF),
            pltpu.VMEM((rows, 2 * HD), BF),
            pltpu.VMEM((rows, 2 * HD), BF),
            pltpu.SemaphoreType.DMA((4,)),
            pltpu.SemaphoreType.DMA,
            pltpu.SemaphoreType.DMA,
        ],
        compiler_params=pltpu.CompilerParams(
            collective_id=ident, has_side_effects=True, vmem_limit_bytes=VMEM_LIMIT
        ),
        cost_estimate=pl.CostEstimate(
            flops=16 * q_width * rows * keys, bytes_accessed=70_000_000, transcendentals=0
        ),
        name="attend_whole",
    )(h, gain, cosine, sines, keys_at[:, None], places[None], length, *w_list)


def attend_whole_back(
    e1, rotated, lse, k_all, kt_all, v_all, w_attn, tables, w_layer, ident, cross
):
    cosine, sines, keys_at, places, length = tables
    q_width, rows = rotated.shape
    keys, width = keys_at.shape[0], e1.shape[1]
    w_list = list(w_attn) if isinstance(w_attn, tuple) else [w_attn]
    crossing_specs = [jax.ShapeDtypeStruct(x.shape, BF) for x in cross]
    return pl.pallas_call(
        functools.partial(attend_whole_back_kernel, w_layer, len(w_list), len(cross)),
        out_shape=(jax.ShapeDtypeStruct((rows, q_width + 2 * HD), BF), *crossing_specs),
        in_specs=[VMEM] * 11 + [ANY] * (len(w_list) + len(cross)),
        out_specs=(VMEM, *[ANY] * len(cross)),
        scratch_shapes=[
            pltpu.VMEM((4, q_width, width // 4), BF),
            pltpu.VMEM((keys, rows), F32),
            pltpu.VMEM((q_width, rows), BF),
            pltpu.VMEM((q_width, rows), F32),
            pltpu.VMEM((keys, HD), F32),
            pltpu.VMEM((keys, HD), F32),
            pltpu.VMEM((rows, 2 * HD), F32),
            pltpu.VMEM((rows, 2 * HD), F32),
            pltpu.SemaphoreType.DMA((4,)),
            pltpu.SemaphoreType.DMA,
            pltpu.SemaphoreType.DMA,
        ]
        + [pltpu.SemaphoreType.DMA] * 2 * len(cross),
        compiler_params=pltpu.CompilerParams(
            collective_id=ident, has_side_effects=True, vmem_limit_bytes=VMEM_LIMIT
        ),
        cost_estimate=pl.CostEstimate(
            flops=40 * q_width * rows * keys, bytes_accessed=90_000_000, transcendentals=0
        ),
        name="attend_whole_back",
    )(
        e1, rotated, lse, k_all, kt_all, v_all, cosine, sines, keys_at[:, None], places[None],
        length, *w_list, *cross,
    )


def line_kernel(
    kind, masked, low, high, deps, gathers, layer, exchange, triples, w_layer, crosses, homing,
    gain_ref, resid_ref, valid_ref, h_ref, square_ref, *rest,
):
    forward = kind in ("out", "mlp")
    wide = kind in ("mlp", "mlp_back")
    if kind == "mlp":
        lhs_refs = []
    elif kind == "mlp_back":
        lhs_refs, rest = rest[:4], rest[4:]
    else:
        lhs_refs, rest = rest[:1], rest[1:]
    w_count = 3 if wide else 1
    w_refs = []
    for triple in triples:
        w_refs.append(rest[: 3 if triple else 1])
        rest = rest[3 if triple else 1 :]
    rest = rest[deps:]
    base_refs, rest = rest[: 2 * gathers], rest[2 * gathers :]
    cross_refs, rest = rest[: len(crosses)], rest[len(crosses) :]
    out_ref, rest = rest[0], rest[1:]
    if kind == "mlp":
        normed_ref, ms_ref, gate_ref, up_ref, hidden_ref = rest[:5]
        rest = rest[5:]
    elif kind == "mlp_back":
        product_refs, rest = rest[:3], rest[3:]
        arrived_refs, rest = rest[:exchange], rest[exchange:]
    block_refs, rest = rest[:gathers], rest[gathers:]
    crossed_refs, rest = rest[: len(crosses)], rest[len(crosses) :]
    if homing:
        home_ref, home_send, home_recv = rest[0], *rest[-2:]
        rest = rest[1:-2]
    if crosses:
        x_send, x_recv = rest[-2:]
        rest = rest[:-2]
    w_alls, rest = rest[:w_count], rest[w_count:]
    (
        part, from_end, from_mid, pair,
        w_sem, up_send, up_recv, mid_send, mid_recv, fin_send, fin_recv,
    ) = rest[:11]
    if gathers:
        far_send, far_recv, near_send, near_recv, cross_send, cross_recv = rest[11:]
    if kind == "mlp_back":
        (
            d_gate_ref, d_up_ref, far_normed, far_dm, far_hidden, far_d_gate, far_d_up, stage,
            give_sem, take_sem, stage_sem,
        ) = rest[11:22]
    if exchange:
        y_stage, y_send, y_recv = rest[22:]
    shard = lax.axis_index("gx")
    far, near = shard ^ 2, shard ^ 1
    section = lax.axis_index("section")
    rows, width = resid_ref.shape
    columns = width // 4
    count = rows // CHUNK
    z = lax.axis_index("gy")
    middle = (z == 1) | (z == 2)
    end_of = jnp.where(z == 1, 0, 3)
    mid_of = jnp.where(z == 0, 1, 2)
    across = 3 - z

    def loading(w, j, cut_of, target, slot):
        whole = w_refs[w]
        copies = [(None, pltpu.make_async_copy(cut_of(whole[0].at[j]), target, w_sem.at[slot]))]
        if triples[w]:
            home = section == w_layer
            copies = [(shard != j, copies[0][1])]
            for ref, holds in zip(whole[1:], (home, jnp.logical_not(home))):
                copy = pltpu.make_async_copy(cut_of(ref), target, w_sem.at[slot])
                copies.append(((shard == j) & holds, copy))
        return copies

    loads, downs = [], []
    if wide:
        hidden_width = w_alls[0].shape[1]
        for x0 in range(0, hidden_width, 512):
            x1 = min(x0 + 512, hidden_width)
            for w in range(2):
                for j in range(4):
                    target = w_alls[w].at[j * columns : (j + 1) * columns, x0:x1]
                    loads.append(loading(w, j, lambda ref: ref.at[:, x0:x1], target, len(loads)))
        for j in range(4):
            downs.append(loading(2, j, lambda ref: ref, w_alls[2].at[j], len(loads) + j))
    else:
        for j in range(4):
            cut_of = lambda ref: ref.at[: ref.shape[0] - GAIN_ROWS, low:high]
            loads.append(loading(0, j, cut_of, w_alls[0].at[j], j))
    for load in downs + loads if kind == "mlp_back" else loads + downs:
        for holds, copy in load:
            if holds is None:
                copy.start()
            else:
                pl.when(holds)(copy.start)
    loads, downs = [x[0][1] for x in loads], [x[0][1] for x in downs]

    barrier = pltpu.get_barrier_semaphore()
    peers = []
    if gathers:
        peers = [{"gx": far}, {"gx": near}, {"section": 1 - section}]
    elif kind == "mlp_back":
        peers = [{"gx": near}] + [{"gx": far}] * (exchange > 0)
    if crosses:
        assert not gathers
        peers.append({"section": 1 - section})
    beside = len(peers)
    for peer in peers:
        pl.semaphore_signal(barrier, inc=1, device_id=peer, device_id_type=MESH)

    @pl.when(middle)
    def _():
        pl.semaphore_signal(barrier, inc=1, device_id={"gy": end_of}, device_id_type=MESH)
        pl.semaphore_signal(barrier, inc=1, device_id={"gy": across}, device_id_type=MESH)
        pl.semaphore_wait(barrier, 2 + beside)

    @pl.when(jnp.logical_not(middle))
    def _():
        pl.semaphore_signal(barrier, inc=1, device_id={"gy": mid_of}, device_id_type=MESH)
        pl.semaphore_wait(barrier, 1 + beside)

    x_peer = {"section": 1 - section}

    def x_copy(k):
        return pltpu.make_async_remote_copy(
            src_ref=cross_refs[k], dst_ref=crossed_refs[k], send_sem=x_send.at[k],
            recv_sem=x_recv.at[k], device_id=x_peer, device_id_type=MESH,
        )

    def home_copy(rows_here):
        return pltpu.make_async_remote_copy(
            src_ref=out_ref.at[rows_here, pl.ds(pl.multiple_of(z * columns, columns), columns)],
            dst_ref=home_ref.at[rows_here, :], send_sem=home_send, recv_sem=home_recv,
            device_id=x_peer, device_id_type=MESH,
        )

    def home_start(i):
        if homing:
            here = pl.ds(pl.multiple_of(i * CHUNK, CHUNK), CHUNK)
            pl.when(section != w_layer)(lambda: home_copy(here).start())

    def x_sends(k):
        return section != crosses[k] if crosses[k] < 2 else section >= 0

    def x_takes(k):
        return section == crosses[k] if crosses[k] < 2 else section >= 0

    for k in range(len(crosses)):
        pl.when(x_sends(k))(lambda k=k: x_copy(k).start())

    def half_of(ref, k, which):
        size = base_refs[2 * k].shape[0] // 2
        return ref.at[pl.ds(pl.multiple_of(which * size, 16), size), :]

    def far_copy(k, source):
        return pltpu.make_async_remote_copy(
            src_ref=half_of(source, k, section),
            dst_ref=half_of(block_refs[k].at[shard], k, section),
            send_sem=far_send.at[k], recv_sem=far_recv.at[k],
            device_id={"gx": far}, device_id_type=MESH,
        )

    def near_copy(k, source):
        return pltpu.make_async_remote_copy(
            src_ref=source, dst_ref=block_refs[k].at[shard], send_sem=near_send.at[3 * k],
            recv_sem=near_recv.at[3 * k], device_id={"gx": near}, device_id_type=MESH,
        )

    def cross_copy(k):
        rows_here = half_of(block_refs[k].at[far], k, section)
        return pltpu.make_async_remote_copy(
            src_ref=rows_here, dst_ref=rows_here, send_sem=cross_send.at[k],
            recv_sem=cross_recv.at[k], device_id=x_peer, device_id_type=MESH,
        )

    def pass_copy(k, late):
        rows_here = half_of(block_refs[k].at[far], k, 1 - section if late else section)
        return pltpu.make_async_remote_copy(
            src_ref=rows_here, dst_ref=rows_here, send_sem=near_send.at[3 * k + 1 + late],
            recv_sem=near_recv.at[3 * k + 1 + late], device_id={"gx": near}, device_id_type=MESH,
        )

    at_home = section == layer

    def from_base(k, starts):
        for ref, holds in zip(base_refs[2 * k : 2 * k + 2], (at_home, jnp.logical_not(at_home))):

            @pl.when(holds)
            def _():
                for make in starts:
                    make(k, ref).start()

    def gather_middle(k):
        far_copy(k, base_refs[2 * k]).wait_recv()
        cross_copy(k).start()
        pass_copy(k, 0).start()

    def gather_late(k):
        cross_copy(k).wait_recv()
        pass_copy(k, 1).start()

    if gathers:
        from_base(0, [far_copy])
    for k in range(gathers):
        from_base(k, [near_copy])

    half = rows // STEPS
    core = lax.rem(shard, 2)

    def give(slot, source, target):
        return pltpu.make_async_remote_copy(
            src_ref=source, dst_ref=target, send_sem=give_sem.at[slot],
            recv_sem=take_sem.at[slot], device_id={"gx": near}, device_id_type=MESH,
        )

    def chip_columns(ref, y, of):
        return ref.at[:, pl.ds(pl.multiple_of((2 * y + of) * columns, columns), columns)]

    def step_rows(ref, step):
        return ref.at[pl.ds(pl.multiple_of(step * half, half), half), :]

    if kind == "mlp_back":
        saved_gate, saved_up, saved_normed, saved_hidden = lhs_refs
        early = [give(0, saved_hidden, far_hidden)]
        for y in range(2):
            early.append(give(1 + y, chip_columns(resid_ref, y, 1 - core), far_dm.at[y]))
        for y in range(2):
            early.append(give(3 + y, chip_columns(saved_normed, y, 1 - core), far_normed.at[y]))
        for copy in early:
            copy.start()

    def give_step(step):
        return [
            give(5 + step, step_rows(d_gate_ref, step), step_rows(far_d_gate, step)),
            give(5 + STEPS + step, step_rows(d_up_ref, step), step_rows(far_d_up, step)),
        ]

    if not wide:
        for load in loads:
            load.wait()

    def at_first(step, copies):
        @pl.when(step == 0)
        def _():
            for copy in copies:
                copy.wait()

    def rows_at(ref, i):
        return ref.at[pl.ds(pl.multiple_of(i * CHUNK, CHUNK), CHUNK), :]

    def up_copy(i):
        return pltpu.make_async_remote_copy(
            src_ref=rows_at(part, i), dst_ref=rows_at(from_end, i), send_sem=up_send.at[i],
            recv_sem=up_recv.at[i], device_id={"gy": mid_of}, device_id_type=MESH,
        )

    def mid_copy(i):
        return pltpu.make_async_remote_copy(
            src_ref=rows_at(pair, i), dst_ref=rows_at(from_mid, i), send_sem=mid_send.at[i],
            recv_sem=mid_recv.at[i], device_id={"gy": across}, device_id_type=MESH,
        )

    def fin_copy(i):
        return pltpu.make_async_remote_copy(
            src_ref=rows_at(out_ref, i), dst_ref=rows_at(out_ref, i), send_sem=fin_send.at[i],
            recv_sem=fin_recv.at[i], device_id={"gy": end_of}, device_id_type=MESH,
        )

    def dot(left, right, transposed=False):
        dims = (((1,), (1 if transposed else 0,)), ((), ()))
        return lax.dot_general(left, right, dims, preferred_element_type=F32)

    def spans(extent):
        return [(x, min(x + 512, extent)) for x in range(0, extent, 512)]

    if wide:
        w_gate, w_up, w_down = w_alls

    def product(step, carry):
        here = pl.ds(pl.multiple_of(step * half, half), half)
        if kind == "mlp":
            values = resid_ref[here, :].astype(F32)
            square = jnp.mean(values * values, axis=1, keepdims=True)
            ms_ref[here, :] = square
            normed_ref[here, :] = (values * lax.rsqrt(square + EPS) * gain_ref[...]).astype(BF)
            for n, (x0, x1) in enumerate(spans(w_gate.shape[1])):
                at_first(step, loads[8 * n : 8 * n + 8])
                gate = dot(normed_ref[here, :], w_gate[:, x0:x1])
                up = dot(normed_ref[here, :], w_up[:, x0:x1])
                gate_ref[here, x0:x1] = gate.astype(BF)
                up_ref[here, x0:x1] = up.astype(BF)
                hidden_ref[here, x0:x1] = (gate * jax.nn.sigmoid(gate) * up).astype(BF)
        if kind == "mlp_back":
            at_first(step, downs)
            for x0, x1 in spans(w_gate.shape[1]):
                d_hidden = sum(
                    dot(resid_ref[here, j * columns : (j + 1) * columns], w_down[j, x0:x1, :], True)
                    for j in range(4)
                )
                gate = saved_gate[here, x0:x1].astype(F32)
                up = saved_up[here, x0:x1].astype(F32)
                sigmoid = jax.nn.sigmoid(gate)
                d_up_ref[here, x0:x1] = (d_hidden * (gate * sigmoid)).astype(BF)
                d_gate_ref[here, x0:x1] = (
                    d_hidden * up * sigmoid * (1.0 + gate * (1.0 - sigmoid))
                ).astype(BF)
            for copy in give_step(step):
                copy.start()
        if wide:
            at_first(step, downs if kind == "mlp" else loads)
        for j in range(4):
            span = slice(j * columns, (j + 1) * columns)
            if kind == "out":
                value = dot(lhs_refs[0][here, :], w_alls[0][j])
            elif kind == "mlp":
                value = dot(hidden_ref[here, :], w_down[j])
            elif kind == "mlp_back":
                value = dot(d_gate_ref[here, :], w_gate[span, :], True)
                value += dot(d_up_ref[here, :], w_up[span, :], True)
            else:
                value = dot(lhs_refs[0][here, :], w_alls[0][j], True)
            part[here, span] = value.astype(BF)

        @pl.when(jnp.logical_not(middle))
        def _():
            def send(i, inner):
                up_copy(step * (count // STEPS) + i).start()
                return inner

            lax.fori_loop(0, count // STEPS, send, 0)

        return carry

    lax.fori_loop(0, STEPS, product, 0)

    def finish(i):
        mid_copy(i).wait_recv()
        here = pl.ds(pl.multiple_of(i * CHUNK, CHUNK), CHUNK)
        total = pair[here, :].astype(F32) + from_mid[here, :].astype(F32)
        resid = resid_ref[here, :].astype(F32)
        if forward:
            result = resid + total
            if masked:
                result = result * valid_ref[here, :]
        else:
            values = h_ref[here, :].astype(F32)
            scaled = total * gain_ref[...]
            ratio = lax.rsqrt(square_ref[here, :] + EPS)
            mean_term = jnp.sum(scaled * values, axis=1, keepdims=True) * (1.0 / width)
            result = resid + ratio * scaled - values * (ratio * ratio * ratio) * mean_term
        out_ref[here, :] = result.astype(BF)
        fin_copy(i).start()
        home_start(i)

    tile = columns // 2

    def tile_rows(sub):
        return pl.ds(pl.multiple_of(sub % 2 * tile, tile), tile)

    def stage_copy(number, sub, slot):
        target = product_refs[number].at[sub // 2, tile_rows(sub), :]
        return pltpu.make_async_copy(stage.at[slot], target, stage_sem.at[slot])

    def y_copy(number, sub, slot):
        return pltpu.make_async_remote_copy(
            src_ref=y_stage.at[2 * number + slot], dst_ref=arrived_refs[number].at[tile_rows(sub), :],
            send_sem=y_send.at[2 * number + slot], recv_sem=y_recv.at[2 * number + slot],
            device_id={"gx": far}, device_id_type=MESH,
        )

    def gradient_tile(number, sub):
        slot = sub % 2
        left, far_left, right, far_right = (
            (resid_ref, far_dm, saved_hidden, far_hidden),
            (saved_normed, far_normed, d_gate_ref, far_d_gate),
            (saved_normed, far_normed, d_up_ref, far_d_up),
        )[number]

        @pl.when(sub == 0)
        def _():
            waits = [early[:3], early[3:] + give_all[:STEPS], give_all[STEPS:]][number]
            for copy in waits:
                copy.wait_recv()

        if number >= exchange:

            @pl.when((sub >= 2) | (number > 0))
            def _():
                stage_copy(number, sub, slot).wait()

        elif number > 0:

            @pl.when(sub >= 2)
            def _():
                stage_copy(number, sub - 2, slot).wait()

        y = sub // 2
        if number < exchange:
            y = jnp.where(sub < 2, 1 - lax.div(shard, 2), lax.div(shard, 2))
        start = (y * 2 + core) * columns + sub % 2 * tile
        mine = left[:, pl.ds(pl.multiple_of(start, tile), tile)]
        theirs = far_left[y, :, tile_rows(sub)]
        value = dot_to(mine, right[...], ((0,), (0,))) + dot_to(theirs, far_right[...], ((0,), (0,)))
        if number < exchange:

            @pl.when(sub < 2)
            def _():
                y_stage[2 * number + slot] = value.astype(BF)
                y_copy(number, sub, slot).start()

            @pl.when(sub >= 2)
            def _():
                stage[slot] = value.astype(BF)
                stage_copy(number, sub - 2, slot).start()

        else:
            stage[slot] = value.astype(BF)
            stage_copy(number, sub, slot).start()

    if kind == "mlp_back":
        give_all = [x for pair in zip(*(give_step(n) for n in range(STEPS))) for x in pair]

    def beside_step(i):
        pass_on(i)
        if kind == "mlp_back":
            for number in range(3):
                first = 3 + 4 * number

                @pl.when((i >= first) & (i < first + 4))
                def _():
                    gradient_tile(number, i - first)

    def pass_on(i):
        if gathers == 2:
            at(2, i, lambda: from_base(1, [far_copy]))
            at(6, i, lambda: gather_middle(0))
            at(10, i, lambda: gather_middle(1))
            at(11, i, lambda: gather_late(0))
            at(15, i, lambda: gather_late(1))

    def at(sixteenth, i, action):
        pl.when(i == count * sixteenth // 16)(action)

    @pl.when(middle)
    def _():
        def step(i, carry):
            up_copy(i).wait_recv()
            here = pl.ds(pl.multiple_of(i * CHUNK, CHUNK), CHUNK)
            pair[here, :] = (part[here, :].astype(F32) + from_end[here, :].astype(F32)).astype(BF)
            mid_copy(i).start()

            @pl.when(i >= 1)
            def _():
                finish(i - 1)

            beside_step(i)
            return carry

        lax.fori_loop(0, count, step, 0)
        finish(count - 1)

        def drain(i, carry):
            mid_copy(i).wait_send()
            fin_copy(i).wait_send()
            return carry

        lax.fori_loop(0, count, drain, 0)

    @pl.when(jnp.logical_not(middle))
    def _():
        def drain(i, carry):
            up_copy(i).wait_send()
            fin_copy(i).wait_recv()
            home_start(i)
            beside_step(i)
            return carry

        lax.fori_loop(0, count, drain, 0)

    if kind == "mlp_back":
        for slot in range(2):
            stage_copy(2, 2 + slot, slot).wait()
        for copy in early + give_all:
            copy.wait_send()
        for number in range(exchange):
            for slot in range(2):
                y_copy(number, slot, slot).wait()
    if homing:
        every = pl.ds(0, rows)
        pl.when(section != w_layer)(lambda: home_copy(every).wait_send())
        pl.when(section == w_layer)(lambda: home_copy(every).wait_recv())
    for k in range(len(crosses)):
        pl.when(x_sends(k))(lambda k=k: x_copy(k).wait_send())
        pl.when(x_takes(k))(lambda k=k: x_copy(k).wait_recv())
    for k in range(gathers):
        far_copy(k, base_refs[2 * k]).wait_send()
        near_copy(k, base_refs[2 * k]).wait()
        cross_copy(k).wait_send()
        pass_copy(k, 0).wait()
        pass_copy(k, 1).wait()


def line_sum(kind, ident, resid, weights, lhs=(), gain=None, valid=None, back=None, low=0, high=0, deps=(), bases=(), layer=0, exchange=0, w_layer=0, crosses=(), homing=False):
    rows, width = resid.shape
    one = jnp.ones((rows, 1), F32)
    h, square = back if back is not None else (jnp.zeros((16, 128), BF), jnp.zeros((8, 1), F32))
    gain = jnp.zeros((1, width), F32) if gain is None else gain
    wide = kind in ("mlp", "mlp_back")
    hidden = 0
    if wide:
        hidden = (weights[2][0] if isinstance(weights[2], tuple) else weights[2]).shape[1]
    w_scratch = []
    triples = [isinstance(w, tuple) for w in weights]
    w_flat = [x for w in weights for x in (w if isinstance(w, tuple) else (w,))]
    for i, w in enumerate(weights):
        _, depth, across = (w[0] if isinstance(w, tuple) else w).shape
        if wide and i < 2:
            w_scratch.append(pltpu.VMEM((width, across), BF))
        else:
            shape = (4, depth, across) if wide else (4, depth - GAIN_ROWS, high - low)
            w_scratch.append(pltpu.VMEM(shape, BF))
    outs, products, beside = [((rows, width), BF)], [], []
    if kind == "mlp":
        outs += [((rows, width), BF), ((rows, 1), F32)] + [((rows, hidden), BF)] * 3
    elif kind == "mlp_back":
        products = [((1 if n < exchange else 2, width // 4, hidden), BF) for n in range(3)]
        products += [((width // 4, hidden), BF)] * exchange
        half_block = pltpu.VMEM((2, rows, width // 4), BF)
        beside = [pltpu.VMEM((rows, hidden), BF)] * 2 + [half_block] * 2
        beside += [pltpu.VMEM((rows, hidden), BF)] * 3 + [pltpu.VMEM((2, width // 8, hidden), BF)]
        beside += [pltpu.SemaphoreType.DMA((n,)) for n in (5 + 2 * STEPS, 5 + 2 * STEPS, 2)]
        if exchange:
            beside += [pltpu.VMEM((2 * exchange, width // 8, hidden), BF)]
            beside += [pltpu.SemaphoreType.DMA((2 * exchange,))] * 2
    blocks = [((4,) + base[0].shape, BF) for base in bases]
    pairs = [x for base in bases for x in base]
    crossed = [(x[0].shape, BF) for x in crosses] + [((rows, width // 4), BF)] * homing
    depth = 3 * hidden if wide else lhs[0].shape[1]
    count = rows // CHUNK
    dma = pltpu.SemaphoreType.DMA
    return pl.pallas_call(
        functools.partial(
            line_kernel, kind, valid is not None, low, high, len(deps), len(bases), layer, exchange,
            triples, w_layer, [x[1] for x in crosses], homing,
        ),
        out_shape=tuple(jax.ShapeDtypeStruct(*o) for o in outs + products + blocks + crossed),
        in_specs=[VMEM] * (5 + len(lhs)) + [ANY] * (len(w_flat) + len(deps) + len(pairs) + len(crosses)),
        out_specs=tuple([VMEM] * len(outs) + [ANY] * len(products + blocks + crossed)),
        scratch_shapes=w_scratch
        + [pltpu.VMEM((rows, width), BF)] * 4
        + [dma((8 * -(-hidden // 512) + 4,))]
        + [dma((count,))] * 6
        + [dma((n * len(bases),)) for n in (1, 1, 3, 3, 1, 1) if bases]
        + beside
        + [dma((len(crosses),))] * 2 * bool(crosses)
        + [dma] * 2 * homing,
        compiler_params=pltpu.CompilerParams(
            collective_id=ident, has_side_effects=True, vmem_limit_bytes=VMEM_LIMIT
        ),
        cost_estimate=pl.CostEstimate(
            flops=2 * rows * depth * width, bytes_accessed=200 * 1024 * 1024, transcendentals=0
        ),
        name="line_" + kind,
    )(
        gain, resid, one if valid is None else valid, h, square, *lhs, *w_flat, *deps, *pairs,
        *(x[0] for x in crosses),
    )


def plain_sum(total):
    return lax.psum(total.astype(BF), "gy").astype(F32)


def normed(h, gain):
    values = h.astype(F32)
    square = jnp.mean(values * values, axis=1, keepdims=True)
    return square, (values * lax.rsqrt(square + EPS) * gain).astype(BF)


def norm_back(d_normed, h, square, gain):
    values = h.astype(F32)
    ratio = lax.rsqrt(square + EPS)
    scaled = d_normed * gain
    mean_term = jnp.mean(scaled * values, axis=1, keepdims=True)
    return ratio * scaled - values * (ratio * ratio * ratio) * mean_term


def attention_forward(h, gain, w_attn, low, tables, ident, bases, layer, w_layer, deps=()):
    rows, width = h.shape
    high = low + width // lax.axis_size("gx")
    q_width = low - 2 * HD
    if fused():
        heads, n1, square, rotated, lse, k_all, kt_all, v_all = attend_whole(
            h, gain, w_attn, low, tables, w_layer, ident + 8
        )
        h1, *stacks = line_sum(
            "out", ident, h, [w_attn], (heads,), low=low, high=high,
            deps=deps, bases=bases, layer=layer, w_layer=w_layer,
        )
        blocks = [(x, *pair) for x, pair in zip(stacks, bases)]
    else:
        cosine, sines = tables[:2]
        square, n1 = normed(h, gain)
        q_down = mm(tall(cut(w_attn, 0, q_width)), n1, ((0,), (1,)))
        kv = mm(n1, tall(cut(w_attn, q_width, low)))
        k_rot = rope_down(kv[:, :HD].T, cosine, sines).T.astype(BF)
        kv = jnp.concatenate([k_rot, kv[:, HD:].astype(BF)], axis=1)
        kv_all = jnp.concatenate([kv, swap_pairs(kv, "gx")], axis=0)
        k_all, v_all = kv_all[:, :HD], kv_all[:, HD:]
        kt_all = k_all.T
        heads, rotated, lse = attend(q_down, k_all, v_all, tables)
        h1 = (h.astype(F32) + plain_sum(mm(heads, side(cut(w_attn, low, high))))).astype(BF)
        blocks = [gather_blocks(chosen(x, layer)) for x in bases]
    return h1, square, blocks, (h, square, n1, rotated, lse, k_all, kt_all, v_all, heads)


def mlp_forward(h1, gain, weights, valid, ident, bases=(), layer=0, w_layer=0):
    if fused():
        result, n2, square, gate, up, hidden, *stacks = line_sum(
            "mlp", ident, h1, weights, gain=gain, valid=valid, bases=bases, layer=layer,
            w_layer=w_layer,
        )
        blocks = [(x, *pair) for x, pair in zip(stacks, bases)]
    else:
        square, n2 = normed(h1, gain)
        gate = mm(n2, tall(weights[0]))
        up = mm(n2, tall(weights[1]))
        hidden = (gate * jax.nn.sigmoid(gate) * up).astype(BF)
        gate, up = gate.astype(BF), up.astype(BF)
        result = h1.astype(F32) + plain_sum(mm(hidden, side(weights[2])))
        result = (result * valid).astype(BF)
        blocks = [gather_blocks(chosen(x, layer)) for x in bases]
    return result, square, blocks, (h1, square, n2, gate, up, hidden)


def mlp_backward(dm, gain, weights, saved, ident, w_layer, crosses=(), deps=(), exchange=1):
    h1, square, n2, gate, up, hidden = saved
    if fused():
        e1, *products = line_sum(
            "mlp_back", ident, dm, weights, (gate, up, n2, hidden), gain=gain,
            back=(h1, square), exchange=exchange, w_layer=w_layer, crosses=crosses, deps=deps,
        )
        return e1, products[:4], products[4:]
    gate, up = gate.astype(F32), up.astype(F32)
    d_hidden = mm(dm, side(weights[2]), ((1,), (1,)))
    sigmoid = jax.nn.sigmoid(gate)
    d_gate = (d_hidden * up * sigmoid * (1.0 + gate * (1.0 - sigmoid))).astype(BF)
    d_up = (d_hidden * (gate * sigmoid)).astype(BF)
    total = mm(d_gate, tall(weights[0]), ((1,), (1,))) + mm(d_up, tall(weights[1]), ((1,), (1,)))
    e1 = (dm.astype(F32) + norm_back(plain_sum(total), h1, square, gain)).astype(BF)
    turn = ((0,), (0,))
    products = [mm(dm, hidden, turn), mm(n2, d_gate, turn), mm(n2, d_up, turn)]
    return e1, [p.astype(BF) for p in products], crossing(crosses)


def crossing(crosses):
    pairs = ([(1, 0)], [(0, 1)], [(0, 1), (1, 0)])
    return [lax.ppermute(x, "section", pairs[way]) for x, way in crosses]


def mlp_sums(products):
    if not fused():
        return [shard_sum(p) for p in products]
    down, gate, up, arrived = products
    first = (down[0].astype(F32) + arrived.astype(F32)).astype(BF)
    return [first, chip_sum(gate), chip_sum(up)]


def attention_backward(e1, w_attn, low, tables, saved, w_layer, ident, cross=()):
    h, square, n1, rotated, lse, k_all, kt_all, v_all, heads = saved
    rows, width = h.shape
    if fused():
        d_qkv, *crossed = attend_whole_back(
            e1, rotated, lse, k_all, kt_all, v_all, w_attn, tables, w_layer, ident, cross
        )
    else:
        cosine, sines = tables[:2]
        w_o = side(cut(w_attn, low, low + width // lax.axis_size("gx")))
        d_down = mm(w_o, e1, ((1,), (1,))).astype(BF)
        dq, dk, dv = attend_back(rotated, k_all, v_all, d_down, lse, tables)
        dkv = jnp.concatenate([dk, dv], axis=1)
        dkv = dkv[:rows] + swap_pairs(dkv[rows:], "gx")
        dk = rope_down(dkv[:, :HD].T, cosine, -sines).T
        d_qkv = jnp.concatenate([dq, dk.astype(BF), dkv[:, HD:].astype(BF)], axis=1)
        crossed = crossing([(x, w_layer) for x in cross])
    turn = ((0,), (0,))
    products = [mm(n1, d_qkv, turn).astype(BF), mm(e1, heads, turn).astype(BF)]
    return d_qkv, jnp.concatenate(products, axis=1), crossed


def attention_end(d_qkv, e1, w_attn, gain, saved, ident, w_layer, deps, crosses):
    h, square = saved[:2]
    qkv_width = d_qkv.shape[1]
    if fused():
        grad, *crossed = line_sum(
            "back", ident, e1, [w_attn], (d_qkv,), gain=gain, back=(h, square),
            low=0, high=qkv_width, deps=deps, crosses=crosses, w_layer=w_layer, homing=True,
        )
        return grad, crossed[-1], crossed[:-1]
    total = plain_sum(mm(d_qkv, tall(cut(w_attn, 0, qkv_width)), ((1,), (1,))))
    grad = (e1.astype(F32) + norm_back(total, h, square, gain)).astype(BF)
    width = grad.shape[1] // lax.axis_size("gy")
    part = lax.dynamic_slice_in_dim(grad, lax.axis_index("gy") * width, width, 1)
    home, *crossed = crossing([(part, w_layer), *crosses])
    return grad, home, crossed


def on_device(
    hidden_in, out_grad, lengths, dealing, attn_gain, w_query, w_key, w_value, w_out,
    mlp_gain, w_gate, w_up, w_down,
):
    shards = lax.axis_size("gx")
    shard = lax.axis_index("gx")
    section = lax.axis_index("section")
    column = lax.axis_index("gy")
    core = shard % 2
    sequence = (shard // 2) * 2 + section
    span, width = hidden_in.shape
    half = span // 2
    seq_length = lax.dynamic_index_in_dim(lengths, sequence, keepdims=False)

    both = jnp.concatenate([hidden_in, out_grad], axis=1)
    mine = core_rows(both, core)
    theirs = swap_pairs(core_rows(both, 1 - core), "gx")
    mine = jnp.where(core == section, mine, theirs)
    h = lax.all_gather(mine[:, :width], "gy", axis=1, tiled=True)

    kv_head = column * (w_query.shape[2] // HD) // (QH // KVH)
    low = w_query.shape[2] + 2 * HD
    both_gains = jnp.stack([attn_gain[0], mlp_gain[0]])
    block_rows = both_gains.shape[1]
    attn_own = jnp.concatenate(
        [
            w_query[0],
            lax.dynamic_slice_in_dim(w_key[0], kv_head * HD, HD, 1),
            lax.dynamic_slice_in_dim(w_value[0], kv_head * HD, HD, 1),
            w_out[0],
        ],
        axis=1,
    )
    gain_rows = jnp.pad(both_gains, ((0, GAIN_ROWS - 2), (0, attn_own.shape[1] - block_rows)))
    attn_own = jnp.concatenate([attn_own, gain_rows + theirs[:1, :1] * 0], axis=0)
    own = (attn_own, w_gate[0], w_up[0], w_down[0])
    first = second = [(array, swap_pairs(array, "section")) for array in own]

    def gains_of(w_attn, pair):
        cut_of = lambda w: w[..., block_rows : block_rows + 2, :block_rows]
        rows = cut_of(w_attn[0] if isinstance(w_attn, tuple) else w_attn)
        if isinstance(w_attn, tuple):
            rows = with_own(rows, [cut_of(x) for x in pair], 1)
        return rows.transpose(1, 0, 2).reshape(2, 1, -1).astype(F32)

    here = core_rows(jnp.arange(span), core)
    there = core_rows(jnp.arange(span), 1 - core)
    keys_at = jnp.concatenate([here, there])
    valid = (here < seq_length)[:, None].astype(F32)
    tables = (*rope_tables(here), keys_at, here, seq_length.reshape(1, 1))

    attn0 = gather_blocks(chosen(first[0], 0) + h[:1, :1] * 0)
    gate0 = gather_blocks(chosen(first[1], 0))
    gains0 = gains_of(attn0, first[0])
    h1, square_a, blocks, saved_a0 = attention_forward(
        h, gains0[0], attn0, low, tables, 0, first[2:], 0, 0, (gate0,)
    )
    mlp0 = [gate0] + blocks
    h, square_m, (attn1, gate1), saved_m0 = mlp_forward(
        h1, gains0[1], mlp0, valid, 1, second[:2], 1
    )
    gains1 = gains_of(attn1, second[0])
    outputs, squares = [h], [square_a, square_m]
    d_mine = mine[:, width:] + h[:1, :1] * 0
    d_out = lax.all_gather(d_mine, "gy", axis=1, tiled=True)
    h1, square_a, blocks, saved_a1 = attention_forward(
        h, gains1[0], attn1, low, tables, 2, second[2:], 1, 1
    )
    mlp1 = [gate1] + blocks
    h, square_m, _, saved_m1 = mlp_forward(h1, gains1[1], mlp1, valid, 3, w_layer=1)
    outputs.append(h)
    squares = jnp.concatenate(squares + [square_a, square_m], axis=1)
    rms = (jnp.sqrt(squares + EPS) * valid).T
    statistics = [rms[:2], rms[2:]]
    outputs = [lax.dynamic_slice_in_dim(x, column * width, width, 1) for x in outputs]

    dm = (d_out.astype(F32) * valid).astype(BF)
    e1, products, _ = mlp_backward(dm, gains1[1], mlp1, saved_m1, 4, 1)
    local1 = mlp_sums(products)

    both = []
    for output, stat in zip(outputs, statistics):
        high = stat.astype(BF)
        rest = (stat - high.astype(F32)).astype(BF)
        parts = jnp.concatenate([high, rest], axis=0).reshape(-1, width)
        parts = jnp.pad(parts, ((0, -parts.shape[0] % 16), (0, 0)))
        both.append(jnp.concatenate([output + e1[:1, :1] * 0, parts], axis=0))
    kept = jnp.where(section == 0, both[0], both[1])
    sent = jnp.where(section == 0, both[1], both[0])

    d_qkv, products, _ = attention_backward(e1, attn1, low, tables, saved_a1, 1, 9)
    local1.append(shard_sum(products))
    crosses = [(sent, 2), (local1[0], 1)]
    grad1, home1, (sent, down1) = attention_end(
        d_qkv, e1, attn1, gains1[0], saved_a1, 5, 1, (products,), crosses
    )
    by_section = jnp.stack([jnp.where(section == 0, kept, sent), jnp.where(section == 0, sent, kept)])
    everything = lax.all_gather(by_section, "gx", axis=0)
    owner = jnp.sum(jnp.where(dealing == shard, jnp.arange(shards), 0))
    halves = lax.dynamic_slice(
        everything, ((owner // 2) * 2, owner % 2, 0, 0), (2, 1) + everything.shape[2:]
    )[:, 0]
    layer_out = join_halves(halves[0, :half], halves[1, :half])
    stat_rows = 4 * half // width
    parts = halves[:, half : half + stat_rows].astype(F32).reshape(2, 4, half)
    stat_halves = parts[:, :2] + parts[:, 2:]
    stats_out = join_halves(stat_halves[0].T, stat_halves[1].T).T

    dm = (grad1.astype(F32) * valid).astype(BF)
    crosses = [(local1[1], 1), (local1[2], 1)]
    e1, products, (gate1, up1) = mlp_backward(dm, gains0[1], mlp0, saved_m0, 6, 0, crosses)
    local0 = mlp_sums(products)
    d_qkv, products, (down0,) = attention_backward(
        e1, attn0, low, tables, saved_a0, 0, 11, local0[:1]
    )
    local0.append(shard_sum(products))
    crosses = [(local1[3], 1), (local0[1], 0)]
    grad0, home0, (attn_sum1, gate0) = attention_end(
        d_qkv, e1, attn0, gains0[0], saved_a0, 7, 0, (products, everything), crosses
    )

    input_grads = [lax.dynamic_slice_in_dim(x, column * width, width, 1) for x in (grad0, grad1)]
    local0[2] = local0[2] + grad0[:1, :1] * 0
    received0 = [down0, gate0] + crossing([(x, 0) for x in local0[2:]])
    received1 = [down1, gate1, up1, attn_sum1]
    totals = [
        jnp.where(section == 0, a0.astype(F32) + r0.astype(F32), a1.astype(F32) + r1.astype(F32))
        for a0, r0, a1, r1 in zip(local0, received0, local1, received1)
    ]
    s_down, s_gate, s_up, s_attn = totals
    s_out = s_attn[:, low:]
    q_width = w_query.shape[2]

    attn_sum = jnp.sum(s_attn[:, :low] * attn_own[:block_rows, :low].astype(F32), axis=1)
    mlp_sum = jnp.sum(s_gate * w_gate[0].astype(F32) + s_up * w_up[0].astype(F32), axis=1)
    sums = jnp.pad(jnp.stack([attn_sum, mlp_sum], axis=1), ((0, 0), (0, 126)))
    spread = jnp.concatenate([s_attn[:, q_width:low], sums], axis=1).astype(BF)
    spread = lax.all_gather(spread, "gy", axis=0).astype(F32)
    gains = jnp.sum(spread[:, :, 2 * HD : 2 * HD + 2], axis=0).T / both_gains.astype(F32)
    kv_sum = spread[:, :, : 2 * HD].reshape(KVH, -1, *spread.shape[1:2], 2, HD).sum(axis=1)
    kv_sum = kv_sum.transpose(2, 1, 0, 3).reshape(2, spread.shape[1], KVH * HD)

    kept = jnp.where(section == 0, input_grads[0], input_grads[1])
    sent = jnp.where(section == 0, home0, home1)
    keep = jnp.where(core == section, kept, sent)
    give = swap_pairs(jnp.where(core == section, sent, kept), "gx")
    back_home = join_halves(jnp.where(core == 0, keep, give), jnp.where(core == 0, give, keep))
    return (
        layer_out[None],
        stats_out[None],
        back_home[None],
        gains[None, 0],
        s_attn[None, :, :q_width],
        kv_sum[None, 0],
        kv_sum[None, 1],
        s_out.T[None],
        gains[None, 1],
        s_gate[None],
        s_up[None],
        s_down.T[None],
    )


def solution(mesh):
    rows_cols = P("section", "gx", "gy")
    cols_rows = P("section", "gy", "gx")
    rows_only = P("section", "gx", None)
    gain = P("section", "gx")
    return jax.shard_map(
        on_device,
        mesh=mesh,
        in_specs=(
            P("gx", "gy"), P("gx", "gy"), P(), P(), gain, rows_cols, rows_only, rows_only,
            cols_rows, gain, rows_cols, rows_cols, cols_rows,
        ),
        out_specs=(
            rows_cols, P("section", None, "gx"), rows_cols, gain, rows_cols, rows_only, rows_only,
            cols_rows, gain, rows_cols, rows_cols, cols_rows,
        ),
        check_vma=False,
    )
```

```python
import functools

import jax
import jax.numpy as jnp
from jax import lax
from jax.experimental import pallas as pl
from jax.experimental.pallas import tpu as pltpu
from jax.sharding import PartitionSpec as P

QH = 32
KVH = 4
HD = 64
LAYERS = 2
EPS = 1e-05
BF = jnp.bfloat16
F32 = jnp.float32
MESH = pl.DeviceIdType.MESH
CHUNK = 32
STEPS = 2
GAIN_ROWS = 32
VMEM_LIMIT = 56 * 1024 * 1024
ANY = pl.BlockSpec(memory_space=pl.ANY)
VMEM = pl.BlockSpec(memory_space=pltpu.VMEM)


def mm(left, right, dims=((1,), (0,))):
    return lax.dot_general(left, right, (dims, ((), ())), preferred_element_type=F32)


def swap_pairs(values, axis, by=1):
    count = lax.axis_size(axis)
    return lax.ppermute(values, axis, [(i, i ^ by) for i in range(count)])


def rope_tables(places):
    half_width = HD // 2
    frequency = jnp.power(10000.0, -2.0 * jnp.arange(half_width).astype(F32) / HD)
    angles = frequency[:, None] * places.astype(F32)[None, :]
    return jnp.cos(angles), jnp.sin(angles)


def core_rows(rows, core):
    quarter = rows.shape[0] // 4
    low = lax.dynamic_slice_in_dim(rows, core * quarter, quarter, 0)
    high = lax.dynamic_slice_in_dim(rows, (3 - core) * quarter, quarter, 0)
    return jnp.concatenate([low, high], axis=0)


def join_halves(first, second):
    quarter = first.shape[0] // 2
    return jnp.concatenate(
        [first[:quarter], second[:quarter], second[quarter:], first[quarter:]], axis=0
    )


def chip_groups():
    return [[0, 2], [1, 3]]


def gather_blocks(base):
    return lax.all_gather(base, "gx", axis=0)


def chosen(pair, layer):
    return jnp.where(lax.axis_index("section") == layer, *pair)


def with_own(stack, pair, layer):
    shard = lax.axis_index("gx")
    return lax.dynamic_update_index_in_dim(stack, chosen(pair, layer), shard, 0)


def fused():
    return lax.axis_size("gx") == 4 and lax.axis_size("gy") == 4


def tall(w):
    return w.reshape(-1, w.shape[-1])


def side(w):
    return jnp.concatenate([w[i] for i in range(w.shape[0])], axis=1)


def cut(w, low, high):
    return w[:, :-GAIN_ROWS, low:high]


def shard_sum(product):
    return lax.psum_scatter(product, "gx", scatter_dimension=0, tiled=True)


def chip_sum(product):
    product = product.reshape(-1, product.shape[-1])
    return lax.psum_scatter(
        product, "gx", scatter_dimension=0, tiled=True, axis_index_groups=[[0, 2], [1, 3]]
    )


def line_gather_kernel(mine_ref, out_ref, right_send, right_recv, left_send, left_recv):
    z = lax.axis_index("gy")
    rows, columns = mine_ref.shape
    half = rows // 2
    barrier = pltpu.get_barrier_semaphore()
    for near, there in ((z - 1, z > 0), (z + 1, z < 3)):

        @pl.when(there)
        def _():
            pl.semaphore_signal(barrier, inc=1, device_id={"gy": near}, device_id_type=MESH)

    inner = (z > 0) & (z < 3)
    pl.when(inner)(lambda: pl.semaphore_wait(barrier, 2))
    pl.when(jnp.logical_not(inner))(lambda: pl.semaphore_wait(barrier, 1))

    def block(of):
        of = jnp.clip(of, 0, 3)
        return pl.ds(pl.multiple_of(of * columns, columns), columns)

    out_ref[:, block(z)] = mine_ref[...]

    def copy(step, p, right):
        here = out_ref.at[p * half : (p + 1) * half, block(z - step if right else z + step)]
        send, recv = (right_send, right_recv) if right else (left_send, left_recv)
        return pltpu.make_async_remote_copy(
            src_ref=here, dst_ref=here, send_sem=send.at[2 * step + p],
            recv_sem=recv.at[2 * step + p], device_id={"gy": z + 1 if right else z - 1},
            device_id_type=MESH,
        )

    right_at = [(z < 3) & (z >= step) for step in range(3)]
    left_at = [(z > 0) & (z <= 3 - step) for step in range(3)]
    for step in range(4):
        for p in range(2):
            if step > 0:
                pl.when(z >= step)(lambda: copy(step - 1, p, True).wait_recv())
                pl.when(z <= 3 - step)(lambda: copy(step - 1, p, False).wait_recv())
            if step < 3:
                pl.when(right_at[step])(lambda: copy(step, p, True).start())
                pl.when(left_at[step])(lambda: copy(step, p, False).start())
    for step in range(3):
        for p in range(2):
            pl.when(right_at[step])(lambda: copy(step, p, True).wait_send())
            pl.when(left_at[step])(lambda: copy(step, p, False).wait_send())


def line_gather(mine):
    if not fused():
        return lax.all_gather(mine, "gy", axis=1, tiled=True)
    rows, columns = mine.shape
    dma = pltpu.SemaphoreType.DMA
    return pl.pallas_call(
        line_gather_kernel,
        out_shape=jax.ShapeDtypeStruct((rows, 4 * columns), BF),
        in_specs=[VMEM],
        out_specs=VMEM,
        scratch_shapes=[dma((6,))] * 4,
        compiler_params=pltpu.CompilerParams(
            collective_id=12, has_side_effects=True, vmem_limit_bytes=VMEM_LIMIT
        ),
        cost_estimate=pl.CostEstimate(flops=0, bytes_accessed=150_000_000, transcendentals=0),
        name="line_gather",
    )(mine)


def rope_down(values, cosine, sines):
    half_width = HD // 2
    first, second = values[:half_width], values[half_width:]
    return jnp.concatenate(
        [first * cosine - second * sines, second * cosine + first * sines], axis=0
    )


def fill_bias(bias_ref, key_ref, query_ref, length_ref):
    keys = key_ref[...]
    allowed = (keys <= query_ref[...]) & (keys < length_ref[...])
    bias_ref[...] = jnp.where(allowed, 0.0, -1e30)


def dot_to(left, right, dims):
    return lax.dot_general(left, right, (dims, ((), ())), preferred_element_type=F32)


def attend_kernel(
    q_ref, k_ref, vt_ref, cos_ref, sin_ref, key_ref, query_ref, length_ref,
    heads_ref, rot_ref, lse_ref, bias_ref, out_ref,
):
    fill_bias(bias_ref, key_ref, query_ref, length_ref)

    def head(h, carry):
        here = pl.ds(pl.multiple_of(h * HD, HD), HD)
        rotated = rope_down(q_ref[here, :], cos_ref[...], sin_ref[...]).astype(BF)
        rot_ref[here, :] = rotated
        scaled = (rotated.astype(F32) * HD ** (-0.5)).astype(BF)
        scores = dot_to(k_ref[...], scaled, ((1,), (0,))) + bias_ref[...]
        top = jnp.max(scores, axis=0, keepdims=True)
        exponent = jnp.exp(scores - top)
        total = jnp.sum(exponent, axis=0, keepdims=True)
        probs = (exponent * (1.0 / total)).astype(BF)
        out_ref[here, :] = dot_to(vt_ref[...], probs, ((1,), (0,)))
        lse_ref[pl.ds(h, 1), :] = top + jnp.log(total)
        return carry

    lax.fori_loop(0, q_ref.shape[0] // HD, head, 0)
    heads_ref[...] = out_ref[...].T.astype(BF)


def attend_back_kernel(
    rot_ref, k_ref, kt_ref, v_ref, d_ref, lse_ref, cos_ref, sin_ref, key_ref, query_ref, length_ref,
    dq_ref, dk_ref, dv_ref, bias_ref, out_ref,
):
    fill_bias(bias_ref, key_ref, query_ref, length_ref)
    dk_ref[...] = jnp.zeros_like(dk_ref)
    dv_ref[...] = jnp.zeros_like(dv_ref)
    scaling = HD ** (-0.5)

    def head(h, carry):
        here = pl.ds(pl.multiple_of(h * HD, HD), HD)
        scaled = (rot_ref[here, :].astype(F32) * scaling).astype(BF)
        scores = dot_to(k_ref[...], scaled, ((1,), (0,))) + bias_ref[...]
        probs = jnp.exp(scores - lse_ref[pl.ds(h, 1), :])
        d_probs = dot_to(v_ref[...], d_ref[here, :], ((1,), (0,)))
        delta = jnp.sum(probs * d_probs, axis=0, keepdims=True)
        d_scores = (probs * (d_probs - delta)).astype(BF)
        dk_ref[...] += dot_to(d_scores, scaled, ((1,), (1,)))
        dv_ref[...] += dot_to(probs.astype(BF), d_ref[here, :], ((1,), (1,)))
        dq = dot_to(kt_ref[...], d_scores, ((1,), (0,))) * scaling
        out_ref[here, :] = rope_down(dq, cos_ref[...], -sin_ref[...])
        return carry

    lax.fori_loop(0, rot_ref.shape[0] // HD, head, 0)
    dq_ref[...] = out_ref[...].T.astype(BF)


def attend(q_down, k_all, v_all, tables):
    cosine, sines, keys_at, places, length = tables
    width, rows = q_down.shape
    return pl.pallas_call(
        attend_kernel,
        out_shape=(
            jax.ShapeDtypeStruct((rows, width), BF),
            jax.ShapeDtypeStruct((width, rows), BF),
            jax.ShapeDtypeStruct((width // HD, rows), F32),
        ),
        in_specs=[VMEM] * 8,
        out_specs=(VMEM,) * 3,
        scratch_shapes=[pltpu.VMEM((k_all.shape[0], rows), F32), pltpu.VMEM((width, rows), F32)],
        compiler_params=pltpu.CompilerParams(vmem_limit_bytes=VMEM_LIMIT),
        cost_estimate=pl.CostEstimate(
            flops=16 * width * rows * k_all.shape[0], bytes_accessed=60_000_000, transcendentals=0
        ),
        name="attend",
    )(q_down, k_all, v_all.T, cosine, sines, keys_at[:, None], places[None], length)


def attend_back(rotated, k_all, v_all, d_down, lse, tables):
    cosine, sines, keys_at, places, length = tables
    width, rows = rotated.shape
    return pl.pallas_call(
        attend_back_kernel,
        out_shape=(
            jax.ShapeDtypeStruct((rows, width), BF),
            jax.ShapeDtypeStruct(k_all.shape, F32),
            jax.ShapeDtypeStruct(k_all.shape, F32),
        ),
        in_specs=[VMEM] * 11,
        out_specs=(VMEM,) * 3,
        scratch_shapes=[pltpu.VMEM((k_all.shape[0], rows), F32), pltpu.VMEM((width, rows), F32)],
        compiler_params=pltpu.CompilerParams(vmem_limit_bytes=VMEM_LIMIT),
        cost_estimate=pl.CostEstimate(
            flops=40 * width * rows * k_all.shape[0], bytes_accessed=80_000_000, transcendentals=0
        ),
        name="attend_back",
    )(
        rotated, k_all, k_all.T, v_all, d_down, lse, cosine, sines,
        keys_at[:, None], places[None], length,
    )


def load_blocks(w_refs, w_layer, low, high, target_of, sem):
    shard, home = lax.axis_index("gx"), lax.axis_index("section") == w_layer
    waits = []
    for j in range(4):

        def copy(ref):
            source = ref.at[: ref.shape[0] - GAIN_ROWS, low:high]
            return pltpu.make_async_copy(source, target_of(j), sem.at[j])

        waits.append(copy(w_refs[0].at[j]))
        if len(w_refs) == 1:
            waits[j].start()
        else:
            pl.when(shard != j)(waits[j].start)
            pl.when((shard == j) & home)(copy(w_refs[1]).start)
            pl.when((shard == j) & jnp.logical_not(home))(copy(w_refs[2]).start)
    return waits


def meet_near(*others):
    near = {"gx": lax.axis_index("gx") ^ 1}
    barrier = pltpu.get_barrier_semaphore()
    for peer in (near, *others):
        pl.semaphore_signal(barrier, inc=1, device_id=peer, device_id_type=MESH)
    pl.semaphore_wait(barrier, 1 + len(others))
    return near


def attend_whole_kernel(
    w_layer, listed,
    h_ref, gain_ref, cos_ref, sin_ref, key_ref, query_ref, length_ref, *rest,
):
    w_refs, rest = rest[:listed], rest[listed:]
    (
        heads_ref, normed_ref, ms_ref, rot_ref, lse_ref, k_ref, kt_ref, v_ref,
        w_all, bias_ref, out_ref, q_ref, vt_ref, kv_mine, kv_far, w_sem, send_sem, recv_sem,
    ) = rest
    rows, width = h_ref.shape
    block = width // 4
    q_width = q_ref.shape[0]
    waits = load_blocks(
        w_refs, w_layer, 0, q_width + 2 * HD, lambda j: w_all.at[j * block : (j + 1) * block], w_sem
    )
    near = meet_near()

    def norm(i, carry):
        here = pl.ds(pl.multiple_of(i * 128, 128), 128)
        values = h_ref[here, :].astype(F32)
        square = jnp.mean(values * values, axis=1, keepdims=True)
        ms_ref[here, :] = square
        normed_ref[here, :] = (values * lax.rsqrt(square + EPS) * gain_ref[...]).astype(BF)
        return carry

    lax.fori_loop(0, rows // 128, norm, 0)
    for wait in waits:
        wait.wait()
    kv = dot_to(normed_ref[...], w_all[:, q_width:], ((1,), (0,))).T
    kv = jnp.concatenate([rope_down(kv[:HD], cos_ref[...], sin_ref[...]), kv[HD:]], axis=0)
    kv_mine[...] = kv.T.astype(BF)
    copy = pltpu.make_async_remote_copy(
        src_ref=kv_mine, dst_ref=kv_far, send_sem=send_sem, recv_sem=recv_sem,
        device_id=near, device_id_type=MESH,
    )
    copy.start()
    q_ref[...] = dot_to(normed_ref[...], w_all[:, :q_width], ((1,), (0,))).T
    fill_bias(bias_ref, key_ref, query_ref, length_ref)
    copy.wait()
    for n, ref in enumerate((kv_mine, kv_far)):
        here = pl.ds(n * rows, rows)
        k_ref[here, :] = ref[:, :HD]
        v_ref[here, :] = ref[:, HD:]
        down = ref[...].astype(F32).T.astype(BF)
        kt_ref[:, here] = down[:HD]
        vt_ref[:, here] = down[HD:]

    def head(h, carry):
        here = pl.ds(pl.multiple_of(h * HD, HD), HD)
        rotated = rope_down(q_ref[here, :], cos_ref[...], sin_ref[...]).astype(BF)
        rot_ref[here, :] = rotated
        scaled = (rotated.astype(F32) * HD ** (-0.5)).astype(BF)
        scores = dot_to(k_ref[...], scaled, ((1,), (0,))) + bias_ref[...]
        top = jnp.max(scores, axis=0, keepdims=True)
        exponent = jnp.exp(scores - top)
        total = jnp.sum(exponent, axis=0, keepdims=True)
        probs = (exponent * (1.0 / total)).astype(BF)
        out_ref[here, :] = dot_to(vt_ref[...], probs, ((1,), (0,)))
        lse_ref[pl.ds(h, 1), :] = top + jnp.log(total)
        return carry

    lax.fori_loop(0, q_width // HD, head, 0)
    heads_ref[...] = out_ref[...].T.astype(BF)


def attend_whole_back_kernel(
    w_layer, listed, crosses,
    e1_ref, rot_ref, lse_ref, k_ref, kt_ref, v_ref, cos_ref, sin_ref, key_ref, query_ref,
    length_ref, *rest,
):
    w_refs, rest = rest[:listed], rest[listed:]
    if crosses:
        source_ref, d_qkv_ref, crossed_ref, *rest, x_send, x_recv = rest
    else:
        d_qkv_ref, *rest = rest
    (
        w_all, bias_ref, d_ref, out_ref, dk_ref, dv_ref, dkv_send, dkv_far,
        w_sem, send_sem, recv_sem,
    ) = rest
    rows, width = e1_ref.shape
    block = width // 4
    q_width = rot_ref.shape[0]
    low = q_width + 2 * HD
    waits = load_blocks(w_refs, w_layer, low, low + block, lambda j: w_all.at[j], w_sem)
    section = lax.axis_index("section")
    x_peer = {"section": 1 - section}
    near = meet_near(x_peer) if crosses else meet_near()

    def x_copy():
        return pltpu.make_async_remote_copy(
            src_ref=source_ref, dst_ref=crossed_ref, send_sem=x_send, recv_sem=x_recv,
            device_id=x_peer, device_id_type=MESH,
        )

    if crosses:
        pl.when(section != w_layer)(lambda: x_copy().start())
    fill_bias(bias_ref, key_ref, query_ref, length_ref)
    dk_ref[...] = jnp.zeros_like(dk_ref)
    dv_ref[...] = jnp.zeros_like(dv_ref)
    scaling = HD ** (-0.5)
    for wait in waits:
        wait.wait()
    d_ref[...] = sum(
        dot_to(w_all[j], e1_ref[:, j * block : (j + 1) * block], ((1,), (1,))) for j in range(4)
    ).astype(BF)

    def head(h, carry):
        here = pl.ds(pl.multiple_of(h * HD, HD), HD)
        scaled = (rot_ref[here, :].astype(F32) * scaling).astype(BF)
        scores = dot_to(k_ref[...], scaled, ((1,), (0,))) + bias_ref[...]
        probs = jnp.exp(scores - lse_ref[pl.ds(h, 1), :])
        d_probs = dot_to(v_ref[...], d_ref[here, :], ((1,), (0,)))
        delta = jnp.sum(probs * d_probs, axis=0, keepdims=True)
        d_scores = (probs * (d_probs - delta)).astype(BF)
        dk_ref[...] += dot_to(d_scores, scaled, ((1,), (1,)))
        dv_ref[...] += dot_to(probs.astype(BF), d_ref[here, :], ((1,), (1,)))
        dq = dot_to(kt_ref[...], d_scores, ((1,), (0,))) * scaling
        out_ref[here, :] = rope_down(dq, cos_ref[...], -sin_ref[...])
        return carry

    lax.fori_loop(0, q_width // HD, head, 0)
    dkv_send[:, :HD] = dk_ref[rows:, :]
    dkv_send[:, HD:] = dv_ref[rows:, :]
    copy = pltpu.make_async_remote_copy(
        src_ref=dkv_send, dst_ref=dkv_far, send_sem=send_sem, recv_sem=recv_sem,
        device_id=near, device_id_type=MESH,
    )
    copy.start()
    d_qkv_ref[:, :q_width] = out_ref[...].T.astype(BF)
    copy.wait()
    down = (dkv_far[...].T)
    dk = rope_down(dk_ref[:rows, :].T + down[:HD], cos_ref[...], -sin_ref[...])
    dkv = jnp.concatenate([dk, dv_ref[:rows, :].T + down[HD:]], axis=0)
    d_qkv_ref[:, q_width:] = dkv.T.astype(BF)
    if crosses:
        pl.when(section != w_layer)(lambda: x_copy().wait_send())
        pl.when(section == w_layer)(lambda: x_copy().wait_recv())


def attend_whole(h, gain, w_attn, low, tables, w_layer, ident):
    cosine, sines, keys_at, places, length = tables
    rows, width = h.shape
    keys, q_width = keys_at.shape[0], low - 2 * HD
    w_list = list(w_attn) if isinstance(w_attn, tuple) else [w_attn]
    outs = [
        ((rows, q_width), BF), ((rows, width), BF), ((rows, 1), F32), ((q_width, rows), BF),
        ((q_width // HD, rows), F32), ((keys, HD), BF), ((HD, keys), BF), ((keys, HD), BF),
    ]
    return pl.pallas_call(
        functools.partial(attend_whole_kernel, w_layer, len(w_list)),
        out_shape=tuple(jax.ShapeDtypeStruct(*o) for o in outs),
        in_specs=[VMEM] * 7 + [ANY] * len(w_list),
        out_specs=(VMEM,) * 8,
        scratch_shapes=[
            pltpu.VMEM((width, low), BF),
            pltpu.VMEM((keys, rows), F32),
            pltpu.VMEM((q_width, rows), F32),
            pltpu.VMEM((q_width, rows), F32),
            pltpu.VMEM((HD, keys), BF),
            pltpu.VMEM((rows, 2 * HD), BF),
            pltpu.VMEM((rows, 2 * HD), BF),
            pltpu.SemaphoreType.DMA((4,)),
            pltpu.SemaphoreType.DMA,
            pltpu.SemaphoreType.DMA,
        ],
        compiler_params=pltpu.CompilerParams(
            collective_id=ident, has_side_effects=True, vmem_limit_bytes=VMEM_LIMIT
        ),
        cost_estimate=pl.CostEstimate(
            flops=16 * q_width * rows * keys, bytes_accessed=70_000_000, transcendentals=0
        ),
        name="attend_whole",
    )(h, gain, cosine, sines, keys_at[:, None], places[None], length, *w_list)


def attend_whole_back(
    e1, rotated, lse, k_all, kt_all, v_all, w_attn, tables, w_layer, ident, cross
):
    cosine, sines, keys_at, places, length = tables
    q_width, rows = rotated.shape
    keys, width = keys_at.shape[0], e1.shape[1]
    w_list = list(w_attn) if isinstance(w_attn, tuple) else [w_attn]
    crossing_specs = [jax.ShapeDtypeStruct(x.shape, BF) for x in cross]
    return pl.pallas_call(
        functools.partial(attend_whole_back_kernel, w_layer, len(w_list), len(cross)),
        out_shape=(jax.ShapeDtypeStruct((rows, q_width + 2 * HD), BF), *crossing_specs),
        in_specs=[VMEM] * 11 + [ANY] * (len(w_list) + len(cross)),
        out_specs=(VMEM, *[ANY] * len(cross)),
        scratch_shapes=[
            pltpu.VMEM((4, q_width, width // 4), BF),
            pltpu.VMEM((keys, rows), F32),
            pltpu.VMEM((q_width, rows), BF),
            pltpu.VMEM((q_width, rows), F32),
            pltpu.VMEM((keys, HD), F32),
            pltpu.VMEM((keys, HD), F32),
            pltpu.VMEM((rows, 2 * HD), F32),
            pltpu.VMEM((rows, 2 * HD), F32),
            pltpu.SemaphoreType.DMA((4,)),
            pltpu.SemaphoreType.DMA,
            pltpu.SemaphoreType.DMA,
        ]
        + [pltpu.SemaphoreType.DMA] * 2 * len(cross),
        compiler_params=pltpu.CompilerParams(
            collective_id=ident, has_side_effects=True, vmem_limit_bytes=VMEM_LIMIT
        ),
        cost_estimate=pl.CostEstimate(
            flops=40 * q_width * rows * keys, bytes_accessed=90_000_000, transcendentals=0
        ),
        name="attend_whole_back",
    )(
        e1, rotated, lse, k_all, kt_all, v_all, cosine, sines, keys_at[:, None], places[None],
        length, *w_list, *cross,
    )


def line_kernel(
    kind, masked, low, high, deps, gathers, layer, exchange, triples, w_layer, crosses, homing,
    gain_ref, resid_ref, valid_ref, h_ref, square_ref, *rest,
):
    forward = kind in ("out", "mlp")
    wide = kind in ("mlp", "mlp_back")
    if kind == "mlp":
        lhs_refs = []
    elif kind == "mlp_back":
        lhs_refs, rest = rest[:4], rest[4:]
    else:
        lhs_refs, rest = rest[:1], rest[1:]
    w_count = 3 if wide else 1
    w_refs = []
    for triple in triples:
        w_refs.append(rest[: 3 if triple else 1])
        rest = rest[3 if triple else 1 :]
    rest = rest[deps:]
    base_refs, rest = rest[: 2 * gathers], rest[2 * gathers :]
    cross_refs, rest = rest[: len(crosses)], rest[len(crosses) :]
    out_ref, rest = rest[0], rest[1:]
    if kind == "mlp":
        normed_ref, ms_ref, gate_ref, up_ref, hidden_ref = rest[:5]
        rest = rest[5:]
    elif kind == "mlp_back":
        product_refs, rest = rest[:3], rest[3:]
        arrived_refs, rest = rest[:exchange], rest[exchange:]
    block_refs, rest = rest[:gathers], rest[gathers:]
    crossed_refs, rest = rest[: len(crosses)], rest[len(crosses) :]
    if homing:
        home_ref, home_send, home_recv = rest[0], *rest[-2:]
        rest = rest[1:-2]
    if crosses:
        x_send, x_recv = rest[-2:]
        rest = rest[:-2]
    w_alls, rest = rest[:w_count], rest[w_count:]
    (
        part, from_end, from_mid, pair,
        w_sem, up_send, up_recv, mid_send, mid_recv, fin_send, fin_recv,
    ) = rest[:11]
    if gathers:
        far_send, far_recv, near_send, near_recv, cross_send, cross_recv = rest[11:]
    if kind == "mlp_back":
        (
            d_gate_ref, d_up_ref, far_normed, far_dm, far_hidden, far_d_gate, far_d_up, stage,
            give_sem, take_sem, stage_sem,
        ) = rest[11:22]
    if exchange:
        y_stage, y_send, y_recv = rest[22:]
    shard = lax.axis_index("gx")
    far, near = shard ^ 2, shard ^ 1
    section = lax.axis_index("section")
    rows, width = resid_ref.shape
    columns = width // 4
    count = rows // CHUNK
    z = lax.axis_index("gy")
    middle = (z == 1) | (z == 2)
    end_of = jnp.where(z == 1, 0, 3)
    mid_of = jnp.where(z == 0, 1, 2)
    across = 3 - z

    def loading(w, j, cut_of, target, slot):
        whole = w_refs[w]
        copies = [(None, pltpu.make_async_copy(cut_of(whole[0].at[j]), target, w_sem.at[slot]))]
        if triples[w]:
            home = section == w_layer
            copies = [(shard != j, copies[0][1])]
            for ref, holds in zip(whole[1:], (home, jnp.logical_not(home))):
                copy = pltpu.make_async_copy(cut_of(ref), target, w_sem.at[slot])
                copies.append(((shard == j) & holds, copy))
        return copies

    loads, downs = [], []
    if wide:
        hidden_width = w_alls[0].shape[1]
        for x0 in range(0, hidden_width, 512):
            x1 = min(x0 + 512, hidden_width)
            for w in range(2):
                for j in range(4):
                    target = w_alls[w].at[j * columns : (j + 1) * columns, x0:x1]
                    loads.append(loading(w, j, lambda ref: ref.at[:, x0:x1], target, len(loads)))
        for j in range(4):
            downs.append(loading(2, j, lambda ref: ref, w_alls[2].at[j], len(loads) + j))
    else:
        for j in range(4):
            cut_of = lambda ref: ref.at[: ref.shape[0] - GAIN_ROWS, low:high]
            loads.append(loading(0, j, cut_of, w_alls[0].at[j], j))
    for load in downs + loads if kind == "mlp_back" else loads + downs:
        for holds, copy in load:
            if holds is None:
                copy.start()
            else:
                pl.when(holds)(copy.start)
    loads, downs = [x[0][1] for x in loads], [x[0][1] for x in downs]

    barrier = pltpu.get_barrier_semaphore()
    peers = []
    if gathers:
        peers = [{"gx": far}, {"gx": near}, {"section": 1 - section}]
    elif kind == "mlp_back":
        peers = [{"gx": near}] + [{"gx": far}] * (exchange > 0)
    if crosses:
        assert not gathers
        peers.append({"section": 1 - section})
    beside = len(peers)
    for peer in peers:
        pl.semaphore_signal(barrier, inc=1, device_id=peer, device_id_type=MESH)

    @pl.when(middle)
    def _():
        pl.semaphore_signal(barrier, inc=1, device_id={"gy": end_of}, device_id_type=MESH)
        pl.semaphore_signal(barrier, inc=1, device_id={"gy": across}, device_id_type=MESH)
        pl.semaphore_wait(barrier, 2 + beside)

    @pl.when(jnp.logical_not(middle))
    def _():
        pl.semaphore_signal(barrier, inc=1, device_id={"gy": mid_of}, device_id_type=MESH)
        pl.semaphore_wait(barrier, 1 + beside)

    x_peer = {"section": 1 - section}

    def x_copy(k):
        return pltpu.make_async_remote_copy(
            src_ref=cross_refs[k], dst_ref=crossed_refs[k], send_sem=x_send.at[k],
            recv_sem=x_recv.at[k], device_id=x_peer, device_id_type=MESH,
        )

    def home_copy(rows_here):
        return pltpu.make_async_remote_copy(
            src_ref=out_ref.at[rows_here, pl.ds(pl.multiple_of(z * columns, columns), columns)],
            dst_ref=home_ref.at[rows_here, :], send_sem=home_send, recv_sem=home_recv,
            device_id=x_peer, device_id_type=MESH,
        )

    def home_start(i):
        if homing:
            here = pl.ds(pl.multiple_of(i * CHUNK, CHUNK), CHUNK)
            pl.when(section != w_layer)(lambda: home_copy(here).start())

    def x_sends(k):
        return section != crosses[k] if crosses[k] < 2 else section >= 0

    def x_takes(k):
        return section == crosses[k] if crosses[k] < 2 else section >= 0

    for k in range(len(crosses)):
        pl.when(x_sends(k))(lambda k=k: x_copy(k).start())

    def half_of(ref, k, which):
        size = base_refs[2 * k].shape[0] // 2
        return ref.at[pl.ds(pl.multiple_of(which * size, 16), size), :]

    def far_copy(k, source):
        return pltpu.make_async_remote_copy(
            src_ref=half_of(source, k, section),
            dst_ref=half_of(block_refs[k].at[shard], k, section),
            send_sem=far_send.at[k], recv_sem=far_recv.at[k],
            device_id={"gx": far}, device_id_type=MESH,
        )

    def near_copy(k, source):
        return pltpu.make_async_remote_copy(
            src_ref=source, dst_ref=block_refs[k].at[shard], send_sem=near_send.at[3 * k],
            recv_sem=near_recv.at[3 * k], device_id={"gx": near}, device_id_type=MESH,
        )

    def cross_copy(k):
        rows_here = half_of(block_refs[k].at[far], k, section)
        return pltpu.make_async_remote_copy(
            src_ref=rows_here, dst_ref=rows_here, send_sem=cross_send.at[k],
            recv_sem=cross_recv.at[k], device_id=x_peer, device_id_type=MESH,
        )

    def pass_copy(k, late):
        rows_here = half_of(block_refs[k].at[far], k, 1 - section if late else section)
        return pltpu.make_async_remote_copy(
            src_ref=rows_here, dst_ref=rows_here, send_sem=near_send.at[3 * k + 1 + late],
            recv_sem=near_recv.at[3 * k + 1 + late], device_id={"gx": near}, device_id_type=MESH,
        )

    at_home = section == layer

    def from_base(k, starts):
        for ref, holds in zip(base_refs[2 * k : 2 * k + 2], (at_home, jnp.logical_not(at_home))):

            @pl.when(holds)
            def _():
                for make in starts:
                    make(k, ref).start()

    def gather_middle(k):
        far_copy(k, base_refs[2 * k]).wait_recv()
        cross_copy(k).start()
        pass_copy(k, 0).start()

    def gather_late(k):
        cross_copy(k).wait_recv()
        pass_copy(k, 1).start()

    if gathers:
        from_base(0, [far_copy])
    for k in range(gathers):
        from_base(k, [near_copy])

    half = rows // STEPS
    core = lax.rem(shard, 2)

    def give(slot, source, target):
        return pltpu.make_async_remote_copy(
            src_ref=source, dst_ref=target, send_sem=give_sem.at[slot],
            recv_sem=take_sem.at[slot], device_id={"gx": near}, device_id_type=MESH,
        )

    def chip_columns(ref, y, of):
        return ref.at[:, pl.ds(pl.multiple_of((2 * y + of) * columns, columns), columns)]

    def step_rows(ref, step):
        return ref.at[pl.ds(pl.multiple_of(step * half, half), half), :]

    if kind == "mlp_back":
        saved_gate, saved_up, saved_normed, saved_hidden = lhs_refs
        early = [give(0, saved_hidden, far_hidden)]
        for y in range(2):
            early.append(give(1 + y, chip_columns(resid_ref, y, 1 - core), far_dm.at[y]))
        for y in range(2):
            early.append(give(3 + y, chip_columns(saved_normed, y, 1 - core), far_normed.at[y]))
        for copy in early:
            copy.start()

    def give_step(step):
        return [
            give(5 + step, step_rows(d_gate_ref, step), step_rows(far_d_gate, step)),
            give(5 + STEPS + step, step_rows(d_up_ref, step), step_rows(far_d_up, step)),
        ]

    if not wide:
        for load in loads:
            load.wait()

    def at_first(step, copies):
        @pl.when(step == 0)
        def _():
            for copy in copies:
                copy.wait()

    def rows_at(ref, i):
        return ref.at[pl.ds(pl.multiple_of(i * CHUNK, CHUNK), CHUNK), :]

    def up_copy(i):
        return pltpu.make_async_remote_copy(
            src_ref=rows_at(part, i), dst_ref=rows_at(from_end, i), send_sem=up_send.at[i],
            recv_sem=up_recv.at[i], device_id={"gy": mid_of}, device_id_type=MESH,
        )

    def mid_copy(i):
        return pltpu.make_async_remote_copy(
            src_ref=rows_at(pair, i), dst_ref=rows_at(from_mid, i), send_sem=mid_send.at[i],
            recv_sem=mid_recv.at[i], device_id={"gy": across}, device_id_type=MESH,
        )

    def fin_copy(i):
        return pltpu.make_async_remote_copy(
            src_ref=rows_at(out_ref, i), dst_ref=rows_at(out_ref, i), send_sem=fin_send.at[i],
            recv_sem=fin_recv.at[i], device_id={"gy": end_of}, device_id_type=MESH,
        )

    def dot(left, right, transposed=False):
        dims = (((1,), (1 if transposed else 0,)), ((), ()))
        return lax.dot_general(left, right, dims, preferred_element_type=F32)

    def spans(extent):
        return [(x, min(x + 512, extent)) for x in range(0, extent, 512)]

    if wide:
        w_gate, w_up, w_down = w_alls

    def product(step, carry):
        here = pl.ds(pl.multiple_of(step * half, half), half)
        if kind == "mlp":
            values = resid_ref[here, :].astype(F32)
            square = jnp.mean(values * values, axis=1, keepdims=True)
            ms_ref[here, :] = square
            normed_ref[here, :] = (values * lax.rsqrt(square + EPS) * gain_ref[...]).astype(BF)
            for n, (x0, x1) in enumerate(spans(w_gate.shape[1])):
                at_first(step, loads[8 * n : 8 * n + 8])
                gate = dot(normed_ref[here, :], w_gate[:, x0:x1])
                up = dot(normed_ref[here, :], w_up[:, x0:x1])
                gate_ref[here, x0:x1] = gate.astype(BF)
                up_ref[here, x0:x1] = up.astype(BF)
                hidden_ref[here, x0:x1] = (gate * jax.nn.sigmoid(gate) * up).astype(BF)
        if kind == "mlp_back":
            at_first(step, downs)
            for x0, x1 in spans(w_gate.shape[1]):
                d_hidden = sum(
                    dot(resid_ref[here, j * columns : (j + 1) * columns], w_down[j, x0:x1, :], True)
                    for j in range(4)
                )
                gate = saved_gate[here, x0:x1].astype(F32)
                up = saved_up[here, x0:x1].astype(F32)
                sigmoid = jax.nn.sigmoid(gate)
                d_up_ref[here, x0:x1] = (d_hidden * (gate * sigmoid)).astype(BF)
                d_gate_ref[here, x0:x1] = (
                    d_hidden * up * sigmoid * (1.0 + gate * (1.0 - sigmoid))
                ).astype(BF)
            for copy in give_step(step):
                copy.start()
        if wide:
            at_first(step, downs if kind == "mlp" else loads)
        for j in range(4):
            span = slice(j * columns, (j + 1) * columns)
            if kind == "out":
                value = dot(lhs_refs[0][here, :], w_alls[0][j])
            elif kind == "mlp":
                value = dot(hidden_ref[here, :], w_down[j])
            elif kind == "mlp_back":
                value = dot(d_gate_ref[here, :], w_gate[span, :], True)
                value += dot(d_up_ref[here, :], w_up[span, :], True)
            else:
                value = dot(lhs_refs[0][here, :], w_alls[0][j], True)
            part[here, span] = value.astype(BF)

        @pl.when(jnp.logical_not(middle))
        def _():
            def send(i, inner):
                up_copy(step * (count // STEPS) + i).start()
                return inner

            lax.fori_loop(0, count // STEPS, send, 0)

        return carry

    lax.fori_loop(0, STEPS, product, 0)

    def finish(i):
        mid_copy(i).wait_recv()
        here = pl.ds(pl.multiple_of(i * CHUNK, CHUNK), CHUNK)
        total = pair[here, :].astype(F32) + from_mid[here, :].astype(F32)
        resid = resid_ref[here, :].astype(F32)
        if forward:
            result = resid + total
            if masked:
                result = result * valid_ref[here, :]
        else:
            values = h_ref[here, :].astype(F32)
            scaled = total * gain_ref[...]
            ratio = lax.rsqrt(square_ref[here, :] + EPS)
            mean_term = jnp.sum(scaled * values, axis=1, keepdims=True) * (1.0 / width)
            result = resid + ratio * scaled - values * (ratio * ratio * ratio) * mean_term
        out_ref[here, :] = result.astype(BF)
        fin_copy(i).start()
        home_start(i)

    tile = columns // 2

    def tile_rows(sub):
        return pl.ds(pl.multiple_of(sub % 2 * tile, tile), tile)

    def stage_copy(number, sub, slot):
        target = product_refs[number].at[sub // 2, tile_rows(sub), :]
        return pltpu.make_async_copy(stage.at[slot], target, stage_sem.at[slot])

    def y_copy(number, sub, slot):
        return pltpu.make_async_remote_copy(
            src_ref=y_stage.at[2 * number + slot], dst_ref=arrived_refs[number].at[tile_rows(sub), :],
            send_sem=y_send.at[2 * number + slot], recv_sem=y_recv.at[2 * number + slot],
            device_id={"gx": far}, device_id_type=MESH,
        )

    def gradient_tile(number, sub):
        slot = sub % 2
        left, far_left, right, far_right = (
            (resid_ref, far_dm, saved_hidden, far_hidden),
            (saved_normed, far_normed, d_gate_ref, far_d_gate),
            (saved_normed, far_normed, d_up_ref, far_d_up),
        )[number]

        @pl.when(sub == 0)
        def _():
            waits = [early[:3], early[3:] + give_all[:STEPS], give_all[STEPS:]][number]
            for copy in waits:
                copy.wait_recv()

        if number >= exchange:

            @pl.when((sub >= 2) | (number > 0))
            def _():
                stage_copy(number, sub, slot).wait()

        elif number > 0:

            @pl.when(sub >= 2)
            def _():
                stage_copy(number, sub - 2, slot).wait()

        y = sub // 2
        if number < exchange:
            y = jnp.where(sub < 2, 1 - lax.div(shard, 2), lax.div(shard, 2))
        start = (y * 2 + core) * columns + sub % 2 * tile
        mine = left[:, pl.ds(pl.multiple_of(start, tile), tile)]
        theirs = far_left[y, :, tile_rows(sub)]
        value = dot_to(mine, right[...], ((0,), (0,))) + dot_to(theirs, far_right[...], ((0,), (0,)))
        if number < exchange:

            @pl.when(sub < 2)
            def _():
                y_stage[2 * number + slot] = value.astype(BF)
                y_copy(number, sub, slot).start()

            @pl.when(sub >= 2)
            def _():
                stage[slot] = value.astype(BF)
                stage_copy(number, sub - 2, slot).start()

        else:
            stage[slot] = value.astype(BF)
            stage_copy(number, sub, slot).start()

    if kind == "mlp_back":
        give_all = [x for pair in zip(*(give_step(n) for n in range(STEPS))) for x in pair]

    def beside_step(i):
        pass_on(i)
        if kind == "mlp_back":
            for number in range(3):
                first = 3 + 4 * number

                @pl.when((i >= first) & (i < first + 4))
                def _():
                    gradient_tile(number, i - first)

    def pass_on(i):
        if gathers == 2:
            at(2, i, lambda: from_base(1, [far_copy]))
            at(6, i, lambda: gather_middle(0))
            at(10, i, lambda: gather_middle(1))
            at(11, i, lambda: gather_late(0))
            at(15, i, lambda: gather_late(1))

    def at(sixteenth, i, action):
        pl.when(i == count * sixteenth // 16)(action)

    @pl.when(middle)
    def _():
        def step(i, carry):
            up_copy(i).wait_recv()
            here = pl.ds(pl.multiple_of(i * CHUNK, CHUNK), CHUNK)
            pair[here, :] = (part[here, :].astype(F32) + from_end[here, :].astype(F32)).astype(BF)
            mid_copy(i).start()

            @pl.when(i >= 1)
            def _():
                finish(i - 1)

            beside_step(i)
            return carry

        lax.fori_loop(0, count, step, 0)
        finish(count - 1)

        def drain(i, carry):
            mid_copy(i).wait_send()
            fin_copy(i).wait_send()
            return carry

        lax.fori_loop(0, count, drain, 0)

    @pl.when(jnp.logical_not(middle))
    def _():
        def drain(i, carry):
            up_copy(i).wait_send()
            fin_copy(i).wait_recv()
            home_start(i)
            beside_step(i)
            return carry

        lax.fori_loop(0, count, drain, 0)

    if kind == "mlp_back":
        for slot in range(2):
            stage_copy(2, 2 + slot, slot).wait()
        for copy in early + give_all:
            copy.wait_send()
        for number in range(exchange):
            for slot in range(2):
                y_copy(number, slot, slot).wait()
    if homing:
        every = pl.ds(0, rows)
        pl.when(section != w_layer)(lambda: home_copy(every).wait_send())
        pl.when(section == w_layer)(lambda: home_copy(every).wait_recv())
    for k in range(len(crosses)):
        pl.when(x_sends(k))(lambda k=k: x_copy(k).wait_send())
        pl.when(x_takes(k))(lambda k=k: x_copy(k).wait_recv())
    for k in range(gathers):
        far_copy(k, base_refs[2 * k]).wait_send()
        near_copy(k, base_refs[2 * k]).wait()
        cross_copy(k).wait_send()
        pass_copy(k, 0).wait()
        pass_copy(k, 1).wait()


def line_sum(kind, ident, resid, weights, lhs=(), gain=None, valid=None, back=None, low=0, high=0, deps=(), bases=(), layer=0, exchange=0, w_layer=0, crosses=(), homing=False):
    rows, width = resid.shape
    one = jnp.ones((rows, 1), F32)
    h, square = back if back is not None else (jnp.zeros((16, 128), BF), jnp.zeros((8, 1), F32))
    gain = jnp.zeros((1, width), F32) if gain is None else gain
    wide = kind in ("mlp", "mlp_back")
    hidden = 0
    if wide:
        hidden = (weights[2][0] if isinstance(weights[2], tuple) else weights[2]).shape[1]
    w_scratch = []
    triples = [isinstance(w, tuple) for w in weights]
    w_flat = [x for w in weights for x in (w if isinstance(w, tuple) else (w,))]
    for i, w in enumerate(weights):
        _, depth, across = (w[0] if isinstance(w, tuple) else w).shape
        if wide and i < 2:
            w_scratch.append(pltpu.VMEM((width, across), BF))
        else:
            shape = (4, depth, across) if wide else (4, depth - GAIN_ROWS, high - low)
            w_scratch.append(pltpu.VMEM(shape, BF))
    outs, products, beside = [((rows, width), BF)], [], []
    if kind == "mlp":
        outs += [((rows, width), BF), ((rows, 1), F32)] + [((rows, hidden), BF)] * 3
    elif kind == "mlp_back":
        products = [((1 if n < exchange else 2, width // 4, hidden), BF) for n in range(3)]
        products += [((width // 4, hidden), BF)] * exchange
        half_block = pltpu.VMEM((2, rows, width // 4), BF)
        beside = [pltpu.VMEM((rows, hidden), BF)] * 2 + [half_block] * 2
        beside += [pltpu.VMEM((rows, hidden), BF)] * 3 + [pltpu.VMEM((2, width // 8, hidden), BF)]
        beside += [pltpu.SemaphoreType.DMA((n,)) for n in (5 + 2 * STEPS, 5 + 2 * STEPS, 2)]
        if exchange:
            beside += [pltpu.VMEM((2 * exchange, width // 8, hidden), BF)]
            beside += [pltpu.SemaphoreType.DMA((2 * exchange,))] * 2
    blocks = [((4,) + base[0].shape, BF) for base in bases]
    pairs = [x for base in bases for x in base]
    crossed = [(x[0].shape, BF) for x in crosses] + [((rows, width // 4), BF)] * homing
    depth = 3 * hidden if wide else lhs[0].shape[1]
    count = rows // CHUNK
    dma = pltpu.SemaphoreType.DMA
    return pl.pallas_call(
        functools.partial(
            line_kernel, kind, valid is not None, low, high, len(deps), len(bases), layer, exchange,
            triples, w_layer, [x[1] for x in crosses], homing,
        ),
        out_shape=tuple(jax.ShapeDtypeStruct(*o) for o in outs + products + blocks + crossed),
        in_specs=[VMEM] * (5 + len(lhs)) + [ANY] * (len(w_flat) + len(deps) + len(pairs) + len(crosses)),
        out_specs=tuple([VMEM] * len(outs) + [ANY] * len(products + blocks + crossed)),
        scratch_shapes=w_scratch
        + [pltpu.VMEM((rows, width), BF)] * 4
        + [dma((8 * -(-hidden // 512) + 4,))]
        + [dma((count,))] * 6
        + [dma((n * len(bases),)) for n in (1, 1, 3, 3, 1, 1) if bases]
        + beside
        + [dma((len(crosses),))] * 2 * bool(crosses)
        + [dma] * 2 * homing,
        compiler_params=pltpu.CompilerParams(
            collective_id=ident, has_side_effects=True, vmem_limit_bytes=VMEM_LIMIT
        ),
        cost_estimate=pl.CostEstimate(
            flops=2 * rows * depth * width, bytes_accessed=200 * 1024 * 1024, transcendentals=0
        ),
        name="line_" + kind,
    )(
        gain, resid, one if valid is None else valid, h, square, *lhs, *w_flat, *deps, *pairs,
        *(x[0] for x in crosses),
    )


def plain_sum(total):
    return lax.psum(total.astype(BF), "gy").astype(F32)


def normed(h, gain):
    values = h.astype(F32)
    square = jnp.mean(values * values, axis=1, keepdims=True)
    return square, (values * lax.rsqrt(square + EPS) * gain).astype(BF)


def norm_back(d_normed, h, square, gain):
    values = h.astype(F32)
    ratio = lax.rsqrt(square + EPS)
    scaled = d_normed * gain
    mean_term = jnp.mean(scaled * values, axis=1, keepdims=True)
    return ratio * scaled - values * (ratio * ratio * ratio) * mean_term


def attention_forward(h, gain, w_attn, low, tables, ident, bases, layer, w_layer, deps=(), late=None):
    rows, width = h.shape
    high = low + width // lax.axis_size("gx")
    q_width = low - 2 * HD
    if fused():
        heads, n1, square, rotated, lse, k_all, kt_all, v_all = attend_whole(
            h, gain, w_attn, low, tables, w_layer, ident + 8
        )
        if late is not None:
            late = line_gather(late + heads[:1, :1] * 0)
            deps = (*deps, late)
        h1, *stacks = line_sum(
            "out", ident, h, [w_attn], (heads,), low=low, high=high,
            deps=deps, bases=bases, layer=layer, w_layer=w_layer,
        )
        blocks = [(x, *pair) for x, pair in zip(stacks, bases)]
    else:
        cosine, sines = tables[:2]
        square, n1 = normed(h, gain)
        q_down = mm(tall(cut(w_attn, 0, q_width)), n1, ((0,), (1,)))
        kv = mm(n1, tall(cut(w_attn, q_width, low)))
        k_rot = rope_down(kv[:, :HD].T, cosine, sines).T.astype(BF)
        kv = jnp.concatenate([k_rot, kv[:, HD:].astype(BF)], axis=1)
        kv_all = jnp.concatenate([kv, swap_pairs(kv, "gx")], axis=0)
        k_all, v_all = kv_all[:, :HD], kv_all[:, HD:]
        kt_all = k_all.T
        heads, rotated, lse = attend(q_down, k_all, v_all, tables)
        h1 = (h.astype(F32) + plain_sum(mm(heads, side(cut(w_attn, low, high))))).astype(BF)
        blocks = [gather_blocks(chosen(x, layer)) for x in bases]
        late = None if late is None else line_gather(late)
    if late is not None:
        blocks.append(late)
    return h1, square, blocks, (h, square, n1, rotated, lse, k_all, kt_all, v_all, heads)


def mlp_forward(h1, gain, weights, valid, ident, bases=(), layer=0, w_layer=0):
    if fused():
        result, n2, square, gate, up, hidden, *stacks = line_sum(
            "mlp", ident, h1, weights, gain=gain, valid=valid, bases=bases, layer=layer,
            w_layer=w_layer,
        )
        blocks = [(x, *pair) for x, pair in zip(stacks, bases)]
    else:
        square, n2 = normed(h1, gain)
        gate = mm(n2, tall(weights[0]))
        up = mm(n2, tall(weights[1]))
        hidden = (gate * jax.nn.sigmoid(gate) * up).astype(BF)
        gate, up = gate.astype(BF), up.astype(BF)
        result = h1.astype(F32) + plain_sum(mm(hidden, side(weights[2])))
        result = (result * valid).astype(BF)
        blocks = [gather_blocks(chosen(x, layer)) for x in bases]
    return result, square, blocks, (h1, square, n2, gate, up, hidden)


def mlp_backward(dm, gain, weights, saved, ident, w_layer, crosses=(), deps=(), exchange=1):
    h1, square, n2, gate, up, hidden = saved
    if fused():
        e1, *products = line_sum(
            "mlp_back", ident, dm, weights, (gate, up, n2, hidden), gain=gain,
            back=(h1, square), exchange=exchange, w_layer=w_layer, crosses=crosses, deps=deps,
        )
        return e1, products[:4], products[4:]
    gate, up = gate.astype(F32), up.astype(F32)
    d_hidden = mm(dm, side(weights[2]), ((1,), (1,)))
    sigmoid = jax.nn.sigmoid(gate)
    d_gate = (d_hidden * up * sigmoid * (1.0 + gate * (1.0 - sigmoid))).astype(BF)
    d_up = (d_hidden * (gate * sigmoid)).astype(BF)
    total = mm(d_gate, tall(weights[0]), ((1,), (1,))) + mm(d_up, tall(weights[1]), ((1,), (1,)))
    e1 = (dm.astype(F32) + norm_back(plain_sum(total), h1, square, gain)).astype(BF)
    turn = ((0,), (0,))
    products = [mm(dm, hidden, turn), mm(n2, d_gate, turn), mm(n2, d_up, turn)]
    return e1, [p.astype(BF) for p in products], crossing(crosses)


def crossing(crosses):
    pairs = ([(1, 0)], [(0, 1)], [(0, 1), (1, 0)])
    return [lax.ppermute(x, "section", pairs[way]) for x, way in crosses]


def mlp_sums(products):
    if not fused():
        return [shard_sum(p) for p in products]
    down, gate, up, arrived = products
    first = (down[0].astype(F32) + arrived.astype(F32)).astype(BF)
    return [first, chip_sum(gate), chip_sum(up)]


def attention_backward(e1, w_attn, low, tables, saved, w_layer, ident, cross=()):
    h, square, n1, rotated, lse, k_all, kt_all, v_all, heads = saved
    rows, width = h.shape
    if fused():
        d_qkv, *crossed = attend_whole_back(
            e1, rotated, lse, k_all, kt_all, v_all, w_attn, tables, w_layer, ident, cross
        )
    else:
        cosine, sines = tables[:2]
        w_o = side(cut(w_attn, low, low + width // lax.axis_size("gx")))
        d_down = mm(w_o, e1, ((1,), (1,))).astype(BF)
        dq, dk, dv = attend_back(rotated, k_all, v_all, d_down, lse, tables)
        dkv = jnp.concatenate([dk, dv], axis=1)
        dkv = dkv[:rows] + swap_pairs(dkv[rows:], "gx")
        dk = rope_down(dkv[:, :HD].T, cosine, -sines).T
        d_qkv = jnp.concatenate([dq, dk.astype(BF), dkv[:, HD:].astype(BF)], axis=1)
        crossed = crossing([(x, w_layer) for x in cross])
    turn = ((0,), (0,))
    products = [mm(n1, d_qkv, turn).astype(BF), mm(e1, heads, turn).astype(BF)]
    return d_qkv, jnp.concatenate(products, axis=1), crossed


def attention_end(d_qkv, e1, w_attn, gain, saved, ident, w_layer, deps, crosses):
    h, square = saved[:2]
    qkv_width = d_qkv.shape[1]
    if fused():
        grad, *crossed = line_sum(
            "back", ident, e1, [w_attn], (d_qkv,), gain=gain, back=(h, square),
            low=0, high=qkv_width, deps=deps, crosses=crosses, w_layer=w_layer, homing=True,
        )
        return grad, crossed[-1], crossed[:-1]
    total = plain_sum(mm(d_qkv, tall(cut(w_attn, 0, qkv_width)), ((1,), (1,))))
    grad = (e1.astype(F32) + norm_back(total, h, square, gain)).astype(BF)
    width = grad.shape[1] // lax.axis_size("gy")
    part = lax.dynamic_slice_in_dim(grad, lax.axis_index("gy") * width, width, 1)
    home, *crossed = crossing([(part, w_layer), *crosses])
    return grad, home, crossed


def on_device(
    hidden_in, out_grad, lengths, dealing, attn_gain, w_query, w_key, w_value, w_out,
    mlp_gain, w_gate, w_up, w_down,
):
    shards = lax.axis_size("gx")
    shard = lax.axis_index("gx")
    section = lax.axis_index("section")
    column = lax.axis_index("gy")
    core = shard % 2
    sequence = (shard // 2) * 2 + section
    span, width = hidden_in.shape
    half = span // 2
    seq_length = lax.dynamic_index_in_dim(lengths, sequence, keepdims=False)

    both = jnp.concatenate([hidden_in, out_grad], axis=1)
    mine = core_rows(both, core)
    theirs = swap_pairs(core_rows(both, 1 - core), "gx")
    mine = jnp.where(core == section, mine, theirs)
    h = line_gather(mine[:, :width])

    kv_head = column * (w_query.shape[2] // HD) // (QH // KVH)
    low = w_query.shape[2] + 2 * HD
    both_gains = jnp.stack([attn_gain[0], mlp_gain[0]])
    block_rows = both_gains.shape[1]
    attn_own = jnp.concatenate(
        [
            w_query[0],
            lax.dynamic_slice_in_dim(w_key[0], kv_head * HD, HD, 1),
            lax.dynamic_slice_in_dim(w_value[0], kv_head * HD, HD, 1),
            w_out[0],
        ],
        axis=1,
    )
    gain_rows = jnp.pad(both_gains, ((0, GAIN_ROWS - 2), (0, attn_own.shape[1] - block_rows)))
    attn_own = jnp.concatenate([attn_own, gain_rows + theirs[:1, :1] * 0], axis=0)
    own = (attn_own, w_gate[0], w_up[0], w_down[0])
    first = second = [(array, swap_pairs(array, "section")) for array in own]

    def gains_of(w_attn, pair):
        cut_of = lambda w: w[..., block_rows : block_rows + 2, :block_rows]
        rows = cut_of(w_attn[0] if isinstance(w_attn, tuple) else w_attn)
        if isinstance(w_attn, tuple):
            rows = with_own(rows, [cut_of(x) for x in pair], 1)
        return rows.transpose(1, 0, 2).reshape(2, 1, -1).astype(F32)

    here = core_rows(jnp.arange(span), core)
    there = core_rows(jnp.arange(span), 1 - core)
    keys_at = jnp.concatenate([here, there])
    valid = (here < seq_length)[:, None].astype(F32)
    tables = (*rope_tables(here), keys_at, here, seq_length.reshape(1, 1))

    attn0 = gather_blocks(chosen(first[0], 0) + h[:1, :1] * 0)
    gate0 = gather_blocks(chosen(first[1], 0) + h[:1, :1] * 0)
    gains0 = gains_of(attn0, first[0])
    h1, square_a, blocks, saved_a0 = attention_forward(
        h, gains0[0], attn0, low, tables, 0, first[2:], 0, 0, (gate0,), mine[:, width:]
    )
    d_out = blocks.pop()
    mlp0 = [gate0] + blocks
    h, square_m, (attn1, gate1), saved_m0 = mlp_forward(
        h1, gains0[1], mlp0, valid, 1, second[:2], 1
    )
    gains1 = gains_of(attn1, second[0])
    outputs, squares = [h], [square_a, square_m]
    h1, square_a, blocks, saved_a1 = attention_forward(
        h, gains1[0], attn1, low, tables, 2, second[2:], 1, 1
    )
    mlp1 = [gate1] + blocks
    h, square_m, _, saved_m1 = mlp_forward(h1, gains1[1], mlp1, valid, 3, w_layer=1)
    outputs.append(h)
    squares = jnp.concatenate(squares + [square_a, square_m], axis=1)
    rms = (jnp.sqrt(squares + EPS) * valid).T
    statistics = [rms[:2], rms[2:]]
    outputs = [lax.dynamic_slice_in_dim(x, column * width, width, 1) for x in outputs]

    dm = (d_out.astype(F32) * valid).astype(BF)
    e1, products, _ = mlp_backward(dm, gains1[1], mlp1, saved_m1, 4, 1)
    local1 = mlp_sums(products)

    both = []
    for output, stat in zip(outputs, statistics):
        high = stat.astype(BF)
        rest = (stat - high.astype(F32)).astype(BF)
        parts = jnp.concatenate([high, rest], axis=0).reshape(-1, width)
        parts = jnp.pad(parts, ((0, -parts.shape[0] % 16), (0, 0)))
        both.append(jnp.concatenate([output + e1[:1, :1] * 0, parts], axis=0))
    kept = jnp.where(section == 0, both[0], both[1])
    sent = jnp.where(section == 0, both[1], both[0])

    d_qkv, products, _ = attention_backward(e1, attn1, low, tables, saved_a1, 1, 9)
    local1.append(shard_sum(products))
    crosses = [(sent, 2), (local1[0], 1)]
    grad1, home1, (sent, down1) = attention_end(
        d_qkv, e1, attn1, gains1[0], saved_a1, 5, 1, (products,), crosses
    )
    by_section = jnp.stack([jnp.where(section == 0, kept, sent), jnp.where(section == 0, sent, kept)])
    everything = lax.all_gather(by_section, "gx", axis=0)
    owner = jnp.sum(jnp.where(dealing == shard, jnp.arange(shards), 0))
    halves = lax.dynamic_slice(
        everything, ((owner // 2) * 2, owner % 2, 0, 0), (2, 1) + everything.shape[2:]
    )[:, 0]
    layer_out = join_halves(halves[0, :half], halves[1, :half])
    stat_rows = 4 * half // width
    parts = halves[:, half : half + stat_rows].astype(F32).reshape(2, 4, half)
    stat_halves = parts[:, :2] + parts[:, 2:]
    stats_out = join_halves(stat_halves[0].T, stat_halves[1].T).T

    dm = (grad1.astype(F32) * valid).astype(BF)
    crosses = [(local1[1], 1), (local1[2], 1)]
    e1, products, (gate1, up1) = mlp_backward(dm, gains0[1], mlp0, saved_m0, 6, 0, crosses)
    local0 = mlp_sums(products)
    d_qkv, products, (down0,) = attention_backward(
        e1, attn0, low, tables, saved_a0, 0, 11, local0[:1]
    )
    local0.append(shard_sum(products))
    crosses = [(local1[3], 1), (local0[1], 0)]
    grad0, home0, (attn_sum1, gate0) = attention_end(
        d_qkv, e1, attn0, gains0[0], saved_a0, 7, 0, (products, everything), crosses
    )

    input_grads = [lax.dynamic_slice_in_dim(x, column * width, width, 1) for x in (grad0, grad1)]
    local0[2] = local0[2] + grad0[:1, :1] * 0
    received0 = [down0, gate0] + crossing([(x, 0) for x in local0[2:]])
    received1 = [down1, gate1, up1, attn_sum1]
    totals = [
        jnp.where(section == 0, a0.astype(F32) + r0.astype(F32), a1.astype(F32) + r1.astype(F32))
        for a0, r0, a1, r1 in zip(local0, received0, local1, received1)
    ]
    s_down, s_gate, s_up, s_attn = totals
    s_out = s_attn[:, low:]
    q_width = w_query.shape[2]

    attn_sum = jnp.sum(s_attn[:, :low] * attn_own[:block_rows, :low].astype(F32), axis=1)
    mlp_sum = jnp.sum(s_gate * w_gate[0].astype(F32) + s_up * w_up[0].astype(F32), axis=1)
    sums = jnp.pad(jnp.stack([attn_sum, mlp_sum], axis=1), ((0, 0), (0, 126)))
    spread = jnp.concatenate([s_attn[:, q_width:low], sums], axis=1).astype(BF)
    spread = lax.all_gather(spread, "gy", axis=0).astype(F32)
    gains = jnp.sum(spread[:, :, 2 * HD : 2 * HD + 2], axis=0).T / both_gains.astype(F32)
    kv_sum = spread[:, :, : 2 * HD].reshape(KVH, -1, *spread.shape[1:2], 2, HD).sum(axis=1)
    kv_sum = kv_sum.transpose(2, 1, 0, 3).reshape(2, spread.shape[1], KVH * HD)

    kept = jnp.where(section == 0, input_grads[0], input_grads[1])
    sent = jnp.where(section == 0, home0, home1)
    keep = jnp.where(core == section, kept, sent)
    give = swap_pairs(jnp.where(core == section, sent, kept), "gx")
    back_home = join_halves(jnp.where(core == 0, keep, give), jnp.where(core == 0, give, keep))
    return (
        layer_out[None],
        stats_out[None],
        back_home[None],
        gains[None, 0],
        s_attn[None, :, :q_width],
        kv_sum[None, 0],
        kv_sum[None, 1],
        s_out.T[None],
        gains[None, 1],
        s_gate[None],
        s_up[None],
        s_down.T[None],
    )


def solution(mesh):
    rows_cols = P("section", "gx", "gy")
    cols_rows = P("section", "gy", "gx")
    rows_only = P("section", "gx", None)
    gain = P("section", "gx")
    return jax.shard_map(
        on_device,
        mesh=mesh,
        in_specs=(
            P("gx", "gy"), P("gx", "gy"), P(), P(), gain, rows_cols, rows_only, rows_only,
            cols_rows, gain, rows_cols, rows_cols, cols_rows,
        ),
        out_specs=(
            rows_cols, P("section", None, "gx"), rows_cols, gain, rows_cols, rows_only, rows_only,
            cols_rows, gain, rows_cols, rows_cols, cols_rows,
        ),
        check_vma=False,
    )
```

```python
import functools

import jax
import jax.numpy as jnp
from jax import lax
from jax.experimental import pallas as pl
from jax.experimental.pallas import tpu as pltpu
from jax.sharding import PartitionSpec as P

QH = 32
KVH = 4
HD = 64
LAYERS = 2
EPS = 1e-05
BF = jnp.bfloat16
F32 = jnp.float32
MESH = pl.DeviceIdType.MESH
CHUNK = 32
STEPS = 2
GAIN_ROWS = 32
VMEM_LIMIT = 56 * 1024 * 1024
ANY = pl.BlockSpec(memory_space=pl.ANY)
VMEM = pl.BlockSpec(memory_space=pltpu.VMEM)


def mm(left, right, dims=((1,), (0,))):
    return lax.dot_general(left, right, (dims, ((), ())), preferred_element_type=F32)


def swap_pairs(values, axis, by=1):
    count = lax.axis_size(axis)
    return lax.ppermute(values, axis, [(i, i ^ by) for i in range(count)])


def rope_tables(places):
    half_width = HD // 2
    frequency = jnp.power(10000.0, -2.0 * jnp.arange(half_width).astype(F32) / HD)
    angles = frequency[:, None] * places.astype(F32)[None, :]
    return jnp.cos(angles), jnp.sin(angles)


def core_rows(rows, core):
    quarter = rows.shape[0] // 4
    low = lax.dynamic_slice_in_dim(rows, core * quarter, quarter, 0)
    high = lax.dynamic_slice_in_dim(rows, (3 - core) * quarter, quarter, 0)
    return jnp.concatenate([low, high], axis=0)


def join_halves(first, second):
    quarter = first.shape[0] // 2
    return jnp.concatenate(
        [first[:quarter], second[:quarter], second[quarter:], first[quarter:]], axis=0
    )


def chip_groups():
    return [[0, 2], [1, 3]]


def gather_blocks(base):
    return lax.all_gather(base, "gx", axis=0)


def chosen(pair, layer):
    return jnp.where(lax.axis_index("section") == layer, *pair)


def with_own(stack, pair, layer):
    shard = lax.axis_index("gx")
    return lax.dynamic_update_index_in_dim(stack, chosen(pair, layer), shard, 0)


def fused():
    return lax.axis_size("gx") == 4 and lax.axis_size("gy") == 4


def tall(w):
    return w.reshape(-1, w.shape[-1])


def side(w):
    return jnp.concatenate([w[i] for i in range(w.shape[0])], axis=1)


def cut(w, low, high):
    return w[:, :-GAIN_ROWS, low:high]


def shard_sum(product):
    return lax.psum_scatter(product, "gx", scatter_dimension=0, tiled=True)


def chip_sum(product):
    product = product.reshape(-1, product.shape[-1])
    return lax.psum_scatter(
        product, "gx", scatter_dimension=0, tiled=True, axis_index_groups=[[0, 2], [1, 3]]
    )


def line_gather_kernel(mine_ref, out_ref, right_send, right_recv, left_send, left_recv):
    z = lax.axis_index("gy")
    rows, columns = mine_ref.shape
    half = rows // 2
    barrier = pltpu.get_barrier_semaphore()
    for near, there in ((z - 1, z > 0), (z + 1, z < 3)):

        @pl.when(there)
        def _():
            pl.semaphore_signal(barrier, inc=1, device_id={"gy": near}, device_id_type=MESH)

    inner = (z > 0) & (z < 3)
    pl.when(inner)(lambda: pl.semaphore_wait(barrier, 2))
    pl.when(jnp.logical_not(inner))(lambda: pl.semaphore_wait(barrier, 1))

    def block(of):
        of = jnp.clip(of, 0, 3)
        return pl.ds(pl.multiple_of(of * columns, columns), columns)

    out_ref[:, block(z)] = mine_ref[...]

    def copy(step, p, right):
        here = out_ref.at[p * half : (p + 1) * half, block(z - step if right else z + step)]
        send, recv = (right_send, right_recv) if right else (left_send, left_recv)
        return pltpu.make_async_remote_copy(
            src_ref=here, dst_ref=here, send_sem=send.at[2 * step + p],
            recv_sem=recv.at[2 * step + p], device_id={"gy": z + 1 if right else z - 1},
            device_id_type=MESH,
        )

    right_at = [(z < 3) & (z >= step) for step in range(3)]
    left_at = [(z > 0) & (z <= 3 - step) for step in range(3)]
    for step in range(4):
        for p in range(2):
            if step > 0:
                pl.when(z >= step)(lambda: copy(step - 1, p, True).wait_recv())
                pl.when(z <= 3 - step)(lambda: copy(step - 1, p, False).wait_recv())
            if step < 3:
                pl.when(right_at[step])(lambda: copy(step, p, True).start())
                pl.when(left_at[step])(lambda: copy(step, p, False).start())
    for step in range(3):
        for p in range(2):
            pl.when(right_at[step])(lambda: copy(step, p, True).wait_send())
            pl.when(left_at[step])(lambda: copy(step, p, False).wait_send())


def line_gather(mine):
    if not fused():
        return lax.all_gather(mine, "gy", axis=1, tiled=True)
    rows, columns = mine.shape
    dma = pltpu.SemaphoreType.DMA
    return pl.pallas_call(
        line_gather_kernel,
        out_shape=jax.ShapeDtypeStruct((rows, 4 * columns), BF),
        in_specs=[VMEM],
        out_specs=VMEM,
        scratch_shapes=[dma((6,))] * 4,
        compiler_params=pltpu.CompilerParams(
            collective_id=12, has_side_effects=True, vmem_limit_bytes=VMEM_LIMIT
        ),
        cost_estimate=pl.CostEstimate(flops=0, bytes_accessed=150_000_000, transcendentals=0),
        name="line_gather",
    )(mine)


def rope_down(values, cosine, sines):
    half_width = HD // 2
    first, second = values[:half_width], values[half_width:]
    return jnp.concatenate(
        [first * cosine - second * sines, second * cosine + first * sines], axis=0
    )


def fill_bias(bias_ref, key_ref, query_ref, length_ref):
    keys = key_ref[...]
    allowed = (keys <= query_ref[...]) & (keys < length_ref[...])
    bias_ref[...] = jnp.where(allowed, 0.0, -1e30)


def dot_to(left, right, dims):
    return lax.dot_general(left, right, (dims, ((), ())), preferred_element_type=F32)


def attend_kernel(
    q_ref, k_ref, vt_ref, cos_ref, sin_ref, key_ref, query_ref, length_ref,
    heads_ref, rot_ref, lse_ref, bias_ref, out_ref,
):
    fill_bias(bias_ref, key_ref, query_ref, length_ref)

    def head(h, carry):
        here = pl.ds(pl.multiple_of(h * HD, HD), HD)
        rotated = rope_down(q_ref[here, :], cos_ref[...], sin_ref[...]).astype(BF)
        rot_ref[here, :] = rotated
        scaled = (rotated.astype(F32) * HD ** (-0.5)).astype(BF)
        scores = dot_to(k_ref[...], scaled, ((1,), (0,))) + bias_ref[...]
        top = jnp.max(scores, axis=0, keepdims=True)
        exponent = jnp.exp(scores - top)
        total = jnp.sum(exponent, axis=0, keepdims=True)
        probs = (exponent * (1.0 / total)).astype(BF)
        out_ref[here, :] = dot_to(vt_ref[...], probs, ((1,), (0,)))
        lse_ref[pl.ds(h, 1), :] = top + jnp.log(total)
        return carry

    lax.fori_loop(0, q_ref.shape[0] // HD, head, 0)
    heads_ref[...] = out_ref[...].T.astype(BF)


def attend_back_kernel(
    rot_ref, k_ref, kt_ref, v_ref, d_ref, lse_ref, cos_ref, sin_ref, key_ref, query_ref, length_ref,
    dq_ref, dk_ref, dv_ref, bias_ref, out_ref,
):
    fill_bias(bias_ref, key_ref, query_ref, length_ref)
    dk_ref[...] = jnp.zeros_like(dk_ref)
    dv_ref[...] = jnp.zeros_like(dv_ref)
    scaling = HD ** (-0.5)

    def head(h, carry):
        here = pl.ds(pl.multiple_of(h * HD, HD), HD)
        scaled = (rot_ref[here, :].astype(F32) * scaling).astype(BF)
        scores = dot_to(k_ref[...], scaled, ((1,), (0,))) + bias_ref[...]
        probs = jnp.exp(scores - lse_ref[pl.ds(h, 1), :])
        d_probs = dot_to(v_ref[...], d_ref[here, :], ((1,), (0,)))
        delta = jnp.sum(probs * d_probs, axis=0, keepdims=True)
        d_scores = (probs * (d_probs - delta)).astype(BF)
        dk_ref[...] += dot_to(d_scores, scaled, ((1,), (1,)))
        dv_ref[...] += dot_to(probs.astype(BF), d_ref[here, :], ((1,), (1,)))
        dq = dot_to(kt_ref[...], d_scores, ((1,), (0,))) * scaling
        out_ref[here, :] = rope_down(dq, cos_ref[...], -sin_ref[...])
        return carry

    lax.fori_loop(0, rot_ref.shape[0] // HD, head, 0)
    dq_ref[...] = out_ref[...].T.astype(BF)


def attend(q_down, k_all, v_all, tables):
    cosine, sines, keys_at, places, length = tables
    width, rows = q_down.shape
    return pl.pallas_call(
        attend_kernel,
        out_shape=(
            jax.ShapeDtypeStruct((rows, width), BF),
            jax.ShapeDtypeStruct((width, rows), BF),
            jax.ShapeDtypeStruct((width // HD, rows), F32),
        ),
        in_specs=[VMEM] * 8,
        out_specs=(VMEM,) * 3,
        scratch_shapes=[pltpu.VMEM((k_all.shape[0], rows), F32), pltpu.VMEM((width, rows), F32)],
        compiler_params=pltpu.CompilerParams(vmem_limit_bytes=VMEM_LIMIT),
        cost_estimate=pl.CostEstimate(
            flops=16 * width * rows * k_all.shape[0], bytes_accessed=60_000_000, transcendentals=0
        ),
        name="attend",
    )(q_down, k_all, v_all.T, cosine, sines, keys_at[:, None], places[None], length)


def attend_back(rotated, k_all, v_all, d_down, lse, tables):
    cosine, sines, keys_at, places, length = tables
    width, rows = rotated.shape
    return pl.pallas_call(
        attend_back_kernel,
        out_shape=(
            jax.ShapeDtypeStruct((rows, width), BF),
            jax.ShapeDtypeStruct(k_all.shape, F32),
            jax.ShapeDtypeStruct(k_all.shape, F32),
        ),
        in_specs=[VMEM] * 11,
        out_specs=(VMEM,) * 3,
        scratch_shapes=[pltpu.VMEM((k_all.shape[0], rows), F32), pltpu.VMEM((width, rows), F32)],
        compiler_params=pltpu.CompilerParams(vmem_limit_bytes=VMEM_LIMIT),
        cost_estimate=pl.CostEstimate(
            flops=40 * width * rows * k_all.shape[0], bytes_accessed=80_000_000, transcendentals=0
        ),
        name="attend_back",
    )(
        rotated, k_all, k_all.T, v_all, d_down, lse, cosine, sines,
        keys_at[:, None], places[None], length,
    )


def load_blocks(w_refs, w_layer, low, high, target_of, sem):
    shard, home = lax.axis_index("gx"), lax.axis_index("section") == w_layer
    waits = []
    for j in range(4):

        def copy(ref):
            source = ref.at[: ref.shape[0] - GAIN_ROWS, low:high]
            return pltpu.make_async_copy(source, target_of(j), sem.at[j])

        waits.append(copy(w_refs[0].at[j]))
        if len(w_refs) == 1:
            waits[j].start()
        else:
            pl.when(shard != j)(waits[j].start)
            pl.when((shard == j) & home)(copy(w_refs[1]).start)
            pl.when((shard == j) & jnp.logical_not(home))(copy(w_refs[2]).start)
    return waits


def meet_near(*others):
    near = {"gx": lax.axis_index("gx") ^ 1}
    barrier = pltpu.get_barrier_semaphore()
    for peer in (near, *others):
        pl.semaphore_signal(barrier, inc=1, device_id=peer, device_id_type=MESH)
    pl.semaphore_wait(barrier, 1 + len(others))
    return near


def attend_whole_kernel(
    w_layer, listed,
    h_ref, gain_ref, cos_ref, sin_ref, key_ref, query_ref, length_ref, *rest,
):
    w_refs, rest = rest[:listed], rest[listed:]
    (
        heads_ref, normed_ref, ms_ref, rot_ref, lse_ref, k_ref, kt_ref, v_ref,
        w_all, bias_ref, out_ref, q_ref, vt_ref, kv_mine, kv_far, w_sem, send_sem, recv_sem,
    ) = rest
    rows, width = h_ref.shape
    block = width // 4
    q_width = q_ref.shape[0]
    waits = load_blocks(
        w_refs, w_layer, 0, q_width + 2 * HD, lambda j: w_all.at[j * block : (j + 1) * block], w_sem
    )
    near = meet_near()

    def norm(i, carry):
        here = pl.ds(pl.multiple_of(i * 128, 128), 128)
        values = h_ref[here, :].astype(F32)
        square = jnp.mean(values * values, axis=1, keepdims=True)
        ms_ref[here, :] = square
        normed_ref[here, :] = (values * lax.rsqrt(square + EPS) * gain_ref[...]).astype(BF)
        return carry

    lax.fori_loop(0, rows // 128, norm, 0)
    for wait in waits:
        wait.wait()
    kv = dot_to(normed_ref[...], w_all[:, q_width:], ((1,), (0,))).T
    kv = jnp.concatenate([rope_down(kv[:HD], cos_ref[...], sin_ref[...]), kv[HD:]], axis=0)
    kv_mine[...] = kv.T.astype(BF)
    copy = pltpu.make_async_remote_copy(
        src_ref=kv_mine, dst_ref=kv_far, send_sem=send_sem, recv_sem=recv_sem,
        device_id=near, device_id_type=MESH,
    )
    copy.start()
    q_ref[...] = dot_to(normed_ref[...], w_all[:, :q_width], ((1,), (0,))).T
    fill_bias(bias_ref, key_ref, query_ref, length_ref)
    copy.wait()
    for n, ref in enumerate((kv_mine, kv_far)):
        here = pl.ds(n * rows, rows)
        k_ref[here, :] = ref[:, :HD]
        v_ref[here, :] = ref[:, HD:]
        down = ref[...].astype(F32).T.astype(BF)
        kt_ref[:, here] = down[:HD]
        vt_ref[:, here] = down[HD:]

    def head(h, carry):
        here = pl.ds(pl.multiple_of(h * HD, HD), HD)
        rotated = rope_down(q_ref[here, :], cos_ref[...], sin_ref[...]).astype(BF)
        rot_ref[here, :] = rotated
        scaled = (rotated.astype(F32) * HD ** (-0.5)).astype(BF)
        scores = dot_to(k_ref[...], scaled, ((1,), (0,))) + bias_ref[...]
        top = jnp.max(scores, axis=0, keepdims=True)
        exponent = jnp.exp(scores - top)
        total = jnp.sum(exponent, axis=0, keepdims=True)
        probs = (exponent * (1.0 / total)).astype(BF)
        out_ref[here, :] = dot_to(vt_ref[...], probs, ((1,), (0,)))
        lse_ref[pl.ds(h, 1), :] = top + jnp.log(total)
        return carry

    lax.fori_loop(0, q_width // HD, head, 0)
    heads_ref[...] = out_ref[...].T.astype(BF)


def attend_whole_back_kernel(
    w_layer, listed, crosses,
    e1_ref, rot_ref, lse_ref, k_ref, kt_ref, v_ref, cos_ref, sin_ref, key_ref, query_ref,
    length_ref, *rest,
):
    w_refs, rest = rest[:listed], rest[listed:]
    if crosses:
        source_ref, d_qkv_ref, crossed_ref, *rest, x_send, x_recv = rest
    else:
        d_qkv_ref, *rest = rest
    (
        w_all, bias_ref, d_ref, out_ref, dk_ref, dv_ref, dkv_send, dkv_far,
        w_sem, send_sem, recv_sem,
    ) = rest
    rows, width = e1_ref.shape
    block = width // 4
    q_width = rot_ref.shape[0]
    low = q_width + 2 * HD
    waits = load_blocks(w_refs, w_layer, low, low + block, lambda j: w_all.at[j], w_sem)
    section = lax.axis_index("section")
    x_peer = {"section": 1 - section}
    near = meet_near(x_peer) if crosses else meet_near()

    def x_copy():
        return pltpu.make_async_remote_copy(
            src_ref=source_ref, dst_ref=crossed_ref, send_sem=x_send, recv_sem=x_recv,
            device_id=x_peer, device_id_type=MESH,
        )

    if crosses:
        pl.when(section != w_layer)(lambda: x_copy().start())
    fill_bias(bias_ref, key_ref, query_ref, length_ref)
    dk_ref[...] = jnp.zeros_like(dk_ref)
    dv_ref[...] = jnp.zeros_like(dv_ref)
    scaling = HD ** (-0.5)
    for wait in waits:
        wait.wait()
    d_ref[...] = sum(
        dot_to(w_all[j], e1_ref[:, j * block : (j + 1) * block], ((1,), (1,))) for j in range(4)
    ).astype(BF)

    def head(h, carry):
        here = pl.ds(pl.multiple_of(h * HD, HD), HD)
        scaled = (rot_ref[here, :].astype(F32) * scaling).astype(BF)
        scores = dot_to(k_ref[...], scaled, ((1,), (0,))) + bias_ref[...]
        probs = jnp.exp(scores - lse_ref[pl.ds(h, 1), :])
        d_probs = dot_to(v_ref[...], d_ref[here, :], ((1,), (0,)))
        delta = jnp.sum(probs * d_probs, axis=0, keepdims=True)
        d_scores = (probs * (d_probs - delta)).astype(BF)
        dk_ref[...] += dot_to(d_scores, scaled, ((1,), (1,)))
        dv_ref[...] += dot_to(probs.astype(BF), d_ref[here, :], ((1,), (1,)))
        dq = dot_to(kt_ref[...], d_scores, ((1,), (0,))) * scaling
        out_ref[here, :] = rope_down(dq, cos_ref[...], -sin_ref[...])
        return carry

    lax.fori_loop(0, q_width // HD, head, 0)
    dkv_send[:, :HD] = dk_ref[rows:, :]
    dkv_send[:, HD:] = dv_ref[rows:, :]
    copy = pltpu.make_async_remote_copy(
        src_ref=dkv_send, dst_ref=dkv_far, send_sem=send_sem, recv_sem=recv_sem,
        device_id=near, device_id_type=MESH,
    )
    copy.start()
    d_qkv_ref[:, :q_width] = out_ref[...].T.astype(BF)
    copy.wait()
    down = (dkv_far[...].T)
    dk = rope_down(dk_ref[:rows, :].T + down[:HD], cos_ref[...], -sin_ref[...])
    dkv = jnp.concatenate([dk, dv_ref[:rows, :].T + down[HD:]], axis=0)
    d_qkv_ref[:, q_width:] = dkv.T.astype(BF)
    if crosses:
        pl.when(section != w_layer)(lambda: x_copy().wait_send())
        pl.when(section == w_layer)(lambda: x_copy().wait_recv())


def attend_whole(h, gain, w_attn, low, tables, w_layer, ident):
    cosine, sines, keys_at, places, length = tables
    rows, width = h.shape
    keys, q_width = keys_at.shape[0], low - 2 * HD
    w_list = list(w_attn) if isinstance(w_attn, tuple) else [w_attn]
    outs = [
        ((rows, q_width), BF), ((rows, width), BF), ((rows, 1), F32), ((q_width, rows), BF),
        ((q_width // HD, rows), F32), ((keys, HD), BF), ((HD, keys), BF), ((keys, HD), BF),
    ]
    return pl.pallas_call(
        functools.partial(attend_whole_kernel, w_layer, len(w_list)),
        out_shape=tuple(jax.ShapeDtypeStruct(*o) for o in outs),
        in_specs=[VMEM] * 7 + [ANY] * len(w_list),
        out_specs=(VMEM,) * 8,
        scratch_shapes=[
            pltpu.VMEM((width, low), BF),
            pltpu.VMEM((keys, rows), F32),
            pltpu.VMEM((q_width, rows), F32),
            pltpu.VMEM((q_width, rows), F32),
            pltpu.VMEM((HD, keys), BF),
            pltpu.VMEM((rows, 2 * HD), BF),
            pltpu.VMEM((rows, 2 * HD), BF),
            pltpu.SemaphoreType.DMA((4,)),
            pltpu.SemaphoreType.DMA,
            pltpu.SemaphoreType.DMA,
        ],
        compiler_params=pltpu.CompilerParams(
            collective_id=ident, has_side_effects=True, vmem_limit_bytes=VMEM_LIMIT
        ),
        cost_estimate=pl.CostEstimate(
            flops=16 * q_width * rows * keys, bytes_accessed=70_000_000, transcendentals=0
        ),
        name="attend_whole",
    )(h, gain, cosine, sines, keys_at[:, None], places[None], length, *w_list)


def attend_whole_back(
    e1, rotated, lse, k_all, kt_all, v_all, w_attn, tables, w_layer, ident, cross
):
    cosine, sines, keys_at, places, length = tables
    q_width, rows = rotated.shape
    keys, width = keys_at.shape[0], e1.shape[1]
    w_list = list(w_attn) if isinstance(w_attn, tuple) else [w_attn]
    crossing_specs = [jax.ShapeDtypeStruct(x.shape, BF) for x in cross]
    return pl.pallas_call(
        functools.partial(attend_whole_back_kernel, w_layer, len(w_list), len(cross)),
        out_shape=(jax.ShapeDtypeStruct((rows, q_width + 2 * HD), BF), *crossing_specs),
        in_specs=[VMEM] * 11 + [ANY] * (len(w_list) + len(cross)),
        out_specs=(VMEM, *[ANY] * len(cross)),
        scratch_shapes=[
            pltpu.VMEM((4, q_width, width // 4), BF),
            pltpu.VMEM((keys, rows), F32),
            pltpu.VMEM((q_width, rows), BF),
            pltpu.VMEM((q_width, rows), F32),
            pltpu.VMEM((keys, HD), F32),
            pltpu.VMEM((keys, HD), F32),
            pltpu.VMEM((rows, 2 * HD), F32),
            pltpu.VMEM((rows, 2 * HD), F32),
            pltpu.SemaphoreType.DMA((4,)),
            pltpu.SemaphoreType.DMA,
            pltpu.SemaphoreType.DMA,
        ]
        + [pltpu.SemaphoreType.DMA] * 2 * len(cross),
        compiler_params=pltpu.CompilerParams(
            collective_id=ident, has_side_effects=True, vmem_limit_bytes=VMEM_LIMIT
        ),
        cost_estimate=pl.CostEstimate(
            flops=40 * q_width * rows * keys, bytes_accessed=90_000_000, transcendentals=0
        ),
        name="attend_whole_back",
    )(
        e1, rotated, lse, k_all, kt_all, v_all, cosine, sines, keys_at[:, None], places[None],
        length, *w_list, *cross,
    )


def line_kernel(
    kind, masked, low, high, deps, gathers, layer, exchange, triples, w_layer, crosses, homing,
    gain_ref, resid_ref, valid_ref, h_ref, square_ref, *rest,
):
    forward = kind in ("out", "mlp")
    wide = kind in ("mlp", "mlp_back")
    if kind == "mlp":
        lhs_refs = []
    elif kind == "mlp_back":
        lhs_refs, rest = rest[:4], rest[4:]
    else:
        lhs_refs, rest = rest[:1], rest[1:]
    w_count = 3 if wide else 1
    w_refs = []
    for triple in triples:
        w_refs.append(rest[: 3 if triple else 1])
        rest = rest[3 if triple else 1 :]
    rest = rest[deps:]
    base_refs, rest = rest[: 2 * gathers], rest[2 * gathers :]
    cross_refs, rest = rest[: len(crosses)], rest[len(crosses) :]
    out_ref, rest = rest[0], rest[1:]
    if kind == "mlp":
        normed_ref, ms_ref, gate_ref, up_ref, hidden_ref = rest[:5]
        rest = rest[5:]
    elif kind == "mlp_back":
        product_refs, rest = rest[:3], rest[3:]
        arrived_refs, rest = rest[:exchange], rest[exchange:]
    block_refs, rest = rest[:gathers], rest[gathers:]
    crossed_refs, rest = rest[: len(crosses)], rest[len(crosses) :]
    if homing:
        home_ref, home_send, home_recv = rest[0], *rest[-2:]
        rest = rest[1:-2]
    if crosses:
        x_send, x_recv = rest[-2:]
        rest = rest[:-2]
    w_alls, rest = rest[:w_count], rest[w_count:]
    (
        part, from_end, from_mid, pair,
        w_sem, up_send, up_recv, mid_send, mid_recv, fin_send, fin_recv,
    ) = rest[:11]
    if gathers:
        far_send, far_recv, near_send, near_recv, cross_send, cross_recv = rest[11:]
    if kind == "mlp_back":
        (
            d_gate_ref, d_up_ref, far_normed, far_dm, far_hidden, far_d_gate, far_d_up, stage,
            give_sem, take_sem, stage_sem,
        ) = rest[11:22]
    if exchange:
        y_stage, y_send, y_recv = rest[22:]
    shard = lax.axis_index("gx")
    far, near = shard ^ 2, shard ^ 1
    section = lax.axis_index("section")
    rows, width = resid_ref.shape
    columns = width // 4
    count = rows // CHUNK
    z = lax.axis_index("gy")
    middle = (z == 1) | (z == 2)
    end_of = jnp.where(z == 1, 0, 3)
    mid_of = jnp.where(z == 0, 1, 2)
    across = 3 - z

    def loading(w, j, cut_of, target, slot):
        whole = w_refs[w]
        copies = [(None, pltpu.make_async_copy(cut_of(whole[0].at[j]), target, w_sem.at[slot]))]
        if triples[w]:
            home = section == w_layer
            copies = [(shard != j, copies[0][1])]
            for ref, holds in zip(whole[1:], (home, jnp.logical_not(home))):
                copy = pltpu.make_async_copy(cut_of(ref), target, w_sem.at[slot])
                copies.append(((shard == j) & holds, copy))
        return copies

    loads, downs = [], []
    if wide:
        hidden_width = w_alls[0].shape[1]
        for x0 in range(0, hidden_width, 512):
            x1 = min(x0 + 512, hidden_width)
            for w in range(2):
                for j in range(4):
                    target = w_alls[w].at[j * columns : (j + 1) * columns, x0:x1]
                    loads.append(loading(w, j, lambda ref: ref.at[:, x0:x1], target, len(loads)))
        for j in range(4):
            downs.append(loading(2, j, lambda ref: ref, w_alls[2].at[j], len(loads) + j))
    else:
        for j in range(4):
            cut_of = lambda ref: ref.at[: ref.shape[0] - GAIN_ROWS, low:high]
            loads.append(loading(0, j, cut_of, w_alls[0].at[j], j))
    for load in downs + loads if kind == "mlp_back" else loads + downs:
        for holds, copy in load:
            if holds is None:
                copy.start()
            else:
                pl.when(holds)(copy.start)
    loads, downs = [x[0][1] for x in loads], [x[0][1] for x in downs]

    barrier = pltpu.get_barrier_semaphore()
    peers = []
    if gathers:
        peers = [{"gx": far}, {"gx": near}, {"section": 1 - section}]
    elif kind == "mlp_back":
        peers = [{"gx": near}] + [{"gx": far}] * (exchange > 0)
    if crosses:
        assert not gathers
        peers.append({"section": 1 - section})
    beside = len(peers)
    for peer in peers:
        pl.semaphore_signal(barrier, inc=1, device_id=peer, device_id_type=MESH)

    @pl.when(middle)
    def _():
        pl.semaphore_signal(barrier, inc=1, device_id={"gy": end_of}, device_id_type=MESH)
        pl.semaphore_signal(barrier, inc=1, device_id={"gy": across}, device_id_type=MESH)
        pl.semaphore_wait(barrier, 2 + beside)

    @pl.when(jnp.logical_not(middle))
    def _():
        pl.semaphore_signal(barrier, inc=1, device_id={"gy": mid_of}, device_id_type=MESH)
        pl.semaphore_wait(barrier, 1 + beside)

    x_peer = {"section": 1 - section}

    def x_copy(k):
        return pltpu.make_async_remote_copy(
            src_ref=cross_refs[k], dst_ref=crossed_refs[k], send_sem=x_send.at[k],
            recv_sem=x_recv.at[k], device_id=x_peer, device_id_type=MESH,
        )

    def home_copy(rows_here):
        return pltpu.make_async_remote_copy(
            src_ref=out_ref.at[rows_here, pl.ds(pl.multiple_of(z * columns, columns), columns)],
            dst_ref=home_ref.at[rows_here, :], send_sem=home_send, recv_sem=home_recv,
            device_id=x_peer, device_id_type=MESH,
        )

    def home_start(i):
        if homing:
            here = pl.ds(pl.multiple_of(i * CHUNK, CHUNK), CHUNK)
            pl.when(section != w_layer)(lambda: home_copy(here).start())

    def x_sends(k):
        return section != crosses[k] if crosses[k] < 2 else section >= 0

    def x_takes(k):
        return section == crosses[k] if crosses[k] < 2 else section >= 0

    for k in range(len(crosses)):
        pl.when(x_sends(k))(lambda k=k: x_copy(k).start())

    def half_of(ref, k, which):
        size = base_refs[2 * k].shape[0] // 2
        return ref.at[pl.ds(pl.multiple_of(which * size, 16), size), :]

    def far_copy(k, source):
        return pltpu.make_async_remote_copy(
            src_ref=half_of(source, k, section),
            dst_ref=half_of(block_refs[k].at[shard], k, section),
            send_sem=far_send.at[k], recv_sem=far_recv.at[k],
            device_id={"gx": far}, device_id_type=MESH,
        )

    def near_copy(k, source):
        return pltpu.make_async_remote_copy(
            src_ref=source, dst_ref=block_refs[k].at[shard], send_sem=near_send.at[3 * k],
            recv_sem=near_recv.at[3 * k], device_id={"gx": near}, device_id_type=MESH,
        )

    def cross_copy(k):
        rows_here = half_of(block_refs[k].at[far], k, section)
        return pltpu.make_async_remote_copy(
            src_ref=rows_here, dst_ref=rows_here, send_sem=cross_send.at[k],
            recv_sem=cross_recv.at[k], device_id=x_peer, device_id_type=MESH,
        )

    def pass_copy(k, late):
        rows_here = half_of(block_refs[k].at[far], k, 1 - section if late else section)
        return pltpu.make_async_remote_copy(
            src_ref=rows_here, dst_ref=rows_here, send_sem=near_send.at[3 * k + 1 + late],
            recv_sem=near_recv.at[3 * k + 1 + late], device_id={"gx": near}, device_id_type=MESH,
        )

    at_home = section == layer

    def from_base(k, starts):
        for ref, holds in zip(base_refs[2 * k : 2 * k + 2], (at_home, jnp.logical_not(at_home))):

            @pl.when(holds)
            def _():
                for make in starts:
                    make(k, ref).start()

    def gather_middle(k):
        far_copy(k, base_refs[2 * k]).wait_recv()
        cross_copy(k).start()
        pass_copy(k, 0).start()

    def gather_late(k):
        cross_copy(k).wait_recv()
        pass_copy(k, 1).start()

    if gathers:
        from_base(0, [far_copy])
    for k in range(gathers):
        from_base(k, [near_copy])

    half = rows // STEPS
    core = lax.rem(shard, 2)

    def give(slot, source, target):
        return pltpu.make_async_remote_copy(
            src_ref=source, dst_ref=target, send_sem=give_sem.at[slot],
            recv_sem=take_sem.at[slot], device_id={"gx": near}, device_id_type=MESH,
        )

    def chip_columns(ref, y, of):
        return ref.at[:, pl.ds(pl.multiple_of((2 * y + of) * columns, columns), columns)]

    def step_rows(ref, step):
        return ref.at[pl.ds(pl.multiple_of(step * half, half), half), :]

    if kind == "mlp_back":
        saved_gate, saved_up, saved_normed, saved_hidden = lhs_refs
        early = [give(0, saved_hidden, far_hidden)]
        for y in range(2):
            early.append(give(1 + y, chip_columns(resid_ref, y, 1 - core), far_dm.at[y]))
        for y in range(2):
            early.append(give(3 + y, chip_columns(saved_normed, y, 1 - core), far_normed.at[y]))
        for copy in early:
            copy.start()

    def give_step(step):
        return [
            give(5 + step, step_rows(d_gate_ref, step), step_rows(far_d_gate, step)),
            give(5 + STEPS + step, step_rows(d_up_ref, step), step_rows(far_d_up, step)),
        ]

    if not wide:
        for load in loads:
            load.wait()

    def at_first(step, copies):
        @pl.when(step == 0)
        def _():
            for copy in copies:
                copy.wait()

    def rows_at(ref, i):
        return ref.at[pl.ds(pl.multiple_of(i * CHUNK, CHUNK), CHUNK), :]

    def up_copy(i):
        return pltpu.make_async_remote_copy(
            src_ref=rows_at(part, i), dst_ref=rows_at(from_end, i), send_sem=up_send.at[i],
            recv_sem=up_recv.at[i], device_id={"gy": mid_of}, device_id_type=MESH,
        )

    def mid_copy(i):
        return pltpu.make_async_remote_copy(
            src_ref=rows_at(pair, i), dst_ref=rows_at(from_mid, i), send_sem=mid_send.at[i],
            recv_sem=mid_recv.at[i], device_id={"gy": across}, device_id_type=MESH,
        )

    def fin_copy(i):
        return pltpu.make_async_remote_copy(
            src_ref=rows_at(out_ref, i), dst_ref=rows_at(out_ref, i), send_sem=fin_send.at[i],
            recv_sem=fin_recv.at[i], device_id={"gy": end_of}, device_id_type=MESH,
        )

    def dot(left, right, transposed=False):
        dims = (((1,), (1 if transposed else 0,)), ((), ()))
        return lax.dot_general(left, right, dims, preferred_element_type=F32)

    def spans(extent):
        return [(x, min(x + 512, extent)) for x in range(0, extent, 512)]

    if wide:
        w_gate, w_up, w_down = w_alls

    def product(step, carry):
        here = pl.ds(pl.multiple_of(step * half, half), half)
        if kind == "mlp":
            values = resid_ref[here, :].astype(F32)
            square = jnp.mean(values * values, axis=1, keepdims=True)
            ms_ref[here, :] = square
            normed_ref[here, :] = (values * lax.rsqrt(square + EPS) * gain_ref[...]).astype(BF)
            for n, (x0, x1) in enumerate(spans(w_gate.shape[1])):
                at_first(step, loads[8 * n : 8 * n + 8])
                gate = dot(normed_ref[here, :], w_gate[:, x0:x1])
                up = dot(normed_ref[here, :], w_up[:, x0:x1])
                gate_ref[here, x0:x1] = gate.astype(BF)
                up_ref[here, x0:x1] = up.astype(BF)
                hidden_ref[here, x0:x1] = (gate * jax.nn.sigmoid(gate) * up).astype(BF)
        if kind == "mlp_back":
            at_first(step, downs)
            for x0, x1 in spans(w_gate.shape[1]):
                d_hidden = sum(
                    dot(resid_ref[here, j * columns : (j + 1) * columns], w_down[j, x0:x1, :], True)
                    for j in range(4)
                )
                gate = saved_gate[here, x0:x1].astype(F32)
                up = saved_up[here, x0:x1].astype(F32)
                sigmoid = jax.nn.sigmoid(gate)
                d_up_ref[here, x0:x1] = (d_hidden * (gate * sigmoid)).astype(BF)
                d_gate_ref[here, x0:x1] = (
                    d_hidden * up * sigmoid * (1.0 + gate * (1.0 - sigmoid))
                ).astype(BF)
            for copy in give_step(step):
                copy.start()
        if wide:
            at_first(step, downs if kind == "mlp" else loads)
        for j in range(4):
            span = slice(j * columns, (j + 1) * columns)
            if kind == "out":
                value = dot(lhs_refs[0][here, :], w_alls[0][j])
            elif kind == "mlp":
                value = dot(hidden_ref[here, :], w_down[j])
            elif kind == "mlp_back":
                value = dot(d_gate_ref[here, :], w_gate[span, :], True)
                value += dot(d_up_ref[here, :], w_up[span, :], True)
            else:
                value = dot(lhs_refs[0][here, :], w_alls[0][j], True)
            part[here, span] = value.astype(BF)

        @pl.when(jnp.logical_not(middle))
        def _():
            def send(i, inner):
                up_copy(step * (count // STEPS) + i).start()
                return inner

            lax.fori_loop(0, count // STEPS, send, 0)

        return carry

    lax.fori_loop(0, STEPS, product, 0)

    def finish(i):
        mid_copy(i).wait_recv()
        here = pl.ds(pl.multiple_of(i * CHUNK, CHUNK), CHUNK)
        total = pair[here, :].astype(F32) + from_mid[here, :].astype(F32)
        resid = resid_ref[here, :].astype(F32)
        if forward:
            result = resid + total
            if masked:
                result = result * valid_ref[here, :]
        else:
            values = h_ref[here, :].astype(F32)
            scaled = total * gain_ref[...]
            ratio = lax.rsqrt(square_ref[here, :] + EPS)
            mean_term = jnp.sum(scaled * values, axis=1, keepdims=True) * (1.0 / width)
            result = resid + ratio * scaled - values * (ratio * ratio * ratio) * mean_term
        out_ref[here, :] = result.astype(BF)
        fin_copy(i).start()
        home_start(i)

    tile = columns // 2

    def tile_rows(sub):
        return pl.ds(pl.multiple_of(sub % 2 * tile, tile), tile)

    def stage_copy(number, sub, slot):
        target = product_refs[number].at[sub // 2, tile_rows(sub), :]
        return pltpu.make_async_copy(stage.at[slot], target, stage_sem.at[slot])

    def y_copy(number, sub, slot):
        return pltpu.make_async_remote_copy(
            src_ref=y_stage.at[2 * number + slot], dst_ref=arrived_refs[number].at[tile_rows(sub), :],
            send_sem=y_send.at[2 * number + slot], recv_sem=y_recv.at[2 * number + slot],
            device_id={"gx": far}, device_id_type=MESH,
        )

    def gradient_tile(number, sub):
        slot = sub % 2
        left, far_left, right, far_right = (
            (resid_ref, far_dm, saved_hidden, far_hidden),
            (saved_normed, far_normed, d_gate_ref, far_d_gate),
            (saved_normed, far_normed, d_up_ref, far_d_up),
        )[number]

        @pl.when(sub == 0)
        def _():
            waits = [early[:3], early[3:] + give_all[:STEPS], give_all[STEPS:]][number]
            for copy in waits:
                copy.wait_recv()

        if number >= exchange:

            @pl.when((sub >= 2) | (number > 0))
            def _():
                stage_copy(number, sub, slot).wait()

        elif number > 0:

            @pl.when(sub >= 2)
            def _():
                stage_copy(number, sub - 2, slot).wait()

        y = sub // 2
        if number < exchange:
            y = jnp.where(sub < 2, 1 - lax.div(shard, 2), lax.div(shard, 2))
        start = (y * 2 + core) * columns + sub % 2 * tile
        mine = left[:, pl.ds(pl.multiple_of(start, tile), tile)]
        theirs = far_left[y, :, tile_rows(sub)]
        value = dot_to(mine, right[...], ((0,), (0,))) + dot_to(theirs, far_right[...], ((0,), (0,)))
        if number < exchange:

            @pl.when(sub < 2)
            def _():
                y_stage[2 * number + slot] = value.astype(BF)
                y_copy(number, sub, slot).start()

            @pl.when(sub >= 2)
            def _():
                stage[slot] = value.astype(BF)
                stage_copy(number, sub - 2, slot).start()

        else:
            stage[slot] = value.astype(BF)
            stage_copy(number, sub, slot).start()

    if kind == "mlp_back":
        give_all = [x for pair in zip(*(give_step(n) for n in range(STEPS))) for x in pair]

    def beside_step(i, ahead=0):
        pass_on(i + ahead)
        if kind == "mlp_back":
            for number in range(3):
                first = 3 + 4 * number

                @pl.when((i >= first) & (i < first + 4))
                def _():
                    gradient_tile(number, i - first)

    def pass_on(i):
        if gathers == 2:
            at(2, i, lambda: from_base(1, [far_copy]))
            at(6, i, lambda: gather_middle(0))
            at(10, i, lambda: gather_middle(1))
            at(11, i, lambda: gather_late(0))
            at(15, i, lambda: gather_late(1))

    def at(sixteenth, i, action):
        pl.when(i == count * sixteenth // 16)(action)

    @pl.when(middle)
    def _():
        def step(i, carry):
            up_copy(i).wait_recv()
            here = pl.ds(pl.multiple_of(i * CHUNK, CHUNK), CHUNK)
            pair[here, :] = (part[here, :].astype(F32) + from_end[here, :].astype(F32)).astype(BF)
            mid_copy(i).start()

            @pl.when(i >= 1)
            def _():
                finish(i - 1)

            beside_step(i)
            return carry

        lax.fori_loop(0, count, step, 0)
        finish(count - 1)

        def drain(i, carry):
            mid_copy(i).wait_send()
            fin_copy(i).wait_send()
            return carry

        lax.fori_loop(0, count, drain, 0)

    @pl.when(jnp.logical_not(middle))
    def _():
        if gathers == 2:
            from_base(1, [far_copy])

        def drain(i, carry):
            up_copy(i).wait_send()
            fin_copy(i).wait_recv()
            home_start(i)
            beside_step(i, 3)
            return carry

        lax.fori_loop(0, count, drain, 0)

    if kind == "mlp_back":
        for slot in range(2):
            stage_copy(2, 2 + slot, slot).wait()
        for copy in early + give_all:
            copy.wait_send()
        for number in range(exchange):
            for slot in range(2):
                y_copy(number, slot, slot).wait()
    if homing:
        every = pl.ds(0, rows)
        pl.when(section != w_layer)(lambda: home_copy(every).wait_send())
        pl.when(section == w_layer)(lambda: home_copy(every).wait_recv())
    for k in range(len(crosses)):
        pl.when(x_sends(k))(lambda k=k: x_copy(k).wait_send())
        pl.when(x_takes(k))(lambda k=k: x_copy(k).wait_recv())
    for k in range(gathers):
        far_copy(k, base_refs[2 * k]).wait_send()
        near_copy(k, base_refs[2 * k]).wait()
        cross_copy(k).wait_send()
        pass_copy(k, 0).wait()
        pass_copy(k, 1).wait()


def line_sum(kind, ident, resid, weights, lhs=(), gain=None, valid=None, back=None, low=0, high=0, deps=(), bases=(), layer=0, exchange=0, w_layer=0, crosses=(), homing=False):
    rows, width = resid.shape
    one = jnp.ones((rows, 1), F32)
    h, square = back if back is not None else (jnp.zeros((16, 128), BF), jnp.zeros((8, 1), F32))
    gain = jnp.zeros((1, width), F32) if gain is None else gain
    wide = kind in ("mlp", "mlp_back")
    hidden = 0
    if wide:
        hidden = (weights[2][0] if isinstance(weights[2], tuple) else weights[2]).shape[1]
    w_scratch = []
    triples = [isinstance(w, tuple) for w in weights]
    w_flat = [x for w in weights for x in (w if isinstance(w, tuple) else (w,))]
    for i, w in enumerate(weights):
        _, depth, across = (w[0] if isinstance(w, tuple) else w).shape
        if wide and i < 2:
            w_scratch.append(pltpu.VMEM((width, across), BF))
        else:
            shape = (4, depth, across) if wide else (4, depth - GAIN_ROWS, high - low)
            w_scratch.append(pltpu.VMEM(shape, BF))
    outs, products, beside = [((rows, width), BF)], [], []
    if kind == "mlp":
        outs += [((rows, width), BF), ((rows, 1), F32)] + [((rows, hidden), BF)] * 3
    elif kind == "mlp_back":
        products = [((1 if n < exchange else 2, width // 4, hidden), BF) for n in range(3)]
        products += [((width // 4, hidden), BF)] * exchange
        half_block = pltpu.VMEM((2, rows, width // 4), BF)
        beside = [pltpu.VMEM((rows, hidden), BF)] * 2 + [half_block] * 2
        beside += [pltpu.VMEM((rows, hidden), BF)] * 3 + [pltpu.VMEM((2, width // 8, hidden), BF)]
        beside += [pltpu.SemaphoreType.DMA((n,)) for n in (5 + 2 * STEPS, 5 + 2 * STEPS, 2)]
        if exchange:
            beside += [pltpu.VMEM((2 * exchange, width // 8, hidden), BF)]
            beside += [pltpu.SemaphoreType.DMA((2 * exchange,))] * 2
    blocks = [((4,) + base[0].shape, BF) for base in bases]
    pairs = [x for base in bases for x in base]
    crossed = [(x[0].shape, BF) for x in crosses] + [((rows, width // 4), BF)] * homing
    depth = 3 * hidden if wide else lhs[0].shape[1]
    count = rows // CHUNK
    dma = pltpu.SemaphoreType.DMA
    return pl.pallas_call(
        functools.partial(
            line_kernel, kind, valid is not None, low, high, len(deps), len(bases), layer, exchange,
            triples, w_layer, [x[1] for x in crosses], homing,
        ),
        out_shape=tuple(jax.ShapeDtypeStruct(*o) for o in outs + products + blocks + crossed),
        in_specs=[VMEM] * (5 + len(lhs)) + [ANY] * (len(w_flat) + len(deps) + len(pairs) + len(crosses)),
        out_specs=tuple([VMEM] * len(outs) + [ANY] * len(products + blocks + crossed)),
        scratch_shapes=w_scratch
        + [pltpu.VMEM((rows, width), BF)] * 4
        + [dma((8 * -(-hidden // 512) + 4,))]
        + [dma((count,))] * 6
        + [dma((n * len(bases),)) for n in (1, 1, 3, 3, 1, 1) if bases]
        + beside
        + [dma((len(crosses),))] * 2 * bool(crosses)
        + [dma] * 2 * homing,
        compiler_params=pltpu.CompilerParams(
            collective_id=ident, has_side_effects=True, vmem_limit_bytes=VMEM_LIMIT
        ),
        cost_estimate=pl.CostEstimate(
            flops=2 * rows * depth * width, bytes_accessed=200 * 1024 * 1024, transcendentals=0
        ),
        name="line_" + kind,
    )(
        gain, resid, one if valid is None else valid, h, square, *lhs, *w_flat, *deps, *pairs,
        *(x[0] for x in crosses),
    )


def plain_sum(total):
    return lax.psum(total.astype(BF), "gy").astype(F32)


def normed(h, gain):
    values = h.astype(F32)
    square = jnp.mean(values * values, axis=1, keepdims=True)
    return square, (values * lax.rsqrt(square + EPS) * gain).astype(BF)


def norm_back(d_normed, h, square, gain):
    values = h.astype(F32)
    ratio = lax.rsqrt(square + EPS)
    scaled = d_normed * gain
    mean_term = jnp.mean(scaled * values, axis=1, keepdims=True)
    return ratio * scaled - values * (ratio * ratio * ratio) * mean_term


def attention_forward(h, gain, w_attn, low, tables, ident, bases, layer, w_layer, deps=()):
    rows, width = h.shape
    high = low + width // lax.axis_size("gx")
    q_width = low - 2 * HD
    if fused():
        heads, n1, square, rotated, lse, k_all, kt_all, v_all = attend_whole(
            h, gain, w_attn, low, tables, w_layer, ident + 8
        )
        h1, *stacks = line_sum(
            "out", ident, h, [w_attn], (heads,), low=low, high=high,
            deps=deps, bases=bases, layer=layer, w_layer=w_layer,
        )
        blocks = [(x, *pair) for x, pair in zip(stacks, bases)]
    else:
        cosine, sines = tables[:2]
        square, n1 = normed(h, gain)
        q_down = mm(tall(cut(w_attn, 0, q_width)), n1, ((0,), (1,)))
        kv = mm(n1, tall(cut(w_attn, q_width, low)))
        k_rot = rope_down(kv[:, :HD].T, cosine, sines).T.astype(BF)
        kv = jnp.concatenate([k_rot, kv[:, HD:].astype(BF)], axis=1)
        kv_all = jnp.concatenate([kv, swap_pairs(kv, "gx")], axis=0)
        k_all, v_all = kv_all[:, :HD], kv_all[:, HD:]
        kt_all = k_all.T
        heads, rotated, lse = attend(q_down, k_all, v_all, tables)
        h1 = (h.astype(F32) + plain_sum(mm(heads, side(cut(w_attn, low, high))))).astype(BF)
        blocks = [gather_blocks(chosen(x, layer)) for x in bases]
    return h1, square, blocks, (h, square, n1, rotated, lse, k_all, kt_all, v_all, heads)


def mlp_forward(h1, gain, weights, valid, ident, bases=(), layer=0, w_layer=0):
    if fused():
        result, n2, square, gate, up, hidden, *stacks = line_sum(
            "mlp", ident, h1, weights, gain=gain, valid=valid, bases=bases, layer=layer,
            w_layer=w_layer,
        )
        blocks = [(x, *pair) for x, pair in zip(stacks, bases)]
    else:
        square, n2 = normed(h1, gain)
        gate = mm(n2, tall(weights[0]))
        up = mm(n2, tall(weights[1]))
        hidden = (gate * jax.nn.sigmoid(gate) * up).astype(BF)
        gate, up = gate.astype(BF), up.astype(BF)
        result = h1.astype(F32) + plain_sum(mm(hidden, side(weights[2])))
        result = (result * valid).astype(BF)
        blocks = [gather_blocks(chosen(x, layer)) for x in bases]
    return result, square, blocks, (h1, square, n2, gate, up, hidden)


def mlp_backward(dm, gain, weights, saved, ident, w_layer, crosses=(), deps=(), exchange=1):
    h1, square, n2, gate, up, hidden = saved
    if fused():
        e1, *products = line_sum(
            "mlp_back", ident, dm, weights, (gate, up, n2, hidden), gain=gain,
            back=(h1, square), exchange=exchange, w_layer=w_layer, crosses=crosses, deps=deps,
        )
        return e1, products[:4], products[4:]
    gate, up = gate.astype(F32), up.astype(F32)
    d_hidden = mm(dm, side(weights[2]), ((1,), (1,)))
    sigmoid = jax.nn.sigmoid(gate)
    d_gate = (d_hidden * up * sigmoid * (1.0 + gate * (1.0 - sigmoid))).astype(BF)
    d_up = (d_hidden * (gate * sigmoid)).astype(BF)
    total = mm(d_gate, tall(weights[0]), ((1,), (1,))) + mm(d_up, tall(weights[1]), ((1,), (1,)))
    e1 = (dm.astype(F32) + norm_back(plain_sum(total), h1, square, gain)).astype(BF)
    turn = ((0,), (0,))
    products = [mm(dm, hidden, turn), mm(n2, d_gate, turn), mm(n2, d_up, turn)]
    return e1, [p.astype(BF) for p in products], crossing(crosses)


def crossing(crosses):
    pairs = ([(1, 0)], [(0, 1)], [(0, 1), (1, 0)])
    return [lax.ppermute(x, "section", pairs[way]) for x, way in crosses]


def mlp_sums(products):
    if not fused():
        return [shard_sum(p) for p in products]
    down, gate, up, arrived = products
    first = (down[0].astype(F32) + arrived.astype(F32)).astype(BF)
    return [first, chip_sum(gate), chip_sum(up)]


def attention_backward(e1, w_attn, low, tables, saved, w_layer, ident, cross=()):
    h, square, n1, rotated, lse, k_all, kt_all, v_all, heads = saved
    rows, width = h.shape
    if fused():
        d_qkv, *crossed = attend_whole_back(
            e1, rotated, lse, k_all, kt_all, v_all, w_attn, tables, w_layer, ident, cross
        )
    else:
        cosine, sines = tables[:2]
        w_o = side(cut(w_attn, low, low + width // lax.axis_size("gx")))
        d_down = mm(w_o, e1, ((1,), (1,))).astype(BF)
        dq, dk, dv = attend_back(rotated, k_all, v_all, d_down, lse, tables)
        dkv = jnp.concatenate([dk, dv], axis=1)
        dkv = dkv[:rows] + swap_pairs(dkv[rows:], "gx")
        dk = rope_down(dkv[:, :HD].T, cosine, -sines).T
        d_qkv = jnp.concatenate([dq, dk.astype(BF), dkv[:, HD:].astype(BF)], axis=1)
        crossed = crossing([(x, w_layer) for x in cross])
    turn = ((0,), (0,))
    products = [mm(n1, d_qkv, turn).astype(BF), mm(e1, heads, turn).astype(BF)]
    return d_qkv, jnp.concatenate(products, axis=1), crossed


def attention_end(d_qkv, e1, w_attn, gain, saved, ident, w_layer, deps, crosses):
    h, square = saved[:2]
    qkv_width = d_qkv.shape[1]
    if fused():
        grad, *crossed = line_sum(
            "back", ident, e1, [w_attn], (d_qkv,), gain=gain, back=(h, square),
            low=0, high=qkv_width, deps=deps, crosses=crosses, w_layer=w_layer, homing=True,
        )
        return grad, crossed[-1], crossed[:-1]
    total = plain_sum(mm(d_qkv, tall(cut(w_attn, 0, qkv_width)), ((1,), (1,))))
    grad = (e1.astype(F32) + norm_back(total, h, square, gain)).astype(BF)
    width = grad.shape[1] // lax.axis_size("gy")
    part = lax.dynamic_slice_in_dim(grad, lax.axis_index("gy") * width, width, 1)
    home, *crossed = crossing([(part, w_layer), *crosses])
    return grad, home, crossed


def on_device(
    hidden_in, out_grad, lengths, dealing, attn_gain, w_query, w_key, w_value, w_out,
    mlp_gain, w_gate, w_up, w_down,
):
    shards = lax.axis_size("gx")
    shard = lax.axis_index("gx")
    section = lax.axis_index("section")
    column = lax.axis_index("gy")
    core = shard % 2
    sequence = (shard // 2) * 2 + section
    span, width = hidden_in.shape
    half = span // 2
    seq_length = lax.dynamic_index_in_dim(lengths, sequence, keepdims=False)

    both = jnp.concatenate([hidden_in, out_grad], axis=1)
    mine = core_rows(both, core)
    theirs = swap_pairs(core_rows(both, 1 - core), "gx")
    mine = jnp.where(core == section, mine, theirs)
    h = line_gather(mine[:, :width])

    kv_head = column * (w_query.shape[2] // HD) // (QH // KVH)
    low = w_query.shape[2] + 2 * HD
    both_gains = jnp.stack([attn_gain[0], mlp_gain[0]])
    block_rows = both_gains.shape[1]
    attn_own = jnp.concatenate(
        [
            w_query[0],
            lax.dynamic_slice_in_dim(w_key[0], kv_head * HD, HD, 1),
            lax.dynamic_slice_in_dim(w_value[0], kv_head * HD, HD, 1),
            w_out[0],
        ],
        axis=1,
    )
    gain_rows = jnp.pad(both_gains, ((0, GAIN_ROWS - 2), (0, attn_own.shape[1] - block_rows)))
    attn_own = jnp.concatenate([attn_own, gain_rows + theirs[:1, :1] * 0], axis=0)
    own = (attn_own, w_gate[0], w_up[0], w_down[0])
    first = second = [(array, swap_pairs(array, "section")) for array in own]

    def gains_of(w_attn, pair):
        cut_of = lambda w: w[..., block_rows : block_rows + 2, :block_rows]
        rows = cut_of(w_attn[0] if isinstance(w_attn, tuple) else w_attn)
        if isinstance(w_attn, tuple):
            rows = with_own(rows, [cut_of(x) for x in pair], 1)
        return rows.transpose(1, 0, 2).reshape(2, 1, -1).astype(F32)

    here = core_rows(jnp.arange(span), core)
    there = core_rows(jnp.arange(span), 1 - core)
    keys_at = jnp.concatenate([here, there])
    valid = (here < seq_length)[:, None].astype(F32)
    tables = (*rope_tables(here), keys_at, here, seq_length.reshape(1, 1))

    attn0 = gather_blocks(chosen(first[0], 0) + h[:1, :1] * 0)
    d_out = line_gather(mine[:, width:] + h[:1, :1] * 0)
    gate0 = gather_blocks(chosen(first[1], 0) + d_out[:1, :1] * 0)
    gains0 = gains_of(attn0, first[0])
    h1, square_a, blocks, saved_a0 = attention_forward(
        h, gains0[0], attn0, low, tables, 0, first[2:], 0, 0, (gate0,)
    )
    mlp0 = [gate0] + blocks
    h, square_m, (attn1, gate1), saved_m0 = mlp_forward(
        h1, gains0[1], mlp0, valid, 1, second[:2], 1
    )
    gains1 = gains_of(attn1, second[0])
    outputs, squares = [h], [square_a, square_m]
    h1, square_a, blocks, saved_a1 = attention_forward(
        h, gains1[0], attn1, low, tables, 2, second[2:], 1, 1
    )
    mlp1 = [gate1] + blocks
    h, square_m, _, saved_m1 = mlp_forward(h1, gains1[1], mlp1, valid, 3, w_layer=1)
    outputs.append(h)
    squares = jnp.concatenate(squares + [square_a, square_m], axis=1)
    rms = (jnp.sqrt(squares + EPS) * valid).T
    statistics = [rms[:2], rms[2:]]
    outputs = [lax.dynamic_slice_in_dim(x, column * width, width, 1) for x in outputs]

    dm = (d_out.astype(F32) * valid).astype(BF)
    e1, products, _ = mlp_backward(dm, gains1[1], mlp1, saved_m1, 4, 1)
    local1 = mlp_sums(products)

    both = []
    for output, stat in zip(outputs, statistics):
        high = stat.astype(BF)
        rest = (stat - high.astype(F32)).astype(BF)
        parts = jnp.concatenate([high, rest], axis=0).reshape(-1, width)
        parts = jnp.pad(parts, ((0, -parts.shape[0] % 16), (0, 0)))
        both.append(jnp.concatenate([output + e1[:1, :1] * 0, parts], axis=0))
    kept = jnp.where(section == 0, both[0], both[1])
    sent = jnp.where(section == 0, both[1], both[0])

    d_qkv, products, _ = attention_backward(e1, attn1, low, tables, saved_a1, 1, 9)
    local1.append(shard_sum(products))
    crosses = [(sent, 2), (local1[0], 1)]
    grad1, home1, (sent, down1) = attention_end(
        d_qkv, e1, attn1, gains1[0], saved_a1, 5, 1, (products,), crosses
    )
    dm = (grad1.astype(F32) * valid).astype(BF)
    crosses = [(local1[1], 1), (local1[2], 1)]
    e1, products, (gate1, up1) = mlp_backward(dm, gains0[1], mlp0, saved_m0, 6, 0, crosses)
    local0 = mlp_sums(products)
    d_qkv, products, (down0,) = attention_backward(
        e1, attn0, low, tables, saved_a0, 0, 11, local0[:1]
    )
    local0.append(shard_sum(products))
    crosses = [(local1[3], 1), (local0[1], 0)]
    grad0, home0, (attn_sum1, gate0) = attention_end(
        d_qkv, e1, attn0, gains0[0], saved_a0, 7, 0, (products,), crosses
    )

    input_grads = [lax.dynamic_slice_in_dim(x, column * width, width, 1) for x in (grad0, grad1)]
    by_section = jnp.stack([jnp.where(section == 0, kept, sent), jnp.where(section == 0, sent, kept)])
    by_section = by_section + local0[3][:1, :1] * 0
    everything = lax.all_gather(by_section, "gx", axis=0)
    owner = jnp.sum(jnp.where(dealing == shard, jnp.arange(shards), 0))
    halves = lax.dynamic_slice(
        everything, ((owner // 2) * 2, owner % 2, 0, 0), (2, 1) + everything.shape[2:]
    )[:, 0]
    layer_out = join_halves(halves[0, :half], halves[1, :half])
    stat_rows = 4 * half // width
    parts = halves[:, half : half + stat_rows].astype(F32).reshape(2, 4, half)
    stat_halves = parts[:, :2] + parts[:, 2:]
    stats_out = join_halves(stat_halves[0].T, stat_halves[1].T).T

    local0[2] = local0[2] + grad0[:1, :1] * 0
    received0 = [down0, gate0] + crossing([(x, 0) for x in local0[2:]])
    received1 = [down1, gate1, up1, attn_sum1]
    totals = [
        jnp.where(section == 0, a0.astype(F32) + r0.astype(F32), a1.astype(F32) + r1.astype(F32))
        for a0, r0, a1, r1 in zip(local0, received0, local1, received1)
    ]
    s_down, s_gate, s_up, s_attn = totals
    s_out = s_attn[:, low:]
    q_width = w_query.shape[2]

    attn_sum = jnp.sum(s_attn[:, :low] * attn_own[:block_rows, :low].astype(F32), axis=1)
    mlp_sum = jnp.sum(s_gate * w_gate[0].astype(F32) + s_up * w_up[0].astype(F32), axis=1)
    sums = jnp.stack([attn_sum, mlp_sum]).reshape(-1, 2 * HD)
    sum_rows = sums.shape[0]
    sums = jnp.pad(sums, ((0, -sum_rows % 16), (0, 0)))
    spread = jnp.concatenate([s_attn[:, q_width:low], sums], axis=0).astype(BF)
    spread = spread + everything[0, 0, :1, :1] * 0
    spread = lax.all_gather(spread, "gy", axis=0).astype(F32)
    gains = jnp.sum(spread[:, block_rows : block_rows + sum_rows], axis=0).reshape(2, block_rows)
    gains = gains / both_gains.astype(F32)
    kv_sum = spread[:, :block_rows].reshape(KVH, -1, block_rows, 2, HD).sum(axis=1)
    kv_sum = kv_sum.transpose(2, 1, 0, 3).reshape(2, block_rows, KVH * HD)

    kept = jnp.where(section == 0, input_grads[0], input_grads[1])
    sent = jnp.where(section == 0, home0, home1)
    keep = jnp.where(core == section, kept, sent)
    give = swap_pairs(jnp.where(core == section, sent, kept), "gx")
    back_home = join_halves(jnp.where(core == 0, keep, give), jnp.where(core == 0, give, keep))
    return (
        layer_out[None],
        stats_out[None],
        back_home[None],
        gains[None, 0],
        s_attn[None, :, :q_width],
        kv_sum[None, 0],
        kv_sum[None, 1],
        s_out.T[None],
        gains[None, 1],
        s_gate[None],
        s_up[None],
        s_down.T[None],
    )


def solution(mesh):
    rows_cols = P("section", "gx", "gy")
    cols_rows = P("section", "gy", "gx")
    rows_only = P("section", "gx", None)
    gain = P("section", "gx")
    return jax.shard_map(
        on_device,
        mesh=mesh,
        in_specs=(
            P("gx", "gy"), P("gx", "gy"), P(), P(), gain, rows_cols, rows_only, rows_only,
            cols_rows, gain, rows_cols, rows_cols, cols_rows,
        ),
        out_specs=(
            rows_cols, P("section", None, "gx"), rows_cols, gain, rows_cols, rows_only, rows_only,
            cols_rows, gain, rows_cols, rows_cols, cols_rows,
        ),
        check_vma=False,
    )
```

```python
import functools

import jax
import jax.numpy as jnp
from jax import lax
from jax.experimental import pallas as pl
from jax.experimental.pallas import tpu as pltpu
from jax.sharding import PartitionSpec as P

QH = 32
KVH = 4
HD = 64
LAYERS = 2
EPS = 1e-05
BF = jnp.bfloat16
F32 = jnp.float32
MESH = pl.DeviceIdType.MESH
CHUNK = 32
STEPS = 2
GAIN_ROWS = 32
VMEM_LIMIT = 56 * 1024 * 1024
ANY = pl.BlockSpec(memory_space=pl.ANY)
VMEM = pl.BlockSpec(memory_space=pltpu.VMEM)


def mm(left, right, dims=((1,), (0,))):
    return lax.dot_general(left, right, (dims, ((), ())), preferred_element_type=F32)


def swap_pairs(values, axis, by=1):
    count = lax.axis_size(axis)
    return lax.ppermute(values, axis, [(i, i ^ by) for i in range(count)])


def rope_tables(places):
    half_width = HD // 2
    frequency = jnp.power(10000.0, -2.0 * jnp.arange(half_width).astype(F32) / HD)
    angles = frequency[:, None] * places.astype(F32)[None, :]
    return jnp.cos(angles), jnp.sin(angles)


def core_rows(rows, core):
    quarter = rows.shape[0] // 4
    low = lax.dynamic_slice_in_dim(rows, core * quarter, quarter, 0)
    high = lax.dynamic_slice_in_dim(rows, (3 - core) * quarter, quarter, 0)
    return jnp.concatenate([low, high], axis=0)


def join_halves(first, second):
    quarter = first.shape[0] // 2
    return jnp.concatenate(
        [first[:quarter], second[:quarter], second[quarter:], first[quarter:]], axis=0
    )


def chip_groups():
    return [[0, 2], [1, 3]]


def gather_blocks(base):
    return lax.all_gather(base, "gx", axis=0)


def chosen(pair, layer):
    return jnp.where(lax.axis_index("section") == layer, *pair)


def with_own(stack, pair, layer):
    shard = lax.axis_index("gx")
    return lax.dynamic_update_index_in_dim(stack, chosen(pair, layer), shard, 0)


def fused():
    return lax.axis_size("gx") == 4 and lax.axis_size("gy") == 4


def tall(w):
    return w.reshape(-1, w.shape[-1])


def side(w):
    return jnp.concatenate([w[i] for i in range(w.shape[0])], axis=1)


def cut(w, low, high):
    return w[:, :-GAIN_ROWS, low:high]


def shard_sum(product):
    return lax.psum_scatter(product, "gx", scatter_dimension=0, tiled=True)


def chip_sum(product):
    product = product.reshape(-1, product.shape[-1])
    return lax.psum_scatter(
        product, "gx", scatter_dimension=0, tiled=True, axis_index_groups=[[0, 2], [1, 3]]
    )


def line_gather_kernel(mine_ref, out_ref, right_send, right_recv, left_send, left_recv):
    z = lax.axis_index("gy")
    rows, columns = mine_ref.shape
    half = rows // 2
    barrier = pltpu.get_barrier_semaphore()
    for near, there in ((z - 1, z > 0), (z + 1, z < 3)):

        @pl.when(there)
        def _():
            pl.semaphore_signal(barrier, inc=1, device_id={"gy": near}, device_id_type=MESH)

    inner = (z > 0) & (z < 3)
    pl.when(inner)(lambda: pl.semaphore_wait(barrier, 2))
    pl.when(jnp.logical_not(inner))(lambda: pl.semaphore_wait(barrier, 1))

    def block(of):
        of = jnp.clip(of, 0, 3)
        return pl.ds(pl.multiple_of(of * columns, columns), columns)

    out_ref[:, block(z)] = mine_ref[...]

    def copy(step, p, right):
        here = out_ref.at[p * half : (p + 1) * half, block(z - step if right else z + step)]
        send, recv = (right_send, right_recv) if right else (left_send, left_recv)
        return pltpu.make_async_remote_copy(
            src_ref=here, dst_ref=here, send_sem=send.at[2 * step + p],
            recv_sem=recv.at[2 * step + p], device_id={"gy": z + 1 if right else z - 1},
            device_id_type=MESH,
        )

    right_at = [(z < 3) & (z >= step) for step in range(3)]
    left_at = [(z > 0) & (z <= 3 - step) for step in range(3)]
    for step in range(4):
        for p in range(2):
            if step > 0:
                pl.when(z >= step)(lambda: copy(step - 1, p, True).wait_recv())
                pl.when(z <= 3 - step)(lambda: copy(step - 1, p, False).wait_recv())
            if step < 3:
                pl.when(right_at[step])(lambda: copy(step, p, True).start())
                pl.when(left_at[step])(lambda: copy(step, p, False).start())
    for step in range(3):
        for p in range(2):
            pl.when(right_at[step])(lambda: copy(step, p, True).wait_send())
            pl.when(left_at[step])(lambda: copy(step, p, False).wait_send())


def line_gather(mine):
    if not fused():
        return lax.all_gather(mine, "gy", axis=1, tiled=True)
    rows, columns = mine.shape
    dma = pltpu.SemaphoreType.DMA
    return pl.pallas_call(
        line_gather_kernel,
        out_shape=jax.ShapeDtypeStruct((rows, 4 * columns), BF),
        in_specs=[VMEM],
        out_specs=VMEM,
        scratch_shapes=[dma((6,))] * 4,
        compiler_params=pltpu.CompilerParams(
            collective_id=12, has_side_effects=True, vmem_limit_bytes=VMEM_LIMIT
        ),
        cost_estimate=pl.CostEstimate(flops=0, bytes_accessed=150_000_000, transcendentals=0),
        name="line_gather",
    )(mine)


def rope_down(values, cosine, sines):
    half_width = HD // 2
    first, second = values[:half_width], values[half_width:]
    return jnp.concatenate(
        [first * cosine - second * sines, second * cosine + first * sines], axis=0
    )


def fill_bias(bias_ref, key_ref, query_ref, length_ref):
    keys = key_ref[...]
    allowed = (keys <= query_ref[...]) & (keys < length_ref[...])
    bias_ref[...] = jnp.where(allowed, 0.0, -1e30)


def dot_to(left, right, dims):
    return lax.dot_general(left, right, (dims, ((), ())), preferred_element_type=F32)


def attend_kernel(
    q_ref, k_ref, vt_ref, cos_ref, sin_ref, key_ref, query_ref, length_ref,
    heads_ref, rot_ref, lse_ref, bias_ref, out_ref,
):
    fill_bias(bias_ref, key_ref, query_ref, length_ref)

    def head(h, carry):
        here = pl.ds(pl.multiple_of(h * HD, HD), HD)
        rotated = rope_down(q_ref[here, :], cos_ref[...], sin_ref[...]).astype(BF)
        rot_ref[here, :] = rotated
        scaled = (rotated.astype(F32) * HD ** (-0.5)).astype(BF)
        scores = dot_to(k_ref[...], scaled, ((1,), (0,))) + bias_ref[...]
        top = jnp.max(scores, axis=0, keepdims=True)
        exponent = jnp.exp(scores - top)
        total = jnp.sum(exponent, axis=0, keepdims=True)
        probs = (exponent * (1.0 / total)).astype(BF)
        out_ref[here, :] = dot_to(vt_ref[...], probs, ((1,), (0,)))
        lse_ref[pl.ds(h, 1), :] = top + jnp.log(total)
        return carry

    lax.fori_loop(0, q_ref.shape[0] // HD, head, 0)
    heads_ref[...] = out_ref[...].T.astype(BF)


def attend_back_kernel(
    rot_ref, k_ref, kt_ref, v_ref, d_ref, lse_ref, cos_ref, sin_ref, key_ref, query_ref, length_ref,
    dq_ref, dk_ref, dv_ref, bias_ref, out_ref,
):
    fill_bias(bias_ref, key_ref, query_ref, length_ref)
    dk_ref[...] = jnp.zeros_like(dk_ref)
    dv_ref[...] = jnp.zeros_like(dv_ref)
    scaling = HD ** (-0.5)

    def head(h, carry):
        here = pl.ds(pl.multiple_of(h * HD, HD), HD)
        scaled = (rot_ref[here, :].astype(F32) * scaling).astype(BF)
        scores = dot_to(k_ref[...], scaled, ((1,), (0,))) + bias_ref[...]
        probs = jnp.exp(scores - lse_ref[pl.ds(h, 1), :])
        d_probs = dot_to(v_ref[...], d_ref[here, :], ((1,), (0,)))
        delta = jnp.sum(probs * d_probs, axis=0, keepdims=True)
        d_scores = (probs * (d_probs - delta)).astype(BF)
        dk_ref[...] += dot_to(d_scores, scaled, ((1,), (1,)))
        dv_ref[...] += dot_to(probs.astype(BF), d_ref[here, :], ((1,), (1,)))
        dq = dot_to(kt_ref[...], d_scores, ((1,), (0,))) * scaling
        out_ref[here, :] = rope_down(dq, cos_ref[...], -sin_ref[...])
        return carry

    lax.fori_loop(0, rot_ref.shape[0] // HD, head, 0)
    dq_ref[...] = out_ref[...].T.astype(BF)


def attend(q_down, k_all, v_all, tables):
    cosine, sines, keys_at, places, length = tables
    width, rows = q_down.shape
    return pl.pallas_call(
        attend_kernel,
        out_shape=(
            jax.ShapeDtypeStruct((rows, width), BF),
            jax.ShapeDtypeStruct((width, rows), BF),
            jax.ShapeDtypeStruct((width // HD, rows), F32),
        ),
        in_specs=[VMEM] * 8,
        out_specs=(VMEM,) * 3,
        scratch_shapes=[pltpu.VMEM((k_all.shape[0], rows), F32), pltpu.VMEM((width, rows), F32)],
        compiler_params=pltpu.CompilerParams(vmem_limit_bytes=VMEM_LIMIT),
        cost_estimate=pl.CostEstimate(
            flops=16 * width * rows * k_all.shape[0], bytes_accessed=60_000_000, transcendentals=0
        ),
        name="attend",
    )(q_down, k_all, v_all.T, cosine, sines, keys_at[:, None], places[None], length)


def attend_back(rotated, k_all, v_all, d_down, lse, tables):
    cosine, sines, keys_at, places, length = tables
    width, rows = rotated.shape
    return pl.pallas_call(
        attend_back_kernel,
        out_shape=(
            jax.ShapeDtypeStruct((rows, width), BF),
            jax.ShapeDtypeStruct(k_all.shape, F32),
            jax.ShapeDtypeStruct(k_all.shape, F32),
        ),
        in_specs=[VMEM] * 11,
        out_specs=(VMEM,) * 3,
        scratch_shapes=[pltpu.VMEM((k_all.shape[0], rows), F32), pltpu.VMEM((width, rows), F32)],
        compiler_params=pltpu.CompilerParams(vmem_limit_bytes=VMEM_LIMIT),
        cost_estimate=pl.CostEstimate(
            flops=40 * width * rows * k_all.shape[0], bytes_accessed=80_000_000, transcendentals=0
        ),
        name="attend_back",
    )(
        rotated, k_all, k_all.T, v_all, d_down, lse, cosine, sines,
        keys_at[:, None], places[None], length,
    )


def load_blocks(w_refs, w_layer, low, high, target_of, sem):
    shard, home = lax.axis_index("gx"), lax.axis_index("section") == w_layer
    waits = []
    for j in range(4):

        def copy(ref):
            source = ref.at[: ref.shape[0] - GAIN_ROWS, low:high]
            return pltpu.make_async_copy(source, target_of(j), sem.at[j])

        waits.append(copy(w_refs[0].at[j]))
        if len(w_refs) == 1:
            waits[j].start()
        else:
            pl.when(shard != j)(waits[j].start)
            pl.when((shard == j) & home)(copy(w_refs[1]).start)
            pl.when((shard == j) & jnp.logical_not(home))(copy(w_refs[2]).start)
    return waits


def meet_near(*others):
    near = {"gx": lax.axis_index("gx") ^ 1}
    barrier = pltpu.get_barrier_semaphore()
    for peer in (near, *others):
        pl.semaphore_signal(barrier, inc=1, device_id=peer, device_id_type=MESH)
    pl.semaphore_wait(barrier, 1 + len(others))
    return near


def attend_whole_kernel(
    w_layer, listed,
    h_ref, gain_ref, cos_ref, sin_ref, key_ref, query_ref, length_ref, *rest,
):
    w_refs, rest = rest[:listed], rest[listed:]
    (
        heads_ref, normed_ref, ms_ref, rot_ref, lse_ref, k_ref, kt_ref, v_ref,
        w_all, bias_ref, out_ref, q_ref, vt_ref, kv_mine, kv_far, w_sem, send_sem, recv_sem,
    ) = rest
    rows, width = h_ref.shape
    block = width // 4
    q_width = q_ref.shape[0]
    waits = load_blocks(
        w_refs, w_layer, 0, q_width + 2 * HD, lambda j: w_all.at[j * block : (j + 1) * block], w_sem
    )
    near = meet_near()

    def norm(i, carry):
        here = pl.ds(pl.multiple_of(i * 128, 128), 128)
        values = h_ref[here, :].astype(F32)
        square = jnp.mean(values * values, axis=1, keepdims=True)
        ms_ref[here, :] = square
        normed_ref[here, :] = (values * lax.rsqrt(square + EPS) * gain_ref[...]).astype(BF)
        return carry

    lax.fori_loop(0, rows // 128, norm, 0)
    for wait in waits:
        wait.wait()
    kv = dot_to(normed_ref[...], w_all[:, q_width:], ((1,), (0,))).T
    kv = jnp.concatenate([rope_down(kv[:HD], cos_ref[...], sin_ref[...]), kv[HD:]], axis=0)
    kv_mine[...] = kv.T.astype(BF)
    copy = pltpu.make_async_remote_copy(
        src_ref=kv_mine, dst_ref=kv_far, send_sem=send_sem, recv_sem=recv_sem,
        device_id=near, device_id_type=MESH,
    )
    copy.start()
    q_ref[...] = dot_to(normed_ref[...], w_all[:, :q_width], ((1,), (0,))).T
    fill_bias(bias_ref, key_ref, query_ref, length_ref)
    copy.wait()
    for n, ref in enumerate((kv_mine, kv_far)):
        here = pl.ds(n * rows, rows)
        k_ref[here, :] = ref[:, :HD]
        v_ref[here, :] = ref[:, HD:]
        down = ref[...].astype(F32).T.astype(BF)
        kt_ref[:, here] = down[:HD]
        vt_ref[:, here] = down[HD:]

    def head(h, carry):
        here = pl.ds(pl.multiple_of(h * HD, HD), HD)
        rotated = rope_down(q_ref[here, :], cos_ref[...], sin_ref[...]).astype(BF)
        rot_ref[here, :] = rotated
        scaled = (rotated.astype(F32) * HD ** (-0.5)).astype(BF)
        scores = dot_to(k_ref[...], scaled, ((1,), (0,))) + bias_ref[...]
        top = jnp.max(scores, axis=0, keepdims=True)
        exponent = jnp.exp(scores - top)
        total = jnp.sum(exponent, axis=0, keepdims=True)
        probs = (exponent * (1.0 / total)).astype(BF)
        out_ref[here, :] = dot_to(vt_ref[...], probs, ((1,), (0,)))
        lse_ref[pl.ds(h, 1), :] = top + jnp.log(total)
        return carry

    lax.fori_loop(0, q_width // HD, head, 0)
    heads_ref[...] = out_ref[...].T.astype(BF)


def attend_whole_back_kernel(
    w_layer, listed, crosses,
    e1_ref, rot_ref, lse_ref, k_ref, kt_ref, v_ref, cos_ref, sin_ref, key_ref, query_ref,
    length_ref, *rest,
):
    w_refs, rest = rest[:listed], rest[listed:]
    if crosses:
        source_ref, d_qkv_ref, crossed_ref, *rest, x_send, x_recv = rest
    else:
        d_qkv_ref, *rest = rest
    (
        w_all, bias_ref, d_ref, out_ref, dk_ref, dv_ref, dkv_send, dkv_far,
        w_sem, send_sem, recv_sem,
    ) = rest
    rows, width = e1_ref.shape
    block = width // 4
    q_width = rot_ref.shape[0]
    low = q_width + 2 * HD
    waits = load_blocks(w_refs, w_layer, low, low + block, lambda j: w_all.at[j], w_sem)
    section = lax.axis_index("section")
    x_peer = {"section": 1 - section}
    near = meet_near(x_peer) if crosses else meet_near()

    def x_copy():
        return pltpu.make_async_remote_copy(
            src_ref=source_ref, dst_ref=crossed_ref, send_sem=x_send, recv_sem=x_recv,
            device_id=x_peer, device_id_type=MESH,
        )

    if crosses:
        pl.when(section != w_layer)(lambda: x_copy().start())
    fill_bias(bias_ref, key_ref, query_ref, length_ref)
    dk_ref[...] = jnp.zeros_like(dk_ref)
    dv_ref[...] = jnp.zeros_like(dv_ref)
    scaling = HD ** (-0.5)
    for wait in waits:
        wait.wait()
    d_ref[...] = sum(
        dot_to(w_all[j], e1_ref[:, j * block : (j + 1) * block], ((1,), (1,))) for j in range(4)
    ).astype(BF)

    def head(h, carry):
        here = pl.ds(pl.multiple_of(h * HD, HD), HD)
        scaled = (rot_ref[here, :].astype(F32) * scaling).astype(BF)
        scores = dot_to(k_ref[...], scaled, ((1,), (0,))) + bias_ref[...]
        probs = jnp.exp(scores - lse_ref[pl.ds(h, 1), :])
        d_probs = dot_to(v_ref[...], d_ref[here, :], ((1,), (0,)))
        delta = jnp.sum(probs * d_probs, axis=0, keepdims=True)
        d_scores = (probs * (d_probs - delta)).astype(BF)
        dk_ref[...] += dot_to(d_scores, scaled, ((1,), (1,)))
        dv_ref[...] += dot_to(probs.astype(BF), d_ref[here, :], ((1,), (1,)))
        dq = dot_to(kt_ref[...], d_scores, ((1,), (0,))) * scaling
        out_ref[here, :] = rope_down(dq, cos_ref[...], -sin_ref[...])
        return carry

    lax.fori_loop(0, q_width // HD, head, 0)
    dkv_send[:, :HD] = dk_ref[rows:, :]
    dkv_send[:, HD:] = dv_ref[rows:, :]
    copy = pltpu.make_async_remote_copy(
        src_ref=dkv_send, dst_ref=dkv_far, send_sem=send_sem, recv_sem=recv_sem,
        device_id=near, device_id_type=MESH,
    )
    copy.start()
    d_qkv_ref[:, :q_width] = out_ref[...].T.astype(BF)
    copy.wait()
    down = (dkv_far[...].T)
    dk = rope_down(dk_ref[:rows, :].T + down[:HD], cos_ref[...], -sin_ref[...])
    dkv = jnp.concatenate([dk, dv_ref[:rows, :].T + down[HD:]], axis=0)
    d_qkv_ref[:, q_width:] = dkv.T.astype(BF)
    if crosses:
        pl.when(section != w_layer)(lambda: x_copy().wait_send())
        pl.when(section == w_layer)(lambda: x_copy().wait_recv())


def attend_whole(h, gain, w_attn, low, tables, w_layer, ident):
    cosine, sines, keys_at, places, length = tables
    rows, width = h.shape
    keys, q_width = keys_at.shape[0], low - 2 * HD
    w_list = list(w_attn) if isinstance(w_attn, tuple) else [w_attn]
    outs = [
        ((rows, q_width), BF), ((rows, width), BF), ((rows, 1), F32), ((q_width, rows), BF),
        ((q_width // HD, rows), F32), ((keys, HD), BF), ((HD, keys), BF), ((keys, HD), BF),
    ]
    return pl.pallas_call(
        functools.partial(attend_whole_kernel, w_layer, len(w_list)),
        out_shape=tuple(jax.ShapeDtypeStruct(*o) for o in outs),
        in_specs=[VMEM] * 7 + [ANY] * len(w_list),
        out_specs=(VMEM,) * 8,
        scratch_shapes=[
            pltpu.VMEM((width, low), BF),
            pltpu.VMEM((keys, rows), F32),
            pltpu.VMEM((q_width, rows), F32),
            pltpu.VMEM((q_width, rows), F32),
            pltpu.VMEM((HD, keys), BF),
            pltpu.VMEM((rows, 2 * HD), BF),
            pltpu.VMEM((rows, 2 * HD), BF),
            pltpu.SemaphoreType.DMA((4,)),
            pltpu.SemaphoreType.DMA,
            pltpu.SemaphoreType.DMA,
        ],
        compiler_params=pltpu.CompilerParams(
            collective_id=ident, has_side_effects=True, vmem_limit_bytes=VMEM_LIMIT
        ),
        cost_estimate=pl.CostEstimate(
            flops=16 * q_width * rows * keys, bytes_accessed=70_000_000, transcendentals=0
        ),
        name="attend_whole",
    )(h, gain, cosine, sines, keys_at[:, None], places[None], length, *w_list)


def attend_whole_back(
    e1, rotated, lse, k_all, kt_all, v_all, w_attn, tables, w_layer, ident, cross
):
    cosine, sines, keys_at, places, length = tables
    q_width, rows = rotated.shape
    keys, width = keys_at.shape[0], e1.shape[1]
    w_list = list(w_attn) if isinstance(w_attn, tuple) else [w_attn]
    crossing_specs = [jax.ShapeDtypeStruct(x.shape, BF) for x in cross]
    return pl.pallas_call(
        functools.partial(attend_whole_back_kernel, w_layer, len(w_list), len(cross)),
        out_shape=(jax.ShapeDtypeStruct((rows, q_width + 2 * HD), BF), *crossing_specs),
        in_specs=[VMEM] * 11 + [ANY] * (len(w_list) + len(cross)),
        out_specs=(VMEM, *[ANY] * len(cross)),
        scratch_shapes=[
            pltpu.VMEM((4, q_width, width // 4), BF),
            pltpu.VMEM((keys, rows), F32),
            pltpu.VMEM((q_width, rows), BF),
            pltpu.VMEM((q_width, rows), F32),
            pltpu.VMEM((keys, HD), F32),
            pltpu.VMEM((keys, HD), F32),
            pltpu.VMEM((rows, 2 * HD), F32),
            pltpu.VMEM((rows, 2 * HD), F32),
            pltpu.SemaphoreType.DMA((4,)),
            pltpu.SemaphoreType.DMA,
            pltpu.SemaphoreType.DMA,
        ]
        + [pltpu.SemaphoreType.DMA] * 2 * len(cross),
        compiler_params=pltpu.CompilerParams(
            collective_id=ident, has_side_effects=True, vmem_limit_bytes=VMEM_LIMIT
        ),
        cost_estimate=pl.CostEstimate(
            flops=40 * q_width * rows * keys, bytes_accessed=90_000_000, transcendentals=0
        ),
        name="attend_whole_back",
    )(
        e1, rotated, lse, k_all, kt_all, v_all, cosine, sines, keys_at[:, None], places[None],
        length, *w_list, *cross,
    )


def line_kernel(
    kind, masked, low, high, deps, gathers, layer, exchange, triples, w_layer, crosses, homing,
    gain_ref, resid_ref, valid_ref, h_ref, square_ref, *rest,
):
    forward = kind in ("out", "mlp")
    wide = kind in ("mlp", "mlp_back")
    if kind == "mlp":
        lhs_refs = []
    elif kind == "mlp_back":
        lhs_refs, rest = rest[:4], rest[4:]
    else:
        lhs_refs, rest = rest[:1], rest[1:]
    w_count = 3 if wide else 1
    w_refs = []
    for triple in triples:
        w_refs.append(rest[: 3 if triple else 1])
        rest = rest[3 if triple else 1 :]
    rest = rest[deps:]
    base_refs, rest = rest[: 2 * gathers], rest[2 * gathers :]
    cross_refs, rest = rest[: len(crosses)], rest[len(crosses) :]
    out_ref, rest = rest[0], rest[1:]
    if kind == "mlp":
        normed_ref, ms_ref, gate_ref, up_ref, hidden_ref = rest[:5]
        rest = rest[5:]
    elif kind == "mlp_back":
        product_refs, rest = rest[:3], rest[3:]
        arrived_refs, rest = rest[:exchange], rest[exchange:]
    block_refs, rest = rest[:gathers], rest[gathers:]
    crossed_refs, rest = rest[: len(crosses)], rest[len(crosses) :]
    if homing:
        home_ref, home_send, home_recv = rest[0], *rest[-2:]
        rest = rest[1:-2]
    if crosses:
        x_send, x_recv = rest[-2:]
        rest = rest[:-2]
    w_alls, rest = rest[:w_count], rest[w_count:]
    (
        part, from_end, from_mid, pair,
        w_sem, up_send, up_recv, mid_send, mid_recv, fin_send, fin_recv,
    ) = rest[:11]
    if gathers:
        far_send, far_recv, near_send, near_recv, cross_send, cross_recv = rest[11:]
    if kind == "mlp_back":
        (
            d_gate_ref, d_up_ref, far_normed, far_dm, far_hidden, far_d_gate, far_d_up, stage,
            give_sem, take_sem, stage_sem,
        ) = rest[11:22]
    if exchange:
        y_stage, y_send, y_recv = rest[22:]
    shard = lax.axis_index("gx")
    far, near = shard ^ 2, shard ^ 1
    section = lax.axis_index("section")
    rows, width = resid_ref.shape
    columns = width // 4
    count = rows // CHUNK
    z = lax.axis_index("gy")
    middle = (z == 1) | (z == 2)
    end_of = jnp.where(z == 1, 0, 3)
    mid_of = jnp.where(z == 0, 1, 2)
    across = 3 - z

    def loading(w, j, cut_of, target, slot):
        whole = w_refs[w]
        copies = [(None, pltpu.make_async_copy(cut_of(whole[0].at[j]), target, w_sem.at[slot]))]
        if triples[w]:
            home = section == w_layer
            copies = [(shard != j, copies[0][1])]
            for ref, holds in zip(whole[1:], (home, jnp.logical_not(home))):
                copy = pltpu.make_async_copy(cut_of(ref), target, w_sem.at[slot])
                copies.append(((shard == j) & holds, copy))
        return copies

    loads, downs = [], []
    if wide:
        hidden_width = w_alls[0].shape[1]
        for x0 in range(0, hidden_width, 512):
            x1 = min(x0 + 512, hidden_width)
            for w in range(2):
                for j in range(4):
                    target = w_alls[w].at[j * columns : (j + 1) * columns, x0:x1]
                    loads.append(loading(w, j, lambda ref: ref.at[:, x0:x1], target, len(loads)))
        for j in range(4):
            downs.append(loading(2, j, lambda ref: ref, w_alls[2].at[j], len(loads) + j))
    else:
        for j in range(4):
            cut_of = lambda ref: ref.at[: ref.shape[0] - GAIN_ROWS, low:high]
            loads.append(loading(0, j, cut_of, w_alls[0].at[j], j))
    for load in downs + loads if kind == "mlp_back" else loads + downs:
        for holds, copy in load:
            if holds is None:
                copy.start()
            else:
                pl.when(holds)(copy.start)
    loads, downs = [x[0][1] for x in loads], [x[0][1] for x in downs]

    barrier = pltpu.get_barrier_semaphore()
    peers = []
    if gathers:
        peers = [{"gx": far}, {"gx": near}, {"section": 1 - section}]
    elif kind == "mlp_back":
        peers = [{"gx": near}] + [{"gx": far}] * (exchange > 0)
    if crosses:
        assert not gathers
        peers.append({"section": 1 - section})
    beside = len(peers)
    for peer in peers:
        pl.semaphore_signal(barrier, inc=1, device_id=peer, device_id_type=MESH)

    @pl.when(middle)
    def _():
        pl.semaphore_signal(barrier, inc=1, device_id={"gy": end_of}, device_id_type=MESH)
        pl.semaphore_signal(barrier, inc=1, device_id={"gy": across}, device_id_type=MESH)
        pl.semaphore_wait(barrier, 2 + beside)

    @pl.when(jnp.logical_not(middle))
    def _():
        pl.semaphore_signal(barrier, inc=1, device_id={"gy": mid_of}, device_id_type=MESH)
        pl.semaphore_wait(barrier, 1 + beside)

    x_peer = {"section": 1 - section}

    def x_copy(k):
        return pltpu.make_async_remote_copy(
            src_ref=cross_refs[k], dst_ref=crossed_refs[k], send_sem=x_send.at[k],
            recv_sem=x_recv.at[k], device_id=x_peer, device_id_type=MESH,
        )

    def home_copy(rows_here):
        return pltpu.make_async_remote_copy(
            src_ref=out_ref.at[rows_here, pl.ds(pl.multiple_of(z * columns, columns), columns)],
            dst_ref=home_ref.at[rows_here, :], send_sem=home_send, recv_sem=home_recv,
            device_id=x_peer, device_id_type=MESH,
        )

    def home_start(i):
        if homing:
            here = pl.ds(pl.multiple_of(i * CHUNK, CHUNK), CHUNK)
            pl.when(section != w_layer)(lambda: home_copy(here).start())

    def x_sends(k):
        return section != crosses[k] if crosses[k] < 2 else section >= 0

    def x_takes(k):
        return section == crosses[k] if crosses[k] < 2 else section >= 0

    for k in range(len(crosses)):
        pl.when(x_sends(k))(lambda k=k: x_copy(k).start())

    def half_of(ref, k, which):
        size = base_refs[2 * k].shape[0] // 2
        return ref.at[pl.ds(pl.multiple_of(which * size, 16), size), :]

    def far_copy(k, source):
        return pltpu.make_async_remote_copy(
            src_ref=half_of(source, k, section),
            dst_ref=half_of(block_refs[k].at[shard], k, section),
            send_sem=far_send.at[k], recv_sem=far_recv.at[k],
            device_id={"gx": far}, device_id_type=MESH,
        )

    def near_copy(k, source):
        return pltpu.make_async_remote_copy(
            src_ref=source, dst_ref=block_refs[k].at[shard], send_sem=near_send.at[3 * k],
            recv_sem=near_recv.at[3 * k], device_id={"gx": near}, device_id_type=MESH,
        )

    def cross_copy(k):
        rows_here = half_of(block_refs[k].at[far], k, section)
        return pltpu.make_async_remote_copy(
            src_ref=rows_here, dst_ref=rows_here, send_sem=cross_send.at[k],
            recv_sem=cross_recv.at[k], device_id=x_peer, device_id_type=MESH,
        )

    def pass_copy(k, late):
        rows_here = half_of(block_refs[k].at[far], k, 1 - section if late else section)
        return pltpu.make_async_remote_copy(
            src_ref=rows_here, dst_ref=rows_here, send_sem=near_send.at[3 * k + 1 + late],
            recv_sem=near_recv.at[3 * k + 1 + late], device_id={"gx": near}, device_id_type=MESH,
        )

    at_home = section == layer

    def from_base(k, starts):
        for ref, holds in zip(base_refs[2 * k : 2 * k + 2], (at_home, jnp.logical_not(at_home))):

            @pl.when(holds)
            def _():
                for make in starts:
                    make(k, ref).start()

    def gather_middle(k):
        far_copy(k, base_refs[2 * k]).wait_recv()
        cross_copy(k).start()
        pass_copy(k, 0).start()

    def gather_late(k):
        cross_copy(k).wait_recv()
        pass_copy(k, 1).start()

    if gathers:
        from_base(0, [far_copy])
    for k in range(gathers):
        from_base(k, [near_copy])

    half = rows // STEPS
    core = lax.rem(shard, 2)

    def give(slot, source, target):
        return pltpu.make_async_remote_copy(
            src_ref=source, dst_ref=target, send_sem=give_sem.at[slot],
            recv_sem=take_sem.at[slot], device_id={"gx": near}, device_id_type=MESH,
        )

    def chip_columns(ref, y, of):
        return ref.at[:, pl.ds(pl.multiple_of((2 * y + of) * columns, columns), columns)]

    def step_rows(ref, step):
        return ref.at[pl.ds(pl.multiple_of(step * half, half), half), :]

    if kind == "mlp_back":
        saved_gate, saved_up, saved_normed, saved_hidden = lhs_refs
        early = [give(0, saved_hidden, far_hidden)]
        for y in range(2):
            early.append(give(1 + y, chip_columns(resid_ref, y, 1 - core), far_dm.at[y]))
        for y in range(2):
            early.append(give(3 + y, chip_columns(saved_normed, y, 1 - core), far_normed.at[y]))
        for copy in early:
            copy.start()

    def give_step(step):
        return [
            give(5 + step, step_rows(d_gate_ref, step), step_rows(far_d_gate, step)),
            give(5 + STEPS + step, step_rows(d_up_ref, step), step_rows(far_d_up, step)),
        ]

    if not wide:
        for load in loads:
            load.wait()

    def at_first(step, copies):
        @pl.when(step == 0)
        def _():
            for copy in copies:
                copy.wait()

    def rows_at(ref, i):
        return ref.at[pl.ds(pl.multiple_of(i * CHUNK, CHUNK), CHUNK), :]

    def up_copy(i):
        return pltpu.make_async_remote_copy(
            src_ref=rows_at(part, i), dst_ref=rows_at(from_end, i), send_sem=up_send.at[i],
            recv_sem=up_recv.at[i], device_id={"gy": mid_of}, device_id_type=MESH,
        )

    def mid_copy(i):
        return pltpu.make_async_remote_copy(
            src_ref=rows_at(pair, i), dst_ref=rows_at(from_mid, i), send_sem=mid_send.at[i],
            recv_sem=mid_recv.at[i], device_id={"gy": across}, device_id_type=MESH,
        )

    def fin_copy(i):
        return pltpu.make_async_remote_copy(
            src_ref=rows_at(out_ref, i), dst_ref=rows_at(out_ref, i), send_sem=fin_send.at[i],
            recv_sem=fin_recv.at[i], device_id={"gy": end_of}, device_id_type=MESH,
        )

    def dot(left, right, transposed=False):
        dims = (((1,), (1 if transposed else 0,)), ((), ()))
        return lax.dot_general(left, right, dims, preferred_element_type=F32)

    def spans(extent):
        return [(x, min(x + 512, extent)) for x in range(0, extent, 512)]

    if wide:
        w_gate, w_up, w_down = w_alls

    def product(step, carry):
        here = pl.ds(pl.multiple_of(step * half, half), half)
        if kind == "mlp":
            values = resid_ref[here, :].astype(F32)
            square = jnp.mean(values * values, axis=1, keepdims=True)
            ms_ref[here, :] = square
            normed_ref[here, :] = (values * lax.rsqrt(square + EPS) * gain_ref[...]).astype(BF)
            for n, (x0, x1) in enumerate(spans(w_gate.shape[1])):
                at_first(step, loads[8 * n : 8 * n + 8])
                gate = dot(normed_ref[here, :], w_gate[:, x0:x1])
                up = dot(normed_ref[here, :], w_up[:, x0:x1])
                gate_ref[here, x0:x1] = gate.astype(BF)
                up_ref[here, x0:x1] = up.astype(BF)
                hidden_ref[here, x0:x1] = (gate * jax.nn.sigmoid(gate) * up).astype(BF)
        if kind == "mlp_back":
            at_first(step, downs)
            for x0, x1 in spans(w_gate.shape[1]):
                d_hidden = sum(
                    dot(resid_ref[here, j * columns : (j + 1) * columns], w_down[j, x0:x1, :], True)
                    for j in range(4)
                )
                gate = saved_gate[here, x0:x1].astype(F32)
                up = saved_up[here, x0:x1].astype(F32)
                sigmoid = jax.nn.sigmoid(gate)
                d_up_ref[here, x0:x1] = (d_hidden * (gate * sigmoid)).astype(BF)
                d_gate_ref[here, x0:x1] = (
                    d_hidden * up * sigmoid * (1.0 + gate * (1.0 - sigmoid))
                ).astype(BF)
            for copy in give_step(step):
                copy.start()
        if wide:
            at_first(step, downs if kind == "mlp" else loads)
        for j in range(4):
            span = slice(j * columns, (j + 1) * columns)
            if kind == "out":
                value = dot(lhs_refs[0][here, :], w_alls[0][j])
            elif kind == "mlp":
                value = dot(hidden_ref[here, :], w_down[j])
            elif kind == "mlp_back":
                value = dot(d_gate_ref[here, :], w_gate[span, :], True)
                value += dot(d_up_ref[here, :], w_up[span, :], True)
            else:
                value = dot(lhs_refs[0][here, :], w_alls[0][j], True)
            part[here, span] = value.astype(BF)

        @pl.when(jnp.logical_not(middle))
        def _():
            def send(i, inner):
                up_copy(step * (count // STEPS) + i).start()
                return inner

            lax.fori_loop(0, count // STEPS, send, 0)

        return carry

    lax.fori_loop(0, STEPS, product, 0)

    def finish(i):
        mid_copy(i).wait_recv()
        here = pl.ds(pl.multiple_of(i * CHUNK, CHUNK), CHUNK)
        total = pair[here, :].astype(F32) + from_mid[here, :].astype(F32)
        resid = resid_ref[here, :].astype(F32)
        if forward:
            result = resid + total
            if masked:
                result = result * valid_ref[here, :]
        else:
            values = h_ref[here, :].astype(F32)
            scaled = total * gain_ref[...]
            ratio = lax.rsqrt(square_ref[here, :] + EPS)
            mean_term = jnp.sum(scaled * values, axis=1, keepdims=True) * (1.0 / width)
            result = resid + ratio * scaled - values * (ratio * ratio * ratio) * mean_term
        out_ref[here, :] = result.astype(BF)
        fin_copy(i).start()
        home_start(i)

    tile = columns // 2

    def tile_rows(sub):
        return pl.ds(pl.multiple_of(sub % 2 * tile, tile), tile)

    def stage_copy(number, sub, slot):
        target = product_refs[number].at[sub // 2, tile_rows(sub), :]
        return pltpu.make_async_copy(stage.at[slot], target, stage_sem.at[slot])

    def y_copy(number, sub, slot):
        return pltpu.make_async_remote_copy(
            src_ref=y_stage.at[2 * number + slot], dst_ref=arrived_refs[number].at[tile_rows(sub), :],
            send_sem=y_send.at[2 * number + slot], recv_sem=y_recv.at[2 * number + slot],
            device_id={"gx": far}, device_id_type=MESH,
        )

    def gradient_tile(number, sub):
        slot = sub % 2
        left, far_left, right, far_right = (
            (resid_ref, far_dm, saved_hidden, far_hidden),
            (saved_normed, far_normed, d_gate_ref, far_d_gate),
            (saved_normed, far_normed, d_up_ref, far_d_up),
        )[number]

        @pl.when(sub == 0)
        def _():
            waits = [early[:3], early[3:] + give_all[:STEPS], give_all[STEPS:]][number]
            for copy in waits:
                copy.wait_recv()

        if number >= exchange:

            @pl.when((sub >= 2) | (number > 0))
            def _():
                stage_copy(number, sub, slot).wait()

        elif number > 0:

            @pl.when(sub >= 2)
            def _():
                stage_copy(number, sub - 2, slot).wait()

        y = sub // 2
        if number < exchange:
            y = jnp.where(sub < 2, 1 - lax.div(shard, 2), lax.div(shard, 2))
        start = (y * 2 + core) * columns + sub % 2 * tile
        mine = left[:, pl.ds(pl.multiple_of(start, tile), tile)]
        theirs = far_left[y, :, tile_rows(sub)]
        value = dot_to(mine, right[...], ((0,), (0,))) + dot_to(theirs, far_right[...], ((0,), (0,)))
        if number < exchange:

            @pl.when(sub < 2)
            def _():
                y_stage[2 * number + slot] = value.astype(BF)
                y_copy(number, sub, slot).start()

            @pl.when(sub >= 2)
            def _():
                stage[slot] = value.astype(BF)
                stage_copy(number, sub - 2, slot).start()

        else:
            stage[slot] = value.astype(BF)
            stage_copy(number, sub, slot).start()

    if kind == "mlp_back":
        give_all = [x for pair in zip(*(give_step(n) for n in range(STEPS))) for x in pair]

    def beside_step(i, ahead=0):
        pass_on(i + ahead)
        if kind == "mlp_back":
            for number in range(3):
                first = 3 + 4 * number

                @pl.when((i >= first) & (i < first + 4))
                def _():
                    gradient_tile(number, i - first)

    def pass_on(i):
        if gathers == 2:
            at(2, i, lambda: from_base(1, [far_copy]))
            at(6, i, lambda: gather_middle(0))
            at(10, i, lambda: gather_middle(1))
            at(11, i, lambda: gather_late(0))
            at(15, i, lambda: gather_late(1))

    def at(sixteenth, i, action):
        pl.when(i == count * sixteenth // 16)(action)

    @pl.when(middle)
    def _():
        def step(i, carry):
            up_copy(i).wait_recv()
            here = pl.ds(pl.multiple_of(i * CHUNK, CHUNK), CHUNK)
            pair[here, :] = (part[here, :].astype(F32) + from_end[here, :].astype(F32)).astype(BF)
            mid_copy(i).start()

            @pl.when(i >= 1)
            def _():
                finish(i - 1)

            beside_step(i)
            return carry

        lax.fori_loop(0, count, step, 0)
        finish(count - 1)

        def drain(i, carry):
            mid_copy(i).wait_send()
            fin_copy(i).wait_send()
            return carry

        lax.fori_loop(0, count, drain, 0)

    @pl.when(jnp.logical_not(middle))
    def _():
        if gathers == 2:
            from_base(1, [far_copy])

        def drain(i, carry):
            up_copy(i).wait_send()
            fin_copy(i).wait_recv()
            home_start(i)
            beside_step(i, 3)
            return carry

        lax.fori_loop(0, count, drain, 0)

    if kind == "mlp_back":
        for slot in range(2):
            stage_copy(2, 2 + slot, slot).wait()
        for copy in early + give_all:
            copy.wait_send()
        for number in range(exchange):
            for slot in range(2):
                y_copy(number, slot, slot).wait()
    if homing:
        every = pl.ds(0, rows)
        pl.when(section != w_layer)(lambda: home_copy(every).wait_send())
        pl.when(section == w_layer)(lambda: home_copy(every).wait_recv())
    for k in range(len(crosses)):
        pl.when(x_sends(k))(lambda k=k: x_copy(k).wait_send())
        pl.when(x_takes(k))(lambda k=k: x_copy(k).wait_recv())
    for k in range(gathers):
        far_copy(k, base_refs[2 * k]).wait_send()
        near_copy(k, base_refs[2 * k]).wait()
        cross_copy(k).wait_send()
        pass_copy(k, 0).wait()
        pass_copy(k, 1).wait()


def line_sum(kind, ident, resid, weights, lhs=(), gain=None, valid=None, back=None, low=0, high=0, deps=(), bases=(), layer=0, exchange=0, w_layer=0, crosses=(), homing=False):
    rows, width = resid.shape
    one = jnp.ones((rows, 1), F32)
    h, square = back if back is not None else (jnp.zeros((16, 128), BF), jnp.zeros((8, 1), F32))
    gain = jnp.zeros((1, width), F32) if gain is None else gain
    wide = kind in ("mlp", "mlp_back")
    hidden = 0
    if wide:
        hidden = (weights[2][0] if isinstance(weights[2], tuple) else weights[2]).shape[1]
    w_scratch = []
    triples = [isinstance(w, tuple) for w in weights]
    w_flat = [x for w in weights for x in (w if isinstance(w, tuple) else (w,))]
    for i, w in enumerate(weights):
        _, depth, across = (w[0] if isinstance(w, tuple) else w).shape
        if wide and i < 2:
            w_scratch.append(pltpu.VMEM((width, across), BF))
        else:
            shape = (4, depth, across) if wide else (4, depth - GAIN_ROWS, high - low)
            w_scratch.append(pltpu.VMEM(shape, BF))
    outs, products, beside = [((rows, width), BF)], [], []
    if kind == "mlp":
        outs += [((rows, width), BF), ((rows, 1), F32)] + [((rows, hidden), BF)] * 3
    elif kind == "mlp_back":
        products = [((1 if n < exchange else 2, width // 4, hidden), BF) for n in range(3)]
        products += [((width // 4, hidden), BF)] * exchange
        half_block = pltpu.VMEM((2, rows, width // 4), BF)
        beside = [pltpu.VMEM((rows, hidden), BF)] * 2 + [half_block] * 2
        beside += [pltpu.VMEM((rows, hidden), BF)] * 3 + [pltpu.VMEM((2, width // 8, hidden), BF)]
        beside += [pltpu.SemaphoreType.DMA((n,)) for n in (5 + 2 * STEPS, 5 + 2 * STEPS, 2)]
        if exchange:
            beside += [pltpu.VMEM((2 * exchange, width // 8, hidden), BF)]
            beside += [pltpu.SemaphoreType.DMA((2 * exchange,))] * 2
    blocks = [((4,) + base[0].shape, BF) for base in bases]
    pairs = [x for base in bases for x in base]
    crossed = [(x[0].shape, BF) for x in crosses] + [((rows, width // 4), BF)] * homing
    depth = 3 * hidden if wide else lhs[0].shape[1]
    count = rows // CHUNK
    dma = pltpu.SemaphoreType.DMA
    return pl.pallas_call(
        functools.partial(
            line_kernel, kind, valid is not None, low, high, len(deps), len(bases), layer, exchange,
            triples, w_layer, [x[1] for x in crosses], homing,
        ),
        out_shape=tuple(jax.ShapeDtypeStruct(*o) for o in outs + products + blocks + crossed),
        in_specs=[VMEM] * (5 + len(lhs)) + [ANY] * (len(w_flat) + len(deps) + len(pairs) + len(crosses)),
        out_specs=tuple([VMEM] * len(outs) + [ANY] * len(products + blocks + crossed)),
        scratch_shapes=w_scratch
        + [pltpu.VMEM((rows, width), BF)] * 4
        + [dma((8 * -(-hidden // 512) + 4,))]
        + [dma((count,))] * 6
        + [dma((n * len(bases),)) for n in (1, 1, 3, 3, 1, 1) if bases]
        + beside
        + [dma((len(crosses),))] * 2 * bool(crosses)
        + [dma] * 2 * homing,
        compiler_params=pltpu.CompilerParams(
            collective_id=ident, has_side_effects=True, vmem_limit_bytes=VMEM_LIMIT
        ),
        cost_estimate=pl.CostEstimate(
            flops=2 * rows * depth * width, bytes_accessed=200 * 1024 * 1024, transcendentals=0
        ),
        name="line_" + kind,
    )(
        gain, resid, one if valid is None else valid, h, square, *lhs, *w_flat, *deps, *pairs,
        *(x[0] for x in crosses),
    )


def plain_sum(total):
    return lax.psum(total.astype(BF), "gy").astype(F32)


def normed(h, gain):
    values = h.astype(F32)
    square = jnp.mean(values * values, axis=1, keepdims=True)
    return square, (values * lax.rsqrt(square + EPS) * gain).astype(BF)


def norm_back(d_normed, h, square, gain):
    values = h.astype(F32)
    ratio = lax.rsqrt(square + EPS)
    scaled = d_normed * gain
    mean_term = jnp.mean(scaled * values, axis=1, keepdims=True)
    return ratio * scaled - values * (ratio * ratio * ratio) * mean_term


def attention_forward(h, gain, w_attn, low, tables, ident, bases, layer, w_layer, deps=(), late=None):
    rows, width = h.shape
    high = low + width // lax.axis_size("gx")
    q_width = low - 2 * HD
    if fused():
        heads, n1, square, rotated, lse, k_all, kt_all, v_all = attend_whole(
            h, gain, w_attn, low, tables, w_layer, ident + 8
        )
        if late is not None:
            late = line_gather(late + heads[:1, :1] * 0)
            deps = (*deps, late)
        h1, *stacks = line_sum(
            "out", ident, h, [w_attn], (heads,), low=low, high=high,
            deps=deps, bases=bases, layer=layer, w_layer=w_layer,
        )
        blocks = [(x, *pair) for x, pair in zip(stacks, bases)]
    else:
        cosine, sines = tables[:2]
        square, n1 = normed(h, gain)
        q_down = mm(tall(cut(w_attn, 0, q_width)), n1, ((0,), (1,)))
        kv = mm(n1, tall(cut(w_attn, q_width, low)))
        k_rot = rope_down(kv[:, :HD].T, cosine, sines).T.astype(BF)
        kv = jnp.concatenate([k_rot, kv[:, HD:].astype(BF)], axis=1)
        kv_all = jnp.concatenate([kv, swap_pairs(kv, "gx")], axis=0)
        k_all, v_all = kv_all[:, :HD], kv_all[:, HD:]
        kt_all = k_all.T
        heads, rotated, lse = attend(q_down, k_all, v_all, tables)
        h1 = (h.astype(F32) + plain_sum(mm(heads, side(cut(w_attn, low, high))))).astype(BF)
        blocks = [gather_blocks(chosen(x, layer)) for x in bases]
        late = None if late is None else line_gather(late)
    if late is not None:
        blocks.append(late)
    return h1, square, blocks, (h, square, n1, rotated, lse, k_all, kt_all, v_all, heads)


def mlp_forward(h1, gain, weights, valid, ident, bases=(), layer=0, w_layer=0):
    if fused():
        result, n2, square, gate, up, hidden, *stacks = line_sum(
            "mlp", ident, h1, weights, gain=gain, valid=valid, bases=bases, layer=layer,
            w_layer=w_layer,
        )
        blocks = [(x, *pair) for x, pair in zip(stacks, bases)]
    else:
        square, n2 = normed(h1, gain)
        gate = mm(n2, tall(weights[0]))
        up = mm(n2, tall(weights[1]))
        hidden = (gate * jax.nn.sigmoid(gate) * up).astype(BF)
        gate, up = gate.astype(BF), up.astype(BF)
        result = h1.astype(F32) + plain_sum(mm(hidden, side(weights[2])))
        result = (result * valid).astype(BF)
        blocks = [gather_blocks(chosen(x, layer)) for x in bases]
    return result, square, blocks, (h1, square, n2, gate, up, hidden)


def mlp_backward(dm, gain, weights, saved, ident, w_layer, crosses=(), deps=(), exchange=1):
    h1, square, n2, gate, up, hidden = saved
    if fused():
        e1, *products = line_sum(
            "mlp_back", ident, dm, weights, (gate, up, n2, hidden), gain=gain,
            back=(h1, square), exchange=exchange, w_layer=w_layer, crosses=crosses, deps=deps,
        )
        return e1, products[:4], products[4:]
    gate, up = gate.astype(F32), up.astype(F32)
    d_hidden = mm(dm, side(weights[2]), ((1,), (1,)))
    sigmoid = jax.nn.sigmoid(gate)
    d_gate = (d_hidden * up * sigmoid * (1.0 + gate * (1.0 - sigmoid))).astype(BF)
    d_up = (d_hidden * (gate * sigmoid)).astype(BF)
    total = mm(d_gate, tall(weights[0]), ((1,), (1,))) + mm(d_up, tall(weights[1]), ((1,), (1,)))
    e1 = (dm.astype(F32) + norm_back(plain_sum(total), h1, square, gain)).astype(BF)
    turn = ((0,), (0,))
    products = [mm(dm, hidden, turn), mm(n2, d_gate, turn), mm(n2, d_up, turn)]
    return e1, [p.astype(BF) for p in products], crossing(crosses)


def crossing(crosses):
    pairs = ([(1, 0)], [(0, 1)], [(0, 1), (1, 0)])
    return [lax.ppermute(x, "section", pairs[way]) for x, way in crosses]


def mlp_sums(products):
    if not fused():
        return [shard_sum(p) for p in products]
    down, gate, up, arrived = products
    first = (down[0].astype(F32) + arrived.astype(F32)).astype(BF)
    return [first, chip_sum(gate), chip_sum(up)]


def attention_backward(e1, w_attn, low, tables, saved, w_layer, ident, cross=()):
    h, square, n1, rotated, lse, k_all, kt_all, v_all, heads = saved
    rows, width = h.shape
    if fused():
        d_qkv, *crossed = attend_whole_back(
            e1, rotated, lse, k_all, kt_all, v_all, w_attn, tables, w_layer, ident, cross
        )
    else:
        cosine, sines = tables[:2]
        w_o = side(cut(w_attn, low, low + width // lax.axis_size("gx")))
        d_down = mm(w_o, e1, ((1,), (1,))).astype(BF)
        dq, dk, dv = attend_back(rotated, k_all, v_all, d_down, lse, tables)
        dkv = jnp.concatenate([dk, dv], axis=1)
        dkv = dkv[:rows] + swap_pairs(dkv[rows:], "gx")
        dk = rope_down(dkv[:, :HD].T, cosine, -sines).T
        d_qkv = jnp.concatenate([dq, dk.astype(BF), dkv[:, HD:].astype(BF)], axis=1)
        crossed = crossing([(x, w_layer) for x in cross])
    turn = ((0,), (0,))
    products = [mm(n1, d_qkv, turn).astype(BF), mm(e1, heads, turn).astype(BF)]
    return d_qkv, jnp.concatenate(products, axis=1), crossed


def attention_end(d_qkv, e1, w_attn, gain, saved, ident, w_layer, deps, crosses):
    h, square = saved[:2]
    qkv_width = d_qkv.shape[1]
    if fused():
        grad, *crossed = line_sum(
            "back", ident, e1, [w_attn], (d_qkv,), gain=gain, back=(h, square),
            low=0, high=qkv_width, deps=deps, crosses=crosses, w_layer=w_layer, homing=True,
        )
        return grad, crossed[-1], crossed[:-1]
    total = plain_sum(mm(d_qkv, tall(cut(w_attn, 0, qkv_width)), ((1,), (1,))))
    grad = (e1.astype(F32) + norm_back(total, h, square, gain)).astype(BF)
    width = grad.shape[1] // lax.axis_size("gy")
    part = lax.dynamic_slice_in_dim(grad, lax.axis_index("gy") * width, width, 1)
    home, *crossed = crossing([(part, w_layer), *crosses])
    return grad, home, crossed


def on_device(
    hidden_in, out_grad, lengths, dealing, attn_gain, w_query, w_key, w_value, w_out,
    mlp_gain, w_gate, w_up, w_down,
):
    shards = lax.axis_size("gx")
    shard = lax.axis_index("gx")
    section = lax.axis_index("section")
    column = lax.axis_index("gy")
    core = shard % 2
    sequence = (shard // 2) * 2 + section
    span, width = hidden_in.shape
    half = span // 2
    seq_length = lax.dynamic_index_in_dim(lengths, sequence, keepdims=False)

    both = jnp.concatenate([hidden_in, out_grad], axis=1)
    mine = core_rows(both, core)
    theirs = swap_pairs(core_rows(both, 1 - core), "gx")
    mine = jnp.where(core == section, mine, theirs)
    h = line_gather(mine[:, :width])

    kv_head = column * (w_query.shape[2] // HD) // (QH // KVH)
    low = w_query.shape[2] + 2 * HD
    both_gains = jnp.stack([attn_gain[0], mlp_gain[0]])
    block_rows = both_gains.shape[1]
    attn_own = jnp.concatenate(
        [
            w_query[0],
            lax.dynamic_slice_in_dim(w_key[0], kv_head * HD, HD, 1),
            lax.dynamic_slice_in_dim(w_value[0], kv_head * HD, HD, 1),
            w_out[0],
        ],
        axis=1,
    )
    gain_rows = jnp.pad(both_gains, ((0, GAIN_ROWS - 2), (0, attn_own.shape[1] - block_rows)))
    attn_own = jnp.concatenate([attn_own, gain_rows + theirs[:1, :1] * 0], axis=0)
    own = (attn_own, w_gate[0], w_up[0], w_down[0])
    first = second = [(array, swap_pairs(array, "section")) for array in own]

    def gains_of(w_attn, pair):
        cut_of = lambda w: w[..., block_rows : block_rows + 2, :block_rows]
        rows = cut_of(w_attn[0] if isinstance(w_attn, tuple) else w_attn)
        if isinstance(w_attn, tuple):
            rows = with_own(rows, [cut_of(x) for x in pair], 1)
        return rows.transpose(1, 0, 2).reshape(2, 1, -1).astype(F32)

    here = core_rows(jnp.arange(span), core)
    there = core_rows(jnp.arange(span), 1 - core)
    keys_at = jnp.concatenate([here, there])
    valid = (here < seq_length)[:, None].astype(F32)
    tables = (*rope_tables(here), keys_at, here, seq_length.reshape(1, 1))

    attn0 = gather_blocks(chosen(first[0], 0) + h[:1, :1] * 0)
    gate0 = gather_blocks(chosen(first[1], 0) + h[:1, :1] * 0)
    gains0 = gains_of(attn0, first[0])
    h1, square_a, blocks, saved_a0 = attention_forward(
        h, gains0[0], attn0, low, tables, 0, first[2:], 0, 0, (gate0,), mine[:, width:]
    )
    d_out = blocks.pop()
    mlp0 = [gate0] + blocks
    h, square_m, (attn1, gate1), saved_m0 = mlp_forward(
        h1, gains0[1], mlp0, valid, 1, second[:2], 1
    )
    gains1 = gains_of(attn1, second[0])
    outputs, squares = [h], [square_a, square_m]
    h1, square_a, blocks, saved_a1 = attention_forward(
        h, gains1[0], attn1, low, tables, 2, second[2:], 1, 1
    )
    mlp1 = [gate1] + blocks
    h, square_m, _, saved_m1 = mlp_forward(h1, gains1[1], mlp1, valid, 3, w_layer=1)
    outputs.append(h)
    squares = jnp.concatenate(squares + [square_a, square_m], axis=1)
    rms = (jnp.sqrt(squares + EPS) * valid).T
    statistics = [rms[:2], rms[2:]]
    outputs = [lax.dynamic_slice_in_dim(x, column * width, width, 1) for x in outputs]

    dm = (d_out.astype(F32) * valid).astype(BF)
    e1, products, _ = mlp_backward(dm, gains1[1], mlp1, saved_m1, 4, 1)
    local1 = mlp_sums(products)

    both = []
    for output, stat in zip(outputs, statistics):
        high = stat.astype(BF)
        rest = (stat - high.astype(F32)).astype(BF)
        parts = jnp.concatenate([high, rest], axis=0).reshape(-1, width)
        parts = jnp.pad(parts, ((0, -parts.shape[0] % 16), (0, 0)))
        both.append(jnp.concatenate([output + e1[:1, :1] * 0, parts], axis=0))
    kept = jnp.where(section == 0, both[0], both[1])
    sent = jnp.where(section == 0, both[1], both[0])

    d_qkv, products, _ = attention_backward(e1, attn1, low, tables, saved_a1, 1, 9)
    local1.append(shard_sum(products))
    crosses = [(sent, 2), (local1[0], 1)]
    grad1, home1, (sent, down1) = attention_end(
        d_qkv, e1, attn1, gains1[0], saved_a1, 5, 1, (products,), crosses
    )
    by_section = jnp.stack([jnp.where(section == 0, kept, sent), jnp.where(section == 0, sent, kept)])
    everything = lax.all_gather(by_section, "gx", axis=0)
    owner = jnp.sum(jnp.where(dealing == shard, jnp.arange(shards), 0))
    halves = lax.dynamic_slice(
        everything, ((owner // 2) * 2, owner % 2, 0, 0), (2, 1) + everything.shape[2:]
    )[:, 0]
    layer_out = join_halves(halves[0, :half], halves[1, :half])
    stat_rows = 4 * half // width
    parts = halves[:, half : half + stat_rows].astype(F32).reshape(2, 4, half)
    stat_halves = parts[:, :2] + parts[:, 2:]
    stats_out = join_halves(stat_halves[0].T, stat_halves[1].T).T

    dm = (grad1.astype(F32) * valid).astype(BF)
    crosses = [(local1[1], 1), (local1[2], 1)]
    e1, products, (gate1, up1) = mlp_backward(dm, gains0[1], mlp0, saved_m0, 6, 0, crosses)
    local0 = mlp_sums(products)
    d_qkv, products, (down0,) = attention_backward(
        e1, attn0, low, tables, saved_a0, 0, 11, local0[:1]
    )
    local0.append(shard_sum(products))
    crosses = [(local1[3], 1), (local0[1], 0)]
    grad0, home0, (attn_sum1, gate0) = attention_end(
        d_qkv, e1, attn0, gains0[0], saved_a0, 7, 0, (products, everything), crosses
    )

    input_grads = [lax.dynamic_slice_in_dim(x, column * width, width, 1) for x in (grad0, grad1)]
    local0[2] = local0[2] + grad0[:1, :1] * 0
    received0 = [down0, gate0] + crossing([(x, 0) for x in local0[2:]])
    received1 = [down1, gate1, up1, attn_sum1]
    totals = [
        jnp.where(section == 0, a0.astype(F32) + r0.astype(F32), a1.astype(F32) + r1.astype(F32))
        for a0, r0, a1, r1 in zip(local0, received0, local1, received1)
    ]
    s_down, s_gate, s_up, s_attn = totals
    s_out = s_attn[:, low:]
    q_width = w_query.shape[2]

    attn_sum = jnp.sum(s_attn[:, :low] * attn_own[:block_rows, :low].astype(F32), axis=1)
    mlp_sum = jnp.sum(s_gate * w_gate[0].astype(F32) + s_up * w_up[0].astype(F32), axis=1)
    sums = jnp.stack([attn_sum, mlp_sum]).reshape(-1, 2 * HD)
    sum_rows = sums.shape[0]
    sums = jnp.pad(sums, ((0, -sum_rows % 16), (0, 0)))
    spread = jnp.concatenate([s_attn[:, q_width:low], sums], axis=0).astype(BF)
    spread = lax.all_gather(spread, "gy", axis=0).astype(F32)
    gains = jnp.sum(spread[:, block_rows : block_rows + sum_rows], axis=0).reshape(2, block_rows)
    gains = gains / both_gains.astype(F32)
    kv_sum = spread[:, :block_rows].reshape(KVH, -1, block_rows, 2, HD).sum(axis=1)
    kv_sum = kv_sum.transpose(2, 1, 0, 3).reshape(2, block_rows, KVH * HD)

    kept = jnp.where(section == 0, input_grads[0], input_grads[1])
    sent = jnp.where(section == 0, home0, home1)
    keep = jnp.where(core == section, kept, sent)
    give = swap_pairs(jnp.where(core == section, sent, kept), "gx")
    back_home = join_halves(jnp.where(core == 0, keep, give), jnp.where(core == 0, give, keep))
    return (
        layer_out[None],
        stats_out[None],
        back_home[None],
        gains[None, 0],
        s_attn[None, :, :q_width],
        kv_sum[None, 0],
        kv_sum[None, 1],
        s_out.T[None],
        gains[None, 1],
        s_gate[None],
        s_up[None],
        s_down.T[None],
    )


def solution(mesh):
    rows_cols = P("section", "gx", "gy")
    cols_rows = P("section", "gy", "gx")
    rows_only = P("section", "gx", None)
    gain = P("section", "gx")
    return jax.shard_map(
        on_device,
        mesh=mesh,
        in_specs=(
            P("gx", "gy"), P("gx", "gy"), P(), P(), gain, rows_cols, rows_only, rows_only,
            cols_rows, gain, rows_cols, rows_cols, cols_rows,
        ),
        out_specs=(
            rows_cols, P("section", None, "gx"), rows_cols, gain, rows_cols, rows_only, rows_only,
            cols_rows, gain, rows_cols, rows_cols, cols_rows,
        ),
        check_vma=False,
    )
```

```python
import functools

import jax
import jax.numpy as jnp
from jax import lax
from jax.experimental import pallas as pl
from jax.experimental.pallas import tpu as pltpu
from jax.sharding import PartitionSpec as P

QH = 32
KVH = 4
HD = 64
LAYERS = 2
EPS = 1e-05
BF = jnp.bfloat16
F32 = jnp.float32
MESH = pl.DeviceIdType.MESH
CHUNK = 32
STEPS = 2
GAIN_ROWS = 32
VMEM_LIMIT = 56 * 1024 * 1024
ANY = pl.BlockSpec(memory_space=pl.ANY)
VMEM = pl.BlockSpec(memory_space=pltpu.VMEM)


def mm(left, right, dims=((1,), (0,))):
    return lax.dot_general(left, right, (dims, ((), ())), preferred_element_type=F32)


def swap_pairs(values, axis, by=1):
    count = lax.axis_size(axis)
    return lax.ppermute(values, axis, [(i, i ^ by) for i in range(count)])


def rope_tables(places):
    half_width = HD // 2
    frequency = jnp.power(10000.0, -2.0 * jnp.arange(half_width).astype(F32) / HD)
    angles = frequency[:, None] * places.astype(F32)[None, :]
    return jnp.cos(angles), jnp.sin(angles)


def core_rows(rows, core):
    quarter = rows.shape[0] // 4
    low = lax.dynamic_slice_in_dim(rows, core * quarter, quarter, 0)
    high = lax.dynamic_slice_in_dim(rows, (3 - core) * quarter, quarter, 0)
    return jnp.concatenate([low, high], axis=0)


def join_halves(first, second):
    quarter = first.shape[0] // 2
    return jnp.concatenate(
        [first[:quarter], second[:quarter], second[quarter:], first[quarter:]], axis=0
    )


def chip_groups():
    return [[0, 2], [1, 3]]


def gather_blocks(base):
    return lax.all_gather(base, "gx", axis=0)


def chosen(pair, layer):
    return jnp.where(lax.axis_index("section") == layer, *pair)


def with_own(stack, pair, layer):
    shard = lax.axis_index("gx")
    return lax.dynamic_update_index_in_dim(stack, chosen(pair, layer), shard, 0)


def fused():
    return lax.axis_size("gx") == 4 and lax.axis_size("gy") == 4


def tall(w):
    return w.reshape(-1, w.shape[-1])


def side(w):
    return jnp.concatenate([w[i] for i in range(w.shape[0])], axis=1)


def cut(w, low, high):
    return w[:, :-GAIN_ROWS, low:high]


def shard_sum(product):
    return lax.psum_scatter(product, "gx", scatter_dimension=0, tiled=True)


def chip_sum(product):
    product = product.reshape(-1, product.shape[-1])
    return lax.psum_scatter(
        product, "gx", scatter_dimension=0, tiled=True, axis_index_groups=[[0, 2], [1, 3]]
    )


def line_gather_kernel(mine_ref, out_ref, right_send, right_recv, left_send, left_recv):
    z = lax.axis_index("gy")
    rows, columns = mine_ref.shape
    half = rows // 2
    barrier = pltpu.get_barrier_semaphore()
    for near, there in ((z - 1, z > 0), (z + 1, z < 3)):

        @pl.when(there)
        def _():
            pl.semaphore_signal(barrier, inc=1, device_id={"gy": near}, device_id_type=MESH)

    inner = (z > 0) & (z < 3)
    pl.when(inner)(lambda: pl.semaphore_wait(barrier, 2))
    pl.when(jnp.logical_not(inner))(lambda: pl.semaphore_wait(barrier, 1))

    def block(of):
        of = jnp.clip(of, 0, 3)
        return pl.ds(pl.multiple_of(of * columns, columns), columns)

    out_ref[:, block(z)] = mine_ref[...]

    def copy(step, p, right):
        here = out_ref.at[p * half : (p + 1) * half, block(z - step if right else z + step)]
        send, recv = (right_send, right_recv) if right else (left_send, left_recv)
        return pltpu.make_async_remote_copy(
            src_ref=here, dst_ref=here, send_sem=send.at[2 * step + p],
            recv_sem=recv.at[2 * step + p], device_id={"gy": z + 1 if right else z - 1},
            device_id_type=MESH,
        )

    right_at = [(z < 3) & (z >= step) for step in range(3)]
    left_at = [(z > 0) & (z <= 3 - step) for step in range(3)]
    for step in range(4):
        for p in range(2):
            if step > 0:
                pl.when(z >= step)(lambda: copy(step - 1, p, True).wait_recv())
                pl.when(z <= 3 - step)(lambda: copy(step - 1, p, False).wait_recv())
            if step < 3:
                pl.when(right_at[step])(lambda: copy(step, p, True).start())
                pl.when(left_at[step])(lambda: copy(step, p, False).start())
    for step in range(3):
        for p in range(2):
            pl.when(right_at[step])(lambda: copy(step, p, True).wait_send())
            pl.when(left_at[step])(lambda: copy(step, p, False).wait_send())


def line_gather(mine):
    if not fused():
        return lax.all_gather(mine, "gy", axis=1, tiled=True)
    rows, columns = mine.shape
    dma = pltpu.SemaphoreType.DMA
    return pl.pallas_call(
        line_gather_kernel,
        out_shape=jax.ShapeDtypeStruct((rows, 4 * columns), BF),
        in_specs=[VMEM],
        out_specs=VMEM,
        scratch_shapes=[dma((6,))] * 4,
        compiler_params=pltpu.CompilerParams(
            collective_id=12, has_side_effects=True, vmem_limit_bytes=VMEM_LIMIT
        ),
        cost_estimate=pl.CostEstimate(flops=0, bytes_accessed=150_000_000, transcendentals=0),
        name="line_gather",
    )(mine)


def rope_down(values, cosine, sines):
    half_width = HD // 2
    first, second = values[:half_width], values[half_width:]
    return jnp.concatenate(
        [first * cosine - second * sines, second * cosine + first * sines], axis=0
    )


def fill_bias(bias_ref, key_ref, query_ref, length_ref):
    keys = key_ref[...]
    allowed = (keys <= query_ref[...]) & (keys < length_ref[...])
    bias_ref[...] = jnp.where(allowed, 0.0, -1e30)


def dot_to(left, right, dims):
    return lax.dot_general(left, right, (dims, ((), ())), preferred_element_type=F32)


def attend_kernel(
    q_ref, k_ref, vt_ref, cos_ref, sin_ref, key_ref, query_ref, length_ref,
    heads_ref, rot_ref, lse_ref, bias_ref, out_ref,
):
    fill_bias(bias_ref, key_ref, query_ref, length_ref)

    def head(h, carry):
        here = pl.ds(pl.multiple_of(h * HD, HD), HD)
        rotated = rope_down(q_ref[here, :], cos_ref[...], sin_ref[...]).astype(BF)
        rot_ref[here, :] = rotated
        scaled = (rotated.astype(F32) * HD ** (-0.5)).astype(BF)
        scores = dot_to(k_ref[...], scaled, ((1,), (0,))) + bias_ref[...]
        top = jnp.max(scores, axis=0, keepdims=True)
        exponent = jnp.exp(scores - top)
        total = jnp.sum(exponent, axis=0, keepdims=True)
        probs = (exponent * (1.0 / total)).astype(BF)
        out_ref[here, :] = dot_to(vt_ref[...], probs, ((1,), (0,)))
        lse_ref[pl.ds(h, 1), :] = top + jnp.log(total)
        return carry

    lax.fori_loop(0, q_ref.shape[0] // HD, head, 0)
    heads_ref[...] = out_ref[...].T.astype(BF)


def attend_back_kernel(
    rot_ref, k_ref, kt_ref, v_ref, d_ref, lse_ref, cos_ref, sin_ref, key_ref, query_ref, length_ref,
    dq_ref, dk_ref, dv_ref, bias_ref, out_ref,
):
    fill_bias(bias_ref, key_ref, query_ref, length_ref)
    dk_ref[...] = jnp.zeros_like(dk_ref)
    dv_ref[...] = jnp.zeros_like(dv_ref)
    scaling = HD ** (-0.5)

    def head(h, carry):
        here = pl.ds(pl.multiple_of(h * HD, HD), HD)
        scaled = (rot_ref[here, :].astype(F32) * scaling).astype(BF)
        scores = dot_to(k_ref[...], scaled, ((1,), (0,))) + bias_ref[...]
        probs = jnp.exp(scores - lse_ref[pl.ds(h, 1), :])
        d_probs = dot_to(v_ref[...], d_ref[here, :], ((1,), (0,)))
        delta = jnp.sum(probs * d_probs, axis=0, keepdims=True)
        d_scores = (probs * (d_probs - delta)).astype(BF)
        dk_ref[...] += dot_to(d_scores, scaled, ((1,), (1,)))
        dv_ref[...] += dot_to(probs.astype(BF), d_ref[here, :], ((1,), (1,)))
        dq = dot_to(kt_ref[...], d_scores, ((1,), (0,))) * scaling
        out_ref[here, :] = rope_down(dq, cos_ref[...], -sin_ref[...])
        return carry

    lax.fori_loop(0, rot_ref.shape[0] // HD, head, 0)
    dq_ref[...] = out_ref[...].T.astype(BF)


def attend(q_down, k_all, v_all, tables):
    cosine, sines, keys_at, places, length = tables
    width, rows = q_down.shape
    return pl.pallas_call(
        attend_kernel,
        out_shape=(
            jax.ShapeDtypeStruct((rows, width), BF),
            jax.ShapeDtypeStruct((width, rows), BF),
            jax.ShapeDtypeStruct((width // HD, rows), F32),
        ),
        in_specs=[VMEM] * 8,
        out_specs=(VMEM,) * 3,
        scratch_shapes=[pltpu.VMEM((k_all.shape[0], rows), F32), pltpu.VMEM((width, rows), F32)],
        compiler_params=pltpu.CompilerParams(vmem_limit_bytes=VMEM_LIMIT),
        cost_estimate=pl.CostEstimate(
            flops=16 * width * rows * k_all.shape[0], bytes_accessed=60_000_000, transcendentals=0
        ),
        name="attend",
    )(q_down, k_all, v_all.T, cosine, sines, keys_at[:, None], places[None], length)


def attend_back(rotated, k_all, v_all, d_down, lse, tables):
    cosine, sines, keys_at, places, length = tables
    width, rows = rotated.shape
    return pl.pallas_call(
        attend_back_kernel,
        out_shape=(
            jax.ShapeDtypeStruct((rows, width), BF),
            jax.ShapeDtypeStruct(k_all.shape, F32),
            jax.ShapeDtypeStruct(k_all.shape, F32),
        ),
        in_specs=[VMEM] * 11,
        out_specs=(VMEM,) * 3,
        scratch_shapes=[pltpu.VMEM((k_all.shape[0], rows), F32), pltpu.VMEM((width, rows), F32)],
        compiler_params=pltpu.CompilerParams(vmem_limit_bytes=VMEM_LIMIT),
        cost_estimate=pl.CostEstimate(
            flops=40 * width * rows * k_all.shape[0], bytes_accessed=80_000_000, transcendentals=0
        ),
        name="attend_back",
    )(
        rotated, k_all, k_all.T, v_all, d_down, lse, cosine, sines,
        keys_at[:, None], places[None], length,
    )


def load_blocks(w_refs, w_layer, low, high, target_of, sem):
    shard, home = lax.axis_index("gx"), lax.axis_index("section") == w_layer
    waits = []
    for j in range(4):

        def copy(ref):
            source = ref.at[: ref.shape[0] - GAIN_ROWS, low:high]
            return pltpu.make_async_copy(source, target_of(j), sem.at[j])

        waits.append(copy(w_refs[0].at[j]))
        if len(w_refs) == 1:
            waits[j].start()
        else:
            pl.when(shard != j)(waits[j].start)
            pl.when((shard == j) & home)(copy(w_refs[1]).start)
            pl.when((shard == j) & jnp.logical_not(home))(copy(w_refs[2]).start)
    return waits


def meet_near(*others):
    near = {"gx": lax.axis_index("gx") ^ 1}
    barrier = pltpu.get_barrier_semaphore()
    for peer in (near, *others):
        pl.semaphore_signal(barrier, inc=1, device_id=peer, device_id_type=MESH)
    pl.semaphore_wait(barrier, 1 + len(others))
    return near


def attend_whole_kernel(
    w_layer, listed,
    h_ref, gain_ref, cos_ref, sin_ref, key_ref, query_ref, length_ref, *rest,
):
    w_refs, rest = rest[:listed], rest[listed:]
    (
        heads_ref, normed_ref, ms_ref, rot_ref, lse_ref, k_ref, kt_ref, v_ref,
        w_all, bias_ref, out_ref, q_ref, vt_ref, kv_mine, kv_far, w_sem, send_sem, recv_sem,
    ) = rest
    rows, width = h_ref.shape
    block = width // 4
    q_width = q_ref.shape[0]
    waits = load_blocks(
        w_refs, w_layer, 0, q_width + 2 * HD, lambda j: w_all.at[j * block : (j + 1) * block], w_sem
    )
    near = meet_near()

    def norm(i, carry):
        here = pl.ds(pl.multiple_of(i * 128, 128), 128)
        values = h_ref[here, :].astype(F32)
        square = jnp.mean(values * values, axis=1, keepdims=True)
        ms_ref[here, :] = square
        normed_ref[here, :] = (values * lax.rsqrt(square + EPS) * gain_ref[...]).astype(BF)
        return carry

    lax.fori_loop(0, rows // 128, norm, 0)
    for wait in waits:
        wait.wait()
    kv = dot_to(normed_ref[...], w_all[:, q_width:], ((1,), (0,))).T
    kv = jnp.concatenate([rope_down(kv[:HD], cos_ref[...], sin_ref[...]), kv[HD:]], axis=0)
    kv_mine[...] = kv.T.astype(BF)
    copy = pltpu.make_async_remote_copy(
        src_ref=kv_mine, dst_ref=kv_far, send_sem=send_sem, recv_sem=recv_sem,
        device_id=near, device_id_type=MESH,
    )
    copy.start()
    q_ref[...] = dot_to(normed_ref[...], w_all[:, :q_width], ((1,), (0,))).T
    fill_bias(bias_ref, key_ref, query_ref, length_ref)
    copy.wait()
    for n, ref in enumerate((kv_mine, kv_far)):
        here = pl.ds(n * rows, rows)
        k_ref[here, :] = ref[:, :HD]
        v_ref[here, :] = ref[:, HD:]
        down = ref[...].astype(F32).T.astype(BF)
        kt_ref[:, here] = down[:HD]
        vt_ref[:, here] = down[HD:]

    def head(h, carry):
        here = pl.ds(pl.multiple_of(h * HD, HD), HD)
        rotated = rope_down(q_ref[here, :], cos_ref[...], sin_ref[...]).astype(BF)
        rot_ref[here, :] = rotated
        scaled = (rotated.astype(F32) * HD ** (-0.5)).astype(BF)
        scores = dot_to(k_ref[...], scaled, ((1,), (0,))) + bias_ref[...]
        top = jnp.max(scores, axis=0, keepdims=True)
        exponent = jnp.exp(scores - top)
        total = jnp.sum(exponent, axis=0, keepdims=True)
        probs = (exponent * (1.0 / total)).astype(BF)
        out_ref[here, :] = dot_to(vt_ref[...], probs, ((1,), (0,)))
        lse_ref[pl.ds(h, 1), :] = top + jnp.log(total)
        return carry

    lax.fori_loop(0, q_width // HD, head, 0)
    heads_ref[...] = out_ref[...].T.astype(BF)


def attend_whole_back_kernel(
    w_layer, listed, crosses,
    e1_ref, rot_ref, lse_ref, k_ref, kt_ref, v_ref, cos_ref, sin_ref, key_ref, query_ref,
    length_ref, *rest,
):
    w_refs, rest = rest[:listed], rest[listed:]
    if crosses:
        source_ref, d_qkv_ref, crossed_ref, *rest, x_send, x_recv = rest
    else:
        d_qkv_ref, *rest = rest
    (
        w_all, bias_ref, d_ref, out_ref, dk_ref, dv_ref, dkv_send, dkv_far,
        w_sem, send_sem, recv_sem,
    ) = rest
    rows, width = e1_ref.shape
    block = width // 4
    q_width = rot_ref.shape[0]
    low = q_width + 2 * HD
    waits = load_blocks(w_refs, w_layer, low, low + block, lambda j: w_all.at[j], w_sem)
    section = lax.axis_index("section")
    x_peer = {"section": 1 - section}
    near = meet_near(x_peer) if crosses else meet_near()

    def x_copy():
        return pltpu.make_async_remote_copy(
            src_ref=source_ref, dst_ref=crossed_ref, send_sem=x_send, recv_sem=x_recv,
            device_id=x_peer, device_id_type=MESH,
        )

    if crosses:
        pl.when(section != w_layer)(lambda: x_copy().start())
    fill_bias(bias_ref, key_ref, query_ref, length_ref)
    dk_ref[...] = jnp.zeros_like(dk_ref)
    dv_ref[...] = jnp.zeros_like(dv_ref)
    scaling = HD ** (-0.5)
    for wait in waits:
        wait.wait()
    d_ref[...] = sum(
        dot_to(w_all[j], e1_ref[:, j * block : (j + 1) * block], ((1,), (1,))) for j in range(4)
    ).astype(BF)

    def head(h, carry):
        here = pl.ds(pl.multiple_of(h * HD, HD), HD)
        scaled = (rot_ref[here, :].astype(F32) * scaling).astype(BF)
        scores = dot_to(k_ref[...], scaled, ((1,), (0,))) + bias_ref[...]
        probs = jnp.exp(scores - lse_ref[pl.ds(h, 1), :])
        d_probs = dot_to(v_ref[...], d_ref[here, :], ((1,), (0,)))
        delta = jnp.sum(probs * d_probs, axis=0, keepdims=True)
        d_scores = (probs * (d_probs - delta)).astype(BF)
        dk_ref[...] += dot_to(d_scores, scaled, ((1,), (1,)))
        dv_ref[...] += dot_to(probs.astype(BF), d_ref[here, :], ((1,), (1,)))
        dq = dot_to(kt_ref[...], d_scores, ((1,), (0,))) * scaling
        out_ref[here, :] = rope_down(dq, cos_ref[...], -sin_ref[...])
        return carry

    lax.fori_loop(0, q_width // HD, head, 0)
    dkv_send[:, :HD] = dk_ref[rows:, :]
    dkv_send[:, HD:] = dv_ref[rows:, :]
    copy = pltpu.make_async_remote_copy(
        src_ref=dkv_send, dst_ref=dkv_far, send_sem=send_sem, recv_sem=recv_sem,
        device_id=near, device_id_type=MESH,
    )
    copy.start()
    d_qkv_ref[:, :q_width] = out_ref[...].T.astype(BF)
    copy.wait()
    down = (dkv_far[...].T)
    dk = rope_down(dk_ref[:rows, :].T + down[:HD], cos_ref[...], -sin_ref[...])
    dkv = jnp.concatenate([dk, dv_ref[:rows, :].T + down[HD:]], axis=0)
    d_qkv_ref[:, q_width:] = dkv.T.astype(BF)
    if crosses:
        pl.when(section != w_layer)(lambda: x_copy().wait_send())
        pl.when(section == w_layer)(lambda: x_copy().wait_recv())


def attend_whole(h, gain, w_attn, low, tables, w_layer, ident):
    cosine, sines, keys_at, places, length = tables
    rows, width = h.shape
    keys, q_width = keys_at.shape[0], low - 2 * HD
    w_list = list(w_attn) if isinstance(w_attn, tuple) else [w_attn]
    outs = [
        ((rows, q_width), BF), ((rows, width), BF), ((rows, 1), F32), ((q_width, rows), BF),
        ((q_width // HD, rows), F32), ((keys, HD), BF), ((HD, keys), BF), ((keys, HD), BF),
    ]
    return pl.pallas_call(
        functools.partial(attend_whole_kernel, w_layer, len(w_list)),
        out_shape=tuple(jax.ShapeDtypeStruct(*o) for o in outs),
        in_specs=[VMEM] * 7 + [ANY] * len(w_list),
        out_specs=(VMEM,) * 8,
        scratch_shapes=[
            pltpu.VMEM((width, low), BF),
            pltpu.VMEM((keys, rows), F32),
            pltpu.VMEM((q_width, rows), F32),
            pltpu.VMEM((q_width, rows), F32),
            pltpu.VMEM((HD, keys), BF),
            pltpu.VMEM((rows, 2 * HD), BF),
            pltpu.VMEM((rows, 2 * HD), BF),
            pltpu.SemaphoreType.DMA((4,)),
            pltpu.SemaphoreType.DMA,
            pltpu.SemaphoreType.DMA,
        ],
        compiler_params=pltpu.CompilerParams(
            collective_id=ident, has_side_effects=True, vmem_limit_bytes=VMEM_LIMIT
        ),
        cost_estimate=pl.CostEstimate(
            flops=16 * q_width * rows * keys, bytes_accessed=70_000_000, transcendentals=0
        ),
        name="attend_whole",
    )(h, gain, cosine, sines, keys_at[:, None], places[None], length, *w_list)


def attend_whole_back(
    e1, rotated, lse, k_all, kt_all, v_all, w_attn, tables, w_layer, ident, cross
):
    cosine, sines, keys_at, places, length = tables
    q_width, rows = rotated.shape
    keys, width = keys_at.shape[0], e1.shape[1]
    w_list = list(w_attn) if isinstance(w_attn, tuple) else [w_attn]
    crossing_specs = [jax.ShapeDtypeStruct(x.shape, BF) for x in cross]
    return pl.pallas_call(
        functools.partial(attend_whole_back_kernel, w_layer, len(w_list), len(cross)),
        out_shape=(jax.ShapeDtypeStruct((rows, q_width + 2 * HD), BF), *crossing_specs),
        in_specs=[VMEM] * 11 + [ANY] * (len(w_list) + len(cross)),
        out_specs=(VMEM, *[ANY] * len(cross)),
        scratch_shapes=[
            pltpu.VMEM((4, q_width, width // 4), BF),
            pltpu.VMEM((keys, rows), F32),
            pltpu.VMEM((q_width, rows), BF),
            pltpu.VMEM((q_width, rows), F32),
            pltpu.VMEM((keys, HD), F32),
            pltpu.VMEM((keys, HD), F32),
            pltpu.VMEM((rows, 2 * HD), F32),
            pltpu.VMEM((rows, 2 * HD), F32),
            pltpu.SemaphoreType.DMA((4,)),
            pltpu.SemaphoreType.DMA,
            pltpu.SemaphoreType.DMA,
        ]
        + [pltpu.SemaphoreType.DMA] * 2 * len(cross),
        compiler_params=pltpu.CompilerParams(
            collective_id=ident, has_side_effects=True, vmem_limit_bytes=VMEM_LIMIT
        ),
        cost_estimate=pl.CostEstimate(
            flops=40 * q_width * rows * keys, bytes_accessed=90_000_000, transcendentals=0
        ),
        name="attend_whole_back",
    )(
        e1, rotated, lse, k_all, kt_all, v_all, cosine, sines, keys_at[:, None], places[None],
        length, *w_list, *cross,
    )


def line_kernel(
    kind, masked, low, high, deps, gathers, layer, exchange, triples, w_layer, crosses, homing,
    gain_ref, resid_ref, valid_ref, h_ref, square_ref, *rest,
):
    forward = kind in ("out", "mlp")
    wide = kind in ("mlp", "mlp_back")
    if kind == "mlp":
        lhs_refs = []
    elif kind == "mlp_back":
        lhs_refs, rest = rest[:4], rest[4:]
    else:
        lhs_refs, rest = rest[:1], rest[1:]
    w_count = 3 if wide else 1
    w_refs = []
    for triple in triples:
        w_refs.append(rest[: 3 if triple else 1])
        rest = rest[3 if triple else 1 :]
    rest = rest[deps:]
    base_refs, rest = rest[: 2 * gathers], rest[2 * gathers :]
    cross_refs, rest = rest[: len(crosses)], rest[len(crosses) :]
    out_ref, rest = rest[0], rest[1:]
    if kind == "mlp":
        normed_ref, ms_ref, gate_ref, up_ref, hidden_ref = rest[:5]
        rest = rest[5:]
    elif kind == "mlp_back":
        product_refs, rest = rest[:3], rest[3:]
        arrived_refs, rest = rest[:exchange], rest[exchange:]
    block_refs, rest = rest[:gathers], rest[gathers:]
    crossed_refs, rest = rest[: len(crosses)], rest[len(crosses) :]
    if homing:
        home_ref, home_send, home_recv = rest[0], *rest[-2:]
        rest = rest[1:-2]
    if crosses:
        x_send, x_recv = rest[-2:]
        rest = rest[:-2]
    w_alls, rest = rest[:w_count], rest[w_count:]
    (
        part, from_end, from_mid, pair,
        w_sem, up_send, up_recv, mid_send, mid_recv, fin_send, fin_recv,
    ) = rest[:11]
    if gathers:
        far_send, far_recv, near_send, near_recv, cross_send, cross_recv = rest[11:]
    if kind == "mlp_back":
        (
            d_gate_ref, d_up_ref, far_normed, far_dm, far_hidden, far_d_gate, far_d_up, stage,
            give_sem, take_sem, stage_sem,
        ) = rest[11:22]
    if exchange:
        y_stage, y_send, y_recv = rest[22:]
    shard = lax.axis_index("gx")
    far, near = shard ^ 2, shard ^ 1
    section = lax.axis_index("section")
    rows, width = resid_ref.shape
    columns = width // 4
    count = rows // CHUNK
    z = lax.axis_index("gy")
    middle = (z == 1) | (z == 2)
    end_of = jnp.where(z == 1, 0, 3)
    mid_of = jnp.where(z == 0, 1, 2)
    across = 3 - z

    def loading(w, j, cut_of, target, slot):
        whole = w_refs[w]
        copies = [(None, pltpu.make_async_copy(cut_of(whole[0].at[j]), target, w_sem.at[slot]))]
        if triples[w]:
            home = section == w_layer
            copies = [(shard != j, copies[0][1])]
            for ref, holds in zip(whole[1:], (home, jnp.logical_not(home))):
                copy = pltpu.make_async_copy(cut_of(ref), target, w_sem.at[slot])
                copies.append(((shard == j) & holds, copy))
        return copies

    loads, downs = [], []
    if wide:
        hidden_width = w_alls[0].shape[1]
        for x0 in range(0, hidden_width, 512):
            x1 = min(x0 + 512, hidden_width)
            for w in range(2):
                for j in range(4):
                    target = w_alls[w].at[j * columns : (j + 1) * columns, x0:x1]
                    loads.append(loading(w, j, lambda ref: ref.at[:, x0:x1], target, len(loads)))
        for j in range(4):
            downs.append(loading(2, j, lambda ref: ref, w_alls[2].at[j], len(loads) + j))
    else:
        for j in range(4):
            cut_of = lambda ref: ref.at[: ref.shape[0] - GAIN_ROWS, low:high]
            loads.append(loading(0, j, cut_of, w_alls[0].at[j], j))
    for load in downs + loads if kind == "mlp_back" else loads + downs:
        for holds, copy in load:
            if holds is None:
                copy.start()
            else:
                pl.when(holds)(copy.start)
    loads, downs = [x[0][1] for x in loads], [x[0][1] for x in downs]

    barrier = pltpu.get_barrier_semaphore()
    peers = []
    if gathers:
        peers = [{"gx": far}, {"gx": near}, {"section": 1 - section}]
    elif kind == "mlp_back":
        peers = [{"gx": near}] + [{"gx": far}] * (exchange > 0)
    if crosses:
        assert not gathers
        peers.append({"section": 1 - section})
    beside = len(peers)
    for peer in peers:
        pl.semaphore_signal(barrier, inc=1, device_id=peer, device_id_type=MESH)

    @pl.when(middle)
    def _():
        pl.semaphore_signal(barrier, inc=1, device_id={"gy": end_of}, device_id_type=MESH)
        pl.semaphore_signal(barrier, inc=1, device_id={"gy": across}, device_id_type=MESH)
        pl.semaphore_wait(barrier, 2 + beside)

    @pl.when(jnp.logical_not(middle))
    def _():
        pl.semaphore_signal(barrier, inc=1, device_id={"gy": mid_of}, device_id_type=MESH)
        pl.semaphore_wait(barrier, 1 + beside)

    x_peer = {"section": 1 - section}

    def x_copy(k):
        return pltpu.make_async_remote_copy(
            src_ref=cross_refs[k], dst_ref=crossed_refs[k], send_sem=x_send.at[k],
            recv_sem=x_recv.at[k], device_id=x_peer, device_id_type=MESH,
        )

    def home_copy(rows_here):
        return pltpu.make_async_remote_copy(
            src_ref=out_ref.at[rows_here, pl.ds(pl.multiple_of(z * columns, columns), columns)],
            dst_ref=home_ref.at[rows_here, :], send_sem=home_send, recv_sem=home_recv,
            device_id=x_peer, device_id_type=MESH,
        )

    def home_start(i):
        if homing:
            here = pl.ds(pl.multiple_of(i * CHUNK, CHUNK), CHUNK)
            pl.when(section != w_layer)(lambda: home_copy(here).start())

    def x_sends(k):
        return section != crosses[k] if crosses[k] < 2 else section >= 0

    def x_takes(k):
        return section == crosses[k] if crosses[k] < 2 else section >= 0

    for k in range(len(crosses)):
        pl.when(x_sends(k))(lambda k=k: x_copy(k).start())

    def half_of(ref, k, which):
        size = base_refs[2 * k].shape[0] // 2
        return ref.at[pl.ds(pl.multiple_of(which * size, 16), size), :]

    def far_copy(k, source):
        return pltpu.make_async_remote_copy(
            src_ref=half_of(source, k, section),
            dst_ref=half_of(block_refs[k].at[shard], k, section),
            send_sem=far_send.at[k], recv_sem=far_recv.at[k],
            device_id={"gx": far}, device_id_type=MESH,
        )

    def near_copy(k, source):
        return pltpu.make_async_remote_copy(
            src_ref=source, dst_ref=block_refs[k].at[shard], send_sem=near_send.at[3 * k],
            recv_sem=near_recv.at[3 * k], device_id={"gx": near}, device_id_type=MESH,
        )

    def cross_copy(k):
        rows_here = half_of(block_refs[k].at[far], k, section)
        return pltpu.make_async_remote_copy(
            src_ref=rows_here, dst_ref=rows_here, send_sem=cross_send.at[k],
            recv_sem=cross_recv.at[k], device_id=x_peer, device_id_type=MESH,
        )

    def pass_copy(k, late):
        rows_here = half_of(block_refs[k].at[far], k, 1 - section if late else section)
        return pltpu.make_async_remote_copy(
            src_ref=rows_here, dst_ref=rows_here, send_sem=near_send.at[3 * k + 1 + late],
            recv_sem=near_recv.at[3 * k + 1 + late], device_id={"gx": near}, device_id_type=MESH,
        )

    at_home = section == layer

    def from_base(k, starts):
        for ref, holds in zip(base_refs[2 * k : 2 * k + 2], (at_home, jnp.logical_not(at_home))):

            @pl.when(holds)
            def _():
                for make in starts:
                    make(k, ref).start()

    def gather_middle(k):
        far_copy(k, base_refs[2 * k]).wait_recv()
        cross_copy(k).start()
        pass_copy(k, 0).start()

    def gather_late(k):
        cross_copy(k).wait_recv()
        pass_copy(k, 1).start()

    if gathers:
        from_base(0, [far_copy])
    for k in range(gathers):
        from_base(k, [near_copy])

    half = rows // STEPS
    core = lax.rem(shard, 2)

    def give(slot, source, target):
        return pltpu.make_async_remote_copy(
            src_ref=source, dst_ref=target, send_sem=give_sem.at[slot],
            recv_sem=take_sem.at[slot], device_id={"gx": near}, device_id_type=MESH,
        )

    def chip_columns(ref, y, of):
        return ref.at[:, pl.ds(pl.multiple_of((2 * y + of) * columns, columns), columns)]

    def step_rows(ref, step):
        return ref.at[pl.ds(pl.multiple_of(step * half, half), half), :]

    if kind == "mlp_back":
        saved_gate, saved_up, saved_normed, saved_hidden = lhs_refs
        early = [give(0, saved_hidden, far_hidden)]
        for y in range(2):
            early.append(give(1 + y, chip_columns(resid_ref, y, 1 - core), far_dm.at[y]))
        for y in range(2):
            early.append(give(3 + y, chip_columns(saved_normed, y, 1 - core), far_normed.at[y]))
        for copy in early:
            copy.start()

    def give_step(step):
        return [
            give(5 + step, step_rows(d_gate_ref, step), step_rows(far_d_gate, step)),
            give(5 + STEPS + step, step_rows(d_up_ref, step), step_rows(far_d_up, step)),
        ]

    if not wide:
        for load in loads:
            load.wait()

    def at_first(step, copies):
        @pl.when(step == 0)
        def _():
            for copy in copies:
                copy.wait()

    def rows_at(ref, i):
        return ref.at[pl.ds(pl.multiple_of(i * CHUNK, CHUNK), CHUNK), :]

    def up_copy(i):
        return pltpu.make_async_remote_copy(
            src_ref=rows_at(part, i), dst_ref=rows_at(from_end, i), send_sem=up_send.at[i],
            recv_sem=up_recv.at[i], device_id={"gy": mid_of}, device_id_type=MESH,
        )

    def mid_copy(i):
        return pltpu.make_async_remote_copy(
            src_ref=rows_at(pair, i), dst_ref=rows_at(from_mid, i), send_sem=mid_send.at[i],
            recv_sem=mid_recv.at[i], device_id={"gy": across}, device_id_type=MESH,
        )

    def fin_copy(i):
        return pltpu.make_async_remote_copy(
            src_ref=rows_at(out_ref, i), dst_ref=rows_at(out_ref, i), send_sem=fin_send.at[i],
            recv_sem=fin_recv.at[i], device_id={"gy": end_of}, device_id_type=MESH,
        )

    def dot(left, right, transposed=False):
        dims = (((1,), (1 if transposed else 0,)), ((), ()))
        return lax.dot_general(left, right, dims, preferred_element_type=F32)

    def spans(extent):
        return [(x, min(x + 512, extent)) for x in range(0, extent, 512)]

    if wide:
        w_gate, w_up, w_down = w_alls

    def product(step, carry):
        here = pl.ds(pl.multiple_of(step * half, half), half)
        if kind == "mlp":
            values = resid_ref[here, :].astype(F32)
            square = jnp.mean(values * values, axis=1, keepdims=True)
            ms_ref[here, :] = square
            normed_ref[here, :] = (values * lax.rsqrt(square + EPS) * gain_ref[...]).astype(BF)
            for n, (x0, x1) in enumerate(spans(w_gate.shape[1])):
                at_first(step, loads[8 * n : 8 * n + 8])
                gate = dot(normed_ref[here, :], w_gate[:, x0:x1])
                up = dot(normed_ref[here, :], w_up[:, x0:x1])
                gate_ref[here, x0:x1] = gate.astype(BF)
                up_ref[here, x0:x1] = up.astype(BF)
                hidden_ref[here, x0:x1] = (gate * jax.nn.sigmoid(gate) * up).astype(BF)
        if kind == "mlp_back":
            at_first(step, downs)
            for x0, x1 in spans(w_gate.shape[1]):
                d_hidden = sum(
                    dot(resid_ref[here, j * columns : (j + 1) * columns], w_down[j, x0:x1, :], True)
                    for j in range(4)
                )
                gate = saved_gate[here, x0:x1].astype(F32)
                up = saved_up[here, x0:x1].astype(F32)
                sigmoid = jax.nn.sigmoid(gate)
                d_up_ref[here, x0:x1] = (d_hidden * (gate * sigmoid)).astype(BF)
                d_gate_ref[here, x0:x1] = (
                    d_hidden * up * sigmoid * (1.0 + gate * (1.0 - sigmoid))
                ).astype(BF)
            for copy in give_step(step):
                copy.start()
        if wide:
            at_first(step, downs if kind == "mlp" else loads)
        for j in range(4):
            span = slice(j * columns, (j + 1) * columns)
            if kind == "out":
                value = dot(lhs_refs[0][here, :], w_alls[0][j])
            elif kind == "mlp":
                value = dot(hidden_ref[here, :], w_down[j])
            elif kind == "mlp_back":
                value = dot(d_gate_ref[here, :], w_gate[span, :], True)
                value += dot(d_up_ref[here, :], w_up[span, :], True)
            else:
                value = dot(lhs_refs[0][here, :], w_alls[0][j], True)
            part[here, span] = value.astype(BF)

        @pl.when(jnp.logical_not(middle))
        def _():
            def send(i, inner):
                up_copy(step * (count // STEPS) + i).start()
                return inner

            lax.fori_loop(0, count // STEPS, send, 0)

        return carry

    lax.fori_loop(0, STEPS, product, 0)

    def finish(i):
        mid_copy(i).wait_recv()
        here = pl.ds(pl.multiple_of(i * CHUNK, CHUNK), CHUNK)
        total = pair[here, :].astype(F32) + from_mid[here, :].astype(F32)
        resid = resid_ref[here, :].astype(F32)
        if forward:
            result = resid + total
            if masked:
                result = result * valid_ref[here, :]
        else:
            values = h_ref[here, :].astype(F32)
            scaled = total * gain_ref[...]
            ratio = lax.rsqrt(square_ref[here, :] + EPS)
            mean_term = jnp.sum(scaled * values, axis=1, keepdims=True) * (1.0 / width)
            result = resid + ratio * scaled - values * (ratio * ratio * ratio) * mean_term
        out_ref[here, :] = result.astype(BF)
        fin_copy(i).start()
        home_start(i)

    tile = columns // 2

    def tile_rows(sub):
        return pl.ds(pl.multiple_of(sub % 2 * tile, tile), tile)

    def stage_copy(number, sub, slot):
        target = product_refs[number].at[sub // 2, tile_rows(sub), :]
        return pltpu.make_async_copy(stage.at[slot], target, stage_sem.at[slot])

    def y_copy(number, sub, slot):
        return pltpu.make_async_remote_copy(
            src_ref=y_stage.at[2 * number + slot], dst_ref=arrived_refs[number].at[tile_rows(sub), :],
            send_sem=y_send.at[2 * number + slot], recv_sem=y_recv.at[2 * number + slot],
            device_id={"gx": far}, device_id_type=MESH,
        )

    def gradient_tile(number, sub):
        slot = sub % 2
        left, far_left, right, far_right = (
            (resid_ref, far_dm, saved_hidden, far_hidden),
            (saved_normed, far_normed, d_gate_ref, far_d_gate),
            (saved_normed, far_normed, d_up_ref, far_d_up),
        )[number]

        @pl.when(sub == 0)
        def _():
            waits = [early[:3], early[3:] + give_all[:STEPS], give_all[STEPS:]][number]
            for copy in waits:
                copy.wait_recv()

        if number >= exchange:

            @pl.when((sub >= 2) | (number > 0))
            def _():
                stage_copy(number, sub, slot).wait()

        elif number > 0:

            @pl.when(sub >= 2)
            def _():
                stage_copy(number, sub - 2, slot).wait()

        y = sub // 2
        if number < exchange:
            y = jnp.where(sub < 2, 1 - lax.div(shard, 2), lax.div(shard, 2))
        start = (y * 2 + core) * columns + sub % 2 * tile
        mine = left[:, pl.ds(pl.multiple_of(start, tile), tile)]
        theirs = far_left[y, :, tile_rows(sub)]
        value = dot_to(mine, right[...], ((0,), (0,))) + dot_to(theirs, far_right[...], ((0,), (0,)))
        if number < exchange:

            @pl.when(sub < 2)
            def _():
                y_stage[2 * number + slot] = value.astype(BF)
                y_copy(number, sub, slot).start()

            @pl.when(sub >= 2)
            def _():
                stage[slot] = value.astype(BF)
                stage_copy(number, sub - 2, slot).start()

        else:
            stage[slot] = value.astype(BF)
            stage_copy(number, sub, slot).start()

    if kind == "mlp_back":
        give_all = [x for pair in zip(*(give_step(n) for n in range(STEPS))) for x in pair]

    def beside_step(i, ahead=0):
        pass_on(i + ahead)
        if kind == "mlp_back":
            for number in range(3):
                first = 3 + 4 * number

                @pl.when((i >= first) & (i < first + 4))
                def _():
                    gradient_tile(number, i - first)

    def pass_on(i):
        if gathers == 2:
            at(2, i, lambda: from_base(1, [far_copy]))
            at(6, i, lambda: gather_middle(0))
            at(10, i, lambda: gather_middle(1))
            at(11, i, lambda: gather_late(0))
            at(15, i, lambda: gather_late(1))

    def at(sixteenth, i, action):
        pl.when(i == count * sixteenth // 16)(action)

    @pl.when(middle)
    def _():
        def step(i, carry):
            up_copy(i).wait_recv()
            here = pl.ds(pl.multiple_of(i * CHUNK, CHUNK), CHUNK)
            pair[here, :] = (part[here, :].astype(F32) + from_end[here, :].astype(F32)).astype(BF)
            mid_copy(i).start()

            @pl.when(i >= 1)
            def _():
                finish(i - 1)

            beside_step(i)
            return carry

        lax.fori_loop(0, count, step, 0)
        finish(count - 1)

        def drain(i, carry):
            mid_copy(i).wait_send()
            fin_copy(i).wait_send()
            return carry

        lax.fori_loop(0, count, drain, 0)

    @pl.when(jnp.logical_not(middle))
    def _():
        if gathers == 2:
            from_base(1, [far_copy])

        def drain(i, carry):
            up_copy(i).wait_send()
            fin_copy(i).wait_recv()
            home_start(i)
            beside_step(i, 3)
            return carry

        lax.fori_loop(0, count, drain, 0)

    if kind == "mlp_back":
        for slot in range(2):
            stage_copy(2, 2 + slot, slot).wait()
        for copy in early + give_all:
            copy.wait_send()
        for number in range(exchange):
            for slot in range(2):
                y_copy(number, slot, slot).wait()
    if homing:
        every = pl.ds(0, rows)
        pl.when(section != w_layer)(lambda: home_copy(every).wait_send())
        pl.when(section == w_layer)(lambda: home_copy(every).wait_recv())
    for k in range(len(crosses)):
        pl.when(x_sends(k))(lambda k=k: x_copy(k).wait_send())
        pl.when(x_takes(k))(lambda k=k: x_copy(k).wait_recv())
    for k in range(gathers):
        far_copy(k, base_refs[2 * k]).wait_send()
        near_copy(k, base_refs[2 * k]).wait()
        cross_copy(k).wait_send()
        pass_copy(k, 0).wait()
        pass_copy(k, 1).wait()


def line_sum(kind, ident, resid, weights, lhs=(), gain=None, valid=None, back=None, low=0, high=0, deps=(), bases=(), layer=0, exchange=0, w_layer=0, crosses=(), homing=False):
    rows, width = resid.shape
    one = jnp.ones((rows, 1), F32)
    h, square = back if back is not None else (jnp.zeros((16, 128), BF), jnp.zeros((8, 1), F32))
    gain = jnp.zeros((1, width), F32) if gain is None else gain
    wide = kind in ("mlp", "mlp_back")
    hidden = 0
    if wide:
        hidden = (weights[2][0] if isinstance(weights[2], tuple) else weights[2]).shape[1]
    w_scratch = []
    triples = [isinstance(w, tuple) for w in weights]
    w_flat = [x for w in weights for x in (w if isinstance(w, tuple) else (w,))]
    for i, w in enumerate(weights):
        _, depth, across = (w[0] if isinstance(w, tuple) else w).shape
        if wide and i < 2:
            w_scratch.append(pltpu.VMEM((width, across), BF))
        else:
            shape = (4, depth, across) if wide else (4, depth - GAIN_ROWS, high - low)
            w_scratch.append(pltpu.VMEM(shape, BF))
    outs, products, beside = [((rows, width), BF)], [], []
    if kind == "mlp":
        outs += [((rows, width), BF), ((rows, 1), F32)] + [((rows, hidden), BF)] * 3
    elif kind == "mlp_back":
        products = [((1 if n < exchange else 2, width // 4, hidden), BF) for n in range(3)]
        products += [((width // 4, hidden), BF)] * exchange
        half_block = pltpu.VMEM((2, rows, width // 4), BF)
        beside = [pltpu.VMEM((rows, hidden), BF)] * 2 + [half_block] * 2
        beside += [pltpu.VMEM((rows, hidden), BF)] * 3 + [pltpu.VMEM((2, width // 8, hidden), BF)]
        beside += [pltpu.SemaphoreType.DMA((n,)) for n in (5 + 2 * STEPS, 5 + 2 * STEPS, 2)]
        if exchange:
            beside += [pltpu.VMEM((2 * exchange, width // 8, hidden), BF)]
            beside += [pltpu.SemaphoreType.DMA((2 * exchange,))] * 2
    blocks = [((4,) + base[0].shape, BF) for base in bases]
    pairs = [x for base in bases for x in base]
    crossed = [(x[0].shape, BF) for x in crosses] + [((rows, width // 4), BF)] * homing
    depth = 3 * hidden if wide else lhs[0].shape[1]
    count = rows // CHUNK
    dma = pltpu.SemaphoreType.DMA
    return pl.pallas_call(
        functools.partial(
            line_kernel, kind, valid is not None, low, high, len(deps), len(bases), layer, exchange,
            triples, w_layer, [x[1] for x in crosses], homing,
        ),
        out_shape=tuple(jax.ShapeDtypeStruct(*o) for o in outs + products + blocks + crossed),
        in_specs=[VMEM] * (5 + len(lhs)) + [ANY] * (len(w_flat) + len(deps) + len(pairs) + len(crosses)),
        out_specs=tuple([VMEM] * len(outs) + [ANY] * len(products + blocks + crossed)),
        scratch_shapes=w_scratch
        + [pltpu.VMEM((rows, width), BF)] * 4
        + [dma((8 * -(-hidden // 512) + 4,))]
        + [dma((count,))] * 6
        + [dma((n * len(bases),)) for n in (1, 1, 3, 3, 1, 1) if bases]
        + beside
        + [dma((len(crosses),))] * 2 * bool(crosses)
        + [dma] * 2 * homing,
        compiler_params=pltpu.CompilerParams(
            collective_id=ident, has_side_effects=True, vmem_limit_bytes=VMEM_LIMIT
        ),
        cost_estimate=pl.CostEstimate(
            flops=2 * rows * depth * width, bytes_accessed=200 * 1024 * 1024, transcendentals=0
        ),
        name="line_" + kind,
    )(
        gain, resid, one if valid is None else valid, h, square, *lhs, *w_flat, *deps, *pairs,
        *(x[0] for x in crosses),
    )


def plain_sum(total):
    return lax.psum(total.astype(BF), "gy").astype(F32)


def normed(h, gain):
    values = h.astype(F32)
    square = jnp.mean(values * values, axis=1, keepdims=True)
    return square, (values * lax.rsqrt(square + EPS) * gain).astype(BF)


def norm_back(d_normed, h, square, gain):
    values = h.astype(F32)
    ratio = lax.rsqrt(square + EPS)
    scaled = d_normed * gain
    mean_term = jnp.mean(scaled * values, axis=1, keepdims=True)
    return ratio * scaled - values * (ratio * ratio * ratio) * mean_term


def attention_forward(h, gain, w_attn, low, tables, ident, bases, layer, w_layer, deps=(), late=None):
    rows, width = h.shape
    high = low + width // lax.axis_size("gx")
    q_width = low - 2 * HD
    if fused():
        heads, n1, square, rotated, lse, k_all, kt_all, v_all = attend_whole(
            h, gain, w_attn, low, tables, w_layer, ident + 8
        )
        if late is not None:
            late = line_gather(late + heads[:1, :1] * 0)
            deps = (*deps, late)
        h1, *stacks = line_sum(
            "out", ident, h, [w_attn], (heads,), low=low, high=high,
            deps=deps, bases=bases, layer=layer, w_layer=w_layer,
        )
        blocks = [(x, *pair) for x, pair in zip(stacks, bases)]
    else:
        cosine, sines = tables[:2]
        square, n1 = normed(h, gain)
        q_down = mm(tall(cut(w_attn, 0, q_width)), n1, ((0,), (1,)))
        kv = mm(n1, tall(cut(w_attn, q_width, low)))
        k_rot = rope_down(kv[:, :HD].T, cosine, sines).T.astype(BF)
        kv = jnp.concatenate([k_rot, kv[:, HD:].astype(BF)], axis=1)
        kv_all = jnp.concatenate([kv, swap_pairs(kv, "gx")], axis=0)
        k_all, v_all = kv_all[:, :HD], kv_all[:, HD:]
        kt_all = k_all.T
        heads, rotated, lse = attend(q_down, k_all, v_all, tables)
        h1 = (h.astype(F32) + plain_sum(mm(heads, side(cut(w_attn, low, high))))).astype(BF)
        blocks = [gather_blocks(chosen(x, layer)) for x in bases]
        late = None if late is None else line_gather(late)
    if late is not None:
        blocks.append(late)
    return h1, square, blocks, (h, square, n1, rotated, lse, k_all, kt_all, v_all, heads)


def mlp_forward(h1, gain, weights, valid, ident, bases=(), layer=0, w_layer=0):
    if fused():
        result, n2, square, gate, up, hidden, *stacks = line_sum(
            "mlp", ident, h1, weights, gain=gain, valid=valid, bases=bases, layer=layer,
            w_layer=w_layer,
        )
        blocks = [(x, *pair) for x, pair in zip(stacks, bases)]
    else:
        square, n2 = normed(h1, gain)
        gate = mm(n2, tall(weights[0]))
        up = mm(n2, tall(weights[1]))
        hidden = (gate * jax.nn.sigmoid(gate) * up).astype(BF)
        gate, up = gate.astype(BF), up.astype(BF)
        result = h1.astype(F32) + plain_sum(mm(hidden, side(weights[2])))
        result = (result * valid).astype(BF)
        blocks = [gather_blocks(chosen(x, layer)) for x in bases]
    return result, square, blocks, (h1, square, n2, gate, up, hidden)


def mlp_backward(dm, gain, weights, saved, ident, w_layer, crosses=(), deps=(), exchange=1):
    h1, square, n2, gate, up, hidden = saved
    if fused():
        e1, *products = line_sum(
            "mlp_back", ident, dm, weights, (gate, up, n2, hidden), gain=gain,
            back=(h1, square), exchange=exchange, w_layer=w_layer, crosses=crosses, deps=deps,
        )
        return e1, products[:4], products[4:]
    gate, up = gate.astype(F32), up.astype(F32)
    d_hidden = mm(dm, side(weights[2]), ((1,), (1,)))
    sigmoid = jax.nn.sigmoid(gate)
    d_gate = (d_hidden * up * sigmoid * (1.0 + gate * (1.0 - sigmoid))).astype(BF)
    d_up = (d_hidden * (gate * sigmoid)).astype(BF)
    total = mm(d_gate, tall(weights[0]), ((1,), (1,))) + mm(d_up, tall(weights[1]), ((1,), (1,)))
    e1 = (dm.astype(F32) + norm_back(plain_sum(total), h1, square, gain)).astype(BF)
    turn = ((0,), (0,))
    products = [mm(dm, hidden, turn), mm(n2, d_gate, turn), mm(n2, d_up, turn)]
    return e1, [p.astype(BF) for p in products], crossing(crosses)


def crossing(crosses):
    pairs = ([(1, 0)], [(0, 1)], [(0, 1), (1, 0)])
    return [lax.ppermute(x, "section", pairs[way]) for x, way in crosses]


def mlp_sums(products):
    if not fused():
        return [shard_sum(p) for p in products]
    down, gate, up, arrived = products
    first = (down[0].astype(F32) + arrived.astype(F32)).astype(BF)
    return [first, chip_sum(gate), chip_sum(up)]


def attention_backward(e1, w_attn, low, tables, saved, w_layer, ident, cross=()):
    h, square, n1, rotated, lse, k_all, kt_all, v_all, heads = saved
    rows, width = h.shape
    if fused():
        d_qkv, *crossed = attend_whole_back(
            e1, rotated, lse, k_all, kt_all, v_all, w_attn, tables, w_layer, ident, cross
        )
    else:
        cosine, sines = tables[:2]
        w_o = side(cut(w_attn, low, low + width // lax.axis_size("gx")))
        d_down = mm(w_o, e1, ((1,), (1,))).astype(BF)
        dq, dk, dv = attend_back(rotated, k_all, v_all, d_down, lse, tables)
        dkv = jnp.concatenate([dk, dv], axis=1)
        dkv = dkv[:rows] + swap_pairs(dkv[rows:], "gx")
        dk = rope_down(dkv[:, :HD].T, cosine, -sines).T
        d_qkv = jnp.concatenate([dq, dk.astype(BF), dkv[:, HD:].astype(BF)], axis=1)
        crossed = crossing([(x, w_layer) for x in cross])
    turn = ((0,), (0,))
    products = [mm(n1, d_qkv, turn).astype(BF), mm(e1, heads, turn).astype(BF)]
    return d_qkv, jnp.concatenate(products, axis=1), crossed


def attention_end(d_qkv, e1, w_attn, gain, saved, ident, w_layer, deps, crosses):
    h, square = saved[:2]
    qkv_width = d_qkv.shape[1]
    if fused():
        grad, *crossed = line_sum(
            "back", ident, e1, [w_attn], (d_qkv,), gain=gain, back=(h, square),
            low=0, high=qkv_width, deps=deps, crosses=crosses, w_layer=w_layer, homing=True,
        )
        return grad, crossed[-1], crossed[:-1]
    total = plain_sum(mm(d_qkv, tall(cut(w_attn, 0, qkv_width)), ((1,), (1,))))
    grad = (e1.astype(F32) + norm_back(total, h, square, gain)).astype(BF)
    width = grad.shape[1] // lax.axis_size("gy")
    part = lax.dynamic_slice_in_dim(grad, lax.axis_index("gy") * width, width, 1)
    home, *crossed = crossing([(part, w_layer), *crosses])
    return grad, home, crossed


def on_device(
    hidden_in, out_grad, lengths, dealing, attn_gain, w_query, w_key, w_value, w_out,
    mlp_gain, w_gate, w_up, w_down,
):
    shards = lax.axis_size("gx")
    shard = lax.axis_index("gx")
    section = lax.axis_index("section")
    column = lax.axis_index("gy")
    core = shard % 2
    sequence = (shard // 2) * 2 + section
    span, width = hidden_in.shape
    half = span // 2
    seq_length = lax.dynamic_index_in_dim(lengths, sequence, keepdims=False)

    both = jnp.concatenate([hidden_in, out_grad], axis=1)
    mine = core_rows(both, core)
    theirs = swap_pairs(core_rows(both, 1 - core), "gx")
    mine = jnp.where(core == section, mine, theirs)
    h = line_gather(mine[:, :width])

    kv_head = column * (w_query.shape[2] // HD) // (QH // KVH)
    low = w_query.shape[2] + 2 * HD
    both_gains = jnp.stack([attn_gain[0], mlp_gain[0]])
    block_rows = both_gains.shape[1]
    attn_own = jnp.concatenate(
        [
            w_query[0],
            lax.dynamic_slice_in_dim(w_key[0], kv_head * HD, HD, 1),
            lax.dynamic_slice_in_dim(w_value[0], kv_head * HD, HD, 1),
            w_out[0],
        ],
        axis=1,
    )
    gain_rows = jnp.pad(both_gains, ((0, GAIN_ROWS - 2), (0, attn_own.shape[1] - block_rows)))
    attn_own = jnp.concatenate([attn_own, gain_rows + theirs[:1, :1] * 0], axis=0)
    own = (attn_own, w_gate[0], w_up[0], w_down[0])
    first = second = [(array, swap_pairs(array, "section")) for array in own]

    def gains_of(w_attn, pair):
        cut_of = lambda w: w[..., block_rows : block_rows + 2, :block_rows]
        rows = cut_of(w_attn[0] if isinstance(w_attn, tuple) else w_attn)
        if isinstance(w_attn, tuple):
            rows = with_own(rows, [cut_of(x) for x in pair], 1)
        return rows.transpose(1, 0, 2).reshape(2, 1, -1).astype(F32)

    here = core_rows(jnp.arange(span), core)
    there = core_rows(jnp.arange(span), 1 - core)
    keys_at = jnp.concatenate([here, there])
    valid = (here < seq_length)[:, None].astype(F32)
    tables = (*rope_tables(here), keys_at, here, seq_length.reshape(1, 1))

    attn0 = gather_blocks(chosen(first[0], 0) + h[:1, :1] * 0)
    gate0 = gather_blocks(chosen(first[1], 0) + h[:1, :1] * 0)
    gains0 = gains_of(attn0, first[0])
    h1, square_a, blocks, saved_a0 = attention_forward(
        h, gains0[0], attn0, low, tables, 0, first[2:], 0, 0, (gate0,), mine[:, width:]
    )
    d_out = blocks.pop()
    mlp0 = [gate0] + blocks
    h, square_m, (attn1, gate1), saved_m0 = mlp_forward(
        h1, gains0[1], mlp0, valid, 1, second[:2], 1
    )
    gains1 = gains_of(attn1, second[0])
    outputs, squares = [h], [square_a, square_m]
    h1, square_a, blocks, saved_a1 = attention_forward(
        h, gains1[0], attn1, low, tables, 2, second[2:], 1, 1
    )
    mlp1 = [gate1] + blocks
    h, square_m, _, saved_m1 = mlp_forward(h1, gains1[1], mlp1, valid, 3, w_layer=1)
    outputs.append(h)
    squares = jnp.concatenate(squares + [square_a, square_m], axis=1)
    rms = (jnp.sqrt(squares + EPS) * valid).T
    statistics = [rms[:2], rms[2:]]
    outputs = [lax.dynamic_slice_in_dim(x, column * width, width, 1) for x in outputs]

    dm = (d_out.astype(F32) * valid).astype(BF)
    e1, products, _ = mlp_backward(dm, gains1[1], mlp1, saved_m1, 4, 1)
    local1 = mlp_sums(products)

    both = []
    for output, stat in zip(outputs, statistics):
        high = stat.astype(BF)
        rest = (stat - high.astype(F32)).astype(BF)
        parts = jnp.concatenate([high, rest], axis=0).reshape(-1, width)
        parts = jnp.pad(parts, ((0, -parts.shape[0] % 16), (0, 0)))
        both.append(jnp.concatenate([output + e1[:1, :1] * 0, parts], axis=0))
    kept = jnp.where(section == 0, both[0], both[1])
    sent = jnp.where(section == 0, both[1], both[0])

    d_qkv, products, _ = attention_backward(e1, attn1, low, tables, saved_a1, 1, 9)
    local1.append(shard_sum(products))
    crosses = [(sent, 2), (local1[0], 1)]
    grad1, home1, (sent, down1) = attention_end(
        d_qkv, e1, attn1, gains1[0], saved_a1, 5, 1, (products,), crosses
    )
    by_section = jnp.stack([jnp.where(section == 0, kept, sent), jnp.where(section == 0, sent, kept)])
    everything = lax.all_gather(by_section, "gx", axis=0)
    owner = jnp.sum(jnp.where(dealing == shard, jnp.arange(shards), 0))
    halves = lax.dynamic_slice(
        everything, ((owner // 2) * 2, owner % 2, 0, 0), (2, 1) + everything.shape[2:]
    )[:, 0]
    layer_out = join_halves(halves[0, :half], halves[1, :half])
    stat_rows = 4 * half // width
    parts = halves[:, half : half + stat_rows].astype(F32).reshape(2, 4, half)
    stat_halves = parts[:, :2] + parts[:, 2:]
    stats_out = join_halves(stat_halves[0].T, stat_halves[1].T).T

    dm = (grad1.astype(F32) * valid).astype(BF)
    crosses = [(local1[1], 1), (local1[2], 1)]
    e1, products, (gate1, up1) = mlp_backward(dm, gains0[1], mlp0, saved_m0, 6, 0, crosses)
    local0 = mlp_sums(products)
    middle = local0[0].shape[0] // 2
    d_qkv, products, (down_low,) = attention_backward(
        e1, attn0, low, tables, saved_a0, 0, 11, [local0[0][:middle]]
    )
    local0.append(shard_sum(products))
    crosses = [(local1[3], 1), (local0[1], 0), (local0[0][middle:], 0)]
    grad0, home0, (attn_sum1, gate0, down_high) = attention_end(
        d_qkv, e1, attn0, gains0[0], saved_a0, 7, 0, (products, everything), crosses
    )

    input_grads = [lax.dynamic_slice_in_dim(x, column * width, width, 1) for x in (grad0, grad1)]
    local0[2] = local0[2] + grad0[:1, :1] * 0
    down0 = jnp.concatenate([down_low, down_high], axis=0)
    received0 = [down0, gate0] + crossing([(x, 0) for x in local0[2:]])
    received1 = [down1, gate1, up1, attn_sum1]
    totals = [
        jnp.where(section == 0, a0.astype(F32) + r0.astype(F32), a1.astype(F32) + r1.astype(F32))
        for a0, r0, a1, r1 in zip(local0, received0, local1, received1)
    ]
    s_down, s_gate, s_up, s_attn = totals
    s_out = s_attn[:, low:]
    q_width = w_query.shape[2]

    attn_sum = jnp.sum(s_attn[:, :low] * attn_own[:block_rows, :low].astype(F32), axis=1)
    mlp_sum = jnp.sum(s_gate * w_gate[0].astype(F32) + s_up * w_up[0].astype(F32), axis=1)
    sums = jnp.stack([attn_sum, mlp_sum]).reshape(-1, 2 * HD)
    sum_rows = sums.shape[0]
    sums = jnp.pad(sums, ((0, -sum_rows % 16), (0, 0)))
    spread = jnp.concatenate([s_attn[:, q_width:low], sums], axis=0).astype(BF)
    spread = lax.all_gather(spread, "gy", axis=0).astype(F32)
    gains = jnp.sum(spread[:, block_rows : block_rows + sum_rows], axis=0).reshape(2, block_rows)
    gains = gains / both_gains.astype(F32)
    kv_sum = spread[:, :block_rows].reshape(KVH, -1, block_rows, 2, HD).sum(axis=1)
    kv_sum = kv_sum.transpose(2, 1, 0, 3).reshape(2, block_rows, KVH * HD)

    kept = jnp.where(section == 0, input_grads[0], input_grads[1])
    sent = jnp.where(section == 0, home0, home1)
    keep = jnp.where(core == section, kept, sent)
    give = swap_pairs(jnp.where(core == section, sent, kept), "gx")
    back_home = join_halves(jnp.where(core == 0, keep, give), jnp.where(core == 0, give, keep))
    return (
        layer_out[None],
        stats_out[None],
        back_home[None],
        gains[None, 0],
        s_attn[None, :, :q_width],
        kv_sum[None, 0],
        kv_sum[None, 1],
        s_out.T[None],
        gains[None, 1],
        s_gate[None],
        s_up[None],
        s_down.T[None],
    )


def solution(mesh):
    rows_cols = P("section", "gx", "gy")
    cols_rows = P("section", "gy", "gx")
    rows_only = P("section", "gx", None)
    gain = P("section", "gx")
    return jax.shard_map(
        on_device,
        mesh=mesh,
        in_specs=(
            P("gx", "gy"), P("gx", "gy"), P(), P(), gain, rows_cols, rows_only, rows_only,
            cols_rows, gain, rows_cols, rows_cols, cols_rows,
        ),
        out_specs=(
            rows_cols, P("section", None, "gx"), rows_cols, gain, rows_cols, rows_only, rows_only,
            cols_rows, gain, rows_cols, rows_cols, cols_rows,
        ),
        check_vma=False,
    )
```
